32 devices in a mesh: batch: 4 (over z), mp: 8 (over y, x, core).
Axes of the slice: x: 2, y: 2, z: 4, core: 2. Of those that a mesh axis runs over, the one named last changes fastest.
Arguments:
- tokens: bfloat16 [8192, 2048], P(('batch', 'mp')), may hold values from -6 to 6
- out_grad: bfloat16 [8192, 2048], P(('batch', 'mp')), may hold values from -6 to 6
- seq_lengths: int32 [8], replicated, may hold values from 1 to 2048, as said below
- seq_scripts: int32 [8], replicated, may hold values from 0 to 2
- seq_place: int32 [8], replicated, may hold values from 0 to 3, as said below
- norm1_gain: float32 [2048], replicated, may hold values from 0.25 to 1.75
- norm1_shift: float32 [2048], replicated, may hold values from -3 to 3
- w_qkv: bfloat16 [3, 2048, 2048], P(None, None, 'mp'), may hold values from -0.1875 to 0.1875
- qv_bias: float32 [2, 2048], P(None, 'mp'), may hold values from -3 to 3
- w_out: bfloat16 [2048, 2048], P('mp'), may hold values from -0.375 to 0.375
- out_bias: float32 [2048], replicated, may hold values from -3 to 3
- norm2_gain: float32 [2048], replicated, may hold values from 0.25 to 1.75
- norm2_shift: float32 [2048], replicated, may hold values from -3 to 3
- w_in: bfloat16 [2048, 8192], P(None, 'mp'), may hold values from -0.125 to 0.125
- in_bias: float32 [8192], P('mp'), may hold values from -3 to 3
- w_down: bfloat16 [8192, 2048], P('mp'), may hold values from -0.0625 to 0.0625
- down_bias: float32 [2048], replicated, may hold values from -3 to 3
Outputs:
- block_out: bfloat16 [8192, 2048], P(('batch', 'mp'))
- input_grad: bfloat16 [8192, 2048], P(('batch', 'mp'))
- norm1_gain_grad: float32 [2048], replicated
- norm1_shift_grad: float32 [2048], replicated
- qkv_weight_grad: float32 [3, 2048, 2048], P(None, 'batch', 'mp')
- qv_bias_grad: float32 [2, 2048], replicated
- out_weight_grad: float32 [2048, 2048], P('mp', 'batch')
- out_bias_grad: float32 [2048], replicated
- norm2_gain_grad: float32 [2048], replicated
- norm2_shift_grad: float32 [2048], replicated
- in_weight_grad: float32 [2048, 8192], P('batch', 'mp')
- in_bias_grad: float32 [8192], replicated
- down_weight_grad: float32 [8192, 2048], P('mp', 'batch')
- down_bias_grad: float32 [2048], replicated
The draws below stay inside these ranges and needn't reach their ends.
Inputs may be any that keep to these rules, and one draw needn't show every extreme that they name: `seq_lengths`: the sequences with one value of seq_place hold 2048 tokens or fewer together; one sequence has exactly 2048 tokens and is the only one of its batch group. `seq_place`: every batch group holds at least one sequence.
All inputs are finite; a program needn't handle non-finite values.
Results may differ from the reference program's by a relative error of at most 0.018.
The reference program's roundings to bfloat16 on the way count: a program that leaves them out, or rounds other values in their place, can miss the bound.
Values may be sent and summed in bfloat16 or wider, within the bound.
A program may use at most 256 MiB of HBM per device.

```python
import jax
import jax.numpy as jnp
from jax import lax

D = 2048
HEADS = 16
HEAD_DIM = 128
FF = 8192
TOK_DEV = 2048
SEQ_GROUP = 2
NSEQ = 8
TOKENS = 8192
N_BATCH = 4


def seq_layout(key):
    groups = NSEQ // SEQ_GROUP
    streams = jax.random.split(jax.random.fold_in(key, 101), 6)
    full = jax.random.randint(streams[0], (), 0, groups)
    first = jax.random.permutation(streams[1], groups)
    extra = jax.random.randint(streams[2], (NSEQ - groups,), 0, groups - 1)
    extra = extra + (extra >= full).astype(jnp.int32)
    place = jnp.concatenate([first.astype(jnp.int32), extra.astype(jnp.int32)])
    place = jax.random.permutation(streams[3], place).astype(jnp.int32)
    loads = jax.random.randint(streams[4], (groups,), TOK_DEV // 4, 5 * TOK_DEV // 8 + 1)
    loads = jnp.where(jnp.arange(groups) == full, TOK_DEV, loads)
    shares = jax.random.randint(streams[5], (NSEQ,), 1, 9)
    member = place[:, None] == jnp.arange(groups)[None, :]
    counts = jnp.sum(member.astype(jnp.int32), axis=0)
    share_sums = jnp.sum(jnp.where(member, shares[:, None], 0), axis=0)
    spare = loads - counts
    lengths = 1 + spare[place] * shares // share_sums[place]
    return (lengths.astype(jnp.int32), place)


def draw_seq_lengths(key, part):
    return seq_layout(key)[0]


def draw_seq_place(key, part):
    return seq_layout(key)[1]


def plant(entries, rng, least, high):
    longest = entries.shape.index(max(entries.shape))
    spots = []
    for shift in (0, 1):
        where = [jax.random.randint(jax.random.fold_in(rng, axis), (), 0, length) for axis, length in enumerate(entries.shape)]
        where[longest] = (where[longest] + shift) % entries.shape[longest]
        spots.append(tuple(where))
    return entries.at[spots[0]].set(least).at[spots[1]].set(high)


def shard_levels(key, extent, cuts, low, high):
    factor_of = 1.0
    for axis_at, blocks in cuts:
        steps = jax.random.uniform(jax.random.fold_in(jax.random.fold_in(key, 6), axis_at), (blocks,), jnp.float32, low / len(cuts), high / len(cuts))
        factor_of = factor_of * jnp.repeat(jnp.exp(steps), extent[axis_at] // blocks).reshape((-1,) + (1,) * (len(extent) - 1 - axis_at))
    return factor_of


def normal_values(own_key, shape, width, reach, cuts=(), kind=jnp.bfloat16):
    loudness = shard_levels(own_key, shape, cuts, -0.22, 0.18) if cuts else 1.0
    entries = jax.random.normal(own_key, shape, jnp.float32) * width * loudness
    return jnp.minimum(jnp.maximum(entries, -reach), reach).astype(kind)


def setup_inputs(seed: int = 0) -> dict:
    key_of = jax.random.split(jax.random.key(seed), 18)
    tokens = normal_values(key_of[0], (TOKENS, D), 1.0, 6.0, ((0, 32),))
    out_grad = normal_values(key_of[1], (TOKENS, D), 1.0, 6.0, ((0, 32),))
    seq_lengths = draw_seq_lengths(jax.random.fold_in(key_of[17], 71), 0)
    seq_scripts = plant(jax.random.randint(key_of[3], (NSEQ,), 0, 3), jax.random.fold_in(key_of[3], 1), 0, 2).astype(jnp.int32)
    seq_place = draw_seq_place(jax.random.fold_in(key_of[17], 71), 0)
    norm1_gain = jnp.clip(1.0 + 0.15 * jax.random.normal(key_of[5], (D,), jnp.float32), 0.25, 1.75)
    norm1_shift = normal_values(key_of[6], (D,), 0.5, 3.0, (), jnp.float32)
    w_qkv = normal_values(key_of[7], (3, D, D), (D // 2) ** -0.5, 0.1875, ((2, 8),))
    qv_bias = normal_values(key_of[8], (2, D), 0.5, 3.0, ((1, 8),), jnp.float32)
    w_out = normal_values(key_of[9], (D, D), (D // 8) ** -0.5, 0.375, ((0, 8),))
    out_bias = normal_values(key_of[10], (D,), 0.5, 3.0, (), jnp.float32)
    norm2_gain = jnp.clip(1.0 + 0.15 * jax.random.normal(key_of[11], (D,), jnp.float32), 0.25, 1.75)
    norm2_shift = normal_values(key_of[12], (D,), 0.5, 3.0, (), jnp.float32)
    w_in = normal_values(key_of[13], (D, FF), D ** -0.5, 0.125, ((1, 8),))
    in_bias = normal_values(key_of[14], (FF,), 0.5, 3.0, ((0, 8),), jnp.float32)
    w_down = normal_values(key_of[15], (FF, D), FF ** -0.5, 0.0625, ((0, 8),))
    down_bias = normal_values(key_of[16], (D,), 0.5, 3.0, (), jnp.float32)
    return dict(tokens=tokens, out_grad=out_grad, seq_lengths=seq_lengths, seq_scripts=seq_scripts, seq_place=seq_place, norm1_gain=norm1_gain, norm1_shift=norm1_shift, w_qkv=w_qkv, qv_bias=qv_bias, w_out=w_out, out_bias=out_bias, norm2_gain=norm2_gain, norm2_shift=norm2_shift, w_in=w_in, in_bias=in_bias, w_down=w_down, down_bias=down_bias)


EPS = 1e-05
MASKED = -1000000000.0
HIGHEST = lax.Precision.HIGHEST

@jax.custom_vjp
def low(v):
    return lax.optimization_barrier(v.astype(jnp.bfloat16)).astype(jnp.float32)

@jax.custom_vjp
def low_back(v):
    return v

def low_keep(v):
    return (low(v), None)

def low_pass(kept, grad):
    return (grad,)

def back_keep(v):
    return (v, None)

def back_low(kept, grad):
    return (low(grad),)
low.defvjp(low_keep, low_pass)
low_back.defvjp(back_keep, back_low)

def segments_of(group, seq_lengths, seq_scripts, seq_place, rows):
    count = seq_lengths.shape[0]
    numbers = jnp.arange(count, dtype=jnp.int32)
    order_key = seq_scripts * count + numbers
    same = seq_place[:, None] == seq_place[None, :]
    before = order_key[None, :] < order_key[:, None]
    offsets = lax.optimization_barrier(jnp.sum(jnp.where(same & before, seq_lengths[None, :], 0), axis=1)).astype(jnp.int32)
    position = jnp.arange(rows, dtype=jnp.int32)[:, None]
    member = (seq_place[None, :] == group) & (position >= offsets[None, :]) & (position < (offsets + seq_lengths)[None, :])
    labels = lax.optimization_barrier(jnp.sum(jnp.where(member, numbers[None, :], 0), axis=1))
    return (labels + jnp.where(jnp.any(member, axis=1), 0, count)).astype(jnp.int32)

def visible(segment, first, block):
    rows = segment.shape[0]
    query_rows = first + jnp.arange(block, dtype=jnp.int32)
    query_labels = lax.dynamic_slice_in_dim(segment, first, block, 0)
    key_rows = jnp.arange(rows, dtype=jnp.int32)
    return (query_labels[:, None] == segment[None, :]) & (key_rows[None, :] <= query_rows[:, None])

def layer_norm(rows, gain, shift):
    mean = lax.optimization_barrier(jnp.mean(rows, axis=-1, keepdims=True))
    centred = rows - mean
    inverse = lax.rsqrt(lax.optimization_barrier(jnp.mean(centred * centred, axis=-1, keepdims=True)) + EPS)
    return centred * inverse * gain + shift

def attention(queries, keys, values, segment):
    heads, rows, size = keys.shape
    block = min(512, rows)
    scale = HEAD_DIM ** (-0.5)

    def one_block(index):
        first = index * block
        query_block = lax.dynamic_slice_in_dim(queries, first, block, 1)
        raw = jnp.einsum('hqd,hkd->hqk', query_block, keys, precision=HIGHEST)
        scores = low_back(raw * scale)
        scores = jnp.where(visible(segment, first, block)[None], scores, MASKED)
        top = lax.optimization_barrier(jnp.max(scores, axis=-1, keepdims=True))
        exps = jnp.exp(scores - top)
        weights = low(exps / lax.optimization_barrier(jnp.sum(exps, axis=-1, keepdims=True)))
        return jnp.einsum('hqk,hkd->hqd', weights, values, precision=HIGHEST)
    blocks = lax.map(jax.checkpoint(one_block), jnp.arange(rows // block, dtype=jnp.int32))
    return jnp.transpose(blocks, (1, 0, 2, 3)).reshape(heads, rows, size)

def forward(inputs, params, segment):
    gain1, shift1, w_qkv, qv_bias, w_out, out_bias, gain2, shift2, w_in, in_bias, w_down, down_bias = params
    rows = inputs.shape[0]

    def split_heads(matrix):
        return jnp.transpose(matrix.reshape(rows, HEADS, HEAD_DIM), (1, 0, 2))
    first = low(layer_norm(inputs, gain1, shift1))
    projected = jnp.einsum('td,cde->cte', first, w_qkv, precision=HIGHEST)
    queries = low(low_back(projected[0] + qv_bias[0]))
    keys = low(low_back(projected[1]))
    values = low(low_back(projected[2] + qv_bias[1]))
    mixed = attention(split_heads(queries), split_heads(keys), split_heads(values), segment)
    attended = low(low_back(jnp.transpose(mixed, (1, 0, 2)).reshape(rows, HEADS * HEAD_DIM)))
    middle = inputs + low_back(jnp.dot(attended, w_out, precision=HIGHEST)) + out_bias
    second = low(layer_norm(middle, gain2, shift2))
    hidden = low_back(jnp.dot(second, w_in, precision=HIGHEST) + in_bias)
    activated = low(jax.nn.gelu(hidden, approximate=True))
    return middle + low_back(jnp.dot(activated, w_down, precision=HIGHEST)) + down_bias

def reference(tokens, out_grad, seq_lengths, seq_scripts, seq_place, norm1_gain, norm1_shift, w_qkv, qv_bias, w_out, out_bias, norm2_gain, norm2_shift, w_in, in_bias, w_down, down_bias):
    params = tuple((array.astype(jnp.float32) for array in (norm1_gain, norm1_shift, w_qkv, qv_bias, w_out, out_bias, norm2_gain, norm2_shift, w_in, in_bias, w_down, down_bias)))
    inputs = tokens.astype(jnp.float32).reshape(N_BATCH, TOK_DEV, D)
    cotangent = out_grad.astype(jnp.float32).reshape(N_BATCH, TOK_DEV, D)

    def group_step(totals, item):
        group, rows, incoming = item
        segment = segments_of(group, seq_lengths, seq_scripts, seq_place, TOK_DEV)
        result, pull = jax.vjp(lambda values, weights: forward(values, weights, segment), rows, params)
        row_grad, param_grads = pull(incoming)
        totals = jax.tree.map(lambda left, right: left + right, totals, param_grads)
        return (totals, (result.astype(jnp.bfloat16), row_grad.astype(jnp.bfloat16)))
    zeros = jax.tree.map(jnp.zeros_like, params)
    totals, (results, row_grads) = lax.scan(group_step, zeros, (jnp.arange(N_BATCH, dtype=jnp.int32), inputs, cotangent))
    gain1_grad, shift1_grad, qkv_grad, qv_grad, out_w_grad, out_b_grad, gain2_grad, shift2_grad, in_w_grad, in_b_grad, down_w_grad, down_b_grad = totals
    return (results.reshape(TOKENS, D), row_grads.reshape(TOKENS, D), gain1_grad, shift1_grad, qkv_grad, qv_grad, out_w_grad, out_b_grad, gain2_grad, shift2_grad, in_w_grad, in_b_grad, down_w_grad, down_b_grad)
```

```python
import functools

import jax
import jax.numpy as jnp
from jax import lax
from jax.experimental import pallas as pl
from jax.experimental.pallas import tpu as pltpu
from jax.sharding import PartitionSpec as P

HEAD_DIM = 128
EPS = 1e-05
NEGATIVE = -1e30
LOG2E = 1.4426950408889634
f32 = jnp.float32
bf16 = jnp.bfloat16
MESH = pl.DeviceIdType.MESH
ANY = pl.BlockSpec(memory_space=pl.ANY)
VMEM = pl.BlockSpec(memory_space=pltpu.VMEM)
SMEM = pl.BlockSpec(memory_space=pltpu.SMEM)


def dot(left, right, contract_left, contract_right):
    return lax.dot_general(
        left,
        right,
        (((contract_left,), (contract_right,)), ((), ())),
        preferred_element_type=f32,
    )


def flip(index, mask):
    bit = 1
    while bit <= mask:
        if mask & bit:
            index = index + bit * (1 - 2 * lax.rem(lax.div(index, bit), 2))
        bit *= 2
    return index


def loop(count, step, body):
    def one(index, carry):
        body(pl.multiple_of(index * step, step))
        return carry

    lax.fori_loop(0, count // step, one, 0)


class Plan:
    def __init__(self, devices):
        bits = []
        bit = 2
        while bit < devices:
            bits.append(bit)
            bit *= 2
        self.devices = devices
        self.bits = bits
        self.orders = [tuple(bits)] + ([tuple(reversed(bits))] if len(bits) > 1 else [])
        self.parts = len(self.orders)
        self.offsets = list(range(0, devices, 2))
        self.keys = [(part, offset) for part in range(self.parts) for offset in self.offsets if offset]
        self.keys.sort(key=lambda key: (bin(key[1]).count("1"), self.last(*key)))
        self.shares = [(part, offset) for offset in self.offsets for part in range(self.parts)]

    def last(self, part, offset):
        steps = [step for step, bit in enumerate(self.orders[part]) if bit & offset]
        return max(steps) if steps else -1

    def bit(self, part, offset):
        return self.orders[part][self.last(part, offset)]

    def later(self, part, offset):
        order = self.orders[part]
        return [offset | order[step] for step in range(self.last(part, offset) + 1, len(order))]


class Place:
    def __init__(self, plan):
        self.plan = plan
        self.batch = lax.axis_index("batch")
        self.me = lax.axis_index("mp")

    def at(self, mask):
        return (self.batch, flip(self.me, mask))

    def barrier(self):
        semaphore = pltpu.get_barrier_semaphore()
        masks = [1] + self.plan.bits
        for mask in masks:
            pl.semaphore_signal(semaphore, inc=1, device_id=self.at(mask), device_id_type=MESH)
        pl.semaphore_wait(semaphore, len(masks))


class Gather:
    def __init__(self, place, buf, own, rows, sems):
        self.place, self.plan, self.buf, self.own, self.rows = place, place.plan, buf, own, rows
        self.link_send, self.link_recv, self.core_send, self.core_recv = sems
        self.part_rows = rows // self.plan.parts

    def span(self, mask, part):
        block = flip(self.place.me, mask)
        start = block * self.rows + part * self.part_rows
        return self.buf.at[pl.ds(pl.multiple_of(start, self.part_rows), self.part_rows), :]

    def source(self, offset, part):
        if offset == 0 and self.own is not None:
            return self.own.at[pl.ds(part * self.part_rows, self.part_rows), :]
        return self.span(offset, part)

    def link(self, key):
        part, offset = key
        bit = self.plan.bit(part, offset)
        index = self.plan.keys.index(key)
        return pltpu.make_async_remote_copy(
            src_ref=self.source(offset ^ bit, part),
            dst_ref=self.span(offset ^ bit, part),
            send_sem=self.link_send.at[index],
            recv_sem=self.link_recv.at[index],
            device_id=self.place.at(bit),
            device_id_type=MESH,
        )

    def core(self, key):
        part, offset = key
        index = self.plan.shares.index(key)
        return pltpu.make_async_remote_copy(
            src_ref=self.source(offset, part),
            dst_ref=self.span(offset, part),
            send_sem=self.core_send.at[index],
            recv_sem=self.core_recv.at[index],
            device_id=self.place.at(1),
            device_id_type=MESH,
        )

    def landed(self, ref, semaphore):
        pltpu.make_async_remote_copy(
            src_ref=ref,
            dst_ref=ref,
            send_sem=semaphore,
            recv_sem=semaphore,
            device_id=self.place.at(1),
            device_id_type=MESH,
        ).wait_recv()

    def start(self):
        for part in range(self.plan.parts):
            self.core((part, 0)).start()
        for key in self.plan.keys:
            if bin(key[1]).count("1") == 1:
                self.link(key).start()

    def arrive(self, key):
        part, offset = key
        self.landed(self.span(offset, part), self.link_recv.at[self.plan.keys.index(key)])
        for target in self.plan.later(part, offset):
            self.link((part, target)).start()
        self.core(key).start()

    def share(self, offset):
        for part in range(self.plan.parts):
            index = self.plan.shares.index((part, offset))
            self.landed(self.span(offset | 1, part), self.core_recv.at[index])

    def steps(self):
        singles = [offset for offset in self.plan.offsets if bin(offset).count("1") == 1]
        rest = [offset for offset in self.plan.offsets if bin(offset).count("1") > 1]
        rest.sort(key=lambda offset: bin(offset).count("1"))
        groups = [[key for key in self.plan.keys if key[1] in singles]]
        groups += [[key for key in self.plan.keys if key[1] == offset] for offset in rest]
        return groups, [singles] + [[offset] for offset in rest]

    def finish(self):
        for key in self.plan.keys:
            self.link(key).wait_send()
        for key in self.plan.shares:
            self.core(key).wait_send()

    @staticmethod
    def semaphores(plan):
        return [pltpu.SemaphoreType.DMA((len(plan.keys),))] * 2 + [
            pltpu.SemaphoreType.DMA((len(plan.shares),))
        ] * 2


class Scatter:
    def __init__(self, place, rows, width, core_out, core_in, kept, link_out, link_in, sems):
        self.place, self.plan, self.rows, self.width = place, place.plan, rows, width
        self.core_out, self.core_in, self.kept = core_out, core_in, kept
        self.link_out, self.link_in = link_out, link_in
        self.link_send, self.link_recv, self.core_send, self.core_recv = sems
        self.part_rows = rows // self.plan.parts
        self.step = min(32, self.part_rows)
        self.order = sorted(self.plan.offsets, key=lambda offset: -bin(offset).count("1"))

    def core(self, offset):
        index = offset // 2
        return pltpu.make_async_remote_copy(
            src_ref=self.core_out.at[index],
            dst_ref=self.core_in.at[index],
            send_sem=self.core_send.at[index],
            recv_sem=self.core_recv.at[index],
            device_id=self.place.at(1),
            device_id_type=MESH,
        )

    def link(self, key):
        index = self.plan.keys.index(key)
        return pltpu.make_async_remote_copy(
            src_ref=self.link_out.at[index],
            dst_ref=self.link_in.at[index],
            send_sem=self.link_send.at[index],
            recv_sem=self.link_recv.at[index],
            device_id=self.place.at(self.plan.bit(*key)),
            device_id_type=MESH,
        )

    def total(self, offset, part, start, arrived):
        rows = pl.ds(pl.multiple_of(part * self.part_rows + start, self.step), self.step)
        value = self.kept[offset // 2, rows, :].astype(f32) + self.core_in[offset // 2, rows, :].astype(f32)
        for key in arrived:
            value += self.link_in[self.plan.keys.index(key), pl.ds(start, self.step), :].astype(f32)
        return value

    def pass_on(self, part, offset):
        arrived = [(part, target) for target in self.plan.later(part, offset)]
        for key in arrived:
            self.link(key).wait_recv()
        index = self.plan.keys.index((part, offset))

        def add(start):
            self.link_out[index, pl.ds(start, self.step), :] = self.total(
                offset, part, start, arrived
            ).astype(bf16)

        loop(self.part_rows, self.step, add)
        self.link((part, offset)).start()

    def begin(self, partial):
        for offset in self.order:
            index = offset // 2
            partial(flip(self.place.me, offset | 1), self.core_out.at[index])
            self.core(offset).start()
            partial(flip(self.place.me, offset), self.kept.at[index])
            self.core(offset).wait_recv()
            for part in range(self.plan.parts):
                if offset and not self.plan.later(part, offset):
                    self.pass_on(part, offset)

    def middle(self):
        for offset in self.order:
            for part in range(self.plan.parts):
                if offset and self.plan.later(part, offset):
                    self.pass_on(part, offset)

    def end(self, use):
        for part in range(self.plan.parts):
            arrived = [(part, target) for target in self.plan.later(part, 0)]
            for key in arrived:
                self.link(key).wait_recv()

            def piece(start):
                row = pl.multiple_of(part * self.part_rows + start, self.step)
                use(row, self.step, self.total(0, part, start, arrived))

            loop(self.part_rows, self.step, piece)

    def finish(self):
        for key in self.plan.keys:
            self.link(key).wait_send()
        for offset in self.plan.offsets:
            self.core(offset).wait_send()

    @staticmethod
    def scratch(plan, rows, width, kept):
        chips, keys = len(plan.offsets), len(plan.keys)
        return [
            pltpu.VMEM((chips, rows, width), bf16),
            pltpu.VMEM((chips, rows, width), bf16),
            pltpu.VMEM((chips, rows, width), kept),
            pltpu.VMEM((keys, rows // plan.parts, width), bf16),
            pltpu.VMEM((keys, rows // plan.parts, width), bf16),
            pltpu.SemaphoreType.DMA((keys,)),
            pltpu.SemaphoreType.DMA((keys,)),
            pltpu.SemaphoreType.DMA((chips,)),
            pltpu.SemaphoreType.DMA((chips,)),
        ]


class Moves:
    def __init__(self, sems):
        self.sems, self.count = sems, 0

    def start(self, source, target):
        copy = pltpu.make_async_copy(source, target, self.sems.at[self.count])
        self.count += 1
        copy.start()
        return copy


def norm_rows(rows):
    mean = jnp.mean(rows, axis=-1, keepdims=True)
    centred = rows - mean
    inverse = lax.rsqrt(jnp.mean(centred * centred, axis=-1, keepdims=True) + EPS)
    return centred * inverse, inverse


def norm_back(grad, unit, inverse, gain):
    scaled = grad * gain
    return inverse * (
        scaled
        - jnp.mean(scaled, axis=-1, keepdims=True)
        - unit * jnp.mean(scaled * unit, axis=-1, keepdims=True)
    )


def segment_starts(bounds, rows):
    position = lax.broadcasted_iota(jnp.int32, (1, rows), 1)
    first = jnp.zeros((1, rows), jnp.int32)
    for index in range(bounds.shape[0]):
        first = jnp.maximum(first, jnp.where(position >= bounds[index], bounds[index], 0))
    return first


def head_columns(part, head, width):
    return pl.ds(part * width + head * HEAD_DIM, HEAD_DIM)


def first_kernel(
    plan, block, tok, gain, shift, w_qkv, qv_bias, bounds, out_grad, first_out, qkv_out, att_out,
    sum_out, grad_out, buf, weights, qkv, starts, sums, attended, local, *sems,
):
    place = Place(plan)
    own, depth = tok.shape
    rows = buf.shape[0]
    width = w_qkv.shape[2]
    moves = Moves(local)
    loads = [
        moves.start(w_qkv.at[part], weights.at[:, pl.ds(part * width, width)]) for part in range(3)
    ]
    place.barrier()
    step = min(32, own)
    mine = pl.multiple_of(place.me * own, own)

    def normalise(start):
        unit, _ = norm_rows(tok[pl.ds(start, step), :].astype(f32))
        buf[pl.ds(pl.multiple_of(mine + start, step), step), :] = (unit * gain[...] + shift[...]).astype(bf16)

    loop(own, step, normalise)
    gather = Gather(place, buf, None, own, sems[:4])
    gather.start()
    stores = [moves.start(out_grad, grad_out.at[pl.ds(mine, own), :])]
    starts[...] = segment_starts(bounds, rows)
    for copy in loads:
        copy.wait()

    def project(offset):
        chip = lax.div(flip(place.me, offset), 2)
        span = pl.ds(pl.multiple_of(chip * 2 * own, 2 * own), 2 * own)
        stores.append(moves.start(buf.at[span, :], first_out.at[span, :]))
        qkv[span, :] = (dot(buf[span, :], weights[...], 1, 0) + qv_bias[...]).astype(bf16)

    gather.share(0)
    project(0)
    arrivals, chips = gather.steps()
    for keys, offsets in zip(arrivals, chips):
        for key in keys:
            gather.arrive(key)
        for offset in offsets:
            gather.share(offset)
            project(offset)
    gather.finish()
    gather = Gather(place, grad_out, out_grad, own, sems[4:])
    gather.start()
    stores.append(moves.start(qkv, qkv_out))

    scale = HEAD_DIM ** (-0.5) * LOG2E
    heads = width // HEAD_DIM
    row_in = lax.broadcasted_iota(jnp.int32, (block, block), 0)
    col_in = lax.broadcasted_iota(jnp.int32, (block, block), 1)
    key_in = lax.broadcasted_iota(jnp.int32, (block, 1), 0)

    def attend(index):
        span = pl.ds(index * block, block)
        first = starts[:, span]
        queries = [qkv[span, head_columns(0, head, width)] for head in range(heads)]

        def against(key_block, carry, diagonal):
            key_span = pl.ds(pl.multiple_of(key_block * block, block), block)
            allowed = key_in + key_block * block >= first
            if diagonal:
                allowed = allowed & (row_in <= col_in)
            result = []
            for head in range(heads):
                top, total, mixed = carry[head]
                keys = qkv[key_span, head_columns(1, head, width)]
                values = qkv[key_span, head_columns(2, head, width)]
                scores = jnp.where(allowed, dot(keys, queries[head], 1, 1) * scale, NEGATIVE)
                new_top = jnp.maximum(top, jnp.max(scores, axis=0, keepdims=True))
                exps = jnp.exp2(scores - new_top)
                fade = jnp.exp2(top - new_top)
                total = total * fade + jnp.sum(exps, axis=0, keepdims=True)
                mixed = mixed * fade + dot(values, exps.astype(bf16), 0, 0)
                result.append((new_top, total, mixed))
            return tuple(result)

        carry = tuple(
            (
                jnp.full((1, block), NEGATIVE, f32),
                jnp.zeros((1, block), f32),
                jnp.zeros((HEAD_DIM, block), f32),
            )
            for head in range(heads)
        )
        if index:
            carry = lax.fori_loop(0, index, lambda key_block, c: against(key_block, c, False), carry)
        carry = against(index, carry, True)
        for head in range(heads):
            top, total, mixed = carry[head]
            attended[span, pl.ds(head * HEAD_DIM, HEAD_DIM)] = (mixed * (1.0 / total)).T.astype(bf16)
            sums[pl.ds(head, 1), span] = top + jnp.log2(total)

    blocks = rows // block
    groups = list(zip(arrivals, chips))
    taken = 0
    for index in range(blocks):
        attend(index)
        if index >= blocks - 2 and taken < len(groups):
            for key in groups[taken][0]:
                gather.arrive(key)
            taken += 1
    stores.append(moves.start(attended, att_out))
    stores.append(moves.start(sums, sum_out))
    while taken < len(groups):
        for key in groups[taken][0]:
            gather.arrive(key)
        taken += 1
    for offset in plan.offsets:
        gather.share(offset)
    gather.finish()
    for copy in stores:
        copy.wait()


def params(number):
    return pltpu.CompilerParams(
        collective_id=number, has_side_effects=True, vmem_limit_bytes=62 * 2**20
    )


def run_first(plan, block, tok, gain, shift, w_qkv, qv_bias, bounds, out_grad):
    own, depth = tok.shape
    rows = own * plan.devices
    width = w_qkv.shape[2]
    heads = width // HEAD_DIM
    return pl.pallas_call(
        functools.partial(first_kernel, plan, block),
        out_shape=(
            jax.ShapeDtypeStruct((rows, depth), bf16),
            jax.ShapeDtypeStruct((rows, 3 * width), bf16),
            jax.ShapeDtypeStruct((rows, width), bf16),
            jax.ShapeDtypeStruct((8, rows), f32),
            jax.ShapeDtypeStruct((rows, depth), bf16),
        ),
        in_specs=[VMEM, VMEM, VMEM, ANY, VMEM, SMEM, ANY],
        out_specs=(ANY,) * 5,
        scratch_shapes=[
            pltpu.VMEM((rows, depth), bf16),
            pltpu.VMEM((depth, 3 * width), bf16),
            pltpu.VMEM((rows, 3 * width), bf16),
            pltpu.VMEM((1, rows), jnp.int32),
            pltpu.VMEM((8, rows), f32),
            pltpu.VMEM((rows, width), bf16),
            pltpu.SemaphoreType.DMA((16,)),
        ]
        + Gather.semaphores(plan) * 2,
        compiler_params=params(0),
        name="first",
    )(tok, gain, shift, w_qkv, qv_bias, bounds, out_grad)


def feed_kernel(
    plan, tok, att, w_out, out_bias, gain, shift, w_in, in_bias, w_down, grad_all,
    second_out, act_out, hidden_out, middle_out, bias_out,
    att_in, w_o, w_i, w_d, grad_in, buf, act, back, middle, local, *rest,
):
    scatter_refs, gather_sems = rest[:9], rest[9:]
    place = Place(plan)
    own, depth = tok.shape
    rows = buf.shape[0]
    hidden_width = w_in.shape[1]
    chip_rows = 2 * own
    moves = Moves(local)
    load_att = moves.start(att, att_in)
    load_out = moves.start(w_out, w_o)
    load_in = moves.start(w_in, w_i)
    load_down = moves.start(w_down, w_d)
    place.barrier()
    scatter = Scatter(place, own, depth, *scatter_refs[:5], scatter_refs[5:])
    load_att.wait()
    load_out.wait()
    tile = min(1024, depth)

    def partial(owner, target):
        lines = att_in[pl.ds(pl.multiple_of(owner * own, own), own), :]

        def columns(start):
            target[:, pl.ds(start, tile)] = dot(lines, w_o[:, pl.ds(start, tile)], 1, 0).astype(target.dtype)

        loop(depth, tile, columns)

    scatter.begin(partial)
    scatter.middle()
    mine = pl.multiple_of(place.me * own, own)

    def close(start, count, value):
        span = pl.ds(start, count)
        total = tok[span, :].astype(f32) + value + out_bias[...]
        middle[span, :] = total
        unit, _ = norm_rows(total)
        buf[pl.ds(pl.multiple_of(mine + start, count), count), :] = (unit * gain[...] + shift[...]).astype(bf16)

    scatter.end(close)
    gather = Gather(place, buf, None, own, gather_sems)
    gather.start()
    scatter.finish()
    stores = [moves.start(middle, middle_out)]
    load_in.wait()
    load_down.wait()
    bias_out[...] = jnp.zeros_like(bias_out)
    part_cols = min(512, hidden_width)

    def chip_span(offset):
        chip = lax.div(flip(place.me, offset), 2)
        return pl.ds(pl.multiple_of(chip * chip_rows, chip_rows), chip_rows)

    order = []

    def prefetch(offset):
        slot = len(order) % 2
        order.append(moves.start(grad_all.at[chip_span(offset), :], grad_in.at[slot]))

    def expand(offset, slot):
        span = chip_span(offset)
        stores.append(moves.start(buf.at[span, :], second_out.at[span, :]))
        order[slot].wait()

        def columns(start):
            cols = pl.ds(start, part_cols)
            pre = dot(buf[span, :], w_i[:, cols], 1, 0) + in_bias[:, cols]
            up = dot(grad_in[slot % 2], w_d[cols, :], 1, 1)
            root = 0.7978845608028654
            square = pre * pre
            inner = jnp.tanh(root * (pre + 0.044715 * (square * pre)))
            half = 0.5 * (1.0 + inner)
            slope = half + 0.5 * pre * (1.0 - inner * inner) * (root * (1.0 + 3 * 0.044715 * square))
            act[span, cols] = (pre * half).astype(bf16)
            down = (up * slope).astype(bf16)
            back[span, cols] = down
            bias_out[:, cols] += jnp.sum(down.astype(f32), axis=0, keepdims=True)

        loop(hidden_width, part_cols, columns)
        stores.append(moves.start(act.at[span, :], act_out.at[span, :]))
        stores.append(moves.start(back.at[span, :], hidden_out.at[span, :]))

    arrivals, chips = gather.steps()
    sequence = [0] + [offset for offsets in chips for offset in offsets]
    prefetch(sequence[0])
    prefetch(sequence[1])
    gather.share(0)
    expand(0, 0)
    number = 1
    for keys, offsets in zip(arrivals, chips):
        for key in keys:
            gather.arrive(key)
        for offset in offsets:
            if number + 1 < len(sequence):
                prefetch(sequence[number + 1])
            gather.share(offset)
            expand(offset, number)
            number += 1
    gather.finish()
    for copy in stores:
        copy.wait()


def run_feed(plan, tok, att, w_out, out_bias, gain, shift, w_in, in_bias, w_down, grad_all):
    own, depth = tok.shape
    rows = own * plan.devices
    width = att.shape[1]
    hidden = w_in.shape[1]
    return pl.pallas_call(
        functools.partial(feed_kernel, plan),
        out_shape=(
            jax.ShapeDtypeStruct((rows, depth), bf16),
            jax.ShapeDtypeStruct((rows, hidden), bf16),
            jax.ShapeDtypeStruct((rows, hidden), bf16),
            jax.ShapeDtypeStruct((own, depth), f32),
            jax.ShapeDtypeStruct((1, hidden), f32),
        ),
        in_specs=[VMEM, ANY, ANY, VMEM, VMEM, VMEM, ANY, VMEM, ANY, ANY],
        out_specs=(ANY, ANY, ANY, ANY, VMEM),
        scratch_shapes=[
            pltpu.VMEM((rows, width), bf16),
            pltpu.VMEM((width, depth), bf16),
            pltpu.VMEM((depth, hidden), bf16),
            pltpu.VMEM((hidden, depth), bf16),
            pltpu.VMEM((2, 2 * own, depth), bf16),
            pltpu.VMEM((rows, depth), bf16),
            pltpu.VMEM((rows, hidden), bf16),
            pltpu.VMEM((rows, hidden), bf16),
            pltpu.VMEM((own, depth), f32),
            pltpu.SemaphoreType.DMA((48,)),
        ]
        + Scatter.scratch(plan, own, depth, bf16)
        + Gather.semaphores(plan),
        compiler_params=params(1),
        name="feed",
    )(tok, att, w_out, out_bias, gain, shift, w_in, in_bias, w_down, grad_all)


def middle_kernel(
    plan, hidden_grad, w_in, middle, out_grad, gain, w_out,
    middle_grad_out, branch_out, att_grad_out, sums_out,
    h_in, w_i, w_o, buf, middle_grad, att_grad, local, *rest,
):
    scatter_refs, gather_sems = rest[:9], rest[9:]
    place = Place(plan)
    own, depth = middle.shape
    chip_rows = 2 * own
    moves = Moves(local)
    loads = [moves.start(hidden_grad, h_in), moves.start(w_in, w_i)]
    load_out = moves.start(w_out, w_o)
    place.barrier()
    scatter = Scatter(place, own, depth, *scatter_refs[:5], scatter_refs[5:])
    for copy in loads:
        copy.wait()
    tile = min(1024, depth)

    def partial(owner, target):
        lines = h_in[pl.ds(pl.multiple_of(owner * own, own), own), :]

        def columns(start):
            target[:, pl.ds(start, tile)] = dot(lines, w_i[pl.ds(start, tile), :], 1, 1).astype(target.dtype)

        loop(depth, tile, columns)

    scatter.begin(partial)
    scatter.middle()
    mine = pl.multiple_of(place.me * own, own)
    sums_out[...] = jnp.zeros_like(sums_out)

    def close(start, count, value):
        span = pl.ds(start, count)
        unit, inverse = norm_rows(middle[span, :])
        total = out_grad[span, :].astype(f32) + norm_back(value, unit, inverse, gain[...])
        middle_grad[span, :] = total
        buf[pl.ds(pl.multiple_of(mine + start, count), count), :] = total.astype(bf16)
        sums_out[0:1, :] += jnp.sum(value * unit, axis=0, keepdims=True)
        sums_out[1:2, :] += jnp.sum(value, axis=0, keepdims=True)
        sums_out[2:3, :] += jnp.sum(total, axis=0, keepdims=True)
        sums_out[3:4, :] += jnp.sum(out_grad[span, :].astype(f32), axis=0, keepdims=True)

    scatter.end(close)
    gather = Gather(place, buf, None, own, gather_sems)
    gather.start()
    scatter.finish()
    stores = [moves.start(middle_grad, middle_grad_out)]
    load_out.wait()

    def project(offset):
        chip = lax.div(flip(place.me, offset), 2)
        span = pl.ds(pl.multiple_of(chip * chip_rows, chip_rows), chip_rows)
        stores.append(moves.start(buf.at[span, :], branch_out.at[span, :]))
        att_grad[span, :] = dot(buf[span, :], w_o[...], 1, 1).astype(bf16)

    gather.share(0)
    project(0)
    arrivals, chips = gather.steps()
    for keys, offsets in zip(arrivals, chips):
        for key in keys:
            gather.arrive(key)
        for offset in offsets:
            gather.share(offset)
            project(offset)
    stores.append(moves.start(att_grad, att_grad_out))
    gather.finish()
    for copy in stores:
        copy.wait()


def run_middle(plan, hidden_grad, w_in, middle, out_grad, gain, w_out):
    own, depth = middle.shape
    rows = own * plan.devices
    width = w_out.shape[0]
    hidden = w_in.shape[1]
    return pl.pallas_call(
        functools.partial(middle_kernel, plan),
        out_shape=(
            jax.ShapeDtypeStruct((own, depth), f32),
            jax.ShapeDtypeStruct((rows, depth), bf16),
            jax.ShapeDtypeStruct((rows, width), bf16),
            jax.ShapeDtypeStruct((8, depth), f32),
        ),
        in_specs=[ANY, ANY, VMEM, VMEM, VMEM, ANY],
        out_specs=(ANY, ANY, ANY, VMEM),
        scratch_shapes=[
            pltpu.VMEM((rows, hidden), bf16),
            pltpu.VMEM((depth, hidden), bf16),
            pltpu.VMEM((width, depth), bf16),
            pltpu.VMEM((rows, depth), bf16),
            pltpu.VMEM((own, depth), f32),
            pltpu.VMEM((rows, width), bf16),
            pltpu.SemaphoreType.DMA((16,)),
        ]
        + Scatter.scratch(plan, own, depth, f32)
        + Gather.semaphores(plan),
        compiler_params=params(2),
        name="middle",
    )(hidden_grad, w_in, middle, out_grad, gain, w_out)


def back_kernel(
    plan, block, bounds, qkv, att, att_grad, sums, activated, w_down, middle, down_bias,
    qkv_grad_out, block_out, bias_out,
    qkv_in, att_in, grad_in, act_in, w_d, starts, key_grad, value_grad, result, local, *rest,
):
    place = Place(plan)
    own, depth = middle.shape
    rows = qkv_in.shape[0]
    width = att_in.shape[1]
    heads = width // HEAD_DIM
    moves = Moves(local)
    feeds = [moves.start(activated, act_in), moves.start(w_down, w_d)]
    loads = [moves.start(qkv, qkv_in), moves.start(att, att_in), moves.start(att_grad, grad_in)]
    place.barrier()
    scatter = Scatter(place, own, depth, *rest[:5], rest[5:])
    for copy in feeds:
        copy.wait()
    tile = min(1024, depth)

    def partial(owner, target):
        lines = act_in[pl.ds(pl.multiple_of(owner * own, own), own), :]

        def columns(start):
            target[:, pl.ds(start, tile)] = dot(lines, w_d[:, pl.ds(start, tile)], 1, 0).astype(target.dtype)

        loop(depth, tile, columns)

    scatter.begin(partial)
    starts[...] = segment_starts(bounds, rows)
    bias_out[...] = jnp.zeros_like(bias_out)
    key_grad[...] = jnp.zeros_like(key_grad)
    value_grad[...] = jnp.zeros_like(value_grad)
    for copy in loads:
        copy.wait()
    scale = HEAD_DIM ** (-0.5)
    row_in = lax.broadcasted_iota(jnp.int32, (block, block), 0)
    col_in = lax.broadcasted_iota(jnp.int32, (block, block), 1)
    key_in = lax.broadcasted_iota(jnp.int32, (block, 1), 0)

    def attend(index):
        span = pl.ds(index * block, block)
        first = starts[:, span]
        queries, outer, inner, logs = [], [], [], []
        for head in range(heads):
            columns = pl.ds(head * HEAD_DIM, HEAD_DIM)
            queries.append(qkv_in[span, head_columns(0, head, width)])
            outer.append(grad_in[span, columns])
            product = grad_in[span, columns].astype(f32) * att_in[span, columns].astype(f32)
            inner.append(jnp.sum(product.T, axis=0, keepdims=True))
            logs.append(sums[pl.ds(head, 1), span])

        def against(key_block, carry, diagonal):
            key_span = pl.ds(pl.multiple_of(key_block * block, block), block)
            allowed = key_in + key_block * block >= first
            if diagonal:
                allowed = allowed & (row_in <= col_in)
            result = []
            for head in range(heads):
                columns = pl.ds(head * HEAD_DIM, HEAD_DIM)
                keys = qkv_in[key_span, head_columns(1, head, width)]
                values = qkv_in[key_span, head_columns(2, head, width)]
                scores = dot(keys, queries[head], 1, 1) * (scale * LOG2E)
                probs = jnp.exp2(jnp.where(allowed, scores - logs[head], NEGATIVE))
                value_grad[key_span, columns] += dot(probs.astype(bf16), outer[head], 1, 0)
                prob_grad = dot(values, outer[head], 1, 1)
                score_grad = (probs * (prob_grad - inner[head])).astype(bf16)
                key_grad[key_span, columns] += dot(score_grad, queries[head], 1, 0)
                result.append(carry[head] + dot(score_grad, keys, 0, 0))
            return tuple(result)

        carry = tuple(jnp.zeros((block, HEAD_DIM), f32) for head in range(heads))
        if index:
            carry = lax.fori_loop(0, index, lambda key_block, c: against(key_block, c, False), carry)
        carry = against(index, carry, True)
        for head in range(heads):
            query_grad = (carry[head] * scale).astype(bf16)
            qkv_in[span, head_columns(0, head, width)] = query_grad
            columns = pl.ds(head * HEAD_DIM, HEAD_DIM)
            bias_out[0:1, columns] += jnp.sum(query_grad.astype(f32), axis=0, keepdims=True)

    blocks = rows // block
    for index in range(blocks):
        attend(index)
        if index == blocks // 2:
            scatter.middle()
    kept = min(256, rows)

    def write(start):
        span = pl.ds(start, kept)
        qkv_in[span, pl.ds(width, width)] = (key_grad[span, :] * scale).astype(bf16)
        rounded = value_grad[span, :].astype(bf16)
        qkv_in[span, pl.ds(2 * width, width)] = rounded
        bias_out[1:2, :] += jnp.sum(rounded.astype(f32), axis=0, keepdims=True)

    loop(rows, kept, write)
    stores = [moves.start(qkv_in, qkv_grad_out)]

    def close(start, count, value):
        span = pl.ds(start, count)
        result[span, :] = (middle[span, :] + value + down_bias[...]).astype(bf16)

    scatter.end(close)
    stores.append(moves.start(result, block_out))
    scatter.finish()
    for copy in stores:
        copy.wait()


def run_back(plan, block, bounds, qkv, att, att_grad, sums, activated, w_down, middle, down_bias):
    own, depth = middle.shape
    rows, width = att.shape
    hidden = w_down.shape[0]
    return pl.pallas_call(
        functools.partial(back_kernel, plan, block),
        out_shape=(
            jax.ShapeDtypeStruct((rows, 3 * width), bf16),
            jax.ShapeDtypeStruct((own, depth), bf16),
            jax.ShapeDtypeStruct((8, width), f32),
        ),
        in_specs=[SMEM, ANY, ANY, ANY, VMEM, ANY, ANY, VMEM, VMEM],
        out_specs=(ANY, ANY, VMEM),
        scratch_shapes=[
            pltpu.VMEM((rows, 3 * width), bf16),
            pltpu.VMEM((rows, width), bf16),
            pltpu.VMEM((rows, width), bf16),
            pltpu.VMEM((rows, hidden), bf16),
            pltpu.VMEM((hidden, depth), bf16),
            pltpu.VMEM((1, rows), jnp.int32),
            pltpu.VMEM((rows, width), f32),
            pltpu.VMEM((rows, width), f32),
            pltpu.VMEM((own, depth), bf16),
            pltpu.SemaphoreType.DMA((16,)),
        ]
        + Scatter.scratch(plan, own, depth, f32),
        compiler_params=params(3),
        name="back",
    )(bounds, qkv, att, att_grad, sums, activated, w_down, middle, down_bias)


def last_kernel(
    plan, qkv_grad, w_qkv, tok, middle_grad, gain, input_out, sums_out, g_in, weights, result, local, *rest
):
    place = Place(plan)
    own, depth = tok.shape
    width = w_qkv.shape[2]
    moves = Moves(local)
    loads = [
        moves.start(w_qkv.at[part], weights.at[:, pl.ds(part * width, width)]) for part in range(3)
    ]
    loads.append(moves.start(qkv_grad, g_in))
    place.barrier()
    scatter = Scatter(place, own, depth, *rest[:5], rest[5:])
    for copy in loads:
        copy.wait()
    tile = min(1024, depth)

    def partial(owner, target):
        lines = g_in[pl.ds(pl.multiple_of(owner * own, own), own), :]

        def columns(start):
            target[:, pl.ds(start, tile)] = dot(lines, weights[pl.ds(start, tile), :], 1, 1).astype(target.dtype)

        loop(depth, tile, columns)

    scatter.begin(partial)
    scatter.middle()
    sums_out[...] = jnp.zeros_like(sums_out)

    def close(start, count, value):
        span = pl.ds(start, count)
        unit, inverse = norm_rows(tok[span, :].astype(f32))
        total = middle_grad[span, :] + norm_back(value, unit, inverse, gain[...])
        result[span, :] = total.astype(bf16)
        sums_out[0:1, :] += jnp.sum(value * unit, axis=0, keepdims=True)
        sums_out[1:2, :] += jnp.sum(value, axis=0, keepdims=True)

    scatter.end(close)
    store = moves.start(result, input_out)
    scatter.finish()
    store.wait()


def run_last(plan, qkv_grad, w_qkv, tok, middle_grad, gain):
    own, depth = tok.shape
    rows = qkv_grad.shape[0]
    width = w_qkv.shape[2]
    return pl.pallas_call(
        functools.partial(last_kernel, plan),
        out_shape=(
            jax.ShapeDtypeStruct((own, depth), bf16),
            jax.ShapeDtypeStruct((8, depth), f32),
        ),
        in_specs=[ANY, ANY, VMEM, VMEM, VMEM],
        out_specs=(ANY, VMEM),
        scratch_shapes=[
            pltpu.VMEM((rows, 3 * width), bf16),
            pltpu.VMEM((depth, 3 * width), bf16),
            pltpu.VMEM((own, depth), bf16),
            pltpu.SemaphoreType.DMA((8,)),
        ]
        + Scatter.scratch(plan, own, depth, f32),
        compiler_params=params(4),
        name="last",
    )(qkv_grad, w_qkv, tok, middle_grad, gain)


def segment_bounds(group, seq_lengths, seq_scripts, seq_place):
    count = seq_lengths.shape[0]
    numbers = jnp.arange(count, dtype=jnp.int32)
    order_key = seq_scripts * count + numbers
    same = seq_place[:, None] == seq_place[None, :]
    before = order_key[None, :] < order_key[:, None]
    offsets = jnp.sum(jnp.where(same & before, seq_lengths[None, :], 0), axis=1)
    mine = seq_place == group
    firsts = jnp.where(mine, offsets, 0)
    total = jnp.sum(jnp.where(mine, seq_lengths, 0))
    return jnp.concatenate([firsts, total[None]]).astype(jnp.int32)


def body(
    tokens,
    out_grad,
    seq_lengths,
    seq_scripts,
    seq_place,
    norm1_gain,
    norm1_shift,
    w_qkv,
    qv_bias,
    w_out,
    out_bias,
    norm2_gain,
    norm2_shift,
    w_in,
    in_bias,
    w_down,
    down_bias,
):
    own, depth = tokens.shape
    devices = lax.axis_size("mp")
    plan = Plan(devices)
    rows = own * devices
    width = w_qkv.shape[2]
    hidden = w_in.shape[1]
    block = min(512, rows)
    column = lax.axis_index("mp")
    bounds = segment_bounds(lax.axis_index("batch"), seq_lengths, seq_scripts, seq_place)

    def line(vector):
        return vector.reshape(1, -1)

    bias3 = jnp.concatenate([qv_bias[0], jnp.zeros_like(qv_bias[0]), qv_bias[1]])
    first_all, qkv, att, sums, grad_all = run_first(
        plan, block, tokens, line(norm1_gain), line(norm1_shift), w_qkv, line(bias3), bounds, out_grad
    )
    second_all, activated, hidden_grad, middle, in_part = run_feed(
        plan, tokens, att, w_out, line(out_bias), line(norm2_gain), line(norm2_shift), w_in, line(in_bias),
        w_down, grad_all,
    )

    def over_batch(partial, dimension):
        return lax.psum_scatter(partial, "batch", scatter_dimension=dimension, tiled=True).astype(f32)

    def weight_part(left, right):
        return dot(left, right, 0, 0).astype(bf16)

    down_weight_grad = over_batch(weight_part(activated, grad_all), 1)
    middle_grad, branch_all, att_grad, sums2 = run_middle(
        plan, hidden_grad, w_in, middle, out_grad, line(norm2_gain), w_out
    )
    in_weight_grad = over_batch(weight_part(second_all, hidden_grad), 0)
    qkv_grad, block_out, qv_part = run_back(
        plan, block, bounds, qkv, att, att_grad, sums, activated, w_down, middle, line(down_bias)
    )
    out_weight_grad = over_batch(weight_part(att, branch_all), 1)
    qkv_part = jnp.stack(
        [weight_part(first_all, qkv_grad[:, part * width : (part + 1) * width]) for part in range(3)]
    )
    qkv_weight_grad = over_batch(qkv_part, 1)
    input_grad, sums1 = run_last(plan, qkv_grad, w_qkv, tokens, middle_grad, line(norm1_gain))

    local = jnp.concatenate([qv_part[0], qv_part[1], in_part[0]])
    spread = lax.dynamic_update_slice(
        jnp.zeros((devices, local.shape[0]), f32), local[None], (column, jnp.int32(0))
    )
    packed = jnp.concatenate([sums1[:2].reshape(-1), sums2[:4].reshape(-1), spread.reshape(-1)])
    packed = lax.psum(packed, ("batch", "mp"))
    vectors = packed[: 6 * depth].reshape(6, depth)
    spread = packed[6 * depth :].reshape(devices, -1)
    qv_bias_grad = jnp.stack([spread[:, :width].reshape(-1), spread[:, width : 2 * width].reshape(-1)])
    return (
        block_out,
        input_grad,
        vectors[0],
        vectors[1],
        qkv_weight_grad,
        qv_bias_grad,
        out_weight_grad,
        vectors[4],
        vectors[2],
        vectors[3],
        in_weight_grad,
        spread[:, 2 * width :].reshape(-1),
        down_weight_grad,
        vectors[5],
    )


def solution(mesh):
    return jax.shard_map(
        body,
        mesh=mesh,
        in_specs=(
            P(("batch", "mp"), None),
            P(("batch", "mp"), None),
            P(),
            P(),
            P(),
            P(),
            P(),
            P(None, None, "mp"),
            P(None, "mp"),
            P("mp", None),
            P(),
            P(),
            P(),
            P(None, "mp"),
            P("mp"),
            P("mp", None),
            P(),
        ),
        out_specs=(
            P(("batch", "mp"), None),
            P(("batch", "mp"), None),
            P(),
            P(),
            P(None, "batch", "mp"),
            P(),
            P("mp", "batch"),
            P(),
            P(),
            P(),
            P("batch", "mp"),
            P(),
            P("mp", "batch"),
            P(),
        ),
        check_vma=False,
    )
```

```python
import functools

import jax
import jax.numpy as jnp
from jax import lax
from jax.experimental import pallas as pl
from jax.experimental.pallas import tpu as pltpu
from jax.sharding import PartitionSpec as P

HEAD_DIM = 128
EPS = 1e-05
NEGATIVE = -1e30
LOG2E = 1.4426950408889634
f32 = jnp.float32
bf16 = jnp.bfloat16
MESH = pl.DeviceIdType.MESH
ANY = pl.BlockSpec(memory_space=pl.ANY)
VMEM = pl.BlockSpec(memory_space=pltpu.VMEM)
SMEM = pl.BlockSpec(memory_space=pltpu.SMEM)


def dot(left, right, contract_left, contract_right):
    return lax.dot_general(
        left,
        right,
        (((contract_left,), (contract_right,)), ((), ())),
        preferred_element_type=f32,
    )


def flip(index, mask):
    bit = 1
    while bit <= mask:
        if mask & bit:
            index = index + bit * (1 - 2 * lax.rem(lax.div(index, bit), 2))
        bit *= 2
    return index


def loop(count, step, body):
    def one(index, carry):
        body(pl.multiple_of(index * step, step))
        return carry

    lax.fori_loop(0, count // step, one, 0)


class Plan:
    def __init__(self, devices):
        bits = []
        bit = 2
        while bit < devices:
            bits.append(bit)
            bit *= 2
        self.devices = devices
        self.bits = bits
        self.orders = [tuple(bits)] + ([tuple(reversed(bits))] if len(bits) > 1 else [])
        self.parts = len(self.orders)
        self.offsets = list(range(0, devices, 2))
        self.keys = [(part, offset) for part in range(self.parts) for offset in self.offsets if offset]
        self.keys.sort(key=lambda key: (bin(key[1]).count("1"), self.last(*key)))
        self.shares = [(part, offset) for offset in self.offsets for part in range(self.parts)]

    def last(self, part, offset):
        steps = [step for step, bit in enumerate(self.orders[part]) if bit & offset]
        return max(steps) if steps else -1

    def bit(self, part, offset):
        return self.orders[part][self.last(part, offset)]

    def later(self, part, offset):
        order = self.orders[part]
        return [offset | order[step] for step in range(self.last(part, offset) + 1, len(order))]


class Place:
    def __init__(self, plan):
        self.plan = plan
        self.batch = lax.axis_index("batch")
        self.groups = lax.axis_size("batch")
        self.me = lax.axis_index("mp")

    def at(self, mask):
        return (self.batch, flip(self.me, mask))

    def beside(self, step):
        return (self.batch + step, self.me)

    def barrier(self, line=False, halves=False):
        semaphore = pltpu.get_barrier_semaphore()
        masks = [1] + self.plan.bits
        for mask in masks:
            pl.semaphore_signal(semaphore, inc=1, device_id=self.at(mask), device_id_type=MESH)
        count = len(masks)
        if line:
            for step, there in ((-1, self.batch > 0), (1, self.batch < self.groups - 1)):

                @pl.when(there)
                def greet():
                    pl.semaphore_signal(semaphore, inc=1, device_id=self.beside(step), device_id_type=MESH)

                count = count + there.astype(jnp.int32)
        if halves:
            for bit in self.group_bits():
                pl.semaphore_signal(semaphore, inc=1, device_id=self.across(bit), device_id_type=MESH)
                count = count + 1
        pl.semaphore_wait(semaphore, count)

    def group_bits(self):
        bits = []
        bit = 1
        while bit < self.groups:
            bits.append(bit)
            bit *= 2
        return bits

    def across(self, bit):
        return (flip(self.batch, bit), self.me)


class Gather:
    def __init__(self, place, buf, own, rows, sems):
        self.place, self.plan, self.buf, self.own, self.rows = place, place.plan, buf, own, rows
        self.link_send, self.link_recv, self.core_send, self.core_recv = sems
        self.part_rows = rows // self.plan.parts

    def span(self, mask, part):
        block = flip(self.place.me, mask)
        start = block * self.rows + part * self.part_rows
        return self.buf.at[pl.ds(pl.multiple_of(start, self.part_rows), self.part_rows), :]

    def source(self, offset, part):
        if offset == 0 and self.own is not None:
            return self.own.at[pl.ds(part * self.part_rows, self.part_rows), :]
        return self.span(offset, part)

    def link(self, key):
        part, offset = key
        bit = self.plan.bit(part, offset)
        index = self.plan.keys.index(key)
        return pltpu.make_async_remote_copy(
            src_ref=self.source(offset ^ bit, part),
            dst_ref=self.span(offset ^ bit, part),
            send_sem=self.link_send.at[index],
            recv_sem=self.link_recv.at[index],
            device_id=self.place.at(bit),
            device_id_type=MESH,
        )

    def core(self, key):
        part, offset = key
        index = self.plan.shares.index(key)
        return pltpu.make_async_remote_copy(
            src_ref=self.source(offset, part),
            dst_ref=self.span(offset, part),
            send_sem=self.core_send.at[index],
            recv_sem=self.core_recv.at[index],
            device_id=self.place.at(1),
            device_id_type=MESH,
        )

    def landed(self, ref, semaphore):
        pltpu.make_async_remote_copy(
            src_ref=ref,
            dst_ref=ref,
            send_sem=semaphore,
            recv_sem=semaphore,
            device_id=self.place.at(1),
            device_id_type=MESH,
        ).wait_recv()

    def start(self):
        for part in range(self.plan.parts):
            self.core((part, 0)).start()
        for key in self.plan.keys:
            if bin(key[1]).count("1") == 1:
                self.link(key).start()

    def arrive(self, key):
        part, offset = key
        self.landed(self.span(offset, part), self.link_recv.at[self.plan.keys.index(key)])
        for target in self.plan.later(part, offset):
            self.link((part, target)).start()
        self.core(key).start()

    def share(self, offset):
        for part in range(self.plan.parts):
            index = self.plan.shares.index((part, offset))
            self.landed(self.span(offset | 1, part), self.core_recv.at[index])

    def steps(self):
        singles = [offset for offset in self.plan.offsets if bin(offset).count("1") == 1]
        rest = [offset for offset in self.plan.offsets if bin(offset).count("1") > 1]
        rest.sort(key=lambda offset: bin(offset).count("1"))
        groups = [[key for key in self.plan.keys if key[1] in singles]]
        groups += [[key for key in self.plan.keys if key[1] == offset] for offset in rest]
        return groups, [singles] + [[offset] for offset in rest]

    def finish(self):
        for key in self.plan.keys:
            self.link(key).wait_send()
        for key in self.plan.shares:
            self.core(key).wait_send()

    @staticmethod
    def semaphores(plan):
        return [pltpu.SemaphoreType.DMA((len(plan.keys),))] * 2 + [
            pltpu.SemaphoreType.DMA((len(plan.shares),))
        ] * 2


class Scatter:
    def __init__(self, place, rows, width, core_out, core_in, kept, link_out, link_in, sems):
        self.place, self.plan, self.rows, self.width = place, place.plan, rows, width
        self.core_out, self.core_in, self.kept = core_out, core_in, kept
        self.link_out, self.link_in = link_out, link_in
        self.link_send, self.link_recv, self.core_send, self.core_recv = sems
        self.part_rows = rows // self.plan.parts
        self.step = min(32, self.part_rows)
        self.order = sorted(self.plan.offsets, key=lambda offset: -bin(offset).count("1"))

    def core(self, offset):
        index = offset // 2
        return pltpu.make_async_remote_copy(
            src_ref=self.core_out.at[index],
            dst_ref=self.core_in.at[index],
            send_sem=self.core_send.at[index],
            recv_sem=self.core_recv.at[index],
            device_id=self.place.at(1),
            device_id_type=MESH,
        )

    def link(self, key):
        index = self.plan.keys.index(key)
        return pltpu.make_async_remote_copy(
            src_ref=self.link_out.at[index],
            dst_ref=self.link_in.at[index],
            send_sem=self.link_send.at[index],
            recv_sem=self.link_recv.at[index],
            device_id=self.place.at(self.plan.bit(*key)),
            device_id_type=MESH,
        )

    def total(self, offset, part, start, arrived):
        rows = pl.ds(pl.multiple_of(part * self.part_rows + start, self.step), self.step)
        value = self.kept[offset // 2, rows, :].astype(f32) + self.core_in[offset // 2, rows, :].astype(f32)
        for key in arrived:
            value += self.link_in[self.plan.keys.index(key), pl.ds(start, self.step), :].astype(f32)
        return value

    def pass_on(self, part, offset):
        arrived = [(part, target) for target in self.plan.later(part, offset)]
        for key in arrived:
            self.link(key).wait_recv()
        index = self.plan.keys.index((part, offset))

        def add(start):
            self.link_out[index, pl.ds(start, self.step), :] = self.total(
                offset, part, start, arrived
            ).astype(bf16)

        loop(self.part_rows, self.step, add)
        self.link((part, offset)).start()

    def begin(self, partial, between=None):
        for number, offset in enumerate(self.order):
            index = offset // 2
            partial(flip(self.place.me, offset | 1), self.core_out.at[index])
            self.core(offset).start()
            partial(flip(self.place.me, offset), self.kept.at[index])
            self.core(offset).wait_recv()
            for part in range(self.plan.parts):
                if offset and not self.plan.later(part, offset):
                    self.pass_on(part, offset)
            if between is not None:
                between(number)

    def middle(self):
        for offset in self.order:
            for part in range(self.plan.parts):
                if offset and self.plan.later(part, offset):
                    self.pass_on(part, offset)

    def end(self, use):
        for part in range(self.plan.parts):
            arrived = [(part, target) for target in self.plan.later(part, 0)]
            for key in arrived:
                self.link(key).wait_recv()

            def piece(start):
                row = pl.multiple_of(part * self.part_rows + start, self.step)
                use(row, self.step, self.total(0, part, start, arrived))

            loop(self.part_rows, self.step, piece)

    def finish(self):
        for key in self.plan.keys:
            self.link(key).wait_send()
        for offset in self.plan.offsets:
            self.core(offset).wait_send()

    @staticmethod
    def scratch(plan, rows, width, kept):
        chips, keys = len(plan.offsets), len(plan.keys)
        return [
            pltpu.VMEM((chips, rows, width), bf16),
            pltpu.VMEM((chips, rows, width), bf16),
            pltpu.VMEM((chips, rows, width), kept),
            pltpu.VMEM((keys, rows // plan.parts, width), bf16),
            pltpu.VMEM((keys, rows // plan.parts, width), bf16),
            pltpu.SemaphoreType.DMA((keys,)),
            pltpu.SemaphoreType.DMA((keys,)),
            pltpu.SemaphoreType.DMA((chips,)),
            pltpu.SemaphoreType.DMA((chips,)),
        ]


class Line:
    def __init__(self, place, own, up, down, pieces, sems):
        self.place, self.own, self.up, self.down, self.pieces = place, own, up, down, pieces
        self.groups, self.batch = place.groups, place.batch
        self.rows = own.shape[1] // pieces
        self.step = min(32, self.rows)
        self.sems = sems

    def span(self, piece):
        start = piece * self.rows
        return pl.ds(start if isinstance(start, int) else pl.multiple_of(start, self.rows), self.rows)

    def slot(self, upward, target):
        return self.up.at[target - 1] if upward else self.down.at[target]

    def copy(self, upward, target, piece, source):
        send, recv = self.sems[:2] if upward else self.sems[2:]
        index = target * self.pieces + piece
        return pltpu.make_async_remote_copy(
            src_ref=source.at[self.span(piece), :],
            dst_ref=self.slot(upward, target).at[self.span(piece), :],
            send_sem=send.at[index],
            recv_sem=recv.at[index],
            device_id=self.place.beside(1 if upward else -1),
            device_id_type=MESH,
        )

    def start(self, target):
        if target > 0:

            @pl.when(self.batch == 0)
            def first():
                for piece in range(self.pieces):
                    self.copy(True, target, piece, self.own.at[target]).start()

        if target < self.groups - 1:

            @pl.when(self.batch == self.groups - 1)
            def last():
                for piece in range(self.pieces):
                    self.copy(False, target, piece, self.own.at[target]).start()

    def order(self):
        count = self.groups
        result = []
        for index in range((count + 1) // 2):
            for target in (count - 1 - index, index):
                if target not in result:
                    result.append(target)
        return result

    def ticks(self):
        return range(1, (self.groups - 1) * self.pieces + self.groups)

    def tick(self, number):
        for upward in (True, False):
            place = self.batch if upward else self.groups - 1 - self.batch
            for distance in range(2, self.groups):
                target = distance if upward else self.groups - 1 - distance
                piece = number - (self.groups - 1 - distance) * self.pieces - place
                due = (place > 0) & (place < distance) & (piece >= 0) & (piece < self.pieces)

                @pl.when(due)
                def forward():
                    slot = self.slot(upward, target)
                    copy = self.copy(upward, target, piece, slot)
                    copy.wait_recv()

                    def add(start):
                        rows = pl.ds(pl.multiple_of(piece * self.rows + start, self.step), self.step)
                        total = slot[rows, :].astype(f32) + self.own[target, rows, :].astype(f32)
                        slot[rows, :] = total.astype(bf16)

                    loop(self.rows, self.step, add)
                    copy.start()

    def end(self, target_ref):
        below, above = self.batch > 0, self.batch < self.groups - 1
        total = self.own.shape[1]

        @pl.when(below)
        def up():
            slot = self.slot(True, self.batch)
            for piece in range(self.pieces):
                self.copy(True, self.batch, piece, slot).wait_recv()

        @pl.when(above)
        def down():
            slot = self.slot(False, self.batch)
            for piece in range(self.pieces):
                self.copy(False, self.batch, piece, slot).wait_recv()

        def add(sides):
            def rows_of(start):
                rows = pl.ds(start, self.step)
                value = self.own[self.batch, rows, :].astype(f32)
                for upward in sides:
                    value += self.slot(upward, self.batch)[rows, :].astype(f32)
                target_ref[rows, :] = value

            loop(total, self.step, rows_of)

        @pl.when(jnp.logical_not(above))
        def at_top():
            add([True])

        @pl.when(jnp.logical_not(below))
        def at_bottom():
            add([False])

        @pl.when(below & above)
        def between():
            add([True, False])

    def finish(self):
        for target in range(self.groups):
            for upward in (True, False):
                if target == (0 if upward else self.groups - 1):
                    continue

                @pl.when(self.batch < target if upward else self.batch > target)
                def sent():
                    slot = self.slot(upward, target)
                    for piece in range(self.pieces):
                        self.copy(upward, target, piece, slot).wait_send()

    @staticmethod
    def scratch(groups, rows, columns, pieces):
        return [
            pltpu.VMEM((groups, rows, columns), bf16),
            pltpu.VMEM((groups - 1, rows, columns), bf16),
            pltpu.VMEM((groups - 1, rows, columns), bf16),
        ] + [pltpu.SemaphoreType.DMA((groups * pieces,))] * 4


class Moves:
    def __init__(self, sems):
        self.sems, self.count = sems, 0

    def start(self, source, target):
        copy = pltpu.make_async_copy(source, target, self.sems.at[self.count])
        self.count += 1
        copy.start()
        return copy


def norm_rows(rows):
    mean = jnp.mean(rows, axis=-1, keepdims=True)
    centred = rows - mean
    inverse = lax.rsqrt(jnp.mean(centred * centred, axis=-1, keepdims=True) + EPS)
    return centred * inverse, inverse


def norm_back(grad, unit, inverse, gain):
    scaled = grad * gain
    return inverse * (
        scaled
        - jnp.mean(scaled, axis=-1, keepdims=True)
        - unit * jnp.mean(scaled * unit, axis=-1, keepdims=True)
    )


def segment_starts(bounds, rows):
    position = lax.broadcasted_iota(jnp.int32, (1, rows), 1)
    first = jnp.zeros((1, rows), jnp.int32)
    for index in range(bounds.shape[0]):
        first = jnp.maximum(first, jnp.where(position >= bounds[index], bounds[index], 0))
    return first


def head_columns(part, head, width):
    return pl.ds(part * width + head * HEAD_DIM, HEAD_DIM)


def first_kernel(
    plan, block, tok, gain, shift, w_qkv, qv_bias, bounds, out_grad, first_out, qkv_out, att_out,
    sum_out, grad_out, buf, weights, qkv, starts, sums, attended, local, *sems,
):
    place = Place(plan)
    own, depth = tok.shape
    rows = buf.shape[0]
    width = w_qkv.shape[2]
    moves = Moves(local)
    loads = [
        moves.start(w_qkv.at[part], weights.at[:, pl.ds(part * width, width)]) for part in range(3)
    ]
    place.barrier()
    step = min(32, own)
    mine = pl.multiple_of(place.me * own, own)

    def normalise(start):
        unit, _ = norm_rows(tok[pl.ds(start, step), :].astype(f32))
        buf[pl.ds(pl.multiple_of(mine + start, step), step), :] = (unit * gain[...] + shift[...]).astype(bf16)

    loop(own, step, normalise)
    gather = Gather(place, buf, None, own, sems[:4])
    gather.start()
    stores = [moves.start(out_grad, grad_out.at[pl.ds(mine, own), :])]
    starts[...] = segment_starts(bounds, rows)
    for copy in loads:
        copy.wait()

    def project(offset):
        chip = lax.div(flip(place.me, offset), 2)
        span = pl.ds(pl.multiple_of(chip * 2 * own, 2 * own), 2 * own)
        stores.append(moves.start(buf.at[span, :], first_out.at[span, :]))
        qkv[span, :] = (dot(buf[span, :], weights[...], 1, 0) + qv_bias[...]).astype(bf16)

    gather.share(0)
    project(0)
    arrivals, chips = gather.steps()
    for keys, offsets in zip(arrivals, chips):
        for key in keys:
            gather.arrive(key)
        for offset in offsets:
            gather.share(offset)
            project(offset)
    gather.finish()
    gather = Gather(place, grad_out, out_grad, own, sems[4:])
    gather.start()
    stores.append(moves.start(qkv, qkv_out))

    scale = HEAD_DIM ** (-0.5) * LOG2E
    heads = width // HEAD_DIM
    row_in = lax.broadcasted_iota(jnp.int32, (block, block), 0)
    col_in = lax.broadcasted_iota(jnp.int32, (block, block), 1)
    key_in = lax.broadcasted_iota(jnp.int32, (block, 1), 0)

    def attend(index):
        span = pl.ds(index * block, block)
        first = starts[:, span]
        queries = [qkv[span, head_columns(0, head, width)] for head in range(heads)]

        def against(key_block, carry, diagonal):
            key_span = pl.ds(pl.multiple_of(key_block * block, block), block)
            allowed = key_in + key_block * block >= first
            if diagonal:
                allowed = allowed & (row_in <= col_in)
            result = []
            for head in range(heads):
                top, total, mixed = carry[head]
                keys = qkv[key_span, head_columns(1, head, width)]
                values = qkv[key_span, head_columns(2, head, width)]
                scores = jnp.where(allowed, dot(keys, queries[head], 1, 1) * scale, NEGATIVE)
                new_top = jnp.maximum(top, jnp.max(scores, axis=0, keepdims=True))
                exps = jnp.exp2(scores - new_top)
                fade = jnp.exp2(top - new_top)
                total = total * fade + jnp.sum(exps, axis=0, keepdims=True)
                mixed = mixed * fade + dot(values, exps.astype(bf16), 0, 0)
                result.append((new_top, total, mixed))
            return tuple(result)

        carry = tuple(
            (
                jnp.full((1, block), NEGATIVE, f32),
                jnp.zeros((1, block), f32),
                jnp.zeros((HEAD_DIM, block), f32),
            )
            for head in range(heads)
        )
        if index:
            carry = lax.fori_loop(0, index, lambda key_block, c: against(key_block, c, False), carry)
        carry = against(index, carry, True)
        for head in range(heads):
            top, total, mixed = carry[head]
            attended[span, pl.ds(head * HEAD_DIM, HEAD_DIM)] = (mixed * (1.0 / total)).T.astype(bf16)
            sums[pl.ds(head, 1), span] = top + jnp.log2(total)

    blocks = rows // block
    groups = list(zip(arrivals, chips))
    taken = 0
    for index in range(blocks):
        attend(index)
        if index >= blocks - 2 and taken < len(groups):
            for key in groups[taken][0]:
                gather.arrive(key)
            taken += 1
    stores.append(moves.start(attended, att_out))
    stores.append(moves.start(sums, sum_out))
    while taken < len(groups):
        for key in groups[taken][0]:
            gather.arrive(key)
        taken += 1
    for offset in plan.offsets:
        gather.share(offset)
    gather.finish()
    for copy in stores:
        copy.wait()


def params(number):
    return pltpu.CompilerParams(
        collective_id=number, has_side_effects=True, vmem_limit_bytes=62 * 2**20
    )


def cost(micros):
    return pl.CostEstimate(flops=micros * 10**9, bytes_accessed=10**7, transcendentals=0)


def run_first(plan, block, tok, gain, shift, w_qkv, qv_bias, bounds, out_grad):
    own, depth = tok.shape
    rows = own * plan.devices
    width = w_qkv.shape[2]
    heads = width // HEAD_DIM
    return pl.pallas_call(
        functools.partial(first_kernel, plan, block),
        out_shape=(
            jax.ShapeDtypeStruct((rows, depth), bf16),
            jax.ShapeDtypeStruct((rows, 3 * width), bf16),
            jax.ShapeDtypeStruct((rows, width), bf16),
            jax.ShapeDtypeStruct((8, rows), f32),
            jax.ShapeDtypeStruct((rows, depth), bf16),
        ),
        in_specs=[VMEM, VMEM, VMEM, ANY, VMEM, SMEM, ANY],
        out_specs=(ANY,) * 5,
        scratch_shapes=[
            pltpu.VMEM((rows, depth), bf16),
            pltpu.VMEM((depth, 3 * width), bf16),
            pltpu.VMEM((rows, 3 * width), bf16),
            pltpu.VMEM((1, rows), jnp.int32),
            pltpu.VMEM((8, rows), f32),
            pltpu.VMEM((rows, width), bf16),
            pltpu.SemaphoreType.DMA((16,)),
        ]
        + Gather.semaphores(plan) * 2,
        compiler_params=params(0),
        name="first",
        cost_estimate=cost(80),
    )(tok, gain, shift, w_qkv, qv_bias, bounds, out_grad)


def feed_kernel(
    plan, tok, att, w_out, out_bias, gain, shift, w_in, in_bias, w_down, grad_all,
    second_out, act_out, hidden_out, middle_out, bias_out,
    att_in, w_o, w_i, w_d, grad_in, buf, act, back, middle, local, *rest,
):
    scatter_refs, gather_sems = rest[:9], rest[9:]
    place = Place(plan)
    own, depth = tok.shape
    rows = buf.shape[0]
    hidden_width = w_in.shape[1]
    chip_rows = 2 * own
    moves = Moves(local)
    load_att = moves.start(att, att_in)
    load_out = moves.start(w_out, w_o)
    load_in = moves.start(w_in, w_i)
    load_down = moves.start(w_down, w_d)
    place.barrier()
    scatter = Scatter(place, own, depth, *scatter_refs[:5], scatter_refs[5:])
    load_att.wait()
    load_out.wait()
    tile = min(1024, depth)

    def partial(owner, target):
        lines = att_in[pl.ds(pl.multiple_of(owner * own, own), own), :]

        def columns(start):
            target[:, pl.ds(start, tile)] = dot(lines, w_o[:, pl.ds(start, tile)], 1, 0).astype(target.dtype)

        loop(depth, tile, columns)

    scatter.begin(partial)
    scatter.middle()
    mine = pl.multiple_of(place.me * own, own)

    def close(start, count, value):
        span = pl.ds(start, count)
        total = tok[span, :].astype(f32) + value + out_bias[...]
        middle[span, :] = total
        unit, _ = norm_rows(total)
        buf[pl.ds(pl.multiple_of(mine + start, count), count), :] = (unit * gain[...] + shift[...]).astype(bf16)

    scatter.end(close)
    gather = Gather(place, buf, None, own, gather_sems)
    gather.start()
    scatter.finish()
    stores = [moves.start(middle, middle_out)]
    load_in.wait()
    load_down.wait()
    bias_out[...] = jnp.zeros_like(bias_out)
    part_cols = min(512, hidden_width)

    def chip_span(offset):
        chip = lax.div(flip(place.me, offset), 2)
        return pl.ds(pl.multiple_of(chip * chip_rows, chip_rows), chip_rows)

    order = []

    def prefetch(offset):
        slot = len(order) % 2
        order.append(moves.start(grad_all.at[chip_span(offset), :], grad_in.at[slot]))

    def expand(offset, slot):
        span = chip_span(offset)
        stores.append(moves.start(buf.at[span, :], second_out.at[span, :]))
        order[slot].wait()

        def columns(start):
            cols = pl.ds(start, part_cols)
            pre = dot(buf[span, :], w_i[:, cols], 1, 0) + in_bias[:, cols]
            up = dot(grad_in[slot % 2], w_d[cols, :], 1, 1)
            root = 0.7978845608028654
            square = pre * pre
            inner = jnp.tanh(root * (pre + 0.044715 * (square * pre)))
            half = 0.5 * (1.0 + inner)
            slope = half + 0.5 * pre * (1.0 - inner * inner) * (root * (1.0 + 3 * 0.044715 * square))
            act[span, cols] = (pre * half).astype(bf16)
            down = (up * slope).astype(bf16)
            back[span, cols] = down
            bias_out[:, cols] += jnp.sum(down.astype(f32), axis=0, keepdims=True)

        loop(hidden_width, part_cols, columns)
        stores.append(moves.start(act.at[span, :], act_out.at[span, :]))
        stores.append(moves.start(back.at[span, :], hidden_out.at[span, :]))

    arrivals, chips = gather.steps()
    sequence = [0] + [offset for offsets in chips for offset in offsets]
    prefetch(sequence[0])
    prefetch(sequence[1])
    gather.share(0)
    expand(0, 0)
    number = 1
    for keys, offsets in zip(arrivals, chips):
        for key in keys:
            gather.arrive(key)
        for offset in offsets:
            if number + 1 < len(sequence):
                prefetch(sequence[number + 1])
            gather.share(offset)
            expand(offset, number)
            number += 1
    gather.finish()
    for copy in stores:
        copy.wait()


def run_feed(plan, tok, att, w_out, out_bias, gain, shift, w_in, in_bias, w_down, grad_all):
    own, depth = tok.shape
    rows = own * plan.devices
    width = att.shape[1]
    hidden = w_in.shape[1]
    return pl.pallas_call(
        functools.partial(feed_kernel, plan),
        out_shape=(
            jax.ShapeDtypeStruct((rows, depth), bf16),
            jax.ShapeDtypeStruct((rows, hidden), bf16),
            jax.ShapeDtypeStruct((rows, hidden), bf16),
            jax.ShapeDtypeStruct((own, depth), f32),
            jax.ShapeDtypeStruct((1, hidden), f32),
        ),
        in_specs=[VMEM, ANY, ANY, VMEM, VMEM, VMEM, ANY, VMEM, ANY, ANY],
        out_specs=(ANY, ANY, ANY, ANY, VMEM),
        scratch_shapes=[
            pltpu.VMEM((rows, width), bf16),
            pltpu.VMEM((width, depth), bf16),
            pltpu.VMEM((depth, hidden), bf16),
            pltpu.VMEM((hidden, depth), bf16),
            pltpu.VMEM((2, 2 * own, depth), bf16),
            pltpu.VMEM((rows, depth), bf16),
            pltpu.VMEM((rows, hidden), bf16),
            pltpu.VMEM((rows, hidden), bf16),
            pltpu.VMEM((own, depth), f32),
            pltpu.SemaphoreType.DMA((48,)),
        ]
        + Scatter.scratch(plan, own, depth, bf16)
        + Gather.semaphores(plan),
        compiler_params=params(1),
        name="feed",
        cost_estimate=cost(90),
    )(tok, att, w_out, out_bias, gain, shift, w_in, in_bias, w_down, grad_all)


PIECES = 2


def middle_kernel(
    plan, hidden_grad, w_in, middle, out_grad, gain, w_out, activated, grad_all, second_all,
    middle_grad_out, branch_out, att_grad_out, sums_out, down_out, in_part_out,
    h_in, w_i, w_o, buf, middle_grad, att_grad, act, staged, total, local, *rest,
):
    scatter_refs, gather_sems, line_refs = rest[:9], rest[9:13], rest[13:]
    place = Place(plan)
    own, depth = middle.shape
    rows = buf.shape[0]
    chip_rows = 2 * own
    hidden = w_in.shape[1]
    groups = place.groups
    cut = depth // groups
    moves = Moves(local)
    loads = [moves.start(hidden_grad, h_in), moves.start(w_in, w_i)]
    load_act = moves.start(activated, act)
    load_grad = moves.start(grad_all, buf)
    load_out = moves.start(w_out, w_o)
    place.barrier(line=True)
    scatter = Scatter(place, own, depth, *scatter_refs[:5], scatter_refs[5:])
    line = Line(place, *line_refs[:3], PIECES, line_refs[3:])
    for copy in loads:
        copy.wait()
    tile = min(1024, depth)

    def partial(owner, target):
        lines = h_in[pl.ds(pl.multiple_of(owner * own, own), own), :]

        def columns(start):
            target[:, pl.ds(start, tile)] = dot(lines, w_i[pl.ds(start, tile), :], 1, 1).astype(target.dtype)

        loop(depth, tile, columns)

    order = line.order()
    part = min(512, hidden)

    def down_slice(target):
        def piece(start):
            line.own[target, pl.ds(start, part), :] = dot(
                act[:, pl.ds(start, part)], buf[:, pl.ds(target * cut, cut)], 0, 0
            ).astype(bf16)

        loop(hidden, part, piece)
        line.start(target)

    def between(number):
        if number == 0:
            load_act.wait()
            load_grad.wait()
            for target in order[:2]:
                down_slice(target)
        if number == 1:
            for target in order[2:]:
                down_slice(target)

    scatter.begin(partial, between)

    in_stores = []
    in_loads = {}

    def load_slice(number):
        columns = pl.ds(number * cut, cut)
        in_loads[number] = moves.start(second_all.at[:, columns], act.at[:, pl.ds((number % 2) * cut, cut)])

    def in_slice(number):
        in_loads[number].wait()
        if number >= 2:
            in_stores[number - 2].wait()
        slot = number % 2

        def piece(start):
            columns = pl.ds(start, part)
            staged[slot, :, columns] = dot(
                act[:, pl.ds(slot * cut, cut)], h_in[:, columns], 0, 0
            ).astype(bf16)

        loop(hidden, part, piece)
        in_stores.append(moves.start(staged.at[slot], in_part_out.at[number]))
        if number + 2 < groups:
            load_slice(number + 2)

    ticks = list(line.ticks())
    for number in range(min(2, groups)):
        load_slice(number)
    line.tick(ticks.pop(0))
    scatter.middle()
    half = groups // 2
    for number in range(half):
        in_slice(number)
    line.tick(ticks.pop(0))
    mine = pl.multiple_of(place.me * own, own)
    sums_out[...] = jnp.zeros_like(sums_out)

    def close(start, count, value):
        span = pl.ds(start, count)
        unit, inverse = norm_rows(middle[span, :])
        sum_rows = out_grad[span, :].astype(f32) + norm_back(value, unit, inverse, gain[...])
        middle_grad[span, :] = sum_rows
        buf[pl.ds(pl.multiple_of(mine + start, count), count), :] = sum_rows.astype(bf16)
        sums_out[0:1, :] += jnp.sum(value * unit, axis=0, keepdims=True)
        sums_out[1:2, :] += jnp.sum(value, axis=0, keepdims=True)
        sums_out[2:3, :] += jnp.sum(sum_rows, axis=0, keepdims=True)
        sums_out[3:4, :] += jnp.sum(out_grad[span, :].astype(f32), axis=0, keepdims=True)

    scatter.end(close)
    gather = Gather(place, buf, None, own, gather_sems)
    gather.start()
    scatter.finish()
    stores = [moves.start(middle_grad, middle_grad_out)]
    load_out.wait()

    def project(offset):
        chip = lax.div(flip(place.me, offset), 2)
        span = pl.ds(pl.multiple_of(chip * chip_rows, chip_rows), chip_rows)
        stores.append(moves.start(buf.at[span, :], branch_out.at[span, :]))
        att_grad[span, :] = dot(buf[span, :], w_o[...], 1, 1).astype(bf16)

    gather.share(0)
    project(0)
    for number in range(half, groups):
        in_slice(number)
    line.tick(ticks.pop(0))
    arrivals, chips = gather.steps()
    for keys, offsets in zip(arrivals, chips):
        for key in keys:
            gather.arrive(key)
        for offset in offsets:
            gather.share(offset)
            project(offset)
        line.tick(ticks.pop(0))
    stores.append(moves.start(att_grad, att_grad_out))
    for number in ticks:
        line.tick(number)
    line.end(total)
    stores.append(moves.start(total, down_out))
    gather.finish()
    line.finish()
    for copy in stores + in_stores[-2:]:
        copy.wait()


def run_middle(plan, groups, hidden_grad, w_in, middle, out_grad, gain, w_out, activated, grad_all, second_all):
    own, depth = middle.shape
    rows = own * plan.devices
    width = w_out.shape[0]
    hidden = w_in.shape[1]
    cut = depth // groups
    return pl.pallas_call(
        functools.partial(middle_kernel, plan),
        out_shape=(
            jax.ShapeDtypeStruct((own, depth), f32),
            jax.ShapeDtypeStruct((rows, depth), bf16),
            jax.ShapeDtypeStruct((rows, width), bf16),
            jax.ShapeDtypeStruct((8, depth), f32),
            jax.ShapeDtypeStruct((hidden, cut), f32),
            jax.ShapeDtypeStruct((groups, cut, hidden), bf16),
        ),
        in_specs=[ANY, ANY, VMEM, VMEM, VMEM, ANY, ANY, ANY, ANY],
        out_specs=(ANY, ANY, ANY, VMEM, ANY, ANY),
        scratch_shapes=[
            pltpu.VMEM((rows, hidden), bf16),
            pltpu.VMEM((depth, hidden), bf16),
            pltpu.VMEM((width, depth), bf16),
            pltpu.VMEM((rows, depth), bf16),
            pltpu.VMEM((own, depth), f32),
            pltpu.VMEM((rows, width), bf16),
            pltpu.VMEM((rows, max(hidden, 2 * cut)), bf16),
            pltpu.VMEM((2, cut, hidden), bf16),
            pltpu.VMEM((hidden, cut), f32),
            pltpu.SemaphoreType.DMA((40,)),
        ]
        + Scatter.scratch(plan, own, depth, bf16)
        + Gather.semaphores(plan)
        + Line.scratch(groups, hidden, cut, PIECES),
        compiler_params=params(2),
        name="middle",
        cost_estimate=cost(80),
    )(hidden_grad, w_in, middle, out_grad, gain, w_out, activated, grad_all, second_all)


def back_kernel(
    plan, block, bounds, qkv, att, att_grad, sums, activated, w_down, middle, down_bias, in_part, branch_all,
    qkv_grad_out, block_out, bias_out, in_out, out_part_out,
    qkv_in, att_in, grad_in, act_in, w_d, starts, key_grad, value_grad, result, branch, staged, total, local,
    *rest,
):
    scatter_refs, line_refs = rest[:9], rest[9:]
    place = Place(plan)
    own, depth = middle.shape
    rows = qkv_in.shape[0]
    width = att_in.shape[1]
    heads = width // HEAD_DIM
    groups = place.groups
    cut = depth // groups
    moves = Moves(local)
    line = Line(place, *line_refs[:3], PIECES, line_refs[3:])
    order = line.order()
    parts = [moves.start(in_part.at[target], line.own.at[target]) for target in order]
    feeds = [moves.start(activated, act_in), moves.start(w_down, w_d)]
    loads = [moves.start(qkv, qkv_in), moves.start(att, att_in), moves.start(att_grad, grad_in)]
    branch_loads = {}

    def load_slice(number):
        branch_loads[number] = moves.start(branch_all.at[:, pl.ds(number * cut, cut)], branch.at[number % 2])

    for number in range(min(2, groups)):
        load_slice(number)
    place.barrier(line=True)
    scatter = Scatter(place, own, depth, *scatter_refs[:5], scatter_refs[5:])
    for target, copy in zip(order, parts):
        copy.wait()
        line.start(target)
    for copy in feeds:
        copy.wait()
    tile = min(1024, depth)

    def partial(owner, target):
        lines = act_in[pl.ds(pl.multiple_of(owner * own, own), own), :]

        def columns(start):
            target[:, pl.ds(start, tile)] = dot(lines, w_d[:, pl.ds(start, tile)], 1, 0).astype(target.dtype)

        loop(depth, tile, columns)

    scatter.begin(partial)
    ticks = list(line.ticks())
    line.tick(ticks.pop(0))
    starts[...] = segment_starts(bounds, rows)
    bias_out[...] = jnp.zeros_like(bias_out)
    key_grad[...] = jnp.zeros_like(key_grad)
    value_grad[...] = jnp.zeros_like(value_grad)
    for copy in loads:
        copy.wait()
    for number in range(groups):
        branch_loads[number].wait()
        staged[number, :, :] = dot(att_in[...], branch[number % 2], 0, 0).astype(bf16)
        if number + 2 < groups:
            load_slice(number + 2)
    stores = [moves.start(staged, out_part_out)]
    scale = HEAD_DIM ** (-0.5)
    row_in = lax.broadcasted_iota(jnp.int32, (block, block), 0)
    col_in = lax.broadcasted_iota(jnp.int32, (block, block), 1)
    key_in = lax.broadcasted_iota(jnp.int32, (block, 1), 0)

    def attend(index):
        span = pl.ds(index * block, block)
        first = starts[:, span]
        queries, outer, inner, logs = [], [], [], []
        for head in range(heads):
            columns = pl.ds(head * HEAD_DIM, HEAD_DIM)
            queries.append(qkv_in[span, head_columns(0, head, width)])
            outer.append(grad_in[span, columns])
            product = grad_in[span, columns].astype(f32) * att_in[span, columns].astype(f32)
            inner.append(jnp.sum(product.T, axis=0, keepdims=True))
            logs.append(sums[pl.ds(head, 1), span])

        def against(key_block, carry, diagonal):
            key_span = pl.ds(pl.multiple_of(key_block * block, block), block)
            allowed = key_in + key_block * block >= first
            if diagonal:
                allowed = allowed & (row_in <= col_in)
            out = []
            for head in range(heads):
                columns = pl.ds(head * HEAD_DIM, HEAD_DIM)
                keys = qkv_in[key_span, head_columns(1, head, width)]
                values = qkv_in[key_span, head_columns(2, head, width)]
                scores = dot(keys, queries[head], 1, 1) * (scale * LOG2E)
                probs = jnp.exp2(jnp.where(allowed, scores - logs[head], NEGATIVE))
                value_grad[key_span, columns] += dot(probs.astype(bf16), outer[head], 1, 0)
                prob_grad = dot(values, outer[head], 1, 1)
                score_grad = (probs * (prob_grad - inner[head])).astype(bf16)
                key_grad[key_span, columns] += dot(score_grad, queries[head], 1, 0)
                out.append(carry[head] + dot(score_grad, keys, 0, 0))
            return tuple(out)

        carry = tuple(jnp.zeros((block, HEAD_DIM), f32) for head in range(heads))
        if index:
            carry = lax.fori_loop(0, index, lambda key_block, c: against(key_block, c, False), carry)
        carry = against(index, carry, True)
        for head in range(heads):
            query_grad = (carry[head] * scale).astype(bf16)
            qkv_in[span, head_columns(0, head, width)] = query_grad
            columns = pl.ds(head * HEAD_DIM, HEAD_DIM)
            bias_out[0:1, columns] += jnp.sum(query_grad.astype(f32), axis=0, keepdims=True)

    blocks = rows // block
    for index in range(blocks):
        attend(index)
        if index == blocks // 2:
            scatter.middle()
        if index:
            line.tick(ticks.pop(0))
    kept = min(256, rows)

    def write(start):
        span = pl.ds(start, kept)
        qkv_in[span, pl.ds(width, width)] = (key_grad[span, :] * scale).astype(bf16)
        rounded = value_grad[span, :].astype(bf16)
        qkv_in[span, pl.ds(2 * width, width)] = rounded
        bias_out[1:2, :] += jnp.sum(rounded.astype(f32), axis=0, keepdims=True)

    loop(rows, kept, write)
    stores.append(moves.start(qkv_in, qkv_grad_out))

    def close(start, count, value):
        span = pl.ds(start, count)
        result[span, :] = (middle[span, :] + value + down_bias[...]).astype(bf16)

    scatter.end(close)
    stores.append(moves.start(result, block_out))
    for number in ticks:
        line.tick(number)
    line.end(total)
    stores.append(moves.start(total, in_out))
    scatter.finish()
    line.finish()
    for copy in stores:
        copy.wait()


def run_back(
    plan, groups, block, bounds, qkv, att, att_grad, sums, activated, w_down, middle, down_bias, in_part, branch_all
):
    own, depth = middle.shape
    rows, width = att.shape
    hidden = w_down.shape[0]
    cut = depth // groups
    return pl.pallas_call(
        functools.partial(back_kernel, plan, block),
        out_shape=(
            jax.ShapeDtypeStruct((rows, 3 * width), bf16),
            jax.ShapeDtypeStruct((own, depth), bf16),
            jax.ShapeDtypeStruct((8, width), f32),
            jax.ShapeDtypeStruct((cut, hidden), f32),
            jax.ShapeDtypeStruct((groups, width, cut), bf16),
        ),
        in_specs=[SMEM, ANY, ANY, ANY, VMEM, ANY, ANY, VMEM, VMEM, ANY, ANY],
        out_specs=(ANY, ANY, VMEM, ANY, ANY),
        scratch_shapes=[
            pltpu.VMEM((rows, 3 * width), bf16),
            pltpu.VMEM((rows, width), bf16),
            pltpu.VMEM((rows, width), bf16),
            pltpu.VMEM((rows, hidden), bf16),
            pltpu.VMEM((hidden, depth), bf16),
            pltpu.VMEM((1, rows), jnp.int32),
            pltpu.VMEM((rows, width), f32),
            pltpu.VMEM((rows, width), f32),
            pltpu.VMEM((own, depth), bf16),
            pltpu.VMEM((2, rows, cut), bf16),
            pltpu.VMEM((groups, width, cut), bf16),
            pltpu.VMEM((cut, hidden), f32),
            pltpu.SemaphoreType.DMA((40,)),
        ]
        + Scatter.scratch(plan, own, depth, bf16)
        + Line.scratch(groups, cut, hidden, PIECES),
        compiler_params=params(3),
        name="back",
        cost_estimate=cost(75),
    )(bounds, qkv, att, att_grad, sums, activated, w_down, middle, down_bias, in_part, branch_all)


def last_kernel(
    plan, qkv_grad, w_qkv, tok, middle_grad, gain, out_part, first_all, sums2, in_sums, qv_sums,
    input_out, out_out, qkv_out, vectors_out, spread_out,
    g_in, weights, result, first, out_total, qkv_total, wide, many, wide_in, many_in, local, *rest,
):
    scatter_refs, rest = rest[:9], rest[9:]
    out_refs, rest = rest[:7], rest[7:]
    qkv_refs, (wide_send, wide_recv, many_send, many_recv) = rest[:7], rest[7:]
    place = Place(plan)
    own, depth = tok.shape
    width = w_qkv.shape[2]
    groups = place.groups
    cut = depth // groups
    moves = Moves(local)
    out_line = Line(place, *out_refs[:3], 1, out_refs[3:])
    qkv_line = Line(place, *qkv_refs[:3], PIECES, qkv_refs[3:])
    order = qkv_line.order()
    parts = [moves.start(out_part.at[target], out_line.own.at[target]) for target in order]
    loads = [
        moves.start(w_qkv.at[part], weights.at[:, pl.ds(part * width, width)]) for part in range(3)
    ]
    loads.append(moves.start(qkv_grad, g_in))
    first_loads = {}

    def load_slice(number):
        columns = pl.ds(order[number] * cut, cut)
        first_loads[number] = moves.start(first_all.at[:, columns], first.at[number % 2])

    for number in range(min(2, groups)):
        load_slice(number)
    place.barrier(line=True, halves=True)
    scatter = Scatter(place, own, depth, *scatter_refs[:5], scatter_refs[5:])
    for target, copy in zip(order, parts):
        copy.wait()
        out_line.start(target)
    for copy in loads:
        copy.wait()
    tile = min(1024, depth)

    def partial(owner, target):
        lines = g_in[pl.ds(pl.multiple_of(owner * own, own), own), :]

        def columns(start):
            target[:, pl.ds(start, tile)] = dot(lines, weights[pl.ds(start, tile), :], 1, 1).astype(target.dtype)

        loop(depth, tile, columns)

    def qkv_slice(number):
        first_loads[number].wait()
        qkv_line.own[order[number]] = dot(first[number % 2], g_in[...], 0, 0).astype(bf16)
        qkv_line.start(order[number])
        if number + 2 < groups:
            load_slice(number + 2)

    def between(number):
        if number == 0:
            for index in range(groups // 2):
                qkv_slice(index)
        if number == 1:
            for index in range(groups // 2, groups):
                qkv_slice(index)

    scatter.begin(partial, between)
    for number in out_line.ticks():
        out_line.tick(number)
    ticks = list(qkv_line.ticks())
    scatter.middle()
    qkv_line.tick(ticks.pop(0))
    out_line.end(out_total)
    stores = [moves.start(out_total, out_out)]
    wide[...] = jnp.zeros_like(wide)
    wide[2:6, :] = sums2[0:4, :]
    mine = lax.broadcasted_iota(jnp.int32, (many.shape[0], 1), 0) == place.me
    many[:, pl.ds(0, width)] = jnp.where(mine, qv_sums[0:1, :], 0.0)
    many[:, pl.ds(width, width)] = jnp.where(mine, qv_sums[1:2, :], 0.0)
    many[:, pl.ds(2 * width, in_sums.shape[1])] = jnp.where(mine, in_sums[...], 0.0)
    qkv_line.tick(ticks.pop(0))

    def close(start, count, value):
        span = pl.ds(start, count)
        unit, inverse = norm_rows(tok[span, :].astype(f32))
        sum_rows = middle_grad[span, :] + norm_back(value, unit, inverse, gain[...])
        result[span, :] = sum_rows.astype(bf16)
        wide[0:1, :] += jnp.sum(value * unit, axis=0, keepdims=True)
        wide[1:2, :] += jnp.sum(value, axis=0, keepdims=True)

    scatter.end(close)
    stores.append(moves.start(result, input_out))
    qkv_line.tick(ticks.pop(0))
    partners = [place.at(mask) for mask in [1] + plan.bits]
    partners += [place.across(bit) for bit in place.group_bits()]
    for index, partner in enumerate(partners):
        copies = [
            pltpu.make_async_remote_copy(
                src_ref=source.at[index],
                dst_ref=target.at[index],
                send_sem=send.at[index],
                recv_sem=recv.at[index],
                device_id=partner,
                device_id_type=MESH,
            )
            for source, target, send, recv in (
                (wide_in[0], wide_in[1], wide_send, wide_recv),
                (many_in[0], many_in[1], many_send, many_recv),
            )
        ]
        wide_in[0][index] = wide[...]
        many_in[0][index] = many[...]
        for copy in copies:
            copy.start()
        for copy in copies:
            copy.wait_recv()
        wide[...] = wide_in[0][index] + wide_in[1][index]
        many[...] = many_in[0][index] + many_in[1][index]
        for copy in copies:
            copy.wait_send()
    vectors_out[...] = wide[...]
    spread_out[...] = many[...]
    for number in ticks:
        qkv_line.tick(number)
    qkv_line.end(qkv_total)
    for part in range(3):
        stores.append(moves.start(qkv_total.at[:, pl.ds(part * width, width)], qkv_out.at[part]))
    scatter.finish()
    out_line.finish()
    qkv_line.finish()
    for copy in stores:
        copy.wait()


def run_last(plan, groups, qkv_grad, w_qkv, tok, middle_grad, gain, out_part, first_all, sums2, in_sums, qv_sums):
    own, depth = tok.shape
    rows = qkv_grad.shape[0]
    width = w_qkv.shape[2]
    cut = depth // groups
    many = (plan.devices, 2 * width + in_sums.shape[1])
    rounds = (plan.devices.bit_length() - 1) + (groups.bit_length() - 1)

    def kernel(*refs):
        head, tail = refs[: 10 + 5 + 8], refs[10 + 5 + 8 :]
        last_kernel(plan, *head, (tail[0], tail[1]), (tail[2], tail[3]), *tail[4:])

    return pl.pallas_call(
        kernel,
        out_shape=(
            jax.ShapeDtypeStruct((own, depth), bf16),
            jax.ShapeDtypeStruct((width, cut), f32),
            jax.ShapeDtypeStruct((3, cut, width), f32),
            jax.ShapeDtypeStruct((8, depth), f32),
            jax.ShapeDtypeStruct(many, f32),
        ),
        in_specs=[ANY, ANY, VMEM, VMEM, VMEM, ANY, ANY, VMEM, VMEM, VMEM],
        out_specs=(ANY, ANY, ANY, VMEM, VMEM),
        scratch_shapes=[
            pltpu.VMEM((rows, 3 * width), bf16),
            pltpu.VMEM((depth, 3 * width), bf16),
            pltpu.VMEM((own, depth), bf16),
            pltpu.VMEM((2, rows, cut), bf16),
            pltpu.VMEM((width, cut), f32),
            pltpu.VMEM((cut, 3 * width), f32),
            pltpu.VMEM((8, depth), f32),
            pltpu.VMEM(many, f32),
            pltpu.VMEM((rounds, 8, depth), f32),
            pltpu.VMEM((rounds, 8, depth), f32),
            pltpu.VMEM((rounds,) + many, f32),
            pltpu.VMEM((rounds,) + many, f32),
            pltpu.SemaphoreType.DMA((40,)),
        ]
        + Scatter.scratch(plan, own, depth, bf16)
        + Line.scratch(groups, width, cut, 1)
        + Line.scratch(groups, cut, 3 * width, PIECES)
        + [pltpu.SemaphoreType.DMA((rounds,))] * 4,
        compiler_params=params(4),
        name="last",
        cost_estimate=cost(75),
    )(qkv_grad, w_qkv, tok, middle_grad, gain, out_part, first_all, sums2, in_sums, qv_sums)


def segment_bounds(group, seq_lengths, seq_scripts, seq_place):
    count = seq_lengths.shape[0]
    numbers = jnp.arange(count, dtype=jnp.int32)
    order_key = seq_scripts * count + numbers
    same = seq_place[:, None] == seq_place[None, :]
    before = order_key[None, :] < order_key[:, None]
    offsets = jnp.sum(jnp.where(same & before, seq_lengths[None, :], 0), axis=1)
    mine = seq_place == group
    firsts = jnp.where(mine, offsets, 0)
    total = jnp.sum(jnp.where(mine, seq_lengths, 0))
    return jnp.concatenate([firsts, total[None]]).astype(jnp.int32)


def body(
    tokens,
    out_grad,
    seq_lengths,
    seq_scripts,
    seq_place,
    norm1_gain,
    norm1_shift,
    w_qkv,
    qv_bias,
    w_out,
    out_bias,
    norm2_gain,
    norm2_shift,
    w_in,
    in_bias,
    w_down,
    down_bias,
):
    own, depth = tokens.shape
    devices = lax.axis_size("mp")
    plan = Plan(devices)
    rows = own * devices
    width = w_qkv.shape[2]
    block = min(512, rows)
    bounds = segment_bounds(lax.axis_index("batch"), seq_lengths, seq_scripts, seq_place)

    def line(vector):
        return vector.reshape(1, -1)

    bias3 = jnp.concatenate([qv_bias[0], jnp.zeros_like(qv_bias[0]), qv_bias[1]])
    first_all, qkv, att, sums, grad_all = run_first(
        plan, block, tokens, line(norm1_gain), line(norm1_shift), w_qkv, line(bias3), bounds, out_grad
    )
    second_all, activated, hidden_grad, middle, in_part = run_feed(
        plan, tokens, att, w_out, line(out_bias), line(norm2_gain), line(norm2_shift), w_in, line(in_bias),
        w_down, grad_all,
    )

    groups = lax.axis_size("batch")
    middle_grad, branch_all, att_grad, sums2, down_weight_grad, in_part2 = run_middle(
        plan, groups, hidden_grad, w_in, middle, out_grad, line(norm2_gain), w_out, activated, grad_all, second_all
    )
    qkv_grad, block_out, qv_part, in_weight_grad, out_part = run_back(
        plan, groups, block, bounds, qkv, att, att_grad, sums, activated, w_down, middle, line(down_bias),
        in_part2, branch_all,
    )
    input_grad, out_weight_grad, qkv_weight_grad, vectors, spread = run_last(
        plan, groups, qkv_grad, w_qkv, tokens, middle_grad, line(norm1_gain), out_part, first_all, sums2, in_part,
        qv_part,
    )
    qv_bias_grad = jnp.stack([spread[:, :width].reshape(-1), spread[:, width : 2 * width].reshape(-1)])
    return (
        block_out,
        input_grad,
        vectors[0],
        vectors[1],
        qkv_weight_grad,
        qv_bias_grad,
        out_weight_grad,
        vectors[4],
        vectors[2],
        vectors[3],
        in_weight_grad,
        spread[:, 2 * width :].reshape(-1),
        down_weight_grad,
        vectors[5],
    )


def solution(mesh):
    return jax.shard_map(
        body,
        mesh=mesh,
        in_specs=(
            P(("batch", "mp"), None),
            P(("batch", "mp"), None),
            P(),
            P(),
            P(),
            P(),
            P(),
            P(None, None, "mp"),
            P(None, "mp"),
            P("mp", None),
            P(),
            P(),
            P(),
            P(None, "mp"),
            P("mp"),
            P("mp", None),
            P(),
        ),
        out_specs=(
            P(("batch", "mp"), None),
            P(("batch", "mp"), None),
            P(),
            P(),
            P(None, "batch", "mp"),
            P(),
            P("mp", "batch"),
            P(),
            P(),
            P(),
            P("batch", "mp"),
            P(),
            P("mp", "batch"),
            P(),
        ),
        check_vma=False,
    )
```

```python
import functools

import jax
import jax.numpy as jnp
from jax import lax
from jax.experimental import pallas as pl
from jax.experimental.pallas import tpu as pltpu
from jax.sharding import PartitionSpec as P

HEAD_DIM = 128
EPS = 1e-05
NEGATIVE = -1e30
LOG2E = 1.4426950408889634
f32 = jnp.float32
bf16 = jnp.bfloat16
MESH = pl.DeviceIdType.MESH
ANY = pl.BlockSpec(memory_space=pl.ANY)
VMEM = pl.BlockSpec(memory_space=pltpu.VMEM)
SMEM = pl.BlockSpec(memory_space=pltpu.SMEM)


def dot(left, right, contract_left, contract_right):
    return lax.dot_general(
        left,
        right,
        (((contract_left,), (contract_right,)), ((), ())),
        preferred_element_type=f32,
    )


def flip(index, mask):
    bit = 1
    while bit <= mask:
        if mask & bit:
            index = index + bit * (1 - 2 * lax.rem(lax.div(index, bit), 2))
        bit *= 2
    return index


def loop(count, step, body):
    def one(index, carry):
        body(pl.multiple_of(index * step, step))
        return carry

    lax.fori_loop(0, count // step, one, 0)


class Plan:
    def __init__(self, devices, halves=1):
        bits = []
        bit = 2
        while bit < devices:
            bits.append(bit)
            bit *= 2
        self.devices = devices
        self.bits = bits
        self.ways = [tuple(bits)] + ([tuple(reversed(bits))] if len(bits) > 1 else [])
        self.halves = halves
        self.orders = self.ways * halves
        self.parts = len(self.orders)
        self.offsets = list(range(0, devices, 2))
        self.keys = [(part, offset) for part in range(self.parts) for offset in self.offsets if offset]
        self.keys.sort(key=lambda key: (self.half(key[0]), bin(key[1]).count("1"), self.last(*key)))
        self.shares = [(part, offset) for offset in self.offsets for part in range(self.parts)]

    def half(self, part):
        return part // len(self.ways)

    def parts_of(self, half):
        return range(half * len(self.ways), (half + 1) * len(self.ways))

    def last(self, part, offset):
        steps = [step for step, bit in enumerate(self.orders[part]) if bit & offset]
        return max(steps) if steps else -1

    def bit(self, part, offset):
        return self.orders[part][self.last(part, offset)]

    def later(self, part, offset):
        order = self.orders[part]
        return [offset | order[step] for step in range(self.last(part, offset) + 1, len(order))]


class Place:
    def __init__(self, plan):
        self.plan = plan
        self.batch = lax.axis_index("batch")
        self.groups = lax.axis_size("batch")
        self.me = lax.axis_index("mp")

    def at(self, mask):
        return (self.batch, flip(self.me, mask))

    def beside(self, step):
        return (self.batch + step, self.me)

    def around(self, step):
        return (lax.rem(self.batch + step, self.groups), self.me)

    def barrier(self, groups=False):
        semaphore = pltpu.get_barrier_semaphore()
        partners = [self.at(mask) for mask in [1] + self.plan.bits]
        if groups:
            partners += [self.around(step) for step in range(1, self.groups)]
        for partner in partners:
            pl.semaphore_signal(semaphore, inc=1, device_id=partner, device_id_type=MESH)
        pl.semaphore_wait(semaphore, len(partners))


class Total:
    def __init__(self, place, value, sent, came, slots, sems):
        self.place, self.value, self.sent, self.came, self.slots = place, value, sent, came, slots
        self.send, self.recv, self.slot_send, self.slot_recv = sems

    def plane(self, others=()):
        totals = (self,) + tuple(others)
        for index, mask in enumerate([1] + self.place.plan.bits):
            copies = [
                pltpu.make_async_remote_copy(
                    src_ref=total.sent.at[index],
                    dst_ref=total.came.at[index],
                    send_sem=total.send.at[index],
                    recv_sem=total.recv.at[index],
                    device_id=self.place.at(mask),
                    device_id_type=MESH,
                )
                for total in totals
            ]
            for total, copy in zip(totals, copies):
                total.sent[index] = total.value[...]
                copy.start()
            for total, copy in zip(totals, copies):
                copy.wait_recv()
                total.value[...] = total.sent[index] + total.came[index]
                copy.wait_send()

    def slot(self, step):
        return pltpu.make_async_remote_copy(
            src_ref=self.value,
            dst_ref=self.slots.at[step],
            send_sem=self.slot_send.at[step - 1],
            recv_sem=self.slot_recv.at[step - 1],
            device_id=self.place.around(step),
            device_id_type=MESH,
        )

    def begin(self):
        self.slots[0] = self.value[...]
        for step in range(1, self.place.groups):
            self.slot(step).start()

    def end(self, result):
        for step in range(1, self.place.groups):
            self.slot(step).wait()
        groups = self.place.groups
        total = self.slots[self.place.batch]
        for group in range(1, groups):
            total = total + self.slots[lax.rem(self.place.batch + groups - group, groups)]
        result[...] = total

    @staticmethod
    def scratch(plan, groups, shape):
        rounds = len(plan.bits) + 1
        return [
            pltpu.VMEM(shape, f32),
            pltpu.VMEM((rounds,) + shape, f32),
            pltpu.VMEM((rounds,) + shape, f32),
            pltpu.VMEM((groups,) + shape, f32),
            pltpu.SemaphoreType.DMA((rounds,)),
            pltpu.SemaphoreType.DMA((rounds,)),
            pltpu.SemaphoreType.DMA((max(groups - 1, 1),)),
            pltpu.SemaphoreType.DMA((max(groups - 1, 1),)),
        ]


class Gather:
    def __init__(self, place, buf, own, rows, sems):
        self.place, self.plan, self.buf, self.own, self.rows = place, place.plan, buf, own, rows
        self.link_send, self.link_recv, self.core_send, self.core_recv = sems
        self.part_rows = rows // self.plan.parts

    def span(self, mask, part):
        block = flip(self.place.me, mask)
        start = block * self.rows + part * self.part_rows
        return self.buf.at[pl.ds(pl.multiple_of(start, self.part_rows), self.part_rows), :]

    def source(self, offset, part):
        if offset == 0 and self.own is not None:
            return self.own.at[pl.ds(part * self.part_rows, self.part_rows), :]
        return self.span(offset, part)

    def link(self, key):
        part, offset = key
        bit = self.plan.bit(part, offset)
        index = self.plan.keys.index(key)
        return pltpu.make_async_remote_copy(
            src_ref=self.source(offset ^ bit, part),
            dst_ref=self.span(offset ^ bit, part),
            send_sem=self.link_send.at[index],
            recv_sem=self.link_recv.at[index],
            device_id=self.place.at(bit),
            device_id_type=MESH,
        )

    def core(self, key):
        part, offset = key
        index = self.plan.shares.index(key)
        return pltpu.make_async_remote_copy(
            src_ref=self.source(offset, part),
            dst_ref=self.span(offset, part),
            send_sem=self.core_send.at[index],
            recv_sem=self.core_recv.at[index],
            device_id=self.place.at(1),
            device_id_type=MESH,
        )

    def landed(self, ref, semaphore):
        pltpu.make_async_remote_copy(
            src_ref=ref,
            dst_ref=ref,
            send_sem=semaphore,
            recv_sem=semaphore,
            device_id=self.place.at(1),
            device_id_type=MESH,
        ).wait_recv()

    def start(self, half=0):
        for part in self.plan.parts_of(half):
            self.core((part, 0)).start()
        for key in self.plan.keys:
            if bin(key[1]).count("1") == 1 and self.plan.half(key[0]) == half:
                self.link(key).start()

    def arrive(self, key):
        part, offset = key
        self.landed(self.span(offset, part), self.link_recv.at[self.plan.keys.index(key)])
        for target in self.plan.later(part, offset):
            self.link((part, target)).start()
        self.core(key).start()

    def share(self, offset, half=0):
        for part in self.plan.parts_of(half):
            index = self.plan.shares.index((part, offset))
            self.landed(self.span(offset | 1, part), self.core_recv.at[index])

    def steps(self):
        result = []
        for half in range(self.plan.halves):
            for count in range(1, len(self.plan.bits) + 1):
                keys = [
                    key
                    for key in self.plan.keys
                    if self.plan.half(key[0]) == half and bin(key[1]).count("1") == count
                ]
                offsets = [offset for offset in self.plan.offsets if bin(offset).count("1") == count]
                result.append((half, keys, offsets))
        return result

    def pieces(self, offset, half):
        count = self.rows // self.plan.halves
        chip = lax.div(flip(self.place.me, offset), 2) * 2
        return [
            pl.ds(pl.multiple_of((chip + core) * self.rows + half * count, count), count) for core in range(2)
        ]

    def finish(self):
        for key in self.plan.keys:
            self.link(key).wait_send()
        for key in self.plan.shares:
            self.core(key).wait_send()

    @staticmethod
    def semaphores(plan):
        return [pltpu.SemaphoreType.DMA((len(plan.keys),))] * 2 + [
            pltpu.SemaphoreType.DMA((len(plan.shares),))
        ] * 2


class Scatter:
    def __init__(self, place, rows, width, core_out, core_in, kept, link_out, link_in, sems):
        self.place, self.plan, self.rows, self.width = place, place.plan, rows, width
        self.core_out, self.core_in, self.kept = core_out, core_in, kept
        self.link_out, self.link_in = link_out, link_in
        self.link_send, self.link_recv, self.core_send, self.core_recv = sems
        self.part_rows = rows // self.plan.parts
        self.step = min(32, self.part_rows)
        self.order = sorted(self.plan.offsets, key=lambda offset: -bin(offset).count("1"))

    def core(self, offset):
        index = offset // 2
        return pltpu.make_async_remote_copy(
            src_ref=self.core_out.at[index],
            dst_ref=self.core_in.at[index],
            send_sem=self.core_send.at[index],
            recv_sem=self.core_recv.at[index],
            device_id=self.place.at(1),
            device_id_type=MESH,
        )

    def link(self, key):
        index = self.plan.keys.index(key)
        return pltpu.make_async_remote_copy(
            src_ref=self.link_out.at[index],
            dst_ref=self.link_in.at[index],
            send_sem=self.link_send.at[index],
            recv_sem=self.link_recv.at[index],
            device_id=self.place.at(self.plan.bit(*key)),
            device_id_type=MESH,
        )

    def total(self, offset, part, start, arrived):
        rows = pl.ds(pl.multiple_of(part * self.part_rows + start, self.step), self.step)
        value = self.kept[offset // 2, rows, :].astype(f32) + self.core_in[offset // 2, rows, :].astype(f32)
        for key in arrived:
            value += self.link_in[self.plan.keys.index(key), pl.ds(start, self.step), :].astype(f32)
        return value

    def pass_on(self, part, offset):
        arrived = [(part, target) for target in self.plan.later(part, offset)]
        for key in arrived:
            self.link(key).wait_recv()
        index = self.plan.keys.index((part, offset))

        def add(start):
            self.link_out[index, pl.ds(start, self.step), :] = self.total(
                offset, part, start, arrived
            ).astype(bf16)

        loop(self.part_rows, self.step, add)
        self.link((part, offset)).start()

    def free(self, offset, half):
        for part in self.plan.parts_of(half):
            if offset and not self.plan.later(part, offset):
                self.pass_on(part, offset)

    def bound(self, half):
        for offset in self.order:
            for part in self.plan.parts_of(half):
                if offset and self.plan.later(part, offset):
                    self.pass_on(part, offset)

    def begin(self, partial, between=None):
        for number, offset in enumerate(self.order):
            index = offset // 2
            if offset == 0:
                self.bound(0)
            partial(flip(self.place.me, offset | 1), self.core_out.at[index])
            self.core(offset).start()
            partial(flip(self.place.me, offset), self.kept.at[index])
            self.core(offset).wait_recv()
            for half in range(self.plan.halves):
                self.free(offset, half)
            if between is not None:
                between(number)

    def middle(self):
        for half in range(1, self.plan.halves):
            self.bound(half)

    def end(self, use, half=0):
        for part in self.plan.parts_of(half):
            arrived = [(part, target) for target in self.plan.later(part, 0)]
            for key in arrived:
                self.link(key).wait_recv()

            def piece(start):
                row = pl.multiple_of(part * self.part_rows + start, self.step)
                use(row, self.step, self.total(0, part, start, arrived))

            loop(self.part_rows, self.step, piece)

    def finish(self):
        for key in self.plan.keys:
            self.link(key).wait_send()
        for offset in self.plan.offsets:
            self.core(offset).wait_send()

    @staticmethod
    def scratch(plan, rows, width, kept):
        chips, keys = len(plan.offsets), len(plan.keys)
        return [
            pltpu.VMEM((chips, rows, width), bf16),
            pltpu.VMEM((chips, rows, width), bf16),
            pltpu.VMEM((chips, rows, width), kept),
            pltpu.VMEM((keys, rows // plan.parts, width), bf16),
            pltpu.VMEM((keys, rows // plan.parts, width), bf16),
            pltpu.SemaphoreType.DMA((keys,)),
            pltpu.SemaphoreType.DMA((keys,)),
            pltpu.SemaphoreType.DMA((chips,)),
            pltpu.SemaphoreType.DMA((chips,)),
        ]


class Line:
    def __init__(self, place, own, up, down, pieces, sems):
        self.place, self.own, self.up, self.down, self.pieces = place, own, up, down, pieces
        self.groups, self.batch = place.groups, place.batch
        self.rows = own.shape[1] // pieces
        self.step = min(32, self.rows)
        self.sems = sems

    def span(self, piece):
        start = piece * self.rows
        return pl.ds(start if isinstance(start, int) else pl.multiple_of(start, self.rows), self.rows)

    def slot(self, upward, target):
        return self.up.at[target - 1] if upward else self.down.at[target]

    def copy(self, upward, target, piece, source):
        send, recv = self.sems[:2] if upward else self.sems[2:]
        index = target * self.pieces + piece
        return pltpu.make_async_remote_copy(
            src_ref=source.at[self.span(piece), :],
            dst_ref=self.slot(upward, target).at[self.span(piece), :],
            send_sem=send.at[index],
            recv_sem=recv.at[index],
            device_id=self.place.beside(1 if upward else -1),
            device_id_type=MESH,
        )

    def start(self, target, near=None, pieces=None):
        if target > 0 and near in (None, target == 1):

            @pl.when(self.batch == 0)
            def first():
                for piece in range(self.pieces) if pieces is None else pieces:
                    self.copy(True, target, piece, self.own.at[target]).start()

        if target < self.groups - 1 and near in (None, target == self.groups - 2):

            @pl.when(self.batch == self.groups - 1)
            def last():
                for piece in range(self.pieces) if pieces is None else pieces:
                    self.copy(False, target, piece, self.own.at[target]).start()

    def start_near(self, pieces=None):
        for target in range(self.groups):
            self.start(target, True, pieces)

    def order(self):
        count = self.groups
        result = []
        for index in range((count + 1) // 2):
            for target in (count - 1 - index, index):
                if target not in result:
                    result.append(target)
        return result

    def ticks(self):
        return range(1, (self.groups - 1) * self.pieces + self.groups)

    def tick(self, number):
        for upward in (True, False):
            place = self.batch if upward else self.groups - 1 - self.batch
            for distance in range(2, self.groups):
                target = distance if upward else self.groups - 1 - distance
                piece = number - (self.groups - 1 - distance) * self.pieces - place
                due = (place > 0) & (place < distance) & (piece >= 0) & (piece < self.pieces)

                @pl.when(due)
                def forward():
                    slot = self.slot(upward, target)
                    copy = self.copy(upward, target, piece, slot)
                    copy.wait_recv()

                    def add(start):
                        rows = pl.ds(pl.multiple_of(piece * self.rows + start, self.step), self.step)
                        total = slot[rows, :].astype(f32) + self.own[target, rows, :].astype(f32)
                        slot[rows, :] = total.astype(bf16)

                    loop(self.rows, self.step, add)
                    copy.start()

    def export(self, outs, moves, columns=None):
        below, above = self.batch > 0, self.batch < self.groups - 1
        jobs = []
        for out, there, upward in ((outs[0], None, None), (outs[1], below, True), (outs[2], above, False)):
            slot = self.own.at[self.batch] if there is None else self.slot(upward, self.batch)
            if columns is None:
                copies = [moves.make(slot, out)]
            else:
                copies = [
                    moves.make(slot.at[:, pl.ds(part * columns, columns)], out.at[part])
                    for part in range(out.shape[0])
                ]
            jobs.append((there, copies))

            def begin():
                if there is not None:
                    for piece in range(self.pieces):
                        self.copy(upward, self.batch, piece, slot).wait_recv()
                for copy in copies:
                    copy.start()

            begin() if there is None else pl.when(there)(begin)

        def wait():
            for there, copies in jobs:

                def done():
                    for copy in copies:
                        copy.wait()

                done() if there is None else pl.when(there)(done)

        return wait

    def finish(self):
        for target in range(self.groups):
            for upward in (True, False):
                if target == (0 if upward else self.groups - 1):
                    continue

                @pl.when(self.batch < target if upward else self.batch > target)
                def sent():
                    slot = self.slot(upward, target)
                    for piece in range(self.pieces):
                        self.copy(upward, target, piece, slot).wait_send()

    @staticmethod
    def scratch(groups, rows, columns, pieces):
        return [
            pltpu.VMEM((groups, rows, columns), bf16),
            pltpu.VMEM((groups - 1, rows, columns), bf16),
            pltpu.VMEM((groups - 1, rows, columns), bf16),
        ] + [pltpu.SemaphoreType.DMA((groups * pieces,))] * 4


class Moves:
    def __init__(self, sems):
        self.sems, self.count = sems, 0

    def make(self, source, target):
        copy = pltpu.make_async_copy(source, target, self.sems.at[self.count])
        self.count += 1
        return copy

    def start(self, source, target):
        copy = self.make(source, target)
        copy.start()
        return copy


def norm_rows(rows):
    mean = jnp.mean(rows, axis=-1, keepdims=True)
    centred = rows - mean
    inverse = lax.rsqrt(jnp.mean(centred * centred, axis=-1, keepdims=True) + EPS)
    return centred * inverse, inverse


def norm_back(grad, unit, inverse, gain):
    scaled = grad * gain
    return inverse * (
        scaled
        - jnp.mean(scaled, axis=-1, keepdims=True)
        - unit * jnp.mean(scaled * unit, axis=-1, keepdims=True)
    )


def segment_starts(group, lengths, scripts, places, rows):
    position = lax.broadcasted_iota(jnp.int32, (1, rows), 1)
    first = jnp.zeros((1, rows), jnp.int32)
    count = lengths.shape[0]
    number = [lengths[index] for index in range(count)]
    script = [scripts[index] for index in range(count)]
    mine = [places[index] == group for index in range(count)]
    own = [jnp.where(mine[index], number[index], 0) for index in range(count)]
    total = own[0]
    for index in range(1, count):
        total = total + own[index]
    for index in range(count):
        offset = jnp.int32(0)
        for other in range(count):
            if other < index:
                offset = offset + jnp.where(script[other] <= script[index], own[other], 0)
            elif other > index:
                offset = offset + jnp.where(script[other] < script[index], own[other], 0)
        bound = jnp.where(mine[index], offset, 0)
        first = jnp.maximum(first, jnp.where(position >= bound, bound, 0))
    return jnp.maximum(first, jnp.where(position >= total, total, 0))


def head_columns(part, head, width):
    return pl.ds(part * width + head * HEAD_DIM, HEAD_DIM)


def first_kernel(
    plan, block, tok, gain, shift, w_qkv, qv_bias, lengths, scripts, places, out_grad, first_out, qkv_out, att_out,
    sum_out, grad_out, buf, weights, qkv, starts, sums, attended, local, *sems,
):
    place = Place(plan)
    own, depth = tok.shape
    rows = buf.shape[0]
    width = w_qkv.shape[2]
    moves = Moves(local)
    loads = [
        moves.start(w_qkv.at[part], weights.at[:, pl.ds(part * width, width)]) for part in range(3)
    ]
    place.barrier()
    step = min(32, own)
    mine = pl.multiple_of(place.me * own, own)

    def normalise(start):
        unit, _ = norm_rows(tok[pl.ds(start, step), :].astype(f32))
        buf[pl.ds(pl.multiple_of(mine + start, step), step), :] = (unit * gain[...] + shift[...]).astype(bf16)

    loop(own, step, normalise)
    gather = Gather(place, buf, None, own, sems[:4])
    gather.start()
    stores = [moves.start(out_grad, grad_out.at[pl.ds(mine, own), :])]
    starts[...] = segment_starts(place.batch, lengths, scripts, places, rows)
    for copy in loads:
        copy.wait()

    def project(offset):
        chip = lax.div(flip(place.me, offset), 2)
        span = pl.ds(pl.multiple_of(chip * 2 * own, 2 * own), 2 * own)
        stores.append(moves.start(buf.at[span, :], first_out.at[span, :]))
        product = dot(buf[span, :], weights[...], 1, 0)
        qkv[span, 0:width] = (product[:, 0:width] + qv_bias[0:1, :]).astype(bf16)
        qkv[span, width : 2 * width] = product[:, width : 2 * width].astype(bf16)
        qkv[span, 2 * width : 3 * width] = (product[:, 2 * width :] + qv_bias[1:2, :]).astype(bf16)

    gather.share(0)
    project(0)
    steps = gather.steps()
    grads = Gather(place, grad_out, out_grad, own, sems[4:])
    for number, (half, keys, offsets) in enumerate(steps):
        for key in keys:
            gather.arrive(key)
        if number == max(len(steps) - 2, 0):
            grads.start()
        for offset in offsets:
            gather.share(offset)
            project(offset)
    gather.finish()
    gather = grads
    stores.append(moves.start(qkv, qkv_out))

    scale = HEAD_DIM ** (-0.5) * LOG2E
    heads = width // HEAD_DIM
    row_in = lax.broadcasted_iota(jnp.int32, (block, block), 0)
    col_in = lax.broadcasted_iota(jnp.int32, (block, block), 1)
    key_in = lax.broadcasted_iota(jnp.int32, (block, 1), 0)

    def attend(index):
        span = pl.ds(index * block, block)
        first = starts[:, span]
        queries = [qkv[span, head_columns(0, head, width)] for head in range(heads)]

        def against(key_block, carry, diagonal):
            key_span = pl.ds(pl.multiple_of(key_block * block, block), block)
            allowed = key_in + key_block * block >= first
            if diagonal:
                allowed = allowed & (row_in <= col_in)
            result = []
            for head in range(heads):
                top, total, mixed = carry[head]
                keys = qkv[key_span, head_columns(1, head, width)]
                values = qkv[key_span, head_columns(2, head, width)]
                scores = jnp.where(allowed, dot(keys, queries[head], 1, 1) * scale, NEGATIVE)
                new_top = jnp.maximum(top, jnp.max(scores, axis=0, keepdims=True))
                exps = jnp.exp2(scores - new_top)
                fade = jnp.exp2(top - new_top)
                total = total * fade + jnp.sum(exps, axis=0, keepdims=True)
                mixed = mixed * fade + dot(values, exps.astype(bf16), 0, 0)
                result.append((new_top, total, mixed))
            return tuple(result)

        carry = tuple(
            (
                jnp.full((1, block), NEGATIVE, f32),
                jnp.zeros((1, block), f32),
                jnp.zeros((HEAD_DIM, block), f32),
            )
            for head in range(heads)
        )
        if index:
            carry = lax.fori_loop(0, index, lambda key_block, c: against(key_block, c, False), carry)
        carry = against(index, carry, True)
        for head in range(heads):
            top, total, mixed = carry[head]
            attended[span, pl.ds(head * HEAD_DIM, HEAD_DIM)] = (mixed * (1.0 / total)).T.astype(bf16)
            sums[pl.ds(head, 1), span] = top + jnp.log2(total)

    blocks = rows // block
    taken = 0
    for index in range(blocks):
        attend(index)
        if index >= blocks - 2 and taken < len(steps):
            for key in steps[taken][1]:
                gather.arrive(key)
            taken += 1
    stores.append(moves.start(attended, att_out))
    stores.append(moves.start(sums, sum_out))
    while taken < len(steps):
        for key in steps[taken][1]:
            gather.arrive(key)
        taken += 1
    for offset in plan.offsets:
        gather.share(offset)
    gather.finish()
    for copy in stores:
        copy.wait()


def params(number):
    return pltpu.CompilerParams(
        collective_id=number, has_side_effects=True, vmem_limit_bytes=62 * 2**20
    )


def cost(micros):
    return pl.CostEstimate(flops=micros * 10**9, bytes_accessed=10**7, transcendentals=0)


def run_first(plan, block, tok, gain, shift, w_qkv, qv_bias, order, out_grad):
    own, depth = tok.shape
    rows = own * plan.devices
    width = w_qkv.shape[2]
    heads = width // HEAD_DIM
    return pl.pallas_call(
        functools.partial(first_kernel, plan, block),
        out_shape=(
            jax.ShapeDtypeStruct((rows, depth), bf16),
            jax.ShapeDtypeStruct((rows, 3 * width), bf16),
            jax.ShapeDtypeStruct((rows, width), bf16),
            jax.ShapeDtypeStruct((8, rows), f32),
            jax.ShapeDtypeStruct((rows, depth), bf16),
        ),
        in_specs=[VMEM, VMEM, VMEM, ANY, VMEM, SMEM, SMEM, SMEM, ANY],
        out_specs=(ANY,) * 5,
        scratch_shapes=[
            pltpu.VMEM((rows, depth), bf16),
            pltpu.VMEM((depth, 3 * width), bf16),
            pltpu.VMEM((rows, 3 * width), bf16),
            pltpu.VMEM((1, rows), jnp.int32),
            pltpu.VMEM((8, rows), f32),
            pltpu.VMEM((rows, width), bf16),
            pltpu.SemaphoreType.DMA((16,)),
        ]
        + Gather.semaphores(plan) * 2,
        compiler_params=params(0),
        name="first",
        cost_estimate=cost(80),
    )(tok, gain, shift, w_qkv, qv_bias, *order, out_grad)


def joined(ref, pieces):
    return jnp.concatenate([ref[piece, :] for piece in pieces], axis=0)


def feed_kernel(
    plan, tok, att, w_out, out_bias, gain, shift, w_in, in_bias, w_down, grad_all,
    second_out, act_out, hidden_out, middle_out, bias_out,
    att_in, w_o, w_i, w_d, grad_in, up, buf, act, back, middle, local, *rest,
):
    scatter_refs, gather_sems = rest[:9], rest[9:]
    place = Place(plan)
    own, depth = tok.shape
    rows = buf.shape[0]
    hidden_width = w_in.shape[1]
    chip_rows = 2 * own
    moves = Moves(local)
    load_att = moves.start(att, att_in)
    load_out = moves.start(w_out, w_o)
    load_down = moves.start(w_down, w_d)
    grad_loads = {}

    def load_grad(number):
        lines = pl.ds(number * chip_rows, chip_rows)
        grad_loads[number] = moves.start(grad_all.at[lines, :], grad_in.at[number % 2])

    load_grad(0)
    load_grad(1)
    load_in = moves.start(w_in, w_i)
    place.barrier()
    scatter = Scatter(place, own, depth, *scatter_refs[:5], scatter_refs[5:])
    load_att.wait()
    load_out.wait()
    tile = min(1024, depth)

    def partial(owner, target):
        lines = att_in[pl.ds(pl.multiple_of(owner * own, own), own), :]

        def columns(start):
            target[:, pl.ds(start, tile)] = dot(lines, w_o[:, pl.ds(start, tile)], 1, 0).astype(target.dtype)

        loop(depth, tile, columns)

    part_cols = min(512, hidden_width)
    chips = rows // chip_rows

    def raise_grad(number):
        grad_loads[number].wait()

        def columns(start):
            cols = pl.ds(start, part_cols)
            up[pl.ds(number * chip_rows, chip_rows), cols] = dot(grad_in[number % 2], w_d[cols, :], 1, 1)

        loop(hidden_width, part_cols, columns)
        if number + 2 < chips:
            load_grad(number + 2)

    scatter.begin(partial)
    scatter.middle()
    load_down.wait()
    for number in range(chips):
        raise_grad(number)
    mine = pl.multiple_of(place.me * own, own)

    def close(start, count, value):
        span = pl.ds(start, count)
        total = tok[span, :].astype(f32) + value + out_bias[...]
        middle[span, :] = total
        unit, _ = norm_rows(total)
        buf[pl.ds(pl.multiple_of(mine + start, count), count), :] = (unit * gain[...] + shift[...]).astype(bf16)

    gather = Gather(place, buf, None, own, gather_sems)
    for half in range(plan.halves):
        scatter.end(close, half)
        gather.start(half)
    scatter.finish()
    stores = [moves.start(middle, middle_out)]
    load_in.wait()
    bias_out[...] = jnp.zeros_like(bias_out)

    def expand(offset, half):
        pieces = gather.pieces(offset, half)
        count = own // plan.halves

        def columns(start):
            cols = pl.ds(start, part_cols)
            pre = dot(joined(buf, pieces), w_i[:, cols], 1, 0) + in_bias[:, cols]
            raised = jnp.concatenate([up[piece, cols] for piece in pieces], axis=0)
            root = 0.7978845608028654
            square = pre * pre
            inner = jnp.tanh(root * (pre + 0.044715 * (square * pre)))
            rise = 0.5 * (1.0 + inner)
            slope = rise + 0.5 * pre * (1.0 - inner * inner) * (root * (1.0 + 3 * 0.044715 * square))
            lifted = (pre * rise).astype(bf16)
            down = (raised * slope).astype(bf16)
            for index, piece in enumerate(pieces):
                act[piece, cols] = lifted[index * count : (index + 1) * count]
                back[piece, cols] = down[index * count : (index + 1) * count]
            bias_out[:, cols] += jnp.sum(down.astype(f32), axis=0, keepdims=True)

        loop(hidden_width, part_cols, columns)
        for piece in pieces:
            stores.append(moves.start(buf.at[piece, :], second_out.at[piece, :]))
            stores.append(moves.start(act.at[piece, :], act_out.at[piece, :]))
            stores.append(moves.start(back.at[piece, :], hidden_out.at[piece, :]))

    for half in range(plan.halves):
        gather.share(0, half)
        expand(0, half)
    for half, keys, offsets in gather.steps():
        for key in keys:
            gather.arrive(key)
        for offset in offsets:
            gather.share(offset, half)
            expand(offset, half)
    gather.finish()
    for copy in stores:
        copy.wait()


def run_feed(plan, tok, att, w_out, out_bias, gain, shift, w_in, in_bias, w_down, grad_all):
    own, depth = tok.shape
    rows = own * plan.devices
    width = att.shape[1]
    hidden = w_in.shape[1]
    return pl.pallas_call(
        functools.partial(feed_kernel, plan),
        out_shape=(
            jax.ShapeDtypeStruct((rows, depth), bf16),
            jax.ShapeDtypeStruct((rows, hidden), bf16),
            jax.ShapeDtypeStruct((rows, hidden), bf16),
            jax.ShapeDtypeStruct((own, depth), f32),
            jax.ShapeDtypeStruct((1, hidden), f32),
        ),
        in_specs=[VMEM, ANY, ANY, VMEM, VMEM, VMEM, ANY, VMEM, ANY, ANY],
        out_specs=(ANY, ANY, ANY, ANY, VMEM),
        scratch_shapes=[
            pltpu.VMEM((rows, width), bf16),
            pltpu.VMEM((width, depth), bf16),
            pltpu.VMEM((depth, hidden), bf16),
            pltpu.VMEM((hidden, depth), bf16),
            pltpu.VMEM((2, 2 * own, depth), bf16),
            pltpu.VMEM((rows, hidden), f32),
            pltpu.VMEM((rows, depth), bf16),
            pltpu.VMEM((rows, hidden), bf16),
            pltpu.VMEM((rows, hidden), bf16),
            pltpu.VMEM((own, depth), f32),
            pltpu.SemaphoreType.DMA((128,)),
        ]
        + Scatter.scratch(plan, own, depth, bf16)
        + Gather.semaphores(plan),
        compiler_params=params(1),
        name="feed",
        cost_estimate=cost(90),
    )(tok, att, w_out, out_bias, gain, shift, w_in, in_bias, w_down, grad_all)


PIECES = 2


def add_parts(place, parts, target):
    below, above = place.batch > 0, place.batch < place.groups - 1
    step = min(32, target.shape[0])

    def add(chosen):
        def rows_of(start):
            rows = pl.ds(start, step)
            value = chosen[0][rows, :].astype(f32)
            for part in chosen[1:]:
                value += part[rows, :].astype(f32)
            target[rows, :] = value

        loop(target.shape[0], step, rows_of)

    pl.when(jnp.logical_not(above))(lambda: add([parts[0], parts[1]]))
    pl.when(jnp.logical_not(below))(lambda: add([parts[0], parts[2]]))
    pl.when(below & above)(lambda: add(parts))


def spread_rows(place, target, rows):
    mine = lax.broadcasted_iota(jnp.int32, (target.shape[0], 1), 0) == place.me
    start = 0
    for row in rows:
        target[:, pl.ds(start, row.shape[1])] = jnp.where(mine, row, 0.0)
        start += row.shape[1]


def middle_kernel(
    plan, hidden_grad, w_in, middle, out_grad, gain, w_out, activated, grad_all, second_all, in_sums,
    middle_grad_out, branch_out, att_grad_out, sums_out, in_sums_out, down_out0, down_out1, down_out2, in_part_out,
    h_in, w_i, w_o, buf, middle_grad, att_grad, act, staged, local, *rest,
):
    down_outs = (down_out0, down_out1, down_out2)
    scatter_refs, gather_sems, line_refs, total_refs = rest[:9], rest[9:13], rest[13:20], rest[20:]
    place = Place(plan)
    own, depth = middle.shape
    rows = buf.shape[0]
    chip_rows = 2 * own
    hidden = w_in.shape[1]
    groups = place.groups
    cut = depth // groups
    moves = Moves(local)
    loads = [moves.start(hidden_grad, h_in), moves.start(w_in, w_i)]
    load_act = moves.start(activated, act)
    order = [index for pair in zip(range(groups - 1, -1, -1), range(groups)) for index in pair][:groups]
    load_grad = [
        moves.start(grad_all.at[:, pl.ds(target * cut, cut)], buf.at[:, pl.ds(target * cut, cut)])
        for target in order
    ]
    load_out = moves.start(w_out, w_o)
    place.barrier(groups=True)
    scatter = Scatter(place, own, depth, *scatter_refs[:5], scatter_refs[5:])
    line = Line(place, *line_refs[:3], PIECES, line_refs[3:])
    tile = min(1024, depth)

    def partial(owner, target):
        lines = h_in[pl.ds(pl.multiple_of(owner * own, own), own), :]

        def columns(start):
            target[:, pl.ds(start, tile)] = dot(lines, w_i[pl.ds(start, tile), :], 1, 1).astype(target.dtype)

        loop(depth, tile, columns)

    part = min(512, hidden)

    def down_slice(index):
        target = order[index]
        load_grad[index].wait()

        def piece(start):
            line.own[target, pl.ds(start, part), :] = dot(
                act[:, pl.ds(start, part)], buf[:, pl.ds(target * cut, cut)], 0, 0
            ).astype(bf16)

        loop(hidden, part, piece)
        line.start(target, False)

    for copy in loads:
        copy.wait()

    def between(number):
        if number == 0:
            load_act.wait()
            for index in range(groups // 2):
                down_slice(index)
        if number == min(2, len(plan.offsets) - 1):
            for index in range(groups // 2, groups):
                down_slice(index)
            line.start_near()

    scatter.begin(partial, between)

    in_stores = []
    in_loads = {}

    def load_slice(number):
        columns = pl.ds(number * cut, cut)
        in_loads[number] = moves.start(second_all.at[:, columns], act.at[:, pl.ds((number % 2) * cut, cut)])

    def in_slice(number):
        in_loads[number].wait()
        if number >= 2:
            in_stores[number - 2].wait()
        slot = number % 2

        def piece(start):
            columns = pl.ds(start, part)
            staged[slot, :, columns] = dot(
                act[:, pl.ds(slot * cut, cut)], h_in[:, columns], 0, 0
            ).astype(bf16)

        loop(hidden, part, piece)
        in_stores.append(moves.start(staged.at[slot], in_part_out.at[number]))
        if number + 2 < groups:
            load_slice(number + 2)

    ticks = list(line.ticks())
    for number in range(min(2, groups)):
        load_slice(number)
    line.tick(ticks.pop(0))
    scatter.middle()
    half_groups = groups // 2
    for number in range(half_groups):
        in_slice(number)
    line.tick(ticks.pop(0))
    mine = pl.multiple_of(place.me * own, own)
    totals = [
        Total(place, *total_refs[index : index + 4], total_refs[index + 4 : index + 8]) for index in (0, 8)
    ]
    own_sums = totals[0].value
    own_sums[...] = jnp.zeros_like(own_sums)
    totals[1].value[...] = in_sums[...]

    def close(start, count, value):
        span = pl.ds(start, count)
        unit, inverse = norm_rows(middle[span, :])
        sum_rows = out_grad[span, :].astype(f32) + norm_back(value, unit, inverse, gain[...])
        middle_grad[span, :] = sum_rows
        buf[pl.ds(pl.multiple_of(mine + start, count), count), :] = sum_rows.astype(bf16)
        own_sums[0:1, :] += jnp.sum(value * unit, axis=0, keepdims=True)
        own_sums[1:2, :] += jnp.sum(value, axis=0, keepdims=True)
        own_sums[2:3, :] += jnp.sum(sum_rows, axis=0, keepdims=True)
        own_sums[3:4, :] += jnp.sum(out_grad[span, :].astype(f32), axis=0, keepdims=True)

    gather = Gather(place, buf, None, own, gather_sems)
    for half in range(plan.halves):
        scatter.end(close, half)
        gather.start(half)
    for total in totals:
        total.begin()
    line.tick(ticks.pop(0))
    scatter.finish()
    stores = [moves.start(middle_grad, middle_grad_out)]
    load_out.wait()

    def project(offset, half):
        pieces = gather.pieces(offset, half)
        count = own // plan.halves
        product = dot(joined(buf, pieces), w_o[...], 1, 1).astype(bf16)
        for index, piece in enumerate(pieces):
            att_grad[piece, :] = product[index * count : (index + 1) * count]
            stores.append(moves.start(buf.at[piece, :], branch_out.at[piece, :]))

    for half in range(plan.halves):
        gather.share(0, half)
        project(0, half)
    for number in range(half_groups, groups):
        in_slice(number)
    line.tick(ticks.pop(0))
    for half, keys, offsets in gather.steps():
        for key in keys:
            gather.arrive(key)
        for offset in offsets:
            gather.share(offset, half)
            project(offset, half)
    stores.append(moves.start(att_grad, att_grad_out))
    for number in ticks:
        line.tick(number)
    exported = line.export(down_outs, moves)
    for total, total_out in zip(totals, (sums_out, in_sums_out)):
        total.end(total_out)
    gather.finish()
    line.finish()
    for copy in stores + in_stores[-2:]:
        copy.wait()
    exported()


def run_middle(plan, groups, hidden_grad, w_in, middle, out_grad, gain, w_out, activated, grad_all, second_all, in_sums):
    own, depth = middle.shape
    rows = own * plan.devices
    width = w_out.shape[0]
    hidden = w_in.shape[1]
    cut = depth // groups
    return pl.pallas_call(
        functools.partial(middle_kernel, plan),
        out_shape=(
            jax.ShapeDtypeStruct((own, depth), f32),
            jax.ShapeDtypeStruct((rows, depth), bf16),
            jax.ShapeDtypeStruct((rows, width), bf16),
            jax.ShapeDtypeStruct((4, depth), f32),
            jax.ShapeDtypeStruct(in_sums.shape, f32),
        )
        + (jax.ShapeDtypeStruct((hidden, cut), bf16),) * 3
        + (jax.ShapeDtypeStruct((groups, cut, hidden), bf16),),
        in_specs=[ANY, ANY, VMEM, VMEM, VMEM, ANY, ANY, ANY, ANY, VMEM],
        out_specs=(ANY, ANY, ANY, VMEM, VMEM, ANY, ANY, ANY, ANY),
        scratch_shapes=[
            pltpu.VMEM((rows, hidden), bf16),
            pltpu.VMEM((depth, hidden), bf16),
            pltpu.VMEM((width, depth), bf16),
            pltpu.VMEM((rows, depth), bf16),
            pltpu.VMEM((own, depth), f32),
            pltpu.VMEM((rows, width), bf16),
            pltpu.VMEM((rows, max(hidden, 2 * cut)), bf16),
            pltpu.VMEM((2, cut, hidden), bf16),
            pltpu.SemaphoreType.DMA((64,)),
        ]
        + Scatter.scratch(plan, own, depth, bf16)
        + Gather.semaphores(plan)
        + Line.scratch(groups, hidden, cut, PIECES)
        + Total.scratch(plan, groups, (4, depth))
        + Total.scratch(plan, groups, in_sums.shape),
        compiler_params=params(2),
        name="middle",
        cost_estimate=cost(80),
    )(hidden_grad, w_in, middle, out_grad, gain, w_out, activated, grad_all, second_all, in_sums)


def back_kernel(
    plan, block, lengths, scripts, places, qkv, att, att_grad, sums, activated, w_down, middle, down_bias, in_part, branch_all, sums2, in_sums,
    down0, down1, down2,
    qkv_grad_out, block_out, down_out, in_out0, in_out1, in_out2, out_part_out, vectors_out, spread_out,
    qkv_in, att_in, grad_in, act_in, w_d, starts, key_grad, value_grad, result, branch, staged, bias_out, down_sum,
    local,
    *rest,
):
    in_outs = (in_out0, in_out1, in_out2)
    scatter_refs, line_refs, total_refs = rest[:9], rest[9:16], rest[16:]
    place = Place(plan)
    own, depth = middle.shape
    rows = qkv_in.shape[0]
    width = att_in.shape[1]
    heads = width // HEAD_DIM
    groups = place.groups
    cut = depth // groups
    moves = Moves(local)
    line = Line(place, *line_refs[:3], PIECES, line_refs[3:])
    order = line.order()
    parts = [moves.start(in_part.at[target], line.own.at[target]) for target in order]
    feeds = [moves.start(activated, act_in), moves.start(w_down, w_d)]
    loads = [moves.start(qkv, qkv_in), moves.start(att, att_in), moves.start(att_grad, grad_in)]
    branch_loads = {}

    def load_slice(number):
        branch_loads[number] = moves.start(branch_all.at[:, pl.ds(number * cut, cut)], branch.at[number % 2])

    for number in range(min(2, groups)):
        load_slice(number)
    place.barrier(groups=True)
    scatter = Scatter(place, own, depth, *scatter_refs[:5], scatter_refs[5:])
    for target, copy in zip(order, parts):
        copy.wait()
        line.start(target, False)
    line.start_near()
    for copy in feeds:
        copy.wait()
    tile = min(1024, depth)

    def partial(owner, target):
        lines = act_in[pl.ds(pl.multiple_of(owner * own, own), own), :]

        def columns(start):
            target[:, pl.ds(start, tile)] = dot(lines, w_d[:, pl.ds(start, tile)], 1, 0).astype(target.dtype)

        loop(depth, tile, columns)

    scatter.begin(partial)
    ticks = list(line.ticks())
    line.tick(ticks.pop(0))
    starts[...] = segment_starts(place.batch, lengths, scripts, places, rows)
    bias_out[...] = jnp.zeros_like(bias_out)
    key_grad[...] = jnp.zeros_like(key_grad)
    value_grad[...] = jnp.zeros_like(value_grad)
    for copy in loads:
        copy.wait()
    for number in range(groups):
        branch_loads[number].wait()
        staged[number, :, :] = dot(att_in[...], branch[number % 2], 0, 0).astype(bf16)
        if number + 2 < groups:
            load_slice(number + 2)
    stores = [moves.start(staged, out_part_out)]
    down_rows = down_sum.shape[0]
    fit = rows // down_rows
    down_parts = [
        branch.at[index // fit, pl.ds((index % fit) * down_rows, down_rows), :] for index in range(3)
    ]
    down_loads = [moves.start(part, target) for part, target in zip((down0, down1, down2), down_parts)]
    scale = HEAD_DIM ** (-0.5)
    row_in = lax.broadcasted_iota(jnp.int32, (block, block), 0)
    col_in = lax.broadcasted_iota(jnp.int32, (block, block), 1)
    key_in = lax.broadcasted_iota(jnp.int32, (block, 1), 0)

    def attend(index):
        span = pl.ds(index * block, block)
        first = starts[:, span]
        queries, outer, inner, logs = [], [], [], []
        for head in range(heads):
            columns = pl.ds(head * HEAD_DIM, HEAD_DIM)
            queries.append(qkv_in[span, head_columns(0, head, width)])
            outer.append(grad_in[span, columns])
            product = grad_in[span, columns].astype(f32) * att_in[span, columns].astype(f32)
            inner.append(jnp.sum(product.T, axis=0, keepdims=True))
            logs.append(sums[pl.ds(head, 1), span])

        def against(key_block, carry, diagonal):
            key_span = pl.ds(pl.multiple_of(key_block * block, block), block)
            allowed = key_in + key_block * block >= first
            if diagonal:
                allowed = allowed & (row_in <= col_in)
            out = []
            for head in range(heads):
                columns = pl.ds(head * HEAD_DIM, HEAD_DIM)
                keys = qkv_in[key_span, head_columns(1, head, width)]
                values = qkv_in[key_span, head_columns(2, head, width)]
                scores = dot(keys, queries[head], 1, 1) * (scale * LOG2E)
                probs = jnp.exp2(jnp.where(allowed, scores - logs[head], NEGATIVE))
                value_grad[key_span, columns] += dot(probs.astype(bf16), outer[head], 1, 0)
                prob_grad = dot(values, outer[head], 1, 1)
                score_grad = (probs * (prob_grad - inner[head])).astype(bf16)
                key_grad[key_span, columns] += dot(score_grad, queries[head], 1, 0)
                out.append(carry[head] + dot(score_grad, keys, 0, 0))
            return tuple(out)

        carry = tuple(jnp.zeros((block, HEAD_DIM), f32) for head in range(heads))
        if index:
            carry = lax.fori_loop(0, index, lambda key_block, c: against(key_block, c, False), carry)
        carry = against(index, carry, True)
        for head in range(heads):
            query_grad = (carry[head] * scale).astype(bf16)
            qkv_in[span, head_columns(0, head, width)] = query_grad
            columns = pl.ds(head * HEAD_DIM, HEAD_DIM)
            bias_out[0:1, columns] += jnp.sum(query_grad.astype(f32), axis=0, keepdims=True)

    blocks = rows // block
    for index in range(blocks):
        attend(index)
        if index == blocks // 2:
            scatter.middle()
        if 0 < index < blocks - 1:
            line.tick(ticks.pop(0))
    kept = min(256, rows)

    def write(start):
        span = pl.ds(start, kept)
        qkv_in[span, pl.ds(width, width)] = (key_grad[span, :] * scale).astype(bf16)
        rounded = value_grad[span, :].astype(bf16)
        qkv_in[span, pl.ds(2 * width, width)] = rounded
        bias_out[1:2, :] += jnp.sum(rounded.astype(f32), axis=0, keepdims=True)

    loop(rows, kept, write)
    stores.append(moves.start(qkv_in, qkv_grad_out))
    for number in ticks:
        line.tick(number)
    for copy in down_loads:
        copy.wait()
    add_parts(place, down_parts, down_sum)
    stores.append(moves.start(down_sum, down_out))

    def close(start, count, value):
        span = pl.ds(start, count)
        result[span, :] = (middle[span, :] + value + down_bias[...]).astype(bf16)

    for half in range(plan.halves):
        scatter.end(close, half)
    stores.append(moves.start(result, block_out))
    vectors = Total(place, *total_refs[:4], total_refs[4:8])
    spread = Total(place, *total_refs[8:12], total_refs[12:])
    vectors.value[...] = sums2[...]
    spread_rows(place, spread.value, [bias_out[0:1, :], bias_out[1:2, :], in_sums[...]])
    vectors.plane([spread])
    vectors_out[...] = vectors.value[...]
    spread_out[...] = spread.value[...]
    exported = line.export(in_outs, moves)
    scatter.finish()
    line.finish()
    for copy in stores:
        copy.wait()
    exported()


def run_back(
    plan, groups, block, order, qkv, att, att_grad, sums, activated, w_down, middle, down_bias, in_part, branch_all,
    sums2, in_sums, down_parts,
):
    own, depth = middle.shape
    rows, width = att.shape
    hidden = w_down.shape[0]
    cut = depth // groups
    return pl.pallas_call(
        functools.partial(back_kernel, plan, block),
        out_shape=(
            jax.ShapeDtypeStruct((rows, 3 * width), bf16),
            jax.ShapeDtypeStruct((own, depth), bf16),
            jax.ShapeDtypeStruct((hidden, cut), f32),
            jax.ShapeDtypeStruct((cut, hidden), bf16),
            jax.ShapeDtypeStruct((cut, hidden), bf16),
            jax.ShapeDtypeStruct((cut, hidden), bf16),
            jax.ShapeDtypeStruct((groups, width, cut), bf16),
            jax.ShapeDtypeStruct(sums2.shape, f32),
            jax.ShapeDtypeStruct((plan.devices, 2 * width + hidden), f32),
        ),
        in_specs=[SMEM, SMEM, SMEM, ANY, ANY, ANY, VMEM, ANY, ANY, VMEM, VMEM, ANY, ANY, VMEM, VMEM, ANY, ANY, ANY],
        out_specs=(ANY, ANY, ANY, ANY, ANY, ANY, ANY, VMEM, VMEM),
        scratch_shapes=[
            pltpu.VMEM((rows, 3 * width), bf16),
            pltpu.VMEM((rows, width), bf16),
            pltpu.VMEM((rows, width), bf16),
            pltpu.VMEM((rows, hidden), bf16),
            pltpu.VMEM((hidden, depth), bf16),
            pltpu.VMEM((1, rows), jnp.int32),
            pltpu.VMEM((rows, width), f32),
            pltpu.VMEM((rows, width), f32),
            pltpu.VMEM((own, depth), bf16),
            pltpu.VMEM((2, rows, cut), bf16),
            pltpu.VMEM((groups, width, cut), bf16),
            pltpu.VMEM((2, width), f32),
            pltpu.VMEM((hidden, cut), f32),
            pltpu.SemaphoreType.DMA((64,)),
        ]
        + Scatter.scratch(plan, own, depth, bf16)
        + Line.scratch(groups, cut, hidden, PIECES)
        + Total.scratch(plan, 1, sums2.shape)
        + Total.scratch(plan, 1, (plan.devices, 2 * width + hidden)),
        compiler_params=params(3),
        name="back",
        cost_estimate=cost(75),
    )(*order, qkv, att, att_grad, sums, activated, w_down, middle, down_bias, in_part, branch_all, sums2, in_sums, *down_parts)


def last_kernel(
    plan, qkv_grad, w_qkv, tok, middle_grad, gain, out_part, first_all, qv_sums,
    in0, in1, in2,
    input_out, in_out, out_out0, out_out1, out_out2, qkv_out0, qkv_out1, qkv_out2, vectors_out, spread_out,
    g_in, weights, result, first, in_parts, in_sum, local, *rest,
):
    out_outs = (out_out0, out_out1, out_out2)
    qkv_outs = (qkv_out0, qkv_out1, qkv_out2)
    scatter_refs, rest = rest[:9], rest[9:]
    out_refs, rest = rest[:7], rest[7:]
    qkv_refs, total_refs = rest[:7], rest[7:]
    place = Place(plan)
    own, depth = tok.shape
    width = w_qkv.shape[2]
    groups = place.groups
    cut = depth // groups
    moves = Moves(local)
    out_line = Line(place, *out_refs[:3], 1, out_refs[3:])
    qkv_line = Line(place, *qkv_refs[:3], PIECES, qkv_refs[3:])
    order = qkv_line.order()
    parts = [moves.start(out_part.at[target], out_line.own.at[target]) for target in order]
    loads = [
        moves.start(w_qkv.at[part], weights.at[:, pl.ds(part * width, width)]) for part in range(3)
    ]
    loads.append(moves.start(qkv_grad, g_in))
    first_loads = {}

    def load_slice(number):
        columns = pl.ds(order[number] * cut, cut)
        first_loads[number] = moves.start(first_all.at[:, columns], first.at[number % 2])

    for number in range(min(2, groups)):
        load_slice(number)
    in_loads = [moves.start(part, in_parts.at[index]) for index, part in enumerate((in0, in1, in2))]
    place.barrier(groups=True)
    scatter = Scatter(place, own, depth, *scatter_refs[:5], scatter_refs[5:])
    for target, copy in zip(order, parts):
        copy.wait()
        out_line.start(target, False)
    out_line.start_near()
    for copy in loads:
        copy.wait()
    tile = min(1024, depth)

    def partial(owner, target):
        lines = g_in[pl.ds(pl.multiple_of(owner * own, own), own), :]

        def columns(start):
            target[:, pl.ds(start, tile)] = dot(lines, weights[pl.ds(start, tile), :], 1, 1).astype(target.dtype)

        loop(depth, tile, columns)

    def qkv_slice(number):
        first_loads[number].wait()
        qkv_line.own[order[number]] = dot(first[number % 2], g_in[...], 0, 0).astype(bf16)
        qkv_line.start(order[number], False)
        if number + 2 < groups:
            load_slice(number + 2)

    def between(number):
        if number == 0:
            for index in range(groups // 2):
                qkv_slice(index)
        if number == 1:
            for index in range(groups // 2, groups):
                qkv_slice(index)
            qkv_line.start_near(range(PIECES - 1))

    scatter.begin(partial, between)
    for number in out_line.ticks():
        out_line.tick(number)
    ticks = list(qkv_line.ticks())
    scatter.middle()
    qkv_line.tick(ticks.pop(0))
    exported = [out_line.export(out_outs, moves)]
    stores = []
    totals = [
        Total(place, *total_refs[index : index + 4], total_refs[index + 4 : index + 8]) for index in (0, 8)
    ]
    vectors, spread = totals
    spread.value[...] = qv_sums[...]
    for copy in in_loads:
        copy.wait()
    add_parts(place, [in_parts.at[index] for index in range(3)], in_sum)
    stores.append(moves.start(in_sum, in_out))
    vectors.value[...] = jnp.zeros_like(vectors.value)
    qkv_line.tick(ticks.pop(0))

    def close(start, count, value):
        span = pl.ds(start, count)
        unit, inverse = norm_rows(tok[span, :].astype(f32))
        sum_rows = middle_grad[span, :] + norm_back(value, unit, inverse, gain[...])
        result[span, :] = sum_rows.astype(bf16)
        vectors.value[0:1, :] += jnp.sum(value * unit, axis=0, keepdims=True)
        vectors.value[1:2, :] += jnp.sum(value, axis=0, keepdims=True)

    for half in range(plan.halves):
        scatter.end(close, half)
    stores.append(moves.start(result, input_out))
    qkv_line.tick(ticks.pop(0))
    vectors.plane()
    for total in totals:
        total.begin()
    qkv_line.start_near([PIECES - 1])
    for number in ticks:
        qkv_line.tick(number)
    exported.append(qkv_line.export(qkv_outs, moves, width))
    scatter.finish()
    out_line.finish()
    qkv_line.finish()
    for total, result_out in zip(totals, (vectors_out, spread_out)):
        total.end(result_out)
    for copy in stores:
        copy.wait()
    for wait in exported:
        wait()


def run_last(plan, groups, qkv_grad, w_qkv, tok, middle_grad, gain, out_part, first_all, qv_sums, in_parts):
    own, depth = tok.shape
    rows = qkv_grad.shape[0]
    width = w_qkv.shape[2]
    cut = depth // groups
    return pl.pallas_call(
        functools.partial(last_kernel, plan),
        out_shape=(
            jax.ShapeDtypeStruct((own, depth), bf16),
            jax.ShapeDtypeStruct(in_parts[0].shape, f32),
        )
        + (jax.ShapeDtypeStruct((width, cut), bf16),) * 3
        + (jax.ShapeDtypeStruct((3, cut, width), bf16),) * 3
        + (
            jax.ShapeDtypeStruct((2, depth), f32),
            jax.ShapeDtypeStruct((plan.devices, 2 * width), f32),
        ),
        in_specs=[ANY, ANY, VMEM, VMEM, VMEM, ANY, ANY, VMEM, ANY, ANY, ANY],
        out_specs=(ANY,) * 8 + (VMEM,) * 2,
        scratch_shapes=[
            pltpu.VMEM((rows, 3 * width), bf16),
            pltpu.VMEM((depth, 3 * width), bf16),
            pltpu.VMEM((own, depth), bf16),
            pltpu.VMEM((2, rows, cut), bf16),
            pltpu.VMEM((3,) + in_parts[0].shape, bf16),
            pltpu.VMEM(in_parts[0].shape, f32),
            pltpu.SemaphoreType.DMA((64,)),
        ]
        + Scatter.scratch(plan, own, depth, bf16)
        + Line.scratch(groups, width, cut, 1)
        + Line.scratch(groups, cut, 3 * width, PIECES)
        + Total.scratch(plan, groups, (2, depth))
        + Total.scratch(plan, groups, (plan.devices, 2 * width)),
        compiler_params=params(4),
        name="last",
        cost_estimate=cost(75),
    )(qkv_grad, w_qkv, tok, middle_grad, gain, out_part, first_all, qv_sums, *in_parts)


def body(
    tokens,
    out_grad,
    seq_lengths,
    seq_scripts,
    seq_place,
    norm1_gain,
    norm1_shift,
    w_qkv,
    qv_bias,
    w_out,
    out_bias,
    norm2_gain,
    norm2_shift,
    w_in,
    in_bias,
    w_down,
    down_bias,
):
    own, depth = tokens.shape
    devices = lax.axis_size("mp")
    plan = Plan(devices)
    fine = Plan(devices, 2)
    rows = own * devices
    width = w_qkv.shape[2]
    block = min(512, rows)
    order = (seq_lengths, seq_scripts, seq_place)

    def line(vector):
        return vector.reshape(1, -1)

    first_all, qkv, att, sums, grad_all = run_first(
        plan, block, tokens, line(norm1_gain), line(norm1_shift), w_qkv, qv_bias, order, out_grad
    )
    second_all, activated, hidden_grad, middle, in_part = run_feed(
        fine, tokens, att, w_out, line(out_bias), line(norm2_gain), line(norm2_shift), w_in, line(in_bias),
        w_down, grad_all,
    )

    groups = lax.axis_size("batch")
    batch = lax.axis_index("batch")

    def added(parts):
        total = parts[0].astype(f32)
        total += jnp.where(batch > 0, parts[1].astype(f32), 0.0)
        return total + jnp.where(batch < groups - 1, parts[2].astype(f32), 0.0)

    middle_grad, branch_all, att_grad, sums2, in_sums, *down_parts, in_part2 = run_middle(
        fine, groups, hidden_grad, w_in, middle, out_grad, line(norm2_gain), w_out, activated, grad_all, second_all,
        in_part,
    )
    qkv_grad, block_out, down_weight_grad, *in_parts, out_part, vectors2, spread2 = run_back(
        plan, groups, block, order, qkv, att, att_grad, sums, activated, w_down, middle, line(down_bias),
        in_part2, branch_all, sums2, in_sums, down_parts,
    )
    input_grad, in_weight_grad, *weight_parts, vectors, spread = run_last(
        plan, groups, qkv_grad, w_qkv, tokens, middle_grad, line(norm1_gain), out_part, first_all,
        spread2[:, : 2 * width], in_parts,
    )
    qv_bias_grad = jnp.stack([spread[:, :width].reshape(-1), spread[:, width:].reshape(-1)])
    return (
        block_out,
        input_grad,
        vectors[0],
        vectors[1],
        added(weight_parts[3:]),
        qv_bias_grad,
        added(weight_parts[:3]),
        vectors2[2],
        vectors2[0],
        vectors2[1],
        in_weight_grad,
        spread2[:, 2 * width :].reshape(-1),
        down_weight_grad,
        vectors2[3],
    )


def solution(mesh):
    return jax.shard_map(
        body,
        mesh=mesh,
        in_specs=(
            P(("batch", "mp"), None),
            P(("batch", "mp"), None),
            P(),
            P(),
            P(),
            P(),
            P(),
            P(None, None, "mp"),
            P(None, "mp"),
            P("mp", None),
            P(),
            P(),
            P(),
            P(None, "mp"),
            P("mp"),
            P("mp", None),
            P(),
        ),
        out_specs=(
            P(("batch", "mp"), None),
            P(("batch", "mp"), None),
            P(),
            P(),
            P(None, "batch", "mp"),
            P(),
            P("mp", "batch"),
            P(),
            P(),
            P(),
            P("batch", "mp"),
            P(),
            P("mp", "batch"),
            P(),
        ),
        check_vma=False,
    )
```

```python
import functools

import jax
import jax.numpy as jnp
from jax import lax
from jax.experimental import pallas as pl
from jax.experimental.pallas import tpu as pltpu
from jax.sharding import PartitionSpec as P

HEAD_DIM = 128
EPS = 1e-05
NEGATIVE = -1e30
LOG2E = 1.4426950408889634
f32 = jnp.float32
bf16 = jnp.bfloat16
MESH = pl.DeviceIdType.MESH
ANY = pl.BlockSpec(memory_space=pl.ANY)
VMEM = pl.BlockSpec(memory_space=pltpu.VMEM)
SMEM = pl.BlockSpec(memory_space=pltpu.SMEM)


def dot(left, right, contract_left, contract_right):
    return lax.dot_general(
        left,
        right,
        (((contract_left,), (contract_right,)), ((), ())),
        preferred_element_type=f32,
    )


def flip(index, mask):
    bit = 1
    while bit <= mask:
        if mask & bit:
            index = index + bit * (1 - 2 * lax.rem(lax.div(index, bit), 2))
        bit *= 2
    return index


def loop(count, step, body):
    def one(index, carry):
        body(pl.multiple_of(index * step, step))
        return carry

    lax.fori_loop(0, count // step, one, 0)


class Plan:
    def __init__(self, devices, halves=1):
        bits = []
        bit = 2
        while bit < devices:
            bits.append(bit)
            bit *= 2
        self.devices = devices
        self.bits = bits
        self.ways = [tuple(bits)] + ([tuple(reversed(bits))] if len(bits) > 1 else [])
        self.halves = halves
        self.orders = self.ways * halves
        self.parts = len(self.orders)
        self.offsets = list(range(0, devices, 2))
        self.keys = [(part, offset) for part in range(self.parts) for offset in self.offsets if offset]
        self.keys.sort(key=lambda key: (self.half(key[0]), bin(key[1]).count("1"), self.last(*key)))
        self.shares = [(part, offset) for offset in self.offsets for part in range(self.parts)]

    def half(self, part):
        return part // len(self.ways)

    def parts_of(self, half):
        return range(half * len(self.ways), (half + 1) * len(self.ways))

    def last(self, part, offset):
        steps = [step for step, bit in enumerate(self.orders[part]) if bit & offset]
        return max(steps) if steps else -1

    def bit(self, part, offset):
        return self.orders[part][self.last(part, offset)]

    def later(self, part, offset):
        order = self.orders[part]
        return [offset | order[step] for step in range(self.last(part, offset) + 1, len(order))]


class Place:
    def __init__(self, plan):
        self.plan = plan
        self.batch = lax.axis_index("batch")
        self.groups = lax.axis_size("batch")
        self.me = lax.axis_index("mp")

    def at(self, mask):
        return (self.batch, flip(self.me, mask))

    def beside(self, step):
        return (self.batch + step, self.me)

    def around(self, step):
        return (lax.rem(self.batch + step, self.groups), self.me)

    def barrier(self, groups=False):
        semaphore = pltpu.get_barrier_semaphore()
        partners = [self.at(mask) for mask in [1] + self.plan.bits]
        if groups:
            partners += [self.around(step) for step in range(1, self.groups)]
        for partner in partners:
            pl.semaphore_signal(semaphore, inc=1, device_id=partner, device_id_type=MESH)
        pl.semaphore_wait(semaphore, len(partners))


class Total:
    def __init__(self, place, value, sent, came, slots, sems):
        self.place, self.value, self.sent, self.came, self.slots = place, value, sent, came, slots
        self.send, self.recv, self.slot_send, self.slot_recv = sems

    def plane(self, others=()):
        totals = (self,) + tuple(others)
        for index, mask in enumerate([1] + self.place.plan.bits):
            copies = [
                pltpu.make_async_remote_copy(
                    src_ref=total.sent.at[index],
                    dst_ref=total.came.at[index],
                    send_sem=total.send.at[index],
                    recv_sem=total.recv.at[index],
                    device_id=self.place.at(mask),
                    device_id_type=MESH,
                )
                for total in totals
            ]
            for total, copy in zip(totals, copies):
                total.sent[index] = total.value[...]
                copy.start()
            for total, copy in zip(totals, copies):
                copy.wait_recv()
                total.value[...] = total.sent[index] + total.came[index]
                copy.wait_send()

    def slot(self, step):
        return pltpu.make_async_remote_copy(
            src_ref=self.value,
            dst_ref=self.slots.at[step],
            send_sem=self.slot_send.at[step - 1],
            recv_sem=self.slot_recv.at[step - 1],
            device_id=self.place.around(step),
            device_id_type=MESH,
        )

    def begin(self):
        self.slots[0] = self.value[...]
        for step in range(1, self.place.groups):
            self.slot(step).start()

    def end(self, result):
        for step in range(1, self.place.groups):
            self.slot(step).wait()
        groups = self.place.groups
        total = self.slots[self.place.batch]
        for group in range(1, groups):
            total = total + self.slots[lax.rem(self.place.batch + groups - group, groups)]
        result[...] = total

    @staticmethod
    def scratch(plan, groups, shape):
        rounds = len(plan.bits) + 1
        return [
            pltpu.VMEM(shape, f32),
            pltpu.VMEM((rounds,) + shape, f32),
            pltpu.VMEM((rounds,) + shape, f32),
            pltpu.VMEM((groups,) + shape, f32),
            pltpu.SemaphoreType.DMA((rounds,)),
            pltpu.SemaphoreType.DMA((rounds,)),
            pltpu.SemaphoreType.DMA((max(groups - 1, 1),)),
            pltpu.SemaphoreType.DMA((max(groups - 1, 1),)),
        ]


class Gather:
    def __init__(self, place, buf, own, rows, sems):
        self.place, self.plan, self.buf, self.own, self.rows = place, place.plan, buf, own, rows
        self.link_send, self.link_recv, self.core_send, self.core_recv = sems
        self.part_rows = rows // self.plan.parts

    def span(self, mask, part):
        block = flip(self.place.me, mask)
        start = block * self.rows + part * self.part_rows
        return self.buf.at[pl.ds(pl.multiple_of(start, self.part_rows), self.part_rows), :]

    def source(self, offset, part):
        if offset == 0 and self.own is not None:
            return self.own.at[pl.ds(part * self.part_rows, self.part_rows), :]
        return self.span(offset, part)

    def link(self, key):
        part, offset = key
        bit = self.plan.bit(part, offset)
        index = self.plan.keys.index(key)
        return pltpu.make_async_remote_copy(
            src_ref=self.source(offset ^ bit, part),
            dst_ref=self.span(offset ^ bit, part),
            send_sem=self.link_send.at[index],
            recv_sem=self.link_recv.at[index],
            device_id=self.place.at(bit),
            device_id_type=MESH,
        )

    def core(self, key):
        part, offset = key
        index = self.plan.shares.index(key)
        return pltpu.make_async_remote_copy(
            src_ref=self.source(offset, part),
            dst_ref=self.span(offset, part),
            send_sem=self.core_send.at[index],
            recv_sem=self.core_recv.at[index],
            device_id=self.place.at(1),
            device_id_type=MESH,
        )

    def landed(self, ref, semaphore):
        pltpu.make_async_remote_copy(
            src_ref=ref,
            dst_ref=ref,
            send_sem=semaphore,
            recv_sem=semaphore,
            device_id=self.place.at(1),
            device_id_type=MESH,
        ).wait_recv()

    def start(self, half=0):
        for part in self.plan.parts_of(half):
            self.core((part, 0)).start()
        for key in self.plan.keys:
            if bin(key[1]).count("1") == 1 and self.plan.half(key[0]) == half:
                self.link(key).start()

    def arrive(self, key):
        part, offset = key
        self.landed(self.span(offset, part), self.link_recv.at[self.plan.keys.index(key)])
        for target in self.plan.later(part, offset):
            self.link((part, target)).start()
        self.core(key).start()

    def share(self, offset, half=0):
        for part in self.plan.parts_of(half):
            index = self.plan.shares.index((part, offset))
            self.landed(self.span(offset | 1, part), self.core_recv.at[index])

    def steps(self):
        result = []
        for half in range(self.plan.halves):
            for count in range(1, len(self.plan.bits) + 1):
                keys = [
                    key
                    for key in self.plan.keys
                    if self.plan.half(key[0]) == half and bin(key[1]).count("1") == count
                ]
                offsets = [offset for offset in self.plan.offsets if bin(offset).count("1") == count]
                result.append((half, keys, offsets))
        return result

    def pieces(self, offset, half):
        count = self.rows // self.plan.halves
        chip = lax.div(flip(self.place.me, offset), 2) * 2
        return [
            pl.ds(pl.multiple_of((chip + core) * self.rows + half * count, count), count) for core in range(2)
        ]

    def finish(self):
        for key in self.plan.keys:
            self.link(key).wait_send()
        for key in self.plan.shares:
            self.core(key).wait_send()

    @staticmethod
    def semaphores(plan):
        return [pltpu.SemaphoreType.DMA((len(plan.keys),))] * 2 + [
            pltpu.SemaphoreType.DMA((len(plan.shares),))
        ] * 2


class Scatter:
    def __init__(self, place, rows, width, core_out, core_in, kept, link_out, link_in, sems):
        self.place, self.plan, self.rows, self.width = place, place.plan, rows, width
        self.core_out, self.core_in, self.kept = core_out, core_in, kept
        self.link_out, self.link_in = link_out, link_in
        self.link_send, self.link_recv, self.core_send, self.core_recv = sems
        self.part_rows = rows // self.plan.parts
        self.step = min(32, self.part_rows)
        self.order = sorted(self.plan.offsets, key=lambda offset: -bin(offset).count("1"))

    def core(self, offset):
        index = offset // 2
        return pltpu.make_async_remote_copy(
            src_ref=self.core_out.at[index],
            dst_ref=self.core_in.at[index],
            send_sem=self.core_send.at[index],
            recv_sem=self.core_recv.at[index],
            device_id=self.place.at(1),
            device_id_type=MESH,
        )

    def link(self, key):
        index = self.plan.keys.index(key)
        return pltpu.make_async_remote_copy(
            src_ref=self.link_out.at[index],
            dst_ref=self.link_in.at[index],
            send_sem=self.link_send.at[index],
            recv_sem=self.link_recv.at[index],
            device_id=self.place.at(self.plan.bit(*key)),
            device_id_type=MESH,
        )

    def total(self, offset, part, start, arrived):
        rows = pl.ds(pl.multiple_of(part * self.part_rows + start, self.step), self.step)
        value = self.kept[offset // 2, rows, :].astype(f32) + self.core_in[offset // 2, rows, :].astype(f32)
        for key in arrived:
            value += self.link_in[self.plan.keys.index(key), pl.ds(start, self.step), :].astype(f32)
        return value

    def pass_on(self, part, offset):
        arrived = [(part, target) for target in self.plan.later(part, offset)]
        for key in arrived:
            self.link(key).wait_recv()
        index = self.plan.keys.index((part, offset))

        def add(start):
            self.link_out[index, pl.ds(start, self.step), :] = self.total(
                offset, part, start, arrived
            ).astype(bf16)

        loop(self.part_rows, self.step, add)
        self.link((part, offset)).start()

    def free(self, offset, half):
        for part in self.plan.parts_of(half):
            if offset and not self.plan.later(part, offset):
                self.pass_on(part, offset)

    def bound(self, half):
        for offset in self.order:
            for part in self.plan.parts_of(half):
                if offset and self.plan.later(part, offset):
                    self.pass_on(part, offset)

    def begin(self, partial, between=None):
        for number, offset in enumerate(self.order):
            index = offset // 2
            if offset == 0:
                self.bound(0)
            partial(flip(self.place.me, offset | 1), self.core_out.at[index])
            self.core(offset).start()
            partial(flip(self.place.me, offset), self.kept.at[index])
            self.core(offset).wait_recv()
            for half in range(self.plan.halves):
                self.free(offset, half)
            if between is not None:
                between(number)

    def middle(self):
        for half in range(1, self.plan.halves):
            self.bound(half)

    def end(self, use, half=0):
        for part in self.plan.parts_of(half):
            arrived = [(part, target) for target in self.plan.later(part, 0)]
            for key in arrived:
                self.link(key).wait_recv()

            def piece(start):
                row = pl.multiple_of(part * self.part_rows + start, self.step)
                use(row, self.step, self.total(0, part, start, arrived))

            loop(self.part_rows, self.step, piece)

    def finish(self):
        for key in self.plan.keys:
            self.link(key).wait_send()
        for offset in self.plan.offsets:
            self.core(offset).wait_send()

    @staticmethod
    def scratch(plan, rows, width, kept):
        chips, keys = len(plan.offsets), len(plan.keys)
        return [
            pltpu.VMEM((chips, rows, width), bf16),
            pltpu.VMEM((chips, rows, width), bf16),
            pltpu.VMEM((chips, rows, width), kept),
            pltpu.VMEM((keys, rows // plan.parts, width), bf16),
            pltpu.VMEM((keys, rows // plan.parts, width), bf16),
            pltpu.SemaphoreType.DMA((keys,)),
            pltpu.SemaphoreType.DMA((keys,)),
            pltpu.SemaphoreType.DMA((chips,)),
            pltpu.SemaphoreType.DMA((chips,)),
        ]


class Line:
    def __init__(self, place, own, up, down, pieces, sems):
        self.place, self.own, self.up, self.down, self.pieces = place, own, up, down, pieces
        self.groups, self.batch = place.groups, place.batch
        self.rows = own.shape[1] // pieces
        self.step = min(32, self.rows)
        self.sems = sems

    def span(self, piece):
        start = piece * self.rows
        return pl.ds(start if isinstance(start, int) else pl.multiple_of(start, self.rows), self.rows)

    def slot(self, upward, target):
        return self.up.at[target - 1] if upward else self.down.at[target]

    def copy(self, upward, target, piece, source):
        send, recv = self.sems[:2] if upward else self.sems[2:]
        index = target * self.pieces + piece
        return pltpu.make_async_remote_copy(
            src_ref=source.at[self.span(piece), :],
            dst_ref=self.slot(upward, target).at[self.span(piece), :],
            send_sem=send.at[index],
            recv_sem=recv.at[index],
            device_id=self.place.beside(1 if upward else -1),
            device_id_type=MESH,
        )

    def start(self, target, near=None, pieces=None):
        if target > 0 and near in (None, target == 1):

            @pl.when(self.batch == 0)
            def first():
                for piece in range(self.pieces) if pieces is None else pieces:
                    self.copy(True, target, piece, self.own.at[target]).start()

        if target < self.groups - 1 and near in (None, target == self.groups - 2):

            @pl.when(self.batch == self.groups - 1)
            def last():
                for piece in range(self.pieces) if pieces is None else pieces:
                    self.copy(False, target, piece, self.own.at[target]).start()

    def start_near(self, pieces=None):
        for target in range(self.groups):
            self.start(target, True, pieces)

    def order(self):
        count = self.groups
        result = []
        for index in range((count + 1) // 2):
            for target in (count - 1 - index, index):
                if target not in result:
                    result.append(target)
        return result

    def ticks(self):
        return range(1, (self.groups - 1) * self.pieces + self.groups)

    def tick(self, number):
        for upward in (True, False):
            place = self.batch if upward else self.groups - 1 - self.batch
            for distance in range(2, self.groups):
                target = distance if upward else self.groups - 1 - distance
                piece = number - (self.groups - 1 - distance) * self.pieces - place
                due = (place > 0) & (place < distance) & (piece >= 0) & (piece < self.pieces)

                @pl.when(due)
                def forward():
                    slot = self.slot(upward, target)
                    copy = self.copy(upward, target, piece, slot)
                    copy.wait_recv()

                    def add(start):
                        rows = pl.ds(pl.multiple_of(piece * self.rows + start, self.step), self.step)
                        total = slot[rows, :].astype(f32) + self.own[target, rows, :].astype(f32)
                        slot[rows, :] = total.astype(bf16)

                    loop(self.rows, self.step, add)
                    copy.start()

    def export(self, outs, moves, columns=None):
        below, above = self.batch > 0, self.batch < self.groups - 1
        jobs = []
        for out, there, upward in ((outs[0], None, None), (outs[1], below, True), (outs[2], above, False)):
            slot = self.own.at[self.batch] if there is None else self.slot(upward, self.batch)
            if columns is None:
                copies = [moves.make(slot, out)]
            else:
                copies = [
                    moves.make(slot.at[:, pl.ds(part * columns, columns)], out.at[part])
                    for part in range(out.shape[0])
                ]
            jobs.append((there, copies))

            def begin():
                if there is not None:
                    for piece in range(self.pieces):
                        self.copy(upward, self.batch, piece, slot).wait_recv()
                for copy in copies:
                    copy.start()

            begin() if there is None else pl.when(there)(begin)

        def wait():
            for there, copies in jobs:

                def done():
                    for copy in copies:
                        copy.wait()

                done() if there is None else pl.when(there)(done)

        return wait

    def finish(self):
        for target in range(self.groups):
            for upward in (True, False):
                if target == (0 if upward else self.groups - 1):
                    continue

                @pl.when(self.batch < target if upward else self.batch > target)
                def sent():
                    slot = self.slot(upward, target)
                    for piece in range(self.pieces):
                        self.copy(upward, target, piece, slot).wait_send()

    @staticmethod
    def scratch(groups, rows, columns, pieces):
        return [
            pltpu.VMEM((groups, rows, columns), bf16),
            pltpu.VMEM((groups - 1, rows, columns), bf16),
            pltpu.VMEM((groups - 1, rows, columns), bf16),
        ] + [pltpu.SemaphoreType.DMA((groups * pieces,))] * 4


class Moves:
    def __init__(self, sems):
        self.sems, self.count = sems, 0

    def make(self, source, target):
        copy = pltpu.make_async_copy(source, target, self.sems.at[self.count])
        self.count += 1
        return copy

    def start(self, source, target):
        copy = self.make(source, target)
        copy.start()
        return copy


def norm_rows(rows):
    mean = jnp.mean(rows, axis=-1, keepdims=True)
    centred = rows - mean
    inverse = lax.rsqrt(jnp.mean(centred * centred, axis=-1, keepdims=True) + EPS)
    return centred * inverse, inverse


def norm_back(grad, unit, inverse, gain):
    scaled = grad * gain
    return inverse * (
        scaled
        - jnp.mean(scaled, axis=-1, keepdims=True)
        - unit * jnp.mean(scaled * unit, axis=-1, keepdims=True)
    )


def segment_starts(group, lengths, scripts, places, rows):
    position = lax.broadcasted_iota(jnp.int32, (1, rows), 1)
    first = jnp.zeros((1, rows), jnp.int32)
    count = lengths.shape[0]
    number = [lengths[index] for index in range(count)]
    script = [scripts[index] for index in range(count)]
    mine = [places[index] == group for index in range(count)]
    own = [jnp.where(mine[index], number[index], 0) for index in range(count)]
    total = own[0]
    for index in range(1, count):
        total = total + own[index]
    for index in range(count):
        offset = jnp.int32(0)
        for other in range(count):
            if other < index:
                offset = offset + jnp.where(script[other] <= script[index], own[other], 0)
            elif other > index:
                offset = offset + jnp.where(script[other] < script[index], own[other], 0)
        bound = jnp.where(mine[index], offset, 0)
        first = jnp.maximum(first, jnp.where(position >= bound, bound, 0))
    return jnp.maximum(first, jnp.where(position >= total, total, 0))


def head_columns(part, head, width):
    return pl.ds(part * width + head * HEAD_DIM, HEAD_DIM)


def params(number):
    return pltpu.CompilerParams(
        collective_id=number, has_side_effects=True, vmem_limit_bytes=62 * 2**20
    )


def cost(micros):
    return pl.CostEstimate(flops=micros * 10**9, bytes_accessed=10**7, transcendentals=0)


def joined(ref, pieces):
    return jnp.concatenate([ref[piece, :] for piece in pieces], axis=0)


def front_kernel(
    plan, fine, block, tok, gain1, shift1, w_qkv, qv_bias, lengths, scripts, places, out_grad,
    w_out, out_bias, gain, shift, w_in, in_bias, w_down,
    first_out, qkv_out, att_out, sum_out, grad_out, second_out, act_out, hidden_out, middle_out, bias_out,
    starts, sums, attended, w_o, w_i, w_d, grad_in, up, buf, act, back, middle, local, *rest,
):
    first_sems, grad_sems, gather_sems, scatter_refs = rest[:4], rest[4:8], rest[8:12], rest[12:]
    place = Place(plan)
    own, depth = tok.shape
    rows = buf.shape[0]
    width = w_qkv.shape[2]
    hidden_width = w_in.shape[1]
    chip_rows = 2 * own
    moves = Moves(local)
    qkv = act.at[:, pl.ds(0, 3 * width)]
    weights = back.at[pl.ds(0, depth), pl.ds(0, 3 * width)]
    loads = [
        moves.start(w_qkv.at[part], back.at[pl.ds(0, depth), pl.ds(part * width, width)]) for part in range(3)
    ]
    load_out = moves.start(w_out, w_o)
    load_down = moves.start(w_down, w_d)
    load_in = moves.start(w_in, w_i)
    place.barrier()
    step = min(32, own)
    mine = pl.multiple_of(place.me * own, own)

    def normalise(start):
        unit, _ = norm_rows(tok[pl.ds(start, step), :].astype(f32))
        buf[pl.ds(pl.multiple_of(mine + start, step), step), :] = (unit * gain1[...] + shift1[...]).astype(bf16)

    loop(own, step, normalise)
    gather = Gather(place, buf, None, own, first_sems)
    gather.start()
    stores = [moves.start(out_grad, grad_out.at[pl.ds(mine, own), :])]
    starts[...] = segment_starts(place.batch, lengths, scripts, places, rows)
    for copy in loads:
        copy.wait()

    def project(offset):
        chip = lax.div(flip(place.me, offset), 2)
        span = pl.ds(pl.multiple_of(chip * chip_rows, chip_rows), chip_rows)
        stores.append(moves.start(buf.at[span, :], first_out.at[span, :]))
        product = dot(buf[span, :], weights[...], 1, 0)
        qkv[span, 0:width] = (product[:, 0:width] + qv_bias[0:1, :]).astype(bf16)
        qkv[span, width : 2 * width] = product[:, width : 2 * width].astype(bf16)
        qkv[span, 2 * width : 3 * width] = (product[:, 2 * width :] + qv_bias[1:2, :]).astype(bf16)

    gather.share(0)
    project(0)
    steps = gather.steps()
    grads = Gather(place, grad_out, out_grad, own, grad_sems)
    for number, (half, keys, offsets) in enumerate(steps):
        for key in keys:
            gather.arrive(key)
        if number == max(len(steps) - 2, 0):
            grads.start()
        for offset in offsets:
            gather.share(offset)
            project(offset)
    gather.finish()
    stores.append(moves.start(qkv, qkv_out))

    scale = HEAD_DIM ** (-0.5) * LOG2E
    heads = width // HEAD_DIM
    row_in = lax.broadcasted_iota(jnp.int32, (block, block), 0)
    col_in = lax.broadcasted_iota(jnp.int32, (block, block), 1)
    key_in = lax.broadcasted_iota(jnp.int32, (block, 1), 0)

    def attend(index):
        span = pl.ds(index * block, block)
        first = starts[:, span]
        queries = [qkv[span, head_columns(0, head, width)] for head in range(heads)]

        def against(key_block, carry, diagonal):
            key_span = pl.ds(pl.multiple_of(key_block * block, block), block)
            allowed = key_in + key_block * block >= first
            if diagonal:
                allowed = allowed & (row_in <= col_in)
            result = []
            for head in range(heads):
                top, total, mixed = carry[head]
                keys = qkv[key_span, head_columns(1, head, width)]
                values = qkv[key_span, head_columns(2, head, width)]
                scores = jnp.where(allowed, dot(keys, queries[head], 1, 1) * scale, NEGATIVE)
                new_top = jnp.maximum(top, jnp.max(scores, axis=0, keepdims=True))
                exps = jnp.exp2(scores - new_top)
                fade = jnp.exp2(top - new_top)
                total = total * fade + jnp.sum(exps, axis=0, keepdims=True)
                mixed = mixed * fade + dot(values, exps.astype(bf16), 0, 0)
                result.append((new_top, total, mixed))
            return tuple(result)

        carry = tuple(
            (
                jnp.full((1, block), NEGATIVE, f32),
                jnp.zeros((1, block), f32),
                jnp.zeros((HEAD_DIM, block), f32),
            )
            for head in range(heads)
        )
        if index:
            carry = lax.fori_loop(0, index, lambda key_block, c: against(key_block, c, False), carry)
        carry = against(index, carry, True)
        for head in range(heads):
            top, total, mixed = carry[head]
            attended[span, pl.ds(head * HEAD_DIM, HEAD_DIM)] = (mixed * (1.0 / total)).T.astype(bf16)
            sums[pl.ds(head, 1), span] = top + jnp.log2(total)

    blocks = rows // block
    waiting = [key for _, keys, _ in steps for key in keys]
    for index in range(blocks):
        attend(index)
        if index == blocks - 2:
            while waiting and plan.later(*waiting[0]) and bin(waiting[0][1]).count("1") == 1:
                grads.arrive(waiting.pop(0))
    for copy in stores:
        copy.wait()
    stores = [moves.start(attended, att_out), moves.start(sums, sum_out)]

    place = Place(fine)
    scatter = Scatter(place, own, depth, *scatter_refs[:5], scatter_refs[5:])
    load_out.wait()
    tile = min(1024, depth)

    def partial(owner, target):
        lines = attended[pl.ds(pl.multiple_of(owner * own, own), own), :]

        def columns(start):
            target[:, pl.ds(start, tile)] = dot(lines, w_o[:, pl.ds(start, tile)], 1, 0).astype(target.dtype)

        loop(depth, tile, columns)

    grad_loads = {}

    def load_grad(number):
        lines = pl.ds(number * own, own)
        grad_loads[number] = moves.start(grad_out.at[lines, :], grad_in.at[number % 2])

    def between(number):
        if number == max(len(plan.offsets) - 2, 0):
            for key in waiting:
                grads.arrive(key)
            for offset in plan.offsets:
                grads.share(offset)
            load_grad(0)
            load_grad(1)

    part_cols = min(512, hidden_width)
    chips = rows // own

    def raise_grad(number):
        grad_loads[number].wait()

        def columns(start):
            cols = pl.ds(start, part_cols)
            up[pl.ds(number * own, own), cols] = dot(grad_in[number % 2], w_d[cols, :], 1, 1)

        loop(hidden_width, part_cols, columns)
        if number + 2 < chips:
            load_grad(number + 2)

    scatter.begin(partial, between)
    load_down.wait()
    for number in range(chips):
        raise_grad(number)
    scatter.middle()
    grads.finish()

    def close(start, count, value):
        span = pl.ds(start, count)
        total = tok[span, :].astype(f32) + value + out_bias[...]
        middle[span, :] = total
        unit, _ = norm_rows(total)
        buf[pl.ds(pl.multiple_of(mine + start, count), count), :] = (unit * gain[...] + shift[...]).astype(bf16)

    gather = Gather(place, buf, None, own, gather_sems)
    for half in range(fine.halves):
        scatter.end(close, half)
        gather.start(half)
    scatter.finish()
    stores.append(moves.start(middle, middle_out))
    load_in.wait()
    bias_out[...] = jnp.zeros_like(bias_out)

    def expand(offset, half):
        pieces = gather.pieces(offset, half)
        count = own // fine.halves

        def columns(start):
            cols = pl.ds(start, part_cols)
            pre = dot(joined(buf, pieces), w_i[:, cols], 1, 0) + in_bias[:, cols]
            raised = jnp.concatenate([up[piece, cols] for piece in pieces], axis=0)
            root = 0.7978845608028654
            square = pre * pre
            inner = jnp.tanh(root * (pre + 0.044715 * (square * pre)))
            rise = 0.5 * (1.0 + inner)
            slope = rise + 0.5 * pre * (1.0 - inner * inner) * (root * (1.0 + 3 * 0.044715 * square))
            lifted = (pre * rise).astype(bf16)
            down = (raised * slope).astype(bf16)
            for index, piece in enumerate(pieces):
                act[piece, cols] = lifted[index * count : (index + 1) * count]
                back[piece, cols] = down[index * count : (index + 1) * count]
            bias_out[:, cols] += jnp.sum(down.astype(f32), axis=0, keepdims=True)

        loop(hidden_width, part_cols, columns)
        for piece in pieces:
            stores.append(moves.start(buf.at[piece, :], second_out.at[piece, :]))
            stores.append(moves.start(act.at[piece, :], act_out.at[piece, :]))
            stores.append(moves.start(back.at[piece, :], hidden_out.at[piece, :]))

    for half in range(fine.halves):
        gather.share(0, half)
        expand(0, half)
    for half, keys, offsets in gather.steps():
        for key in keys:
            gather.arrive(key)
        for offset in offsets:
            gather.share(offset, half)
            expand(offset, half)
    gather.finish()
    for copy in stores:
        copy.wait()


def run_front(
    plan, fine, block, tok, gain1, shift1, w_qkv, qv_bias, order, out_grad, w_out, out_bias, gain, shift, w_in, in_bias,
    w_down,
):
    own, depth = tok.shape
    rows = own * plan.devices
    width = w_qkv.shape[2]
    hidden = w_in.shape[1]
    return pl.pallas_call(
        functools.partial(front_kernel, plan, fine, block),
        out_shape=(
            jax.ShapeDtypeStruct((rows, depth), bf16),
            jax.ShapeDtypeStruct((rows, 3 * width), bf16),
            jax.ShapeDtypeStruct((rows, width), bf16),
            jax.ShapeDtypeStruct((8, rows), f32),
            jax.ShapeDtypeStruct((rows, depth), bf16),
            jax.ShapeDtypeStruct((rows, depth), bf16),
            jax.ShapeDtypeStruct((rows, hidden), bf16),
            jax.ShapeDtypeStruct((rows, hidden), bf16),
            jax.ShapeDtypeStruct((own, depth), f32),
            jax.ShapeDtypeStruct((1, hidden), f32),
        ),
        in_specs=[VMEM, VMEM, VMEM, ANY, VMEM, SMEM, SMEM, SMEM, ANY, ANY, VMEM, VMEM, VMEM, ANY, VMEM, ANY],
        out_specs=(ANY,) * 9 + (VMEM,),
        scratch_shapes=[
            pltpu.VMEM((1, rows), jnp.int32),
            pltpu.VMEM((8, rows), f32),
            pltpu.VMEM((rows, width), bf16),
            pltpu.VMEM((width, depth), bf16),
            pltpu.VMEM((depth, hidden), bf16),
            pltpu.VMEM((hidden, depth), bf16),
            pltpu.VMEM((2, own, depth), bf16),
            pltpu.VMEM((rows, hidden), f32),
            pltpu.VMEM((rows, depth), bf16),
            pltpu.VMEM((rows, hidden), bf16),
            pltpu.VMEM((max(rows, depth), hidden), bf16),
            pltpu.VMEM((own, depth), f32),
            pltpu.SemaphoreType.DMA((160,)),
        ]
        + Gather.semaphores(plan) * 2
        + Gather.semaphores(fine)
        + Scatter.scratch(fine, own, depth, bf16),
        compiler_params=params(0),
        name="front",
        cost_estimate=cost(150),
    )(tok, gain1, shift1, w_qkv, qv_bias, *order, out_grad, w_out, out_bias, gain, shift, w_in, in_bias, w_down)


PIECES = 2


def add_parts(place, parts, target):
    below, above = place.batch > 0, place.batch < place.groups - 1
    step = min(32, target.shape[0])

    def add(chosen):
        def rows_of(start):
            rows = pl.ds(start, step)
            value = chosen[0][rows, :].astype(f32)
            for part in chosen[1:]:
                value += part[rows, :].astype(f32)
            target[rows, :] = value

        loop(target.shape[0], step, rows_of)

    pl.when(jnp.logical_not(above))(lambda: add([parts[0], parts[1]]))
    pl.when(jnp.logical_not(below))(lambda: add([parts[0], parts[2]]))
    pl.when(below & above)(lambda: add(parts))


def spread_rows(place, target, rows):
    mine = lax.broadcasted_iota(jnp.int32, (target.shape[0], 1), 0) == place.me
    start = 0
    for row in rows:
        target[:, pl.ds(start, row.shape[1])] = jnp.where(mine, row, 0.0)
        start += row.shape[1]


def middle_kernel(
    plan, hidden_grad, w_in, middle, out_grad, gain, w_out, activated, grad_all, second_all, in_sums,
    middle_grad_out, branch_out, att_grad_out, sums_out, in_sums_out, down_out0, down_out1, down_out2, in_part_out,
    h_in, w_i, w_o, buf, middle_grad, att_grad, act, staged, local, *rest,
):
    down_outs = (down_out0, down_out1, down_out2)
    scatter_refs, gather_sems, line_refs, total_refs = rest[:9], rest[9:13], rest[13:20], rest[20:]
    place = Place(plan)
    own, depth = middle.shape
    rows = buf.shape[0]
    chip_rows = 2 * own
    hidden = w_in.shape[1]
    groups = place.groups
    cut = depth // groups
    moves = Moves(local)
    loads = [moves.start(hidden_grad, h_in), moves.start(w_in, w_i)]
    load_act = moves.start(activated, act)
    order = [index for pair in zip(range(groups - 1, -1, -1), range(groups)) for index in pair][:groups]
    load_grad = [
        moves.start(grad_all.at[:, pl.ds(target * cut, cut)], buf.at[:, pl.ds(target * cut, cut)])
        for target in order
    ]
    load_out = moves.start(w_out, w_o)
    place.barrier(groups=True)
    scatter = Scatter(place, own, depth, *scatter_refs[:5], scatter_refs[5:])
    line = Line(place, *line_refs[:3], PIECES, line_refs[3:])
    tile = min(1024, depth)

    def partial(owner, target):
        lines = h_in[pl.ds(pl.multiple_of(owner * own, own), own), :]

        def columns(start):
            target[:, pl.ds(start, tile)] = dot(lines, w_i[pl.ds(start, tile), :], 1, 1).astype(target.dtype)

        loop(depth, tile, columns)

    part = min(512, hidden)

    def down_slice(index):
        target = order[index]
        load_grad[index].wait()

        def piece(start):
            line.own[target, pl.ds(start, part), :] = dot(
                act[:, pl.ds(start, part)], buf[:, pl.ds(target * cut, cut)], 0, 0
            ).astype(bf16)

        loop(hidden, part, piece)
        line.start(target, False)

    for copy in loads:
        copy.wait()

    def between(number):
        if number == 0:
            load_act.wait()
            for index in range(groups // 2):
                down_slice(index)
        if number == min(2, len(plan.offsets) - 1):
            for index in range(groups // 2, groups):
                down_slice(index)
            line.start_near()

    scatter.begin(partial, between)

    in_stores = []
    in_loads = {}

    def load_slice(number):
        columns = pl.ds(number * cut, cut)
        in_loads[number] = moves.start(second_all.at[:, columns], act.at[:, pl.ds((number % 2) * cut, cut)])

    def in_slice(number):
        in_loads[number].wait()
        if number >= 2:
            in_stores[number - 2].wait()
        slot = number % 2

        def piece(start):
            columns = pl.ds(start, part)
            staged[slot, :, columns] = dot(
                act[:, pl.ds(slot * cut, cut)], h_in[:, columns], 0, 0
            ).astype(bf16)

        loop(hidden, part, piece)
        in_stores.append(moves.start(staged.at[slot], in_part_out.at[number]))
        if number + 2 < groups:
            load_slice(number + 2)

    ticks = list(line.ticks())
    for number in range(min(2, groups)):
        load_slice(number)
    line.tick(ticks.pop(0))
    scatter.middle()
    half_groups = groups // 2
    for number in range(half_groups):
        in_slice(number)
    line.tick(ticks.pop(0))
    mine = pl.multiple_of(place.me * own, own)
    totals = [
        Total(place, *total_refs[index : index + 4], total_refs[index + 4 : index + 8]) for index in (0, 8)
    ]
    own_sums = totals[0].value
    own_sums[...] = jnp.zeros_like(own_sums)
    totals[1].value[...] = in_sums[...]

    def close(start, count, value):
        span = pl.ds(start, count)
        unit, inverse = norm_rows(middle[span, :])
        sum_rows = out_grad[span, :].astype(f32) + norm_back(value, unit, inverse, gain[...])
        middle_grad[span, :] = sum_rows
        buf[pl.ds(pl.multiple_of(mine + start, count), count), :] = sum_rows.astype(bf16)
        own_sums[0:1, :] += jnp.sum(value * unit, axis=0, keepdims=True)
        own_sums[1:2, :] += jnp.sum(value, axis=0, keepdims=True)
        own_sums[2:3, :] += jnp.sum(sum_rows, axis=0, keepdims=True)
        own_sums[3:4, :] += jnp.sum(out_grad[span, :].astype(f32), axis=0, keepdims=True)

    gather = Gather(place, buf, None, own, gather_sems)
    for half in range(plan.halves):
        scatter.end(close, half)
        gather.start(half)
    for total in totals:
        total.begin()
    line.tick(ticks.pop(0))
    scatter.finish()
    stores = [moves.start(middle_grad, middle_grad_out)]
    load_out.wait()

    def project(offset, half):
        pieces = gather.pieces(offset, half)
        count = own // plan.halves
        product = dot(joined(buf, pieces), w_o[...], 1, 1).astype(bf16)
        for index, piece in enumerate(pieces):
            att_grad[piece, :] = product[index * count : (index + 1) * count]
            stores.append(moves.start(buf.at[piece, :], branch_out.at[piece, :]))

    for half in range(plan.halves):
        gather.share(0, half)
        project(0, half)
    for number in range(half_groups, groups):
        in_slice(number)
    line.tick(ticks.pop(0))
    for half, keys, offsets in gather.steps():
        for key in keys:
            gather.arrive(key)
        for offset in offsets:
            gather.share(offset, half)
            project(offset, half)
    stores.append(moves.start(att_grad, att_grad_out))
    for number in ticks:
        line.tick(number)
    exported = line.export(down_outs, moves)
    for total, total_out in zip(totals, (sums_out, in_sums_out)):
        total.end(total_out)
    gather.finish()
    line.finish()
    for copy in stores + in_stores[-2:]:
        copy.wait()
    exported()


def run_middle(plan, groups, hidden_grad, w_in, middle, out_grad, gain, w_out, activated, grad_all, second_all, in_sums):
    own, depth = middle.shape
    rows = own * plan.devices
    width = w_out.shape[0]
    hidden = w_in.shape[1]
    cut = depth // groups
    return pl.pallas_call(
        functools.partial(middle_kernel, plan),
        out_shape=(
            jax.ShapeDtypeStruct((own, depth), f32),
            jax.ShapeDtypeStruct((rows, depth), bf16),
            jax.ShapeDtypeStruct((rows, width), bf16),
            jax.ShapeDtypeStruct((4, depth), f32),
            jax.ShapeDtypeStruct(in_sums.shape, f32),
        )
        + (jax.ShapeDtypeStruct((hidden, cut), bf16),) * 3
        + (jax.ShapeDtypeStruct((groups, cut, hidden), bf16),),
        in_specs=[ANY, ANY, VMEM, VMEM, VMEM, ANY, ANY, ANY, ANY, VMEM],
        out_specs=(ANY, ANY, ANY, VMEM, VMEM, ANY, ANY, ANY, ANY),
        scratch_shapes=[
            pltpu.VMEM((rows, hidden), bf16),
            pltpu.VMEM((depth, hidden), bf16),
            pltpu.VMEM((width, depth), bf16),
            pltpu.VMEM((rows, depth), bf16),
            pltpu.VMEM((own, depth), f32),
            pltpu.VMEM((rows, width), bf16),
            pltpu.VMEM((rows, max(hidden, 2 * cut)), bf16),
            pltpu.VMEM((2, cut, hidden), bf16),
            pltpu.SemaphoreType.DMA((64,)),
        ]
        + Scatter.scratch(plan, own, depth, bf16)
        + Gather.semaphores(plan)
        + Line.scratch(groups, hidden, cut, PIECES)
        + Total.scratch(plan, groups, (4, depth))
        + Total.scratch(plan, groups, in_sums.shape),
        compiler_params=params(2),
        name="middle",
        cost_estimate=cost(80),
    )(hidden_grad, w_in, middle, out_grad, gain, w_out, activated, grad_all, second_all, in_sums)


def back_kernel(
    plan, block, lengths, scripts, places, qkv, att, att_grad, sums, activated, w_down, middle, down_bias, in_part, branch_all, sums2, in_sums,
    down0, down1, down2,
    qkv_grad_out, block_out, down_out, in_out0, in_out1, in_out2, out_part_out, vectors_out, spread_out,
    qkv_in, att_in, grad_in, act_in, w_d, starts, key_grad, value_grad, result, branch, staged, bias_out, down_sum,
    local,
    *rest,
):
    in_outs = (in_out0, in_out1, in_out2)
    scatter_refs, line_refs, total_refs = rest[:9], rest[9:16], rest[16:]
    place = Place(plan)
    own, depth = middle.shape
    rows = qkv_in.shape[0]
    width = att_in.shape[1]
    heads = width // HEAD_DIM
    groups = place.groups
    cut = depth // groups
    moves = Moves(local)
    line = Line(place, *line_refs[:3], PIECES, line_refs[3:])
    order = line.order()
    parts = [moves.start(in_part.at[target], line.own.at[target]) for target in order]
    feeds = [moves.start(activated, act_in), moves.start(w_down, w_d)]
    loads = [moves.start(qkv, qkv_in), moves.start(att, att_in), moves.start(att_grad, grad_in)]
    branch_loads = {}

    def load_slice(number):
        branch_loads[number] = moves.start(branch_all.at[:, pl.ds(number * cut, cut)], branch.at[number % 2])

    for number in range(min(2, groups)):
        load_slice(number)
    place.barrier(groups=True)
    scatter = Scatter(place, own, depth, *scatter_refs[:5], scatter_refs[5:])
    for target, copy in zip(order, parts):
        copy.wait()
        line.start(target, False)
    line.start_near()
    for copy in feeds:
        copy.wait()
    tile = min(1024, depth)

    def partial(owner, target):
        lines = act_in[pl.ds(pl.multiple_of(owner * own, own), own), :]

        def columns(start):
            target[:, pl.ds(start, tile)] = dot(lines, w_d[:, pl.ds(start, tile)], 1, 0).astype(target.dtype)

        loop(depth, tile, columns)

    scatter.begin(partial)
    ticks = list(line.ticks())
    line.tick(ticks.pop(0))
    starts[...] = segment_starts(place.batch, lengths, scripts, places, rows)
    bias_out[...] = jnp.zeros_like(bias_out)
    key_grad[...] = jnp.zeros_like(key_grad)
    value_grad[...] = jnp.zeros_like(value_grad)
    for copy in loads:
        copy.wait()
    for number in range(groups):
        branch_loads[number].wait()
        staged[number, :, :] = dot(att_in[...], branch[number % 2], 0, 0).astype(bf16)
        if number + 2 < groups:
            load_slice(number + 2)
    stores = [moves.start(staged, out_part_out)]
    down_rows = down_sum.shape[0]
    fit = rows // down_rows
    down_parts = [
        branch.at[index // fit, pl.ds((index % fit) * down_rows, down_rows), :] for index in range(3)
    ]
    down_loads = [moves.start(part, target) for part, target in zip((down0, down1, down2), down_parts)]
    scale = HEAD_DIM ** (-0.5)
    row_in = lax.broadcasted_iota(jnp.int32, (block, block), 0)
    col_in = lax.broadcasted_iota(jnp.int32, (block, block), 1)
    key_in = lax.broadcasted_iota(jnp.int32, (block, 1), 0)

    def attend(index):
        span = pl.ds(index * block, block)
        first = starts[:, span]
        queries, outer, inner, logs = [], [], [], []
        for head in range(heads):
            columns = pl.ds(head * HEAD_DIM, HEAD_DIM)
            queries.append(qkv_in[span, head_columns(0, head, width)])
            outer.append(grad_in[span, columns])
            product = grad_in[span, columns].astype(f32) * att_in[span, columns].astype(f32)
            inner.append(jnp.sum(product.T, axis=0, keepdims=True))
            logs.append(sums[pl.ds(head, 1), span])

        def against(key_block, carry, diagonal):
            key_span = pl.ds(pl.multiple_of(key_block * block, block), block)
            allowed = key_in + key_block * block >= first
            if diagonal:
                allowed = allowed & (row_in <= col_in)
            out = []
            for head in range(heads):
                columns = pl.ds(head * HEAD_DIM, HEAD_DIM)
                keys = qkv_in[key_span, head_columns(1, head, width)]
                values = qkv_in[key_span, head_columns(2, head, width)]
                scores = dot(keys, queries[head], 1, 1) * (scale * LOG2E)
                probs = jnp.exp2(jnp.where(allowed, scores - logs[head], NEGATIVE))
                value_grad[key_span, columns] += dot(probs.astype(bf16), outer[head], 1, 0)
                prob_grad = dot(values, outer[head], 1, 1)
                score_grad = (probs * (prob_grad - inner[head])).astype(bf16)
                key_grad[key_span, columns] += dot(score_grad, queries[head], 1, 0)
                out.append(carry[head] + dot(score_grad, keys, 0, 0))
            return tuple(out)

        carry = tuple(jnp.zeros((block, HEAD_DIM), f32) for head in range(heads))
        if index:
            carry = lax.fori_loop(0, index, lambda key_block, c: against(key_block, c, False), carry)
        carry = against(index, carry, True)
        for head in range(heads):
            query_grad = (carry[head] * scale).astype(bf16)
            qkv_in[span, head_columns(0, head, width)] = query_grad
            columns = pl.ds(head * HEAD_DIM, HEAD_DIM)
            bias_out[0:1, columns] += jnp.sum(query_grad.astype(f32), axis=0, keepdims=True)

    blocks = rows // block
    for index in range(blocks):
        attend(index)
        if index == blocks // 2:
            scatter.middle()
        if 0 < index < blocks - 1:
            line.tick(ticks.pop(0))
    kept = min(256, rows)

    def write(start):
        span = pl.ds(start, kept)
        qkv_in[span, pl.ds(width, width)] = (key_grad[span, :] * scale).astype(bf16)
        rounded = value_grad[span, :].astype(bf16)
        qkv_in[span, pl.ds(2 * width, width)] = rounded
        bias_out[1:2, :] += jnp.sum(rounded.astype(f32), axis=0, keepdims=True)

    loop(rows, kept, write)
    stores.append(moves.start(qkv_in, qkv_grad_out))
    for number in ticks:
        line.tick(number)
    for copy in down_loads:
        copy.wait()
    add_parts(place, down_parts, down_sum)
    stores.append(moves.start(down_sum, down_out))

    def close(start, count, value):
        span = pl.ds(start, count)
        result[span, :] = (middle[span, :] + value + down_bias[...]).astype(bf16)

    for half in range(plan.halves):
        scatter.end(close, half)
    stores.append(moves.start(result, block_out))
    vectors = Total(place, *total_refs[:4], total_refs[4:8])
    spread = Total(place, *total_refs[8:12], total_refs[12:])
    vectors.value[...] = sums2[...]
    spread_rows(place, spread.value, [bias_out[0:1, :], bias_out[1:2, :], in_sums[...]])
    vectors.plane([spread])
    vectors_out[...] = vectors.value[...]
    spread_out[...] = spread.value[...]
    exported = line.export(in_outs, moves)
    scatter.finish()
    line.finish()
    for copy in stores:
        copy.wait()
    exported()


def run_back(
    plan, groups, block, order, qkv, att, att_grad, sums, activated, w_down, middle, down_bias, in_part, branch_all,
    sums2, in_sums, down_parts,
):
    own, depth = middle.shape
    rows, width = att.shape
    hidden = w_down.shape[0]
    cut = depth // groups
    return pl.pallas_call(
        functools.partial(back_kernel, plan, block),
        out_shape=(
            jax.ShapeDtypeStruct((rows, 3 * width), bf16),
            jax.ShapeDtypeStruct((own, depth), bf16),
            jax.ShapeDtypeStruct((hidden, cut), f32),
            jax.ShapeDtypeStruct((cut, hidden), bf16),
            jax.ShapeDtypeStruct((cut, hidden), bf16),
            jax.ShapeDtypeStruct((cut, hidden), bf16),
            jax.ShapeDtypeStruct((groups, width, cut), bf16),
            jax.ShapeDtypeStruct(sums2.shape, f32),
            jax.ShapeDtypeStruct((plan.devices, 2 * width + hidden), f32),
        ),
        in_specs=[SMEM, SMEM, SMEM, ANY, ANY, ANY, VMEM, ANY, ANY, VMEM, VMEM, ANY, ANY, VMEM, VMEM, ANY, ANY, ANY],
        out_specs=(ANY, ANY, ANY, ANY, ANY, ANY, ANY, VMEM, VMEM),
        scratch_shapes=[
            pltpu.VMEM((rows, 3 * width), bf16),
            pltpu.VMEM((rows, width), bf16),
            pltpu.VMEM((rows, width), bf16),
            pltpu.VMEM((rows, hidden), bf16),
            pltpu.VMEM((hidden, depth), bf16),
            pltpu.VMEM((1, rows), jnp.int32),
            pltpu.VMEM((rows, width), f32),
            pltpu.VMEM((rows, width), f32),
            pltpu.VMEM((own, depth), bf16),
            pltpu.VMEM((2, rows, cut), bf16),
            pltpu.VMEM((groups, width, cut), bf16),
            pltpu.VMEM((2, width), f32),
            pltpu.VMEM((hidden, cut), f32),
            pltpu.SemaphoreType.DMA((64,)),
        ]
        + Scatter.scratch(plan, own, depth, bf16)
        + Line.scratch(groups, cut, hidden, PIECES)
        + Total.scratch(plan, 1, sums2.shape)
        + Total.scratch(plan, 1, (plan.devices, 2 * width + hidden)),
        compiler_params=params(3),
        name="back",
        cost_estimate=cost(75),
    )(*order, qkv, att, att_grad, sums, activated, w_down, middle, down_bias, in_part, branch_all, sums2, in_sums, *down_parts)


def last_kernel(
    plan, qkv_grad, w_qkv, tok, middle_grad, gain, out_part, first_all, qv_sums,
    in0, in1, in2,
    input_out, in_out, out_out0, out_out1, out_out2, qkv_out0, qkv_out1, qkv_out2, vectors_out, spread_out,
    g_in, weights, result, first, in_parts, in_sum, local, *rest,
):
    out_outs = (out_out0, out_out1, out_out2)
    qkv_outs = (qkv_out0, qkv_out1, qkv_out2)
    scatter_refs, rest = rest[:9], rest[9:]
    out_refs, rest = rest[:7], rest[7:]
    qkv_refs, total_refs = rest[:7], rest[7:]
    place = Place(plan)
    own, depth = tok.shape
    width = w_qkv.shape[2]
    groups = place.groups
    cut = depth // groups
    moves = Moves(local)
    out_line = Line(place, *out_refs[:3], 1, out_refs[3:])
    qkv_line = Line(place, *qkv_refs[:3], PIECES, qkv_refs[3:])
    order = qkv_line.order()
    parts = [moves.start(out_part.at[target], out_line.own.at[target]) for target in order]
    loads = [
        moves.start(w_qkv.at[part], weights.at[:, pl.ds(part * width, width)]) for part in range(3)
    ]
    loads.append(moves.start(qkv_grad, g_in))
    first_loads = {}

    def load_slice(number):
        columns = pl.ds(order[number] * cut, cut)
        first_loads[number] = moves.start(first_all.at[:, columns], first.at[number % 2])

    for number in range(min(2, groups)):
        load_slice(number)
    in_loads = [moves.start(part, in_parts.at[index]) for index, part in enumerate((in0, in1, in2))]
    place.barrier(groups=True)
    scatter = Scatter(place, own, depth, *scatter_refs[:5], scatter_refs[5:])
    for target, copy in zip(order, parts):
        copy.wait()
        out_line.start(target, False)
    out_line.start_near()
    for copy in loads:
        copy.wait()
    tile = min(1024, depth)

    def partial(owner, target):
        lines = g_in[pl.ds(pl.multiple_of(owner * own, own), own), :]

        def columns(start):
            target[:, pl.ds(start, tile)] = dot(lines, weights[pl.ds(start, tile), :], 1, 1).astype(target.dtype)

        loop(depth, tile, columns)

    def qkv_slice(number):
        first_loads[number].wait()
        qkv_line.own[order[number]] = dot(first[number % 2], g_in[...], 0, 0).astype(bf16)
        qkv_line.start(order[number], False)
        if number + 2 < groups:
            load_slice(number + 2)

    def between(number):
        if number == 0:
            for index in range(groups // 2):
                qkv_slice(index)
        if number == 1:
            for index in range(groups // 2, groups):
                qkv_slice(index)
            qkv_line.start_near(range(PIECES - 1))

    scatter.begin(partial, between)
    for number in out_line.ticks():
        out_line.tick(number)
    ticks = list(qkv_line.ticks())
    scatter.middle()
    qkv_line.tick(ticks.pop(0))
    exported = [out_line.export(out_outs, moves)]
    stores = []
    totals = [
        Total(place, *total_refs[index : index + 4], total_refs[index + 4 : index + 8]) for index in (0, 8)
    ]
    vectors, spread = totals
    spread.value[...] = qv_sums[:, 0 : 2 * width]
    for copy in in_loads:
        copy.wait()
    add_parts(place, [in_parts.at[index] for index in range(3)], in_sum)
    stores.append(moves.start(in_sum, in_out))
    vectors.value[...] = jnp.zeros_like(vectors.value)
    qkv_line.tick(ticks.pop(0))

    def close(start, count, value):
        span = pl.ds(start, count)
        unit, inverse = norm_rows(tok[span, :].astype(f32))
        sum_rows = middle_grad[span, :] + norm_back(value, unit, inverse, gain[...])
        result[span, :] = sum_rows.astype(bf16)
        vectors.value[0:1, :] += jnp.sum(value * unit, axis=0, keepdims=True)
        vectors.value[1:2, :] += jnp.sum(value, axis=0, keepdims=True)

    for half in range(plan.halves):
        scatter.end(close, half)
    stores.append(moves.start(result, input_out))
    qkv_line.tick(ticks.pop(0))
    vectors.plane()
    for total in totals:
        total.begin()
    qkv_line.start_near([PIECES - 1])
    for number in ticks:
        qkv_line.tick(number)
    exported.append(qkv_line.export(qkv_outs, moves, width))
    scatter.finish()
    out_line.finish()
    qkv_line.finish()
    for total, result_out in zip(totals, (vectors_out, spread_out)):
        total.end(result_out)
    for copy in stores:
        copy.wait()
    for wait in exported:
        wait()


def run_last(plan, groups, qkv_grad, w_qkv, tok, middle_grad, gain, out_part, first_all, qv_sums, in_parts):
    own, depth = tok.shape
    rows = qkv_grad.shape[0]
    width = w_qkv.shape[2]
    cut = depth // groups
    return pl.pallas_call(
        functools.partial(last_kernel, plan),
        out_shape=(
            jax.ShapeDtypeStruct((own, depth), bf16),
            jax.ShapeDtypeStruct(in_parts[0].shape, f32),
        )
        + (jax.ShapeDtypeStruct((width, cut), bf16),) * 3
        + (jax.ShapeDtypeStruct((3, cut, width), bf16),) * 3
        + (
            jax.ShapeDtypeStruct((2, depth), f32),
            jax.ShapeDtypeStruct((plan.devices, 2 * width), f32),
        ),
        in_specs=[ANY, ANY, VMEM, VMEM, VMEM, ANY, ANY, VMEM, ANY, ANY, ANY],
        out_specs=(ANY,) * 8 + (VMEM,) * 2,
        scratch_shapes=[
            pltpu.VMEM((rows, 3 * width), bf16),
            pltpu.VMEM((depth, 3 * width), bf16),
            pltpu.VMEM((own, depth), bf16),
            pltpu.VMEM((2, rows, cut), bf16),
            pltpu.VMEM((3,) + in_parts[0].shape, bf16),
            pltpu.VMEM(in_parts[0].shape, f32),
            pltpu.SemaphoreType.DMA((64,)),
        ]
        + Scatter.scratch(plan, own, depth, bf16)
        + Line.scratch(groups, width, cut, 1)
        + Line.scratch(groups, cut, 3 * width, PIECES)
        + Total.scratch(plan, groups, (2, depth))
        + Total.scratch(plan, groups, (plan.devices, 2 * width)),
        compiler_params=params(4),
        name="last",
        cost_estimate=cost(75),
    )(qkv_grad, w_qkv, tok, middle_grad, gain, out_part, first_all, qv_sums, *in_parts)


def body(
    tokens,
    out_grad,
    seq_lengths,
    seq_scripts,
    seq_place,
    norm1_gain,
    norm1_shift,
    w_qkv,
    qv_bias,
    w_out,
    out_bias,
    norm2_gain,
    norm2_shift,
    w_in,
    in_bias,
    w_down,
    down_bias,
):
    own, depth = tokens.shape
    devices = lax.axis_size("mp")
    plan = Plan(devices)
    fine = Plan(devices, 2)
    rows = own * devices
    width = w_qkv.shape[2]
    block = min(512, rows)
    order = (seq_lengths, seq_scripts, seq_place)

    def line(vector):
        return vector.reshape(1, -1)

    (
        first_all, qkv, att, sums, grad_all, second_all, activated, hidden_grad, middle, in_part,
    ) = run_front(
        plan, fine, block, tokens, line(norm1_gain), line(norm1_shift), w_qkv, qv_bias, order, out_grad,
        w_out, line(out_bias), line(norm2_gain), line(norm2_shift), w_in, line(in_bias), w_down,
    )
    groups = lax.axis_size("batch")
    batch = lax.axis_index("batch")

    def added(parts):
        total = parts[0].astype(f32)
        total += jnp.where(batch > 0, parts[1].astype(f32), 0.0)
        return total + jnp.where(batch < groups - 1, parts[2].astype(f32), 0.0)

    middle_grad, branch_all, att_grad, sums2, in_sums, *down_parts, in_part2 = run_middle(
        fine, groups, hidden_grad, w_in, middle, out_grad, line(norm2_gain), w_out, activated, grad_all, second_all,
        in_part,
    )
    qkv_grad, block_out, down_weight_grad, *in_parts, out_part, vectors2, spread2 = run_back(
        plan, groups, block, order, qkv, att, att_grad, sums, activated, w_down, middle, line(down_bias),
        in_part2, branch_all, sums2, in_sums, down_parts,
    )
    input_grad, in_weight_grad, *weight_parts, vectors, spread = run_last(
        plan, groups, qkv_grad, w_qkv, tokens, middle_grad, line(norm1_gain), out_part, first_all,
        spread2, in_parts,
    )
    qv_bias_grad = jnp.stack([spread[:, :width].reshape(-1), spread[:, width:].reshape(-1)])
    return (
        block_out,
        input_grad,
        vectors[0],
        vectors[1],
        added(weight_parts[3:]),
        qv_bias_grad,
        added(weight_parts[:3]),
        vectors2[2],
        vectors2[0],
        vectors2[1],
        in_weight_grad,
        spread2[:, 2 * width :].reshape(-1),
        down_weight_grad,
        vectors2[3],
    )


def solution(mesh):
    return jax.shard_map(
        body,
        mesh=mesh,
        in_specs=(
            P(("batch", "mp"), None),
            P(("batch", "mp"), None),
            P(),
            P(),
            P(),
            P(),
            P(),
            P(None, None, "mp"),
            P(None, "mp"),
            P("mp", None),
            P(),
            P(),
            P(),
            P(None, "mp"),
            P("mp"),
            P("mp", None),
            P(),
        ),
        out_specs=(
            P(("batch", "mp"), None),
            P(("batch", "mp"), None),
            P(),
            P(),
            P(None, "batch", "mp"),
            P(),
            P("mp", "batch"),
            P(),
            P(),
            P(),
            P("batch", "mp"),
            P(),
            P("mp", "batch"),
            P(),
        ),
        check_vma=False,
    )
```

```python
import functools

import jax
import jax.numpy as jnp
from jax import lax
from jax.experimental import pallas as pl
from jax.experimental.pallas import tpu as pltpu
from jax.sharding import PartitionSpec as P

HEAD_DIM = 128
EPS = 1e-05
NEGATIVE = -1e30
LOG2E = 1.4426950408889634
f32 = jnp.float32
bf16 = jnp.bfloat16
MESH = pl.DeviceIdType.MESH
ANY = pl.BlockSpec(memory_space=pl.ANY)
VMEM = pl.BlockSpec(memory_space=pltpu.VMEM)
SMEM = pl.BlockSpec(memory_space=pltpu.SMEM)


def dot(left, right, contract_left, contract_right):
    return lax.dot_general(
        left,
        right,
        (((contract_left,), (contract_right,)), ((), ())),
        preferred_element_type=f32,
    )


def flip(index, mask):
    bit = 1
    while bit <= mask:
        if mask & bit:
            index = index + bit * (1 - 2 * lax.rem(lax.div(index, bit), 2))
        bit *= 2
    return index


def loop(count, step, body):
    def one(index, carry):
        body(pl.multiple_of(index * step, step))
        return carry

    lax.fori_loop(0, count // step, one, 0)


class Plan:
    def __init__(self, devices, halves=1):
        bits = []
        bit = 2
        while bit < devices:
            bits.append(bit)
            bit *= 2
        self.devices = devices
        self.bits = bits
        self.ways = [tuple(bits)] + ([tuple(reversed(bits))] if len(bits) > 1 else [])
        self.halves = halves
        self.orders = self.ways * halves
        self.parts = len(self.orders)
        self.offsets = list(range(0, devices, 2))
        self.keys = [(part, offset) for part in range(self.parts) for offset in self.offsets if offset]
        self.keys.sort(key=lambda key: (self.half(key[0]), bin(key[1]).count("1"), self.last(*key)))
        self.shares = [(part, offset) for offset in self.offsets for part in range(self.parts)]

    def half(self, part):
        return part // len(self.ways)

    def parts_of(self, half):
        return range(half * len(self.ways), (half + 1) * len(self.ways))

    def last(self, part, offset):
        steps = [step for step, bit in enumerate(self.orders[part]) if bit & offset]
        return max(steps) if steps else -1

    def bit(self, part, offset):
        return self.orders[part][self.last(part, offset)]

    def later(self, part, offset):
        order = self.orders[part]
        return [offset | order[step] for step in range(self.last(part, offset) + 1, len(order))]


class Place:
    def __init__(self, plan):
        self.plan = plan
        self.batch = lax.axis_index("batch")
        self.groups = lax.axis_size("batch")
        self.me = lax.axis_index("mp")

    def at(self, mask):
        return (self.batch, flip(self.me, mask))

    def beside(self, step):
        return (self.batch + step, self.me)

    def around(self, step):
        return (lax.rem(self.batch + step, self.groups), self.me)

    def barrier(self, groups=False):
        semaphore = pltpu.get_barrier_semaphore()
        partners = [self.at(mask) for mask in [1] + self.plan.bits]
        if groups:
            partners += [self.around(step) for step in range(1, self.groups)]
        for partner in partners:
            pl.semaphore_signal(semaphore, inc=1, device_id=partner, device_id_type=MESH)
        pl.semaphore_wait(semaphore, len(partners))


class Total:
    def __init__(self, place, value, sent, came, slots, sems):
        self.place, self.value, self.sent, self.came, self.slots = place, value, sent, came, slots
        self.send, self.recv, self.slot_send, self.slot_recv = sems

    def plane(self, others=()):
        totals = (self,) + tuple(others)
        for index, mask in enumerate([1] + self.place.plan.bits):
            copies = [
                pltpu.make_async_remote_copy(
                    src_ref=total.sent.at[index],
                    dst_ref=total.came.at[index],
                    send_sem=total.send.at[index],
                    recv_sem=total.recv.at[index],
                    device_id=self.place.at(mask),
                    device_id_type=MESH,
                )
                for total in totals
            ]
            for total, copy in zip(totals, copies):
                total.sent[index] = total.value[...]
                copy.start()
            for total, copy in zip(totals, copies):
                copy.wait_recv()
                total.value[...] = total.sent[index] + total.came[index]
                copy.wait_send()

    def slot(self, step):
        return pltpu.make_async_remote_copy(
            src_ref=self.value,
            dst_ref=self.slots.at[step],
            send_sem=self.slot_send.at[step - 1],
            recv_sem=self.slot_recv.at[step - 1],
            device_id=self.place.around(step),
            device_id_type=MESH,
        )

    def begin(self):
        self.slots[0] = self.value[...]
        for step in range(1, self.place.groups):
            self.slot(step).start()

    def end(self, result):
        for step in range(1, self.place.groups):
            self.slot(step).wait()
        groups = self.place.groups
        total = self.slots[self.place.batch]
        for group in range(1, groups):
            total = total + self.slots[lax.rem(self.place.batch + groups - group, groups)]
        result[...] = total

    @staticmethod
    def scratch(plan, groups, shape):
        rounds = len(plan.bits) + 1
        return [
            pltpu.VMEM(shape, f32),
            pltpu.VMEM((rounds,) + shape, f32),
            pltpu.VMEM((rounds,) + shape, f32),
            pltpu.VMEM((groups,) + shape, f32),
            pltpu.SemaphoreType.DMA((rounds,)),
            pltpu.SemaphoreType.DMA((rounds,)),
            pltpu.SemaphoreType.DMA((max(groups - 1, 1),)),
            pltpu.SemaphoreType.DMA((max(groups - 1, 1),)),
        ]


class Gather:
    def __init__(self, place, buf, own, rows, sems):
        self.place, self.plan, self.buf, self.own, self.rows = place, place.plan, buf, own, rows
        self.link_send, self.link_recv, self.core_send, self.core_recv = sems
        self.part_rows = rows // self.plan.parts

    def span(self, mask, part):
        block = flip(self.place.me, mask)
        start = block * self.rows + part * self.part_rows
        return self.buf.at[pl.ds(pl.multiple_of(start, self.part_rows), self.part_rows), :]

    def source(self, offset, part):
        if offset == 0 and self.own is not None:
            return self.own.at[pl.ds(part * self.part_rows, self.part_rows), :]
        return self.span(offset, part)

    def link(self, key):
        part, offset = key
        bit = self.plan.bit(part, offset)
        index = self.plan.keys.index(key)
        return pltpu.make_async_remote_copy(
            src_ref=self.source(offset ^ bit, part),
            dst_ref=self.span(offset ^ bit, part),
            send_sem=self.link_send.at[index],
            recv_sem=self.link_recv.at[index],
            device_id=self.place.at(bit),
            device_id_type=MESH,
        )

    def core(self, key):
        part, offset = key
        index = self.plan.shares.index(key)
        return pltpu.make_async_remote_copy(
            src_ref=self.source(offset, part),
            dst_ref=self.span(offset, part),
            send_sem=self.core_send.at[index],
            recv_sem=self.core_recv.at[index],
            device_id=self.place.at(1),
            device_id_type=MESH,
        )

    def landed(self, ref, semaphore):
        pltpu.make_async_remote_copy(
            src_ref=ref,
            dst_ref=ref,
            send_sem=semaphore,
            recv_sem=semaphore,
            device_id=self.place.at(1),
            device_id_type=MESH,
        ).wait_recv()

    def start(self, half=0):
        for part in self.plan.parts_of(half):
            self.core((part, 0)).start()
        for key in self.plan.keys:
            if bin(key[1]).count("1") == 1 and self.plan.half(key[0]) == half:
                self.link(key).start()

    def arrive(self, key):
        part, offset = key
        self.landed(self.span(offset, part), self.link_recv.at[self.plan.keys.index(key)])
        for target in self.plan.later(part, offset):
            self.link((part, target)).start()
        self.core(key).start()

    def share(self, offset, half=0):
        for part in self.plan.parts_of(half):
            index = self.plan.shares.index((part, offset))
            self.landed(self.span(offset | 1, part), self.core_recv.at[index])

    def steps(self):
        result = []
        for half in range(self.plan.halves):
            for count in range(1, len(self.plan.bits) + 1):
                keys = [
                    key
                    for key in self.plan.keys
                    if self.plan.half(key[0]) == half and bin(key[1]).count("1") == count
                ]
                offsets = [offset for offset in self.plan.offsets if bin(offset).count("1") == count]
                result.append((half, keys, offsets))
        return result

    def pieces(self, offset, half):
        count = self.rows // self.plan.halves
        chip = lax.div(flip(self.place.me, offset), 2) * 2
        return [
            pl.ds(pl.multiple_of((chip + core) * self.rows + half * count, count), count) for core in range(2)
        ]

    def finish(self):
        for key in self.plan.keys:
            self.link(key).wait_send()
        for key in self.plan.shares:
            self.core(key).wait_send()

    @staticmethod
    def semaphores(plan):
        return [pltpu.SemaphoreType.DMA((len(plan.keys),))] * 2 + [
            pltpu.SemaphoreType.DMA((len(plan.shares),))
        ] * 2


class Spread:
    dtype = bf16

    def __init__(self, refs):
        self.refs = refs

    def __setitem__(self, index, value):
        count = self.refs[0].shape[0]
        for number, ref in enumerate(self.refs):
            ref[index] = value[number * count : (number + 1) * count]


class Scatter:
    def __init__(self, place, rows, width, core_out, core_in, kept, link_out, link_in, sems):
        self.place, self.plan, self.rows, self.width = place, place.plan, rows, width
        self.core_out, self.core_in, self.kept = core_out, core_in, kept
        self.link_out, self.link_in = link_out, link_in
        self.link_send, self.link_recv, self.core_send, self.core_recv = sems
        self.part_rows = rows // self.plan.parts
        self.step = min(32, self.part_rows)
        self.order = sorted(self.plan.offsets, key=lambda offset: -bin(offset).count("1"))

    def core(self, offset):
        index = offset // 2
        return pltpu.make_async_remote_copy(
            src_ref=self.core_out.at[index],
            dst_ref=self.core_in.at[index],
            send_sem=self.core_send.at[index],
            recv_sem=self.core_recv.at[index],
            device_id=self.place.at(1),
            device_id_type=MESH,
        )

    def link(self, key):
        index = self.plan.keys.index(key)
        return pltpu.make_async_remote_copy(
            src_ref=self.link_out.at[index],
            dst_ref=self.link_in.at[index],
            send_sem=self.link_send.at[index],
            recv_sem=self.link_recv.at[index],
            device_id=self.place.at(self.plan.bit(*key)),
            device_id_type=MESH,
        )

    def keep(self, offset):
        if offset == 0:
            return self.kept
        return Spread([self.link_out.at[self.plan.keys.index((part, offset))] for part in range(self.plan.parts)])

    def total(self, offset, part, start, arrived):
        rows = pl.ds(pl.multiple_of(part * self.part_rows + start, self.step), self.step)
        if offset:
            value = self.link_out[self.plan.keys.index((part, offset)), pl.ds(start, self.step), :].astype(f32)
        else:
            value = self.kept[rows, :].astype(f32)
        value += self.core_in[offset // 2, rows, :].astype(f32)
        for key in arrived:
            value += self.link_in[self.plan.keys.index(key), pl.ds(start, self.step), :].astype(f32)
        return value

    def pass_on(self, part, offset):
        arrived = [(part, target) for target in self.plan.later(part, offset)]
        for key in arrived:
            self.link(key).wait_recv()
        index = self.plan.keys.index((part, offset))

        def add(start):
            self.link_out[index, pl.ds(start, self.step), :] = self.total(
                offset, part, start, arrived
            ).astype(bf16)

        loop(self.part_rows, self.step, add)
        self.link((part, offset)).start()

    def free(self, offset, half):
        for part in self.plan.parts_of(half):
            if offset and not self.plan.later(part, offset):
                self.pass_on(part, offset)

    def bound(self, half):
        for offset in self.order:
            for part in self.plan.parts_of(half):
                if offset and self.plan.later(part, offset):
                    self.pass_on(part, offset)

    def begin(self, partial, between=None):
        for number, offset in enumerate(self.order):
            index = offset // 2
            if offset == 0:
                self.bound(0)
            partial(flip(self.place.me, offset | 1), self.core_out.at[index])
            self.core(offset).start()
            partial(flip(self.place.me, offset), self.keep(offset))
            self.core(offset).wait_recv()
            for half in range(self.plan.halves):
                self.free(offset, half)
            if between is not None:
                between(number)

    def middle(self):
        for half in range(1, self.plan.halves):
            self.bound(half)

    def end(self, use, half=0):
        for part in self.plan.parts_of(half):
            arrived = [(part, target) for target in self.plan.later(part, 0)]
            for key in arrived:
                self.link(key).wait_recv()

            def piece(start):
                row = pl.multiple_of(part * self.part_rows + start, self.step)
                use(row, self.step, self.total(0, part, start, arrived))

            loop(self.part_rows, self.step, piece)

    def finish(self):
        for key in self.plan.keys:
            self.link(key).wait_send()
        for offset in self.plan.offsets:
            self.core(offset).wait_send()

    @staticmethod
    def scratch(plan, rows, width, kept):
        chips, keys = len(plan.offsets), len(plan.keys)
        return [
            pltpu.VMEM((chips, rows, width), bf16),
            pltpu.VMEM((chips, rows, width), bf16),
            pltpu.VMEM((rows, width), kept),
            pltpu.VMEM((keys, rows // plan.parts, width), bf16),
            pltpu.VMEM((keys, rows // plan.parts, width), bf16),
            pltpu.SemaphoreType.DMA((keys,)),
            pltpu.SemaphoreType.DMA((keys,)),
            pltpu.SemaphoreType.DMA((chips,)),
            pltpu.SemaphoreType.DMA((chips,)),
        ]


class Slices:
    def __init__(self, ref, rows, columns):
        self.ref, self.shape = ref, (None, rows, columns)

    def part(self, target):
        rows = self.shape[1]
        start = target * rows
        start = start if isinstance(start, int) else pl.multiple_of(start, rows)
        return self.ref.at[pl.ds(start, rows), pl.ds(0, self.shape[2])]


def add_columns(parts, target, columns):
    rows, width = parts[0].shape
    step = min(32, rows)

    def rows_of(start):
        value = parts[0][pl.ds(start, step), :].astype(f32)
        for part in parts[1:]:
            value += part[pl.ds(start, step), :].astype(f32)
        for index in range(width // columns):
            lines = pl.ds(pl.multiple_of(index * rows + start, step), step)
            target[lines, :] = value[:, index * columns : (index + 1) * columns]

    loop(rows, step, rows_of)


def column_pieces(target, rows, width, columns):
    return [target.at[pl.ds(index * rows, rows), :] for index in range(width // columns)]


class Line:
    def __init__(self, place, own, up, down, pieces, sems):
        self.place, self.own, self.up, self.down, self.pieces = place, own, up, down, pieces
        self.groups, self.batch = place.groups, place.batch
        self.rows = own.shape[1] // pieces
        self.step = min(32, self.rows)
        self.sems = sems

    def span(self, piece):
        start = piece * self.rows
        return pl.ds(start if isinstance(start, int) else pl.multiple_of(start, self.rows), self.rows)

    def part(self, target):
        return self.own.part(target) if isinstance(self.own, Slices) else self.own.at[target]

    def slot(self, upward, target):
        return self.up.at[target - 1] if upward else self.down.at[target]

    def copy(self, upward, target, piece, source):
        send, recv = self.sems[:2] if upward else self.sems[2:]
        index = target * self.pieces + piece
        return pltpu.make_async_remote_copy(
            src_ref=source.at[self.span(piece), :],
            dst_ref=self.slot(upward, target).at[self.span(piece), :],
            send_sem=send.at[index],
            recv_sem=recv.at[index],
            device_id=self.place.beside(1 if upward else -1),
            device_id_type=MESH,
        )

    def start(self, target, near=None, pieces=None):
        if target > 0 and near in (None, target == 1):

            @pl.when(self.batch == 0)
            def first():
                for piece in range(self.pieces) if pieces is None else pieces:
                    self.copy(True, target, piece, self.part(target)).start()

        if target < self.groups - 1 and near in (None, target == self.groups - 2):

            @pl.when(self.batch == self.groups - 1)
            def last():
                for piece in range(self.pieces) if pieces is None else pieces:
                    self.copy(False, target, piece, self.part(target)).start()

    def start_near(self, pieces=None):
        for target in range(self.groups):
            self.start(target, True, pieces)

    def order(self):
        count = self.groups
        result = []
        for index in range((count + 1) // 2):
            for target in (count - 1 - index, index):
                if target not in result:
                    result.append(target)
        return result

    def ticks(self):
        return range(1, (self.groups - 1) * self.pieces + self.groups)

    def tick(self, number):
        for upward in (True, False):
            place = self.batch if upward else self.groups - 1 - self.batch
            for distance in range(2, self.groups):
                target = distance if upward else self.groups - 1 - distance
                piece = number - (self.groups - 1 - distance) * self.pieces - place
                due = (place > 0) & (place < distance) & (piece >= 0) & (piece < self.pieces)

                @pl.when(due)
                def forward():
                    slot = self.slot(upward, target)
                    copy = self.copy(upward, target, piece, slot)
                    copy.wait_recv()

                    def add(start):
                        rows = pl.ds(pl.multiple_of(piece * self.rows + start, self.step), self.step)
                        total = slot[rows, :].astype(f32) + self.part(target)[rows, :].astype(f32)
                        slot[rows, :] = total.astype(bf16)

                    loop(self.rows, self.step, add)
                    copy.start()

    def export(self, outs, moves, columns=None):
        below, above = self.batch > 0, self.batch < self.groups - 1
        jobs = []
        for out, there, upward in ((outs[0], None, None), (outs[1], below, True), (outs[2], above, False)):
            slot = self.part(self.batch) if there is None else self.slot(upward, self.batch)
            if columns is None:
                copies = [moves.make(slot, out)]
            else:
                copies = [
                    moves.make(slot.at[:, pl.ds(part * columns, columns)], out.at[part])
                    for part in range(out.shape[0])
                ]
            jobs.append((there, copies))

            def begin():
                if there is not None:
                    for piece in range(self.pieces):
                        self.copy(upward, self.batch, piece, slot).wait_recv()
                for copy in copies:
                    copy.start()

            begin() if there is None else pl.when(there)(begin)

        def wait():
            for there, copies in jobs:

                def done():
                    for copy in copies:
                        copy.wait()

                done() if there is None else pl.when(there)(done)

        return wait

    def add(self, target, columns):
        below, above = self.batch > 0, self.batch < self.groups - 1
        for there, upward in ((below, True), (above, False)):

            @pl.when(there)
            def come():
                slot = self.slot(upward, self.batch)
                for piece in range(self.pieces):
                    self.copy(upward, self.batch, piece, slot).wait_recv()

        own = self.part(self.batch)

        def sides(chosen):
            slots = [self.slot(upward, self.batch) for upward in chosen]
            add_columns([own] + slots, target, columns)

        pl.when(jnp.logical_not(above))(lambda: sides([True]))
        pl.when(jnp.logical_not(below))(lambda: sides([False]))
        pl.when(below & above)(lambda: sides([True, False]))
        return column_pieces(target, own.shape[0], own.shape[1], columns)

    def finish(self):
        for target in range(self.groups):
            for upward in (True, False):
                if target == (0 if upward else self.groups - 1):
                    continue

                @pl.when(self.batch < target if upward else self.batch > target)
                def sent():
                    slot = self.slot(upward, target)
                    for piece in range(self.pieces):
                        self.copy(upward, target, piece, slot).wait_send()

    @staticmethod
    def scratch(groups, rows, columns, pieces):
        return [
            pltpu.VMEM((groups, rows, columns), bf16),
            pltpu.VMEM((groups - 1, rows, columns), bf16),
            pltpu.VMEM((groups - 1, rows, columns), bf16),
        ] + [pltpu.SemaphoreType.DMA((groups * pieces,))] * 4


class Moves:
    def __init__(self, sems):
        self.sems, self.count = sems, 0

    def make(self, source, target):
        copy = pltpu.make_async_copy(source, target, self.sems.at[self.count])
        self.count += 1
        return copy

    def start(self, source, target):
        copy = self.make(source, target)
        copy.start()
        return copy


def norm_rows(rows):
    mean = jnp.mean(rows, axis=-1, keepdims=True)
    centred = rows - mean
    inverse = lax.rsqrt(jnp.mean(centred * centred, axis=-1, keepdims=True) + EPS)
    return centred * inverse, inverse


def norm_back(grad, unit, inverse, gain):
    scaled = grad * gain
    return inverse * (
        scaled
        - jnp.mean(scaled, axis=-1, keepdims=True)
        - unit * jnp.mean(scaled * unit, axis=-1, keepdims=True)
    )


def segment_starts(group, lengths, scripts, places, rows):
    position = lax.broadcasted_iota(jnp.int32, (1, rows), 1)
    first = jnp.zeros((1, rows), jnp.int32)
    count = lengths.shape[0]
    number = [lengths[index] for index in range(count)]
    script = [scripts[index] for index in range(count)]
    mine = [places[index] == group for index in range(count)]
    own = [jnp.where(mine[index], number[index], 0) for index in range(count)]
    total = own[0]
    for index in range(1, count):
        total = total + own[index]
    for index in range(count):
        offset = jnp.int32(0)
        for other in range(count):
            if other < index:
                offset = offset + jnp.where(script[other] <= script[index], own[other], 0)
            elif other > index:
                offset = offset + jnp.where(script[other] < script[index], own[other], 0)
        bound = jnp.where(mine[index], offset, 0)
        first = jnp.maximum(first, jnp.where(position >= bound, bound, 0))
    return jnp.maximum(first, jnp.where(position >= total, total, 0))


def head_columns(part, head, width):
    return pl.ds(part * width + head * HEAD_DIM, HEAD_DIM)


def params(number):
    return pltpu.CompilerParams(
        collective_id=number, has_side_effects=True, vmem_limit_bytes=62 * 2**20
    )


def cost(micros):
    return pl.CostEstimate(flops=micros * 10**9, bytes_accessed=10**7, transcendentals=0)


def joined(ref, pieces):
    return jnp.concatenate([ref[piece, :] for piece in pieces], axis=0)


def front_kernel(
    plan, fine, block, tok, gain1, shift1, w_qkv, qv_bias, lengths, scripts, places, out_grad,
    w_out, out_bias, gain, shift, w_in, in_bias, w_down,
    first_out, qkv_out, att_out, sum_out, grad_out, second_out, act_out, hidden_out, middle_out, bias_out,
    starts, sums, attended, w_o, w_i, w_d, grad_in, up, buf, act, back, middle, local, *rest,
):
    first_sems, grad_sems, gather_sems, scatter_refs = rest[:4], rest[4:8], rest[8:12], rest[12:]
    place = Place(plan)
    own, depth = tok.shape
    rows = buf.shape[0]
    width = w_qkv.shape[2]
    hidden_width = w_in.shape[1]
    chip_rows = 2 * own
    moves = Moves(local)
    qkv = act.at[:, pl.ds(0, 3 * width)]
    weights = back.at[pl.ds(0, depth), pl.ds(0, 3 * width)]
    loads = [
        moves.start(w_qkv.at[part], back.at[pl.ds(0, depth), pl.ds(part * width, width)]) for part in range(3)
    ]
    load_out = moves.start(w_out, w_o)
    load_down = moves.start(w_down, w_d)
    load_in = moves.start(w_in, w_i)
    place.barrier()
    step = min(32, own)
    mine = pl.multiple_of(place.me * own, own)

    def normalise(start):
        unit, _ = norm_rows(tok[pl.ds(start, step), :].astype(f32))
        buf[pl.ds(pl.multiple_of(mine + start, step), step), :] = (unit * gain1[...] + shift1[...]).astype(bf16)

    loop(own, step, normalise)
    gather = Gather(place, buf, None, own, first_sems)
    gather.start()
    stores = [moves.start(out_grad, grad_out.at[pl.ds(mine, own), :])]
    starts[...] = segment_starts(place.batch, lengths, scripts, places, rows)
    for copy in loads:
        copy.wait()

    def project(offset):
        chip = lax.div(flip(place.me, offset), 2)
        span = pl.ds(pl.multiple_of(chip * chip_rows, chip_rows), chip_rows)
        stores.append(moves.start(buf.at[span, :], first_out.at[span, :]))
        product = dot(buf[span, :], weights[...], 1, 0)
        qkv[span, 0:width] = (product[:, 0:width] + qv_bias[0:1, :]).astype(bf16)
        qkv[span, width : 2 * width] = product[:, width : 2 * width].astype(bf16)
        qkv[span, 2 * width : 3 * width] = (product[:, 2 * width :] + qv_bias[1:2, :]).astype(bf16)

    gather.share(0)
    project(0)
    steps = gather.steps()
    grads = Gather(place, grad_out, out_grad, own, grad_sems)
    for number, (half, keys, offsets) in enumerate(steps):
        for key in keys:
            gather.arrive(key)
        if number == max(len(steps) - 2, 0):
            grads.start()
        for offset in offsets:
            gather.share(offset)
            project(offset)
    gather.finish()
    stores.append(moves.start(qkv, qkv_out))

    scale = HEAD_DIM ** (-0.5) * LOG2E
    heads = width // HEAD_DIM
    row_in = lax.broadcasted_iota(jnp.int32, (block, block), 0)
    col_in = lax.broadcasted_iota(jnp.int32, (block, block), 1)
    key_in = lax.broadcasted_iota(jnp.int32, (block, 1), 0)

    def attend(index):
        span = pl.ds(index * block, block)
        first = starts[:, span]
        queries = [qkv[span, head_columns(0, head, width)] for head in range(heads)]

        def against(key_block, carry, diagonal):
            key_span = pl.ds(pl.multiple_of(key_block * block, block), block)
            allowed = key_in + key_block * block >= first
            if diagonal:
                allowed = allowed & (row_in <= col_in)
            result = []
            for head in range(heads):
                top, total, mixed = carry[head]
                keys = qkv[key_span, head_columns(1, head, width)]
                values = qkv[key_span, head_columns(2, head, width)]
                scores = jnp.where(allowed, dot(keys, queries[head], 1, 1) * scale, NEGATIVE)
                new_top = jnp.maximum(top, jnp.max(scores, axis=0, keepdims=True))
                exps = jnp.exp2(scores - new_top)
                fade = jnp.exp2(top - new_top)
                total = total * fade + jnp.sum(exps, axis=0, keepdims=True)
                mixed = mixed * fade + dot(values, exps.astype(bf16), 0, 0)
                result.append((new_top, total, mixed))
            return tuple(result)

        carry = tuple(
            (
                jnp.full((1, block), NEGATIVE, f32),
                jnp.zeros((1, block), f32),
                jnp.zeros((HEAD_DIM, block), f32),
            )
            for head in range(heads)
        )
        if index:
            carry = lax.fori_loop(0, index, lambda key_block, c: against(key_block, c, False), carry)
        carry = against(index, carry, True)
        for head in range(heads):
            top, total, mixed = carry[head]
            attended[span, pl.ds(head * HEAD_DIM, HEAD_DIM)] = (mixed * (1.0 / total)).T.astype(bf16)
            sums[pl.ds(head, 1), span] = top + jnp.log2(total)

    blocks = rows // block
    waiting = [key for _, keys, _ in steps for key in keys]
    for index in range(blocks):
        attend(index)
        if index == blocks - 2:
            while waiting and plan.later(*waiting[0]) and bin(waiting[0][1]).count("1") == 1:
                grads.arrive(waiting.pop(0))
    for copy in stores:
        copy.wait()
    stores = [moves.start(attended, att_out), moves.start(sums, sum_out)]

    place = Place(fine)
    scatter = Scatter(place, own, depth, *scatter_refs[:5], scatter_refs[5:])
    load_out.wait()
    tile = min(1024, depth)

    def partial(owner, target):
        lines = attended[pl.ds(pl.multiple_of(owner * own, own), own), :]

        def columns(start):
            target[:, pl.ds(start, tile)] = dot(lines, w_o[:, pl.ds(start, tile)], 1, 0).astype(target.dtype)

        loop(depth, tile, columns)

    grad_loads = {}

    def load_grad(number):
        lines = pl.ds(number * own, own)
        grad_loads[number] = moves.start(grad_out.at[lines, :], grad_in.at[number % 2])

    def between(number):
        if number == max(len(plan.offsets) - 2, 0):
            for key in waiting:
                grads.arrive(key)
            for offset in plan.offsets:
                grads.share(offset)
            load_grad(0)
            load_grad(1)

    part_cols = min(512, hidden_width)
    chips = rows // own

    def raise_grad(number):
        grad_loads[number].wait()

        def columns(start):
            cols = pl.ds(start, part_cols)
            up[pl.ds(number * own, own), cols] = dot(grad_in[number % 2], w_d[cols, :], 1, 1)

        loop(hidden_width, part_cols, columns)
        if number + 2 < chips:
            load_grad(number + 2)

    scatter.begin(partial, between)
    load_down.wait()
    for number in range(chips):
        raise_grad(number)
    scatter.middle()
    grads.finish()

    def close(start, count, value):
        span = pl.ds(start, count)
        total = tok[span, :].astype(f32) + value + out_bias[...]
        middle[span, :] = total
        unit, _ = norm_rows(total)
        buf[pl.ds(pl.multiple_of(mine + start, count), count), :] = (unit * gain[...] + shift[...]).astype(bf16)

    gather = Gather(place, buf, None, own, gather_sems)
    for half in range(fine.halves):
        scatter.end(close, half)
        gather.start(half)
    scatter.finish()
    stores.append(moves.start(middle, middle_out))
    load_in.wait()
    bias_out[...] = jnp.zeros_like(bias_out)

    def expand(offset, half):
        pieces = gather.pieces(offset, half)
        count = own // fine.halves

        def columns(start):
            cols = pl.ds(start, part_cols)
            pre = dot(joined(buf, pieces), w_i[:, cols], 1, 0) + in_bias[:, cols]
            raised = jnp.concatenate([up[piece, cols] for piece in pieces], axis=0)
            root = 0.7978845608028654
            square = pre * pre
            inner = jnp.tanh(root * (pre + 0.044715 * (square * pre)))
            rise = 0.5 * (1.0 + inner)
            slope = rise + 0.5 * pre * (1.0 - inner * inner) * (root * (1.0 + 3 * 0.044715 * square))
            lifted = (pre * rise).astype(bf16)
            down = (raised * slope).astype(bf16)
            for index, piece in enumerate(pieces):
                act[piece, cols] = lifted[index * count : (index + 1) * count]
                back[piece, cols] = down[index * count : (index + 1) * count]
            bias_out[:, cols] += jnp.sum(down.astype(f32), axis=0, keepdims=True)

        loop(hidden_width, part_cols, columns)
        for piece in pieces:
            stores.append(moves.start(buf.at[piece, :], second_out.at[piece, :]))
            stores.append(moves.start(act.at[piece, :], act_out.at[piece, :]))
            stores.append(moves.start(back.at[piece, :], hidden_out.at[piece, :]))

    for half in range(fine.halves):
        gather.share(0, half)
        expand(0, half)
    for half, keys, offsets in gather.steps():
        for key in keys:
            gather.arrive(key)
        for offset in offsets:
            gather.share(offset, half)
            expand(offset, half)
    gather.finish()
    for copy in stores:
        copy.wait()


def run_front(
    plan, fine, block, tok, gain1, shift1, w_qkv, qv_bias, order, out_grad, w_out, out_bias, gain, shift, w_in, in_bias,
    w_down,
):
    own, depth = tok.shape
    rows = own * plan.devices
    width = w_qkv.shape[2]
    hidden = w_in.shape[1]
    return pl.pallas_call(
        functools.partial(front_kernel, plan, fine, block),
        out_shape=(
            jax.ShapeDtypeStruct((rows, depth), bf16),
            jax.ShapeDtypeStruct((rows, 3 * width), bf16),
            jax.ShapeDtypeStruct((rows, width), bf16),
            jax.ShapeDtypeStruct((8, rows), f32),
            jax.ShapeDtypeStruct((rows, depth), bf16),
            jax.ShapeDtypeStruct((rows, depth), bf16),
            jax.ShapeDtypeStruct((rows, hidden), bf16),
            jax.ShapeDtypeStruct((rows, hidden), bf16),
            jax.ShapeDtypeStruct((own, depth), f32),
            jax.ShapeDtypeStruct((1, hidden), f32),
        ),
        in_specs=[VMEM, VMEM, VMEM, ANY, VMEM, SMEM, SMEM, SMEM, ANY, ANY, VMEM, VMEM, VMEM, ANY, VMEM, ANY],
        out_specs=(ANY,) * 9 + (VMEM,),
        scratch_shapes=[
            pltpu.VMEM((1, rows), jnp.int32),
            pltpu.VMEM((8, rows), f32),
            pltpu.VMEM((rows, width), bf16),
            pltpu.VMEM((width, depth), bf16),
            pltpu.VMEM((depth, hidden), bf16),
            pltpu.VMEM((hidden, depth), bf16),
            pltpu.VMEM((2, own, depth), bf16),
            pltpu.VMEM((rows, hidden), f32),
            pltpu.VMEM((rows, depth), bf16),
            pltpu.VMEM((rows, hidden), bf16),
            pltpu.VMEM((max(rows, depth), hidden), bf16),
            pltpu.VMEM((own, depth), f32),
            pltpu.SemaphoreType.DMA((160,)),
        ]
        + Gather.semaphores(plan) * 2
        + Gather.semaphores(fine)
        + Scatter.scratch(fine, own, depth, bf16),
        compiler_params=params(0),
        name="front",
        cost_estimate=cost(150),
    )(tok, gain1, shift1, w_qkv, qv_bias, *order, out_grad, w_out, out_bias, gain, shift, w_in, in_bias, w_down)


PIECES = 2


def add_parts(place, parts, target, columns):
    below, above = place.batch > 0, place.batch < place.groups - 1
    pl.when(jnp.logical_not(above))(lambda: add_columns([parts[0], parts[1]], target, columns))
    pl.when(jnp.logical_not(below))(lambda: add_columns([parts[0], parts[2]], target, columns))
    pl.when(below & above)(lambda: add_columns(parts, target, columns))


def spread_rows(place, target, rows):
    mine = lax.broadcasted_iota(jnp.int32, (target.shape[0], 1), 0) == place.me
    start = 0
    for row in rows:
        target[:, pl.ds(start, row.shape[1])] = jnp.where(mine, row, 0.0)
        start += row.shape[1]


def middle_kernel(
    plan, hidden_grad, w_in, middle, out_grad, gain, w_out, activated, grad_all, second_all, in_sums,
    middle_grad_out, branch_out, att_grad_out, sums_out, in_sums_out, down_out0, down_out1, down_out2, in_part_out,
    h_in, w_i, w_o, buf, middle_grad, att_grad, act, staged, local, *rest,
):
    down_outs = (down_out0, down_out1, down_out2)
    scatter_refs, gather_sems, line_refs, total_refs = rest[:9], rest[9:13], rest[13:20], rest[20:]
    place = Place(plan)
    own, depth = middle.shape
    rows = buf.shape[0]
    chip_rows = 2 * own
    hidden = w_in.shape[1]
    groups = place.groups
    cut = depth // groups
    moves = Moves(local)
    loads = [moves.start(hidden_grad, h_in), moves.start(w_in, w_i)]
    load_act = moves.start(activated, act)
    order = [index for pair in zip(range(groups - 1, -1, -1), range(groups)) for index in pair][:groups]
    load_grad = [
        moves.start(grad_all.at[:, pl.ds(target * cut, cut)], buf.at[:, pl.ds(target * cut, cut)])
        for target in order
    ]
    load_out = moves.start(w_out, w_o)
    place.barrier(groups=True)
    scatter = Scatter(place, own, depth, *scatter_refs[:5], scatter_refs[5:])
    line = Line(place, *line_refs[:3], PIECES, line_refs[3:])
    tile = min(1024, depth)

    def partial(owner, target):
        lines = h_in[pl.ds(pl.multiple_of(owner * own, own), own), :]

        def columns(start):
            target[:, pl.ds(start, tile)] = dot(lines, w_i[pl.ds(start, tile), :], 1, 1).astype(target.dtype)

        loop(depth, tile, columns)

    part = min(512, hidden)

    def down_slice(index):
        target = order[index]
        load_grad[index].wait()

        def piece(start):
            line.own[target, pl.ds(start, part), :] = dot(
                act[:, pl.ds(start, part)], buf[:, pl.ds(target * cut, cut)], 0, 0
            ).astype(bf16)

        loop(hidden, part, piece)
        line.start(target, False)

    for copy in loads:
        copy.wait()

    def between(number):
        if number == 0:
            load_act.wait()
            for index in range(groups // 2):
                down_slice(index)
        if number == min(2, len(plan.offsets) - 1):
            for index in range(groups // 2, groups):
                down_slice(index)
            line.start_near()

    scatter.begin(partial, between)

    in_stores = []
    in_loads = {}

    def load_slice(number):
        columns = pl.ds(number * cut, cut)
        in_loads[number] = moves.start(second_all.at[:, columns], act.at[:, pl.ds((number % 2) * cut, cut)])

    def in_slice(number):
        in_loads[number].wait()
        if number >= 2:
            in_stores[number - 2].wait()
        slot = number % 2

        def piece(start):
            columns = pl.ds(start, part)
            staged[slot, :, columns] = dot(
                act[:, pl.ds(slot * cut, cut)], h_in[:, columns], 0, 0
            ).astype(bf16)

        loop(hidden, part, piece)
        in_stores.append(moves.start(staged.at[slot], in_part_out.at[number]))
        if number + 2 < groups:
            load_slice(number + 2)

    ticks = list(line.ticks())
    for number in range(min(2, groups)):
        load_slice(number)
    line.tick(ticks.pop(0))
    scatter.middle()
    half_groups = groups // 2
    for number in range(half_groups):
        in_slice(number)
    line.tick(ticks.pop(0))
    mine = pl.multiple_of(place.me * own, own)
    totals = [
        Total(place, *total_refs[index : index + 4], total_refs[index + 4 : index + 8]) for index in (0, 8)
    ]
    own_sums = totals[0].value
    own_sums[...] = jnp.zeros_like(own_sums)
    totals[1].value[...] = in_sums[...]

    def close(start, count, value):
        span = pl.ds(start, count)
        unit, inverse = norm_rows(middle[span, :])
        sum_rows = out_grad[span, :].astype(f32) + norm_back(value, unit, inverse, gain[...])
        middle_grad[span, :] = sum_rows
        buf[pl.ds(pl.multiple_of(mine + start, count), count), :] = sum_rows.astype(bf16)
        own_sums[0:1, :] += jnp.sum(value * unit, axis=0, keepdims=True)
        own_sums[1:2, :] += jnp.sum(value, axis=0, keepdims=True)
        own_sums[2:3, :] += jnp.sum(sum_rows, axis=0, keepdims=True)
        own_sums[3:4, :] += jnp.sum(out_grad[span, :].astype(f32), axis=0, keepdims=True)

    gather = Gather(place, buf, None, own, gather_sems)
    for half in range(plan.halves):
        scatter.end(close, half)
        gather.start(half)
    for total in totals:
        total.begin()
    line.tick(ticks.pop(0))
    scatter.finish()
    stores = [moves.start(middle_grad, middle_grad_out)]
    load_out.wait()

    def project(offset, half):
        pieces = gather.pieces(offset, half)
        count = own // plan.halves
        product = dot(joined(buf, pieces), w_o[...], 1, 1).astype(bf16)
        for index, piece in enumerate(pieces):
            att_grad[piece, :] = product[index * count : (index + 1) * count]
            stores.append(moves.start(buf.at[piece, :], branch_out.at[piece, :]))

    for half in range(plan.halves):
        gather.share(0, half)
        project(0, half)
    for number in range(half_groups, groups):
        in_slice(number)
    line.tick(ticks.pop(0))
    for half, keys, offsets in gather.steps():
        for key in keys:
            gather.arrive(key)
        for offset in offsets:
            gather.share(offset, half)
            project(offset, half)
    stores.append(moves.start(att_grad, att_grad_out))
    for number in ticks:
        line.tick(number)
    exported = line.export(down_outs, moves)
    for total, total_out in zip(totals, (sums_out, in_sums_out)):
        total.end(total_out)
    gather.finish()
    line.finish()
    for copy in stores + in_stores[-2:]:
        copy.wait()
    exported()


def run_middle(plan, groups, hidden_grad, w_in, middle, out_grad, gain, w_out, activated, grad_all, second_all, in_sums):
    own, depth = middle.shape
    rows = own * plan.devices
    width = w_out.shape[0]
    hidden = w_in.shape[1]
    cut = depth // groups
    return pl.pallas_call(
        functools.partial(middle_kernel, plan),
        out_shape=(
            jax.ShapeDtypeStruct((own, depth), f32),
            jax.ShapeDtypeStruct((rows, depth), bf16),
            jax.ShapeDtypeStruct((rows, width), bf16),
            jax.ShapeDtypeStruct((4, depth), f32),
            jax.ShapeDtypeStruct(in_sums.shape, f32),
        )
        + (jax.ShapeDtypeStruct((hidden, cut), bf16),) * 3
        + (jax.ShapeDtypeStruct((groups, cut, hidden), bf16),),
        in_specs=[ANY, ANY, VMEM, VMEM, VMEM, ANY, ANY, ANY, ANY, VMEM],
        out_specs=(ANY, ANY, ANY, VMEM, VMEM, ANY, ANY, ANY, ANY),
        scratch_shapes=[
            pltpu.VMEM((rows, hidden), bf16),
            pltpu.VMEM((depth, hidden), bf16),
            pltpu.VMEM((width, depth), bf16),
            pltpu.VMEM((rows, depth), bf16),
            pltpu.VMEM((own, depth), f32),
            pltpu.VMEM((rows, width), bf16),
            pltpu.VMEM((rows, max(hidden, 2 * cut)), bf16),
            pltpu.VMEM((2, cut, hidden), bf16),
            pltpu.SemaphoreType.DMA((64,)),
        ]
        + Scatter.scratch(plan, own, depth, bf16)
        + Gather.semaphores(plan)
        + Line.scratch(groups, hidden, cut, PIECES)
        + Total.scratch(plan, groups, (4, depth))
        + Total.scratch(plan, groups, in_sums.shape),
        compiler_params=params(2),
        name="middle",
        cost_estimate=cost(80),
    )(hidden_grad, w_in, middle, out_grad, gain, w_out, activated, grad_all, second_all, in_sums)


def back_kernel(
    plan, block, lengths, scripts, places, qkv, att, att_grad, sums, activated, w_down, middle, down_bias, in_part,
    branch_all, sums2, in_sums, down0, down1, down2, w_qkv, tok, middle_grad, gain, first_all,
    block_out, input_out, down_out, in_out, out_out, qkv_out, vectors2_out, spread2_out, vectors_out, spread_out,
    qkv_in, att_in, grad_in, act_in, w_d, mid, starts, key_grad, value_grad, result, branch, bias_out, local, free, *rest,
):
    feed_refs, first_sems, rest = rest[:9], rest[9:13], rest[13:]
    in_refs, out_refs, qkv_refs, total_refs = rest[:7], rest[7:14], rest[14:20], rest[20:]
    place = Place(plan)
    own, depth = tok.shape
    rows = qkv_in.shape[0]
    width = att_in.shape[1]
    hidden = w_down.shape[0]
    heads = width // HEAD_DIM
    groups = place.groups
    cut = depth // groups
    moves = Moves(local)
    line = Line(place, *in_refs[:3], PIECES, in_refs[3:])
    out_line = Line(place, *out_refs[:3], 1, out_refs[3:])
    qkv_line = Line(place, Slices(act_in, cut, 3 * width), *qkv_refs[:2], PIECES, qkv_refs[2:])
    order = line.order()
    parts = [moves.start(in_part.at[target], line.own.at[target]) for target in order]
    feeds = [moves.start(activated, act_in), moves.start(w_down, w_d)]
    loads = [moves.start(qkv, qkv_in), moves.start(att, att_in), moves.start(att_grad, grad_in)]
    load_middle = moves.start(middle, mid)
    slice_loads = {}

    def load_slice(source, number, name):
        columns = pl.ds(number * cut, cut)
        slice_loads[name] = moves.start(source.at[:, columns], branch.at[name[1] % 2])

    for index in range(min(2, groups)):
        load_slice(branch_all, order[index], ("out", index))
    place.barrier(groups=True)
    scatter = Scatter(place, own, depth, *feed_refs[:5], feed_refs[5:])
    for target, copy in zip(order, parts):
        copy.wait()
        line.start(target, False)
    line.start_near()
    for copy in feeds:
        copy.wait()
    tile = min(1024, depth)

    def partial(owner, target):
        lines = act_in[pl.ds(pl.multiple_of(owner * own, own), own), :]

        def columns(start):
            target[:, pl.ds(start, tile)] = dot(lines, w_d[:, pl.ds(start, tile)], 1, 0).astype(target.dtype)

        loop(depth, tile, columns)

    scatter.begin(partial)
    turns = depth // hidden
    weight_loads = [
        moves.start(
            w_qkv.at[part, pl.ds(turn * hidden, hidden), :],
            w_d.at[:, pl.ds((turn * 3 + part) * width, width)],
        )
        for turn in range(turns)
        for part in range(3)
    ]
    ticks = list(line.ticks())
    line.tick(ticks.pop(0))
    starts[...] = segment_starts(place.batch, lengths, scripts, places, rows)
    bias_out[...] = jnp.zeros_like(bias_out)
    key_grad[...] = jnp.zeros_like(key_grad)
    value_grad[...] = jnp.zeros_like(value_grad)
    for copy in loads:
        copy.wait()
    for index, target in enumerate(order):
        slice_loads["out", index].wait()
        out_line.own[target, :, :] = dot(att_in[...], branch[index % 2], 0, 0).astype(bf16)
        out_line.start(target, False)
        if index + 2 < groups:
            load_slice(branch_all, order[index + 2], ("out", index + 2))
    out_line.start_near()
    fit = rows // hidden
    down_parts = [branch.at[index // fit, pl.ds((index % fit) * hidden, hidden), :] for index in range(3)]
    down_loads = [moves.start(part, target) for part, target in zip((down0, down1, down2), down_parts)]
    scale = HEAD_DIM ** (-0.5)
    row_in = lax.broadcasted_iota(jnp.int32, (block, block), 0)
    col_in = lax.broadcasted_iota(jnp.int32, (block, block), 1)
    key_in = lax.broadcasted_iota(jnp.int32, (block, 1), 0)

    def attend(index):
        span = pl.ds(index * block, block)
        first = starts[:, span]
        queries, outer, inner, logs = [], [], [], []
        for head in range(heads):
            columns = pl.ds(head * HEAD_DIM, HEAD_DIM)
            queries.append(qkv_in[span, head_columns(0, head, width)])
            outer.append(grad_in[span, columns])
            product = grad_in[span, columns].astype(f32) * att_in[span, columns].astype(f32)
            inner.append(jnp.sum(product.T, axis=0, keepdims=True))
            logs.append(sums[pl.ds(head, 1), span])

        def against(key_block, carry, diagonal):
            key_span = pl.ds(pl.multiple_of(key_block * block, block), block)
            allowed = key_in + key_block * block >= first
            if diagonal:
                allowed = allowed & (row_in <= col_in)
            out = []
            for head in range(heads):
                columns = pl.ds(head * HEAD_DIM, HEAD_DIM)
                keys = qkv_in[key_span, head_columns(1, head, width)]
                values = qkv_in[key_span, head_columns(2, head, width)]
                scores = dot(keys, queries[head], 1, 1) * (scale * LOG2E)
                probs = jnp.exp2(jnp.where(allowed, scores - logs[head], NEGATIVE))
                value_grad[key_span, columns] += dot(probs.astype(bf16), outer[head], 1, 0)
                prob_grad = dot(values, outer[head], 1, 1)
                score_grad = (probs * (prob_grad - inner[head])).astype(bf16)
                key_grad[key_span, columns] += dot(score_grad, queries[head], 1, 0)
                out.append(carry[head] + dot(score_grad, keys, 0, 0))
            return tuple(out)

        carry = tuple(jnp.zeros((block, HEAD_DIM), f32) for head in range(heads))
        if index:
            carry = lax.fori_loop(0, index, lambda key_block, c: against(key_block, c, False), carry)
        carry = against(index, carry, True)
        for head in range(heads):
            query_grad = (carry[head] * scale).astype(bf16)
            qkv_in[span, head_columns(0, head, width)] = query_grad
            columns = pl.ds(head * HEAD_DIM, HEAD_DIM)
            bias_out[0:1, columns] += jnp.sum(query_grad.astype(f32), axis=0, keepdims=True)

    blocks = rows // block
    for index in range(blocks):
        attend(index)
        if index == blocks // 2:
            scatter.middle()
        if 0 < index < blocks - 1:
            line.tick(ticks.pop(0))
    kept = min(256, rows)

    def write(start):
        span = pl.ds(start, kept)
        qkv_in[span, pl.ds(width, width)] = (key_grad[span, :] * scale).astype(bf16)
        rounded = value_grad[span, :].astype(bf16)
        qkv_in[span, pl.ds(2 * width, width)] = rounded
        bias_out[1:2, :] += jnp.sum(rounded.astype(f32), axis=0, keepdims=True)

    loop(rows, kept, write)
    for number in ticks:
        line.tick(number)
    load_middle.wait()

    def close(start, count, value):
        span = pl.ds(start, count)
        result[span, :] = (mid[span, :] + value + down_bias[...]).astype(bf16)

    for half in range(plan.halves):
        scatter.end(close, half)
    stores = [moves.start(result, block_out)]
    load_grad = moves.start(middle_grad, mid)
    totals = [
        Total(place, *total_refs[index : index + 4], total_refs[index + 4 : index + 8]) for index in (0, 8, 16, 24)
    ]
    vectors2, spread2, vectors, spread = totals
    vectors2.value[...] = sums2[...]
    spread_rows(place, spread2.value, [bias_out[0:1, :], bias_out[1:2, :], in_sums[...]])
    vectors.value[...] = jnp.zeros_like(vectors.value)
    masks = [1] + plan.bits
    for mask in masks:
        pl.semaphore_signal(free, inc=1, device_id=place.at(mask), device_id_type=MESH)
    scatter.finish()
    scatter = Scatter(place, own, depth, *feed_refs[:5], first_sems)
    for copy in weight_loads:
        copy.wait()

    def first_partial(owner, target):
        lines = qkv_in[pl.ds(pl.multiple_of(owner * own, own), own), :]
        for turn in range(turns):
            target[:, pl.ds(turn * hidden, hidden)] = dot(
                lines, w_d[:, pl.ds(turn * 3 * width, 3 * width)], 1, 1
            ).astype(target.dtype)

    def qkv_slice(index):
        slice_loads["qkv", index].wait()
        qkv_line.part(order[index])[...] = dot(branch[index % 2], qkv_in[...], 0, 0).astype(bf16)
        qkv_line.start(order[index], False)
        if index + 2 < groups:
            load_slice(first_all, order[index + 2], ("qkv", index + 2))

    pl.semaphore_wait(free, len(masks))
    scatter.begin(first_partial)
    for copy in down_loads:
        copy.wait()
    add_parts(place, down_parts, key_grad, width)
    down_stores = [
        moves.start(piece, down_out.at[:, pl.ds(index * width, width)])
        for index, piece in enumerate(column_pieces(key_grad, hidden, cut, width))
    ]
    for index in range(min(2, groups)):
        load_slice(first_all, order[index], ("qkv", index))
    for index in range(groups):
        qkv_slice(index)
    qkv_line.start_near(range(PIECES - 1))
    for number in out_line.ticks():
        out_line.tick(number)
    scatter.middle()
    pieces = line.add(value_grad, width)
    in_stores = [
        moves.start(piece, in_out.at[:, pl.ds(index * width, width)]) for index, piece in enumerate(pieces)
    ]
    ticks = list(qkv_line.ticks())
    qkv_line.tick(ticks.pop(0))
    load_grad.wait()
    stores.pop(0).wait()
    load_tok = moves.start(tok, result)
    load_tok.wait()

    def close_first(start, count, value):
        span = pl.ds(start, count)
        unit, inverse = norm_rows(result[span, :].astype(f32))
        sum_rows = mid[span, :] + norm_back(value, unit, inverse, gain[...])
        result[span, :] = sum_rows.astype(bf16)
        vectors.value[0:1, :] += jnp.sum(value * unit, axis=0, keepdims=True)
        vectors.value[1:2, :] += jnp.sum(value, axis=0, keepdims=True)

    for half in range(plan.halves):
        scatter.end(close_first, half)
    stores.append(moves.start(result, input_out))
    qkv_line.tick(ticks.pop(0))
    vectors.plane([vectors2, spread2])
    spread.value[...] = spread2.value[:, 0 : 2 * width]
    for total in (vectors, spread):
        total.begin()
    qkv_line.start_near([PIECES - 1])
    for number in ticks:
        qkv_line.tick(number)
    for copy in in_stores + down_stores:
        copy.wait()
    pieces = out_line.add(key_grad, width)
    stores += [
        moves.start(piece, out_out.at[:, pl.ds(index * width, width)]) for index, piece in enumerate(pieces)
    ]
    pieces = qkv_line.add(value_grad, width)
    stores += [moves.start(piece, qkv_out.at[index]) for index, piece in enumerate(pieces)]
    scatter.finish()
    line.finish()
    out_line.finish()
    qkv_line.finish()
    vectors2_out[...] = vectors2.value[...]
    spread2_out[...] = spread2.value[...]
    vectors.end(vectors_out)
    spread.end(spread_out)
    for copy in stores:
        copy.wait()


def run_back(
    plan, groups, block, order, qkv, att, att_grad, sums, activated, w_down, middle, down_bias, in_part, branch_all,
    sums2, in_sums, down_parts, w_qkv, tok, middle_grad, gain, first_all,
):
    own, depth = tok.shape
    rows, width = att.shape
    hidden = w_down.shape[0]
    cut = depth // groups
    return pl.pallas_call(
        functools.partial(back_kernel, plan, block),
        out_shape=(
            jax.ShapeDtypeStruct((own, depth), bf16),
            jax.ShapeDtypeStruct((own, depth), bf16),
            jax.ShapeDtypeStruct((hidden, cut), f32),
            jax.ShapeDtypeStruct((cut, hidden), f32),
            jax.ShapeDtypeStruct((width, cut), f32),
            jax.ShapeDtypeStruct((3, cut, width), f32),
            jax.ShapeDtypeStruct(sums2.shape, f32),
            jax.ShapeDtypeStruct((plan.devices, 2 * width + hidden), f32),
            jax.ShapeDtypeStruct((2, depth), f32),
            jax.ShapeDtypeStruct((plan.devices, 2 * width), f32),
        ),
        in_specs=[SMEM] * 3
        + [ANY, ANY, ANY, VMEM, ANY, ANY, ANY, VMEM, ANY, ANY, VMEM, VMEM, ANY, ANY, ANY, ANY, ANY, ANY, VMEM, ANY],
        out_specs=(ANY,) * 6 + (VMEM,) * 4,
        scratch_shapes=[
            pltpu.VMEM((rows, 3 * width), bf16),
            pltpu.VMEM((rows, width), bf16),
            pltpu.VMEM((rows, width), bf16),
            pltpu.VMEM((rows, hidden), bf16),
            pltpu.VMEM((hidden, depth), bf16),
            pltpu.VMEM((own, depth), f32),
            pltpu.VMEM((1, rows), jnp.int32),
            pltpu.VMEM((rows, width), f32),
            pltpu.VMEM((rows, width), f32),
            pltpu.VMEM((own, depth), bf16),
            pltpu.VMEM((2, rows, cut), bf16),
            pltpu.VMEM((2, width), f32),
            pltpu.SemaphoreType.DMA((96,)),
            pltpu.SemaphoreType.REGULAR,
        ]
        + Scatter.scratch(plan, own, depth, bf16)
        + Scatter.scratch(plan, own, depth, bf16)[5:]
        + Line.scratch(groups, cut, hidden, PIECES)
        + Line.scratch(groups, width, cut, 1)
        + Line.scratch(groups, cut, 3 * width, PIECES)[1:]
        + Total.scratch(plan, 1, sums2.shape)
        + Total.scratch(plan, 1, (plan.devices, 2 * width + hidden))
        + Total.scratch(plan, groups, (2, depth))
        + Total.scratch(plan, groups, (plan.devices, 2 * width)),
        compiler_params=params(3),
        name="back",
        cost_estimate=cost(145),
    )(
        *order, qkv, att, att_grad, sums, activated, w_down, middle, down_bias, in_part, branch_all, sums2, in_sums,
        *down_parts, w_qkv, tok, middle_grad, gain, first_all,
    )


def body(
    tokens,
    out_grad,
    seq_lengths,
    seq_scripts,
    seq_place,
    norm1_gain,
    norm1_shift,
    w_qkv,
    qv_bias,
    w_out,
    out_bias,
    norm2_gain,
    norm2_shift,
    w_in,
    in_bias,
    w_down,
    down_bias,
):
    own, depth = tokens.shape
    devices = lax.axis_size("mp")
    plan = Plan(devices)
    fine = Plan(devices, 2)
    rows = own * devices
    width = w_qkv.shape[2]
    block = min(512, rows)
    order = (seq_lengths, seq_scripts, seq_place)

    def line(vector):
        return vector.reshape(1, -1)

    (
        first_all, qkv, att, sums, grad_all, second_all, activated, hidden_grad, middle, in_part,
    ) = run_front(
        plan, fine, block, tokens, line(norm1_gain), line(norm1_shift), w_qkv, qv_bias, order, out_grad,
        w_out, line(out_bias), line(norm2_gain), line(norm2_shift), w_in, line(in_bias), w_down,
    )
    groups = lax.axis_size("batch")
    middle_grad, branch_all, att_grad, sums2, in_sums, *down_parts, in_part2 = run_middle(
        fine, groups, hidden_grad, w_in, middle, out_grad, line(norm2_gain), w_out, activated, grad_all, second_all,
        in_part,
    )
    (
        block_out, input_grad, down_weight_grad, in_weight_grad, out_weight_grad, qkv_weight_grad,
        vectors2, spread2, vectors, spread,
    ) = run_back(
        plan, groups, block, order, qkv, att, att_grad, sums, activated, w_down, middle, line(down_bias),
        in_part2, branch_all, sums2, in_sums, down_parts, w_qkv, tokens, middle_grad, line(norm1_gain), first_all,
    )
    qv_bias_grad = jnp.stack([spread[:, :width].reshape(-1), spread[:, width:].reshape(-1)])
    return (
        block_out,
        input_grad,
        vectors[0],
        vectors[1],
        qkv_weight_grad,
        qv_bias_grad,
        out_weight_grad,
        vectors2[2],
        vectors2[0],
        vectors2[1],
        in_weight_grad,
        spread2[:, 2 * width :].reshape(-1),
        down_weight_grad,
        vectors2[3],
    )


def solution(mesh):
    return jax.shard_map(
        body,
        mesh=mesh,
        in_specs=(
            P(("batch", "mp"), None),
            P(("batch", "mp"), None),
            P(),
            P(),
            P(),
            P(),
            P(),
            P(None, None, "mp"),
            P(None, "mp"),
            P("mp", None),
            P(),
            P(),
            P(),
            P(None, "mp"),
            P("mp"),
            P("mp", None),
            P(),
        ),
        out_specs=(
            P(("batch", "mp"), None),
            P(("batch", "mp"), None),
            P(),
            P(),
            P(None, "batch", "mp"),
            P(),
            P("mp", "batch"),
            P(),
            P(),
            P(),
            P("batch", "mp"),
            P(),
            P("mp", "batch"),
            P(),
        ),
        check_vma=False,
    )
```

```python
import functools

import jax
import jax.numpy as jnp
from jax import lax
from jax.experimental import pallas as pl
from jax.experimental.pallas import tpu as pltpu
from jax.sharding import PartitionSpec as P

HEAD_DIM = 128
EPS = 1e-05
NEGATIVE = -1e30
LOG2E = 1.4426950408889634
f32 = jnp.float32
bf16 = jnp.bfloat16
MESH = pl.DeviceIdType.MESH
ANY = pl.BlockSpec(memory_space=pl.ANY)
VMEM = pl.BlockSpec(memory_space=pltpu.VMEM)
SMEM = pl.BlockSpec(memory_space=pltpu.SMEM)


def dot(left, right, contract_left, contract_right):
    return lax.dot_general(
        left,
        right,
        (((contract_left,), (contract_right,)), ((), ())),
        preferred_element_type=f32,
    )


def flip(index, mask):
    bit = 1
    while bit <= mask:
        if mask & bit:
            index = index + bit * (1 - 2 * lax.rem(lax.div(index, bit), 2))
        bit *= 2
    return index


def loop(count, step, body):
    def one(index, carry):
        body(pl.multiple_of(index * step, step))
        return carry

    lax.fori_loop(0, count // step, one, 0)


class Plan:
    def __init__(self, devices, halves=1):
        bits = []
        bit = 2
        while bit < devices:
            bits.append(bit)
            bit *= 2
        self.devices = devices
        self.bits = bits
        self.ways = [tuple(bits)] + ([tuple(reversed(bits))] if len(bits) > 1 else [])
        self.halves = halves
        self.orders = self.ways * halves
        self.parts = len(self.orders)
        self.offsets = list(range(0, devices, 2))
        self.keys = [(part, offset) for part in range(self.parts) for offset in self.offsets if offset]
        self.keys.sort(key=lambda key: (self.half(key[0]), bin(key[1]).count("1"), self.last(*key)))
        self.shares = [(part, offset) for offset in self.offsets for part in range(self.parts)]

    def half(self, part):
        return part // len(self.ways)

    def parts_of(self, half):
        return range(half * len(self.ways), (half + 1) * len(self.ways))

    def last(self, part, offset):
        steps = [step for step, bit in enumerate(self.orders[part]) if bit & offset]
        return max(steps) if steps else -1

    def bit(self, part, offset):
        return self.orders[part][self.last(part, offset)]

    def later(self, part, offset):
        order = self.orders[part]
        return [offset | order[step] for step in range(self.last(part, offset) + 1, len(order))]


class Place:
    def __init__(self, plan):
        self.plan = plan
        self.batch = lax.axis_index("batch")
        self.groups = lax.axis_size("batch")
        self.me = lax.axis_index("mp")

    def at(self, mask):
        return (self.batch, flip(self.me, mask))

    def beside(self, step):
        return (self.batch + step, self.me)

    def around(self, step):
        return (lax.rem(self.batch + step, self.groups), self.me)

    def barrier(self, groups=False):
        semaphore = pltpu.get_barrier_semaphore()
        partners = [self.at(mask) for mask in [1] + self.plan.bits]
        if groups:
            partners += [self.around(step) for step in range(1, self.groups)]
        for partner in partners:
            pl.semaphore_signal(semaphore, inc=1, device_id=partner, device_id_type=MESH)
        pl.semaphore_wait(semaphore, len(partners))


class Total:
    def __init__(self, place, value, sent, came, slots, sems):
        self.place, self.value, self.sent, self.came, self.slots = place, value, sent, came, slots
        self.send, self.recv, self.slot_send, self.slot_recv = sems

    def plane(self, others=()):
        totals = (self,) + tuple(others)
        for index, mask in enumerate([1] + self.place.plan.bits):
            copies = [
                pltpu.make_async_remote_copy(
                    src_ref=total.sent.at[index],
                    dst_ref=total.came.at[index],
                    send_sem=total.send.at[index],
                    recv_sem=total.recv.at[index],
                    device_id=self.place.at(mask),
                    device_id_type=MESH,
                )
                for total in totals
            ]
            for total, copy in zip(totals, copies):
                total.sent[index] = total.value[...]
                copy.start()
            for total, copy in zip(totals, copies):
                copy.wait_recv()
                total.value[...] = total.sent[index] + total.came[index]
                copy.wait_send()

    def slot(self, step):
        return pltpu.make_async_remote_copy(
            src_ref=self.value,
            dst_ref=self.slots.at[step],
            send_sem=self.slot_send.at[step - 1],
            recv_sem=self.slot_recv.at[step - 1],
            device_id=self.place.around(step),
            device_id_type=MESH,
        )

    def begin(self):
        self.slots[0] = self.value[...]
        for step in range(1, self.place.groups):
            self.slot(step).start()

    def end(self, result):
        for step in range(1, self.place.groups):
            self.slot(step).wait()
        groups = self.place.groups
        total = self.slots[self.place.batch]
        for group in range(1, groups):
            total = total + self.slots[lax.rem(self.place.batch + groups - group, groups)]
        result[...] = total

    @staticmethod
    def scratch(plan, groups, shape):
        rounds = len(plan.bits) + 1
        return [
            pltpu.VMEM(shape, f32),
            pltpu.VMEM((rounds,) + shape, f32),
            pltpu.VMEM((rounds,) + shape, f32),
            pltpu.VMEM((groups,) + shape, f32),
            pltpu.SemaphoreType.DMA((rounds,)),
            pltpu.SemaphoreType.DMA((rounds,)),
            pltpu.SemaphoreType.DMA((max(groups - 1, 1),)),
            pltpu.SemaphoreType.DMA((max(groups - 1, 1),)),
        ]


class Gather:
    def __init__(self, place, buf, own, rows, sems):
        self.place, self.plan, self.buf, self.own, self.rows = place, place.plan, buf, own, rows
        self.link_send, self.link_recv, self.core_send, self.core_recv = sems
        self.part_rows = rows // self.plan.parts

    def span(self, mask, part):
        block = flip(self.place.me, mask)
        start = block * self.rows + part * self.part_rows
        return self.buf.at[pl.ds(pl.multiple_of(start, self.part_rows), self.part_rows), :]

    def source(self, offset, part):
        if offset == 0 and self.own is not None:
            return self.own.at[pl.ds(part * self.part_rows, self.part_rows), :]
        return self.span(offset, part)

    def link(self, key):
        part, offset = key
        bit = self.plan.bit(part, offset)
        index = self.plan.keys.index(key)
        return pltpu.make_async_remote_copy(
            src_ref=self.source(offset ^ bit, part),
            dst_ref=self.span(offset ^ bit, part),
            send_sem=self.link_send.at[index],
            recv_sem=self.link_recv.at[index],
            device_id=self.place.at(bit),
            device_id_type=MESH,
        )

    def core(self, key):
        part, offset = key
        index = self.plan.shares.index(key)
        return pltpu.make_async_remote_copy(
            src_ref=self.source(offset, part),
            dst_ref=self.span(offset, part),
            send_sem=self.core_send.at[index],
            recv_sem=self.core_recv.at[index],
            device_id=self.place.at(1),
            device_id_type=MESH,
        )

    def landed(self, ref, semaphore):
        pltpu.make_async_remote_copy(
            src_ref=ref,
            dst_ref=ref,
            send_sem=semaphore,
            recv_sem=semaphore,
            device_id=self.place.at(1),
            device_id_type=MESH,
        ).wait_recv()

    def start(self, half=0, ahead=None):
        if ahead in (None, False):
            for part in self.plan.parts_of(half):
                self.core((part, 0)).start()
        for key in self.plan.keys:
            if bin(key[1]).count("1") == 1 and self.plan.half(key[0]) == half:
                if ahead is None or ahead == (self.plan.last(*key) == 0):
                    self.link(key).start()

    def arrive(self, key):
        part, offset = key
        self.landed(self.span(offset, part), self.link_recv.at[self.plan.keys.index(key)])
        for target in self.plan.later(part, offset):
            self.link((part, target)).start()
        self.core(key).start()

    def share(self, offset, half=0):
        for part in self.plan.parts_of(half):
            index = self.plan.shares.index((part, offset))
            self.landed(self.span(offset | 1, part), self.core_recv.at[index])

    def steps(self):
        result = []
        for half in range(self.plan.halves):
            for count in range(1, len(self.plan.bits) + 1):
                keys = [
                    key
                    for key in self.plan.keys
                    if self.plan.half(key[0]) == half and bin(key[1]).count("1") == count
                ]
                offsets = [offset for offset in self.plan.offsets if bin(offset).count("1") == count]
                result.append((half, keys, offsets))
        return result

    def pieces(self, offset, half):
        count = self.rows // self.plan.halves
        chip = lax.div(flip(self.place.me, offset), 2) * 2
        return [
            pl.ds(pl.multiple_of((chip + core) * self.rows + half * count, count), count) for core in range(2)
        ]

    def finish(self):
        for key in self.plan.keys:
            self.link(key).wait_send()
        for key in self.plan.shares:
            self.core(key).wait_send()

    @staticmethod
    def semaphores(plan):
        return [pltpu.SemaphoreType.DMA((len(plan.keys),))] * 2 + [
            pltpu.SemaphoreType.DMA((len(plan.shares),))
        ] * 2


class Spread:
    dtype = bf16

    def __init__(self, refs):
        self.refs = refs

    def __setitem__(self, index, value):
        count = self.refs[0].shape[0]
        for number, ref in enumerate(self.refs):
            ref[index] = value[number * count : (number + 1) * count]


class Scatter:
    def __init__(self, place, rows, width, core_out, core_in, kept, link_out, link_in, sems):
        self.place, self.plan, self.rows, self.width = place, place.plan, rows, width
        self.core_out, self.core_in, self.kept = core_out, core_in, kept
        self.link_out, self.link_in = link_out, link_in
        self.link_send, self.link_recv, self.core_send, self.core_recv = sems
        self.part_rows = rows // self.plan.parts
        self.step = min(32, self.part_rows)
        self.order = sorted(self.plan.offsets, key=lambda offset: -bin(offset).count("1"))

    def core(self, offset):
        index = offset // 2
        return pltpu.make_async_remote_copy(
            src_ref=self.core_out.at[index],
            dst_ref=self.core_in.at[index],
            send_sem=self.core_send.at[index],
            recv_sem=self.core_recv.at[index],
            device_id=self.place.at(1),
            device_id_type=MESH,
        )

    def link(self, key):
        index = self.plan.keys.index(key)
        return pltpu.make_async_remote_copy(
            src_ref=self.link_out.at[index],
            dst_ref=self.link_in.at[index],
            send_sem=self.link_send.at[index],
            recv_sem=self.link_recv.at[index],
            device_id=self.place.at(self.plan.bit(*key)),
            device_id_type=MESH,
        )

    def keep(self, offset):
        if offset == 0:
            return self.kept
        return Spread([self.link_out.at[self.plan.keys.index((part, offset))] for part in range(self.plan.parts)])

    def total(self, offset, part, start, arrived):
        rows = pl.ds(pl.multiple_of(part * self.part_rows + start, self.step), self.step)
        if offset:
            value = self.link_out[self.plan.keys.index((part, offset)), pl.ds(start, self.step), :].astype(f32)
        else:
            value = self.kept[rows, :].astype(f32)
        value += self.core_in[offset // 2, rows, :].astype(f32)
        for key in arrived:
            value += self.link_in[self.plan.keys.index(key), pl.ds(start, self.step), :].astype(f32)
        return value

    def pass_on(self, part, offset):
        arrived = [(part, target) for target in self.plan.later(part, offset)]
        for key in arrived:
            self.link(key).wait_recv()
        index = self.plan.keys.index((part, offset))

        def add(start):
            self.link_out[index, pl.ds(start, self.step), :] = self.total(
                offset, part, start, arrived
            ).astype(bf16)

        loop(self.part_rows, self.step, add)
        self.link((part, offset)).start()

    def free(self, offset, half):
        for part in self.plan.parts_of(half):
            if offset and not self.plan.later(part, offset):
                self.pass_on(part, offset)

    def bound(self, half):
        for offset in self.order:
            for part in self.plan.parts_of(half):
                if offset and self.plan.later(part, offset):
                    self.pass_on(part, offset)

    def begin(self, partial, between=None):
        for number, offset in enumerate(self.order):
            index = offset // 2
            if offset == 0:
                self.bound(0)
            partial(flip(self.place.me, offset | 1), self.core_out.at[index])
            self.core(offset).start()
            partial(flip(self.place.me, offset), self.keep(offset))
            self.core(offset).wait_recv()
            for half in range(self.plan.halves):
                self.free(offset, half)
            if between is not None:
                between(number)

    def middle(self):
        for half in range(1, self.plan.halves):
            self.bound(half)

    def end(self, use, half=0):
        for part in self.plan.parts_of(half):
            arrived = [(part, target) for target in self.plan.later(part, 0)]
            for key in arrived:
                self.link(key).wait_recv()

            def piece(start):
                row = pl.multiple_of(part * self.part_rows + start, self.step)
                use(row, self.step, self.total(0, part, start, arrived))

            loop(self.part_rows, self.step, piece)

    def finish(self):
        for key in self.plan.keys:
            self.link(key).wait_send()
        for offset in self.plan.offsets:
            self.core(offset).wait_send()

    @staticmethod
    def scratch(plan, rows, width, kept):
        chips, keys = len(plan.offsets), len(plan.keys)
        return [
            pltpu.VMEM((chips, rows, width), bf16),
            pltpu.VMEM((chips, rows, width), bf16),
            pltpu.VMEM((rows, width), kept),
            pltpu.VMEM((keys, rows // plan.parts, width), bf16),
            pltpu.VMEM((keys, rows // plan.parts, width), bf16),
            pltpu.SemaphoreType.DMA((keys,)),
            pltpu.SemaphoreType.DMA((keys,)),
            pltpu.SemaphoreType.DMA((chips,)),
            pltpu.SemaphoreType.DMA((chips,)),
        ]


class Slices:
    def __init__(self, ref, rows, columns):
        self.ref, self.shape = ref, (None, rows, columns)

    def part(self, target):
        rows = self.shape[1]
        start = target * rows
        start = start if isinstance(start, int) else pl.multiple_of(start, rows)
        return self.ref.at[pl.ds(start, rows), pl.ds(0, self.shape[2])]


def add_columns(parts, target, columns):
    rows, width = parts[0].shape
    step = min(32, rows)

    def rows_of(start):
        value = parts[0][pl.ds(start, step), :].astype(f32)
        for part in parts[1:]:
            value += part[pl.ds(start, step), :].astype(f32)
        for index in range(width // columns):
            lines = pl.ds(pl.multiple_of(index * rows + start, step), step)
            target[lines, :] = value[:, index * columns : (index + 1) * columns]

    loop(rows, step, rows_of)


def column_pieces(target, rows, width, columns):
    return [target.at[pl.ds(index * rows, rows), :] for index in range(width // columns)]


class Line:
    def __init__(self, place, own, up, down, pieces, sems, early=False):
        self.place, self.own, self.up, self.down, self.pieces = place, own, up, down, pieces
        self.early = early and place.groups > 2
        self.groups, self.batch = place.groups, place.batch
        self.rows = own.shape[1] // pieces
        self.step = min(32, self.rows)
        self.sems = sems

    def span(self, piece):
        start = piece * self.rows
        return pl.ds(start if isinstance(start, int) else pl.multiple_of(start, self.rows), self.rows)

    def part(self, target):
        return self.own.part(target) if isinstance(self.own, Slices) else self.own.at[target]

    def slot(self, upward, target):
        return self.up.at[target - 1] if upward else self.down.at[target]

    def copy(self, upward, target, piece, source):
        send, recv = self.sems[:2] if upward else self.sems[2:]
        index = target * self.pieces + piece
        return pltpu.make_async_remote_copy(
            src_ref=source.at[self.span(piece), :],
            dst_ref=self.slot(upward, target).at[self.span(piece), :],
            send_sem=send.at[index],
            recv_sem=recv.at[index],
            device_id=self.place.beside(1 if upward else -1),
            device_id_type=MESH,
        )

    def sent(self, target, farthest, pieces=None):
        pieces = list(range(self.pieces) if pieces is None else pieces)
        return [piece for piece in pieces if not (self.early and target == farthest and piece == 0)]

    def start(self, target, near=None, pieces=None):
        if target > 0 and near in (None, target == 1):

            @pl.when(self.batch == 0)
            def first():
                for piece in self.sent(target, self.groups - 1, pieces):
                    self.copy(True, target, piece, self.part(target)).start()

        if target < self.groups - 1 and near in (None, target == self.groups - 2):

            @pl.when(self.batch == self.groups - 1)
            def last():
                for piece in self.sent(target, 0, pieces):
                    self.copy(False, target, piece, self.part(target)).start()

    def start_near(self, pieces=None):
        for target in range(self.groups):
            self.start(target, True, pieces)

    def order(self):
        count = self.groups
        result = []
        for index in range((count + 1) // 2):
            for target in (count - 1 - index, index):
                if target not in result:
                    result.append(target)
        return result

    def ticks(self):
        return range(1, (self.groups - 1) * self.pieces + self.groups)

    def tick(self, number):
        for upward in (True, False):
            place = self.batch if upward else self.groups - 1 - self.batch
            for distance in range(2, self.groups):
                target = distance if upward else self.groups - 1 - distance
                piece = number - (self.groups - 1 - distance) * self.pieces - place
                due = (place > 0) & (place < distance) & (piece >= 0) & (piece < self.pieces)

                @pl.when(due)
                def forward():
                    slot = self.slot(upward, target)
                    copy = self.copy(upward, target, piece, slot)
                    if not (self.early and number == 1):
                        copy.wait_recv()

                    def add(start):
                        rows = pl.ds(pl.multiple_of(piece * self.rows + start, self.step), self.step)
                        total = slot[rows, :].astype(f32) + self.part(target)[rows, :].astype(f32)
                        slot[rows, :] = total.astype(bf16)

                    loop(self.rows, self.step, add)
                    copy.start()

    def export(self, outs, moves, columns=None):
        below, above = self.batch > 0, self.batch < self.groups - 1
        jobs = []
        for out, there, upward in ((outs[0], None, None), (outs[1], below, True), (outs[2], above, False)):
            slot = self.part(self.batch) if there is None else self.slot(upward, self.batch)
            if columns is None:
                copies = [moves.make(slot, out)]
            else:
                copies = [
                    moves.make(slot.at[:, pl.ds(part * columns, columns)], out.at[part])
                    for part in range(out.shape[0])
                ]
            jobs.append((there, copies))

            def begin():
                if there is not None:
                    for piece in range(self.pieces):
                        self.copy(upward, self.batch, piece, slot).wait_recv()
                for copy in copies:
                    copy.start()

            begin() if there is None else pl.when(there)(begin)

        def wait():
            for there, copies in jobs:

                def done():
                    for copy in copies:
                        copy.wait()

                done() if there is None else pl.when(there)(done)

        return wait

    def add(self, target, columns):
        below, above = self.batch > 0, self.batch < self.groups - 1
        for there, upward in ((below, True), (above, False)):

            @pl.when(there)
            def come():
                slot = self.slot(upward, self.batch)
                for piece in range(self.pieces):
                    self.copy(upward, self.batch, piece, slot).wait_recv()

        own = self.part(self.batch)

        def sides(chosen):
            slots = [self.slot(upward, self.batch) for upward in chosen]
            add_columns([own] + slots, target, columns)

        pl.when(jnp.logical_not(above))(lambda: sides([True]))
        pl.when(jnp.logical_not(below))(lambda: sides([False]))
        pl.when(below & above)(lambda: sides([True, False]))
        return column_pieces(target, own.shape[0], own.shape[1], columns)

    def finish(self):
        for target in range(self.groups):
            for upward in (True, False):
                if target == (0 if upward else self.groups - 1):
                    continue

                slot = self.slot(upward, target)
                farthest = self.groups - 1 if upward else 0
                passes = self.batch < target if upward else self.batch > target
                inner = self.batch > 0 if upward else self.batch < self.groups - 1

                @pl.when(passes)
                def sent():
                    for piece in self.sent(target, farthest):
                        self.copy(upward, target, piece, slot).wait_send()

                if self.early and target == farthest:

                    @pl.when(passes & inner)
                    def sent_first():
                        self.copy(upward, target, 0, slot).wait_send()

    @staticmethod
    def scratch(groups, rows, columns, pieces):
        return [
            pltpu.VMEM((groups, rows, columns), bf16),
            pltpu.VMEM((groups - 1, rows, columns), bf16),
            pltpu.VMEM((groups - 1, rows, columns), bf16),
        ] + [pltpu.SemaphoreType.DMA((groups * pieces,))] * 4


class Moves:
    def __init__(self, sems):
        self.sems, self.count = sems, 0

    def make(self, source, target):
        copy = pltpu.make_async_copy(source, target, self.sems.at[self.count])
        self.count += 1
        return copy

    def start(self, source, target):
        copy = self.make(source, target)
        copy.start()
        return copy


def norm_rows(rows):
    mean = jnp.mean(rows, axis=-1, keepdims=True)
    centred = rows - mean
    inverse = lax.rsqrt(jnp.mean(centred * centred, axis=-1, keepdims=True) + EPS)
    return centred * inverse, inverse


def norm_back(grad, unit, inverse, gain):
    scaled = grad * gain
    return inverse * (
        scaled
        - jnp.mean(scaled, axis=-1, keepdims=True)
        - unit * jnp.mean(scaled * unit, axis=-1, keepdims=True)
    )


def segment_starts(group, lengths, scripts, places, rows):
    position = lax.broadcasted_iota(jnp.int32, (1, rows), 1)
    first = jnp.zeros((1, rows), jnp.int32)
    count = lengths.shape[0]
    number = [lengths[index] for index in range(count)]
    script = [scripts[index] for index in range(count)]
    mine = [places[index] == group for index in range(count)]
    own = [jnp.where(mine[index], number[index], 0) for index in range(count)]
    total = own[0]
    for index in range(1, count):
        total = total + own[index]
    for index in range(count):
        offset = jnp.int32(0)
        for other in range(count):
            if other < index:
                offset = offset + jnp.where(script[other] <= script[index], own[other], 0)
            elif other > index:
                offset = offset + jnp.where(script[other] < script[index], own[other], 0)
        bound = jnp.where(mine[index], offset, 0)
        first = jnp.maximum(first, jnp.where(position >= bound, bound, 0))
    return jnp.maximum(first, jnp.where(position >= total, total, 0))


def head_columns(part, head, width):
    return pl.ds(part * width + head * HEAD_DIM, HEAD_DIM)


def params(number):
    return pltpu.CompilerParams(
        collective_id=number, has_side_effects=True, vmem_limit_bytes=62 * 2**20
    )


def cost(micros):
    return pl.CostEstimate(flops=micros * 10**9, bytes_accessed=10**7, transcendentals=0)


def joined(ref, pieces):
    return jnp.concatenate([ref[piece, :] for piece in pieces], axis=0)


def front_kernel(
    plan, fine, block, tok, gain1, shift1, w_qkv, qv_bias, lengths, scripts, places, out_grad,
    w_out, out_bias, gain, shift, w_in, in_bias, w_down,
    first_out, qkv_out, att_out, sum_out, grad_out, second_out, act_out, hidden_out, middle_out, bias_out,
    starts, sums, attended, w_o, w_i, w_d, grad_in, up, buf, act, back, middle, local, *rest,
):
    first_sems, grad_sems, gather_sems, scatter_refs = rest[:4], rest[4:8], rest[8:12], rest[12:]
    place = Place(plan)
    own, depth = tok.shape
    rows = buf.shape[0]
    width = w_qkv.shape[2]
    hidden_width = w_in.shape[1]
    chip_rows = 2 * own
    moves = Moves(local)
    qkv = act.at[:, pl.ds(0, 3 * width)]
    weights = back.at[pl.ds(0, depth), pl.ds(0, 3 * width)]
    loads = [
        moves.start(w_qkv.at[part], back.at[pl.ds(0, depth), pl.ds(part * width, width)]) for part in range(3)
    ]
    load_out = moves.start(w_out, w_o)
    load_down = moves.start(w_down, w_d)
    load_in = moves.start(w_in, w_i)
    place.barrier()
    grads = Gather(place, grad_out, out_grad, own, grad_sems)
    grads.start(0, True)
    step = min(32, own)
    mine = pl.multiple_of(place.me * own, own)

    def normalise(start):
        unit, _ = norm_rows(tok[pl.ds(start, step), :].astype(f32))
        buf[pl.ds(pl.multiple_of(mine + start, step), step), :] = (unit * gain1[...] + shift1[...]).astype(bf16)

    loop(own, step, normalise)
    gather = Gather(place, buf, None, own, first_sems)
    gather.start()
    stores = [moves.start(out_grad, grad_out.at[pl.ds(mine, own), :])]
    starts[...] = segment_starts(place.batch, lengths, scripts, places, rows)
    for copy in loads:
        copy.wait()

    def project(offset):
        chip = lax.div(flip(place.me, offset), 2)
        span = pl.ds(pl.multiple_of(chip * chip_rows, chip_rows), chip_rows)
        stores.append(moves.start(buf.at[span, :], first_out.at[span, :]))
        product = dot(buf[span, :], weights[...], 1, 0)
        qkv[span, 0:width] = (product[:, 0:width] + qv_bias[0:1, :]).astype(bf16)
        qkv[span, width : 2 * width] = product[:, width : 2 * width].astype(bf16)
        qkv[span, 2 * width : 3 * width] = (product[:, 2 * width :] + qv_bias[1:2, :]).astype(bf16)

    gather.share(0)
    project(0)
    steps = gather.steps()
    for number, (half, keys, offsets) in enumerate(steps):
        for key in keys:
            gather.arrive(key)
        if number == max(len(steps) - 2, 0):
            grads.start(0, False)
        for offset in offsets:
            gather.share(offset)
            project(offset)
    gather.finish()
    stores.append(moves.start(qkv, qkv_out))

    scale = HEAD_DIM ** (-0.5) * LOG2E
    heads = width // HEAD_DIM
    row_in = lax.broadcasted_iota(jnp.int32, (block, block), 0)
    col_in = lax.broadcasted_iota(jnp.int32, (block, block), 1)
    key_in = lax.broadcasted_iota(jnp.int32, (block, 1), 0)

    def attend(index):
        span = pl.ds(index * block, block)
        first = starts[:, span]
        queries = [qkv[span, head_columns(0, head, width)] for head in range(heads)]

        def against(key_block, carry, diagonal):
            key_span = pl.ds(pl.multiple_of(key_block * block, block), block)
            allowed = key_in + key_block * block >= first
            if diagonal:
                allowed = allowed & (row_in <= col_in)
            result = []
            for head in range(heads):
                top, total, mixed = carry[head]
                keys = qkv[key_span, head_columns(1, head, width)]
                values = qkv[key_span, head_columns(2, head, width)]
                scores = jnp.where(allowed, dot(keys, queries[head], 1, 1) * scale, NEGATIVE)
                new_top = jnp.maximum(top, jnp.max(scores, axis=0, keepdims=True))
                exps = jnp.exp2(scores - new_top)
                fade = jnp.exp2(top - new_top)
                total = total * fade + jnp.sum(exps, axis=0, keepdims=True)
                mixed = mixed * fade + dot(values, exps.astype(bf16), 0, 0)
                result.append((new_top, total, mixed))
            return tuple(result)

        carry = tuple(
            (
                jnp.full((1, block), NEGATIVE, f32),
                jnp.zeros((1, block), f32),
                jnp.zeros((HEAD_DIM, block), f32),
            )
            for head in range(heads)
        )
        if index:
            carry = lax.fori_loop(0, index, lambda key_block, c: against(key_block, c, False), carry)
        carry = against(index, carry, True)
        for head in range(heads):
            top, total, mixed = carry[head]
            attended[span, pl.ds(head * HEAD_DIM, HEAD_DIM)] = (mixed * (1.0 / total)).T.astype(bf16)
            sums[pl.ds(head, 1), span] = top + jnp.log2(total)

    blocks = rows // block
    waiting = [key for _, keys, _ in steps for key in keys]
    for index in range(blocks):
        attend(index)
        if index == blocks - 2:
            while waiting and plan.later(*waiting[0]) and bin(waiting[0][1]).count("1") == 1:
                grads.arrive(waiting.pop(0))
    for copy in stores:
        copy.wait()
    stores = [moves.start(attended, att_out), moves.start(sums, sum_out)]

    place = Place(fine)
    scatter = Scatter(place, own, depth, *scatter_refs[:5], scatter_refs[5:])
    load_out.wait()
    tile = min(1024, depth)

    def partial(owner, target):
        lines = attended[pl.ds(pl.multiple_of(owner * own, own), own), :]

        def columns(start):
            target[:, pl.ds(start, tile)] = dot(lines, w_o[:, pl.ds(start, tile)], 1, 0).astype(target.dtype)

        loop(depth, tile, columns)

    grad_loads = {}

    def load_grad(number):
        lines = pl.ds(number * own, own)
        grad_loads[number] = moves.start(grad_out.at[lines, :], grad_in.at[number % 2])

    def between(number):
        if number == max(len(plan.offsets) - 2, 0):
            for key in waiting:
                grads.arrive(key)
            for offset in plan.offsets:
                grads.share(offset)
            load_grad(0)
            load_grad(1)

    part_cols = min(512, hidden_width)
    chips = rows // own

    def raise_grad(number):
        grad_loads[number].wait()

        def columns(start):
            cols = pl.ds(start, part_cols)
            up[pl.ds(number * own, own), cols] = dot(grad_in[number % 2], w_d[cols, :], 1, 1)

        loop(hidden_width, part_cols, columns)
        if number + 2 < chips:
            load_grad(number + 2)

    scatter.begin(partial, between)
    load_down.wait()
    for number in range(chips):
        raise_grad(number)
    scatter.middle()
    grads.finish()

    def close(start, count, value):
        span = pl.ds(start, count)
        total = tok[span, :].astype(f32) + value + out_bias[...]
        middle[span, :] = total
        unit, _ = norm_rows(total)
        buf[pl.ds(pl.multiple_of(mine + start, count), count), :] = (unit * gain[...] + shift[...]).astype(bf16)

    gather = Gather(place, buf, None, own, gather_sems)
    for half in range(fine.halves):
        scatter.end(close, half)
        gather.start(half)
    scatter.finish()
    stores.append(moves.start(middle, middle_out))
    load_in.wait()
    bias_out[...] = jnp.zeros_like(bias_out)

    def expand(offset, half):
        pieces = gather.pieces(offset, half)
        count = own // fine.halves

        def columns(start):
            cols = pl.ds(start, part_cols)
            pre = dot(joined(buf, pieces), w_i[:, cols], 1, 0) + in_bias[:, cols]
            raised = jnp.concatenate([up[piece, cols] for piece in pieces], axis=0)
            root = 0.7978845608028654
            square = pre * pre
            inner = jnp.tanh(root * (pre + 0.044715 * (square * pre)))
            rise = 0.5 * (1.0 + inner)
            slope = rise + 0.5 * pre * (1.0 - inner * inner) * (root * (1.0 + 3 * 0.044715 * square))
            lifted = (pre * rise).astype(bf16)
            down = (raised * slope).astype(bf16)
            for index, piece in enumerate(pieces):
                act[piece, cols] = lifted[index * count : (index + 1) * count]
                back[piece, cols] = down[index * count : (index + 1) * count]
            bias_out[:, cols] += jnp.sum(down.astype(f32), axis=0, keepdims=True)

        loop(hidden_width, part_cols, columns)
        for piece in pieces:
            stores.append(moves.start(buf.at[piece, :], second_out.at[piece, :]))
            stores.append(moves.start(act.at[piece, :], act_out.at[piece, :]))
            stores.append(moves.start(back.at[piece, :], hidden_out.at[piece, :]))

    for half in range(fine.halves):
        gather.share(0, half)
        expand(0, half)
    for half, keys, offsets in gather.steps():
        for key in keys:
            gather.arrive(key)
        for offset in offsets:
            gather.share(offset, half)
            expand(offset, half)
    gather.finish()
    for copy in stores:
        copy.wait()


def run_front(
    plan, fine, block, tok, gain1, shift1, w_qkv, qv_bias, order, out_grad, w_out, out_bias, gain, shift, w_in, in_bias,
    w_down,
):
    own, depth = tok.shape
    rows = own * plan.devices
    width = w_qkv.shape[2]
    hidden = w_in.shape[1]
    return pl.pallas_call(
        functools.partial(front_kernel, plan, fine, block),
        out_shape=(
            jax.ShapeDtypeStruct((rows, depth), bf16),
            jax.ShapeDtypeStruct((rows, 3 * width), bf16),
            jax.ShapeDtypeStruct((rows, width), bf16),
            jax.ShapeDtypeStruct((8, rows), f32),
            jax.ShapeDtypeStruct((rows, depth), bf16),
            jax.ShapeDtypeStruct((rows, depth), bf16),
            jax.ShapeDtypeStruct((rows, hidden), bf16),
            jax.ShapeDtypeStruct((rows, hidden), bf16),
            jax.ShapeDtypeStruct((own, depth), f32),
            jax.ShapeDtypeStruct((1, hidden), f32),
        ),
        in_specs=[VMEM, VMEM, VMEM, ANY, VMEM, SMEM, SMEM, SMEM, ANY, ANY, VMEM, VMEM, VMEM, ANY, VMEM, ANY],
        out_specs=(ANY,) * 9 + (VMEM,),
        scratch_shapes=[
            pltpu.VMEM((1, rows), jnp.int32),
            pltpu.VMEM((8, rows), f32),
            pltpu.VMEM((rows, width), bf16),
            pltpu.VMEM((width, depth), bf16),
            pltpu.VMEM((depth, hidden), bf16),
            pltpu.VMEM((hidden, depth), bf16),
            pltpu.VMEM((2, own, depth), bf16),
            pltpu.VMEM((rows, hidden), f32),
            pltpu.VMEM((rows, depth), bf16),
            pltpu.VMEM((rows, hidden), bf16),
            pltpu.VMEM((max(rows, depth), hidden), bf16),
            pltpu.VMEM((own, depth), f32),
            pltpu.SemaphoreType.DMA((160,)),
        ]
        + Gather.semaphores(plan) * 2
        + Gather.semaphores(fine)
        + Scatter.scratch(fine, own, depth, bf16),
        compiler_params=params(0),
        name="front",
        cost_estimate=cost(150),
    )(tok, gain1, shift1, w_qkv, qv_bias, *order, out_grad, w_out, out_bias, gain, shift, w_in, in_bias, w_down)


PIECES = 2


def add_parts(place, parts, target, columns):
    below, above = place.batch > 0, place.batch < place.groups - 1
    pl.when(jnp.logical_not(above))(lambda: add_columns([parts[0], parts[1]], target, columns))
    pl.when(jnp.logical_not(below))(lambda: add_columns([parts[0], parts[2]], target, columns))
    pl.when(below & above)(lambda: add_columns(parts, target, columns))


def spread_rows(place, target, rows):
    mine = lax.broadcasted_iota(jnp.int32, (target.shape[0], 1), 0) == place.me
    start = 0
    for row in rows:
        target[:, pl.ds(start, row.shape[1])] = jnp.where(mine, row, 0.0)
        start += row.shape[1]


def middle_kernel(
    plan, hidden_grad, w_in, middle, out_grad, gain, w_out, activated, grad_all, second_all, in_sums,
    middle_grad_out, branch_out, att_grad_out, sums_out, in_sums_out, down_out0, down_out1, down_out2, in_part_out, early_out,
    h_in, w_i, w_o, buf, middle_grad, att_grad, act, staged, local, early_send, early_recv, *rest,
):
    down_outs = (down_out0, down_out1, down_out2)
    scatter_refs, gather_sems, line_refs, total_refs = rest[:9], rest[9:13], rest[13:20], rest[20:]
    place = Place(plan)
    own, depth = middle.shape
    rows = buf.shape[0]
    chip_rows = 2 * own
    hidden = w_in.shape[1]
    groups = place.groups
    cut = depth // groups
    moves = Moves(local)
    loads = [moves.start(hidden_grad, h_in), moves.start(w_in, w_i)]
    load_act = moves.start(activated, act)
    order = [index for pair in zip(range(groups - 1, -1, -1), range(groups)) for index in pair][:groups]
    load_grad = [
        moves.start(grad_all.at[:, pl.ds(target * cut, cut)], buf.at[:, pl.ds(target * cut, cut)])
        for target in order
    ]
    load_out = moves.start(w_out, w_o)
    place.barrier(groups=True)
    scatter = Scatter(place, own, depth, *scatter_refs[:5], scatter_refs[5:])
    line = Line(place, *line_refs[:3], PIECES, line_refs[3:])
    tile = min(1024, depth)

    def partial(owner, target):
        lines = h_in[pl.ds(pl.multiple_of(owner * own, own), own), :]

        def columns(start):
            target[:, pl.ds(start, tile)] = dot(lines, w_i[pl.ds(start, tile), :], 1, 1).astype(target.dtype)

        loop(depth, tile, columns)

    part = min(512, hidden)

    def down_slice(index):
        target = order[index]
        load_grad[index].wait()

        def piece(start):
            line.own[target, pl.ds(start, part), :] = dot(
                act[:, pl.ds(start, part)], buf[:, pl.ds(target * cut, cut)], 0, 0
            ).astype(bf16)

        loop(hidden, part, piece)
        line.start(target, False)

    for copy in loads:
        copy.wait()

    def between(number):
        if number == 0:
            load_act.wait()
            for index in range(groups // 2):
                down_slice(index)
        if number == min(2, len(plan.offsets) - 1):
            for index in range(groups // 2, groups):
                down_slice(index)
            line.start_near()

    scatter.begin(partial, between)

    in_stores = []
    in_loads = {}
    kept = set()

    def stored(number):
        if number not in kept:
            kept.add(number)
            in_stores[number].wait()

    def load_slice(number):
        columns = pl.ds(order[number] * cut, cut)
        in_loads[number] = moves.start(second_all.at[:, columns], act.at[:, pl.ds((number % 2) * cut, cut)])

    def in_slice(number):
        in_loads[number].wait()
        if number >= 2:
            stored(number - 2)
        slot = number % 2

        def piece(start):
            columns = pl.ds(start, part)
            staged[slot, :, columns] = dot(
                act[:, pl.ds(slot * cut, cut)], h_in[:, columns], 0, 0
            ).astype(bf16)

        loop(hidden, part, piece)
        in_stores.append(moves.start(staged.at[slot], in_part_out.at[order[number]]))
        if number + 2 < groups:
            load_slice(number + 2)

    ticks = list(line.ticks())
    for number in range(min(2, groups)):
        load_slice(number)
    line.tick(ticks.pop(0))
    scatter.middle()
    half_groups = groups // 2
    for number in range(half_groups):
        in_slice(number)
    line.tick(ticks.pop(0))
    mine = pl.multiple_of(place.me * own, own)
    totals = [
        Total(place, *total_refs[index : index + 4], total_refs[index + 4 : index + 8]) for index in (0, 8)
    ]
    own_sums = totals[0].value
    own_sums[...] = jnp.zeros_like(own_sums)
    totals[1].value[...] = in_sums[...]

    def close(start, count, value):
        span = pl.ds(start, count)
        unit, inverse = norm_rows(middle[span, :])
        sum_rows = out_grad[span, :].astype(f32) + norm_back(value, unit, inverse, gain[...])
        middle_grad[span, :] = sum_rows
        buf[pl.ds(pl.multiple_of(mine + start, count), count), :] = sum_rows.astype(bf16)
        own_sums[0:1, :] += jnp.sum(value * unit, axis=0, keepdims=True)
        own_sums[1:2, :] += jnp.sum(value, axis=0, keepdims=True)
        own_sums[2:3, :] += jnp.sum(sum_rows, axis=0, keepdims=True)
        own_sums[3:4, :] += jnp.sum(out_grad[span, :].astype(f32), axis=0, keepdims=True)

    gather = Gather(place, buf, None, own, gather_sems)
    for half in range(plan.halves):
        scatter.end(close, half)
        gather.start(half)
    for total in totals:
        total.begin()
    piece_rows = pl.ds(0, cut // PIECES)
    early = []
    if groups > 2:
        for index, (edge, step, target) in enumerate(((0, 1, groups - 1), (groups - 1, -1, 0))):
            early.append(
                (
                    edge,
                    step,
                    pltpu.make_async_remote_copy(
                        src_ref=in_part_out.at[target, piece_rows, :],
                        dst_ref=early_out.at[index],
                        send_sem=early_send.at[index],
                        recv_sem=early_recv.at[index],
                        device_id=place.beside(step),
                        device_id_type=MESH,
                    ),
                )
            )
        for number in range(2):
            stored(number)
        for edge, step, copy in early:
            pl.when(place.batch == edge)(copy.start)
    line.tick(ticks.pop(0))
    scatter.finish()
    stores = [moves.start(middle_grad, middle_grad_out)]
    load_out.wait()

    def project(offset, half):
        pieces = gather.pieces(offset, half)
        count = own // plan.halves
        product = dot(joined(buf, pieces), w_o[...], 1, 1).astype(bf16)
        for index, piece in enumerate(pieces):
            att_grad[piece, :] = product[index * count : (index + 1) * count]
            stores.append(moves.start(buf.at[piece, :], branch_out.at[piece, :]))

    for half in range(plan.halves):
        gather.share(0, half)
        project(0, half)
    for number in range(half_groups, groups):
        in_slice(number)
    line.tick(ticks.pop(0))
    for half, keys, offsets in gather.steps():
        for key in keys:
            gather.arrive(key)
        for offset in offsets:
            gather.share(offset, half)
            project(offset, half)
    stores.append(moves.start(att_grad, att_grad_out))
    for number in ticks:
        line.tick(number)
    exported = line.export(down_outs, moves)
    for total, total_out in zip(totals, (sums_out, in_sums_out)):
        total.end(total_out)
    gather.finish()
    line.finish()
    for edge, step, copy in early:
        pl.when(place.batch == edge)(copy.wait_send)
        pl.when(place.batch == edge + step)(copy.wait_recv)
    for number in range(groups):
        stored(number)
    for copy in stores:
        copy.wait()
    exported()


def run_middle(plan, groups, hidden_grad, w_in, middle, out_grad, gain, w_out, activated, grad_all, second_all, in_sums):
    own, depth = middle.shape
    rows = own * plan.devices
    width = w_out.shape[0]
    hidden = w_in.shape[1]
    cut = depth // groups
    return pl.pallas_call(
        functools.partial(middle_kernel, plan),
        out_shape=(
            jax.ShapeDtypeStruct((own, depth), f32),
            jax.ShapeDtypeStruct((rows, depth), bf16),
            jax.ShapeDtypeStruct((rows, width), bf16),
            jax.ShapeDtypeStruct((4, depth), f32),
            jax.ShapeDtypeStruct(in_sums.shape, f32),
        )
        + (jax.ShapeDtypeStruct((hidden, cut), bf16),) * 3
        + (
            jax.ShapeDtypeStruct((groups, cut, hidden), bf16),
            jax.ShapeDtypeStruct((2, cut // PIECES, hidden), bf16),
        ),
        in_specs=[ANY, ANY, VMEM, VMEM, VMEM, ANY, ANY, ANY, ANY, VMEM],
        out_specs=(ANY, ANY, ANY, VMEM, VMEM, ANY, ANY, ANY, ANY, ANY),
        scratch_shapes=[
            pltpu.VMEM((rows, hidden), bf16),
            pltpu.VMEM((depth, hidden), bf16),
            pltpu.VMEM((width, depth), bf16),
            pltpu.VMEM((rows, depth), bf16),
            pltpu.VMEM((own, depth), f32),
            pltpu.VMEM((rows, width), bf16),
            pltpu.VMEM((rows, max(hidden, 2 * cut)), bf16),
            pltpu.VMEM((2, cut, hidden), bf16),
            pltpu.SemaphoreType.DMA((64,)),
            pltpu.SemaphoreType.DMA((2,)),
            pltpu.SemaphoreType.DMA((2,)),
        ]
        + Scatter.scratch(plan, own, depth, bf16)
        + Gather.semaphores(plan)
        + Line.scratch(groups, hidden, cut, PIECES)
        + Total.scratch(plan, groups, (4, depth))
        + Total.scratch(plan, groups, in_sums.shape),
        compiler_params=params(2),
        name="middle",
        cost_estimate=cost(80),
    )(hidden_grad, w_in, middle, out_grad, gain, w_out, activated, grad_all, second_all, in_sums)


def back_kernel(
    plan, block, lengths, scripts, places, qkv, att, att_grad, sums, activated, w_down, middle, down_bias, in_part,
    branch_all, sums2, in_sums, down0, down1, down2, early, w_qkv, tok, middle_grad, gain, first_all,
    block_out, input_out, down_out, in_out, out_out, qkv_out, vectors2_out, spread2_out, vectors_out, spread_out,
    qkv_in, att_in, grad_in, act_in, w_d, mid, starts, key_grad, value_grad, result, branch, bias_out, local, free, *rest,
):
    feed_refs, first_sems, rest = rest[:9], rest[9:13], rest[13:]
    in_refs, out_refs, qkv_refs, total_refs = rest[:7], rest[7:14], rest[14:20], rest[20:]
    place = Place(plan)
    own, depth = tok.shape
    rows = qkv_in.shape[0]
    width = att_in.shape[1]
    hidden = w_down.shape[0]
    heads = width // HEAD_DIM
    groups = place.groups
    cut = depth // groups
    moves = Moves(local)
    line = Line(place, *in_refs[:3], PIECES, in_refs[3:], early=True)
    out_line = Line(place, *out_refs[:3], 1, out_refs[3:])
    qkv_line = Line(place, Slices(act_in, cut, 3 * width), *qkv_refs[:2], PIECES, qkv_refs[2:])
    order = line.order()
    parts = [moves.start(in_part.at[target], line.own.at[target]) for target in order]
    feeds = [moves.start(activated, act_in), moves.start(w_down, w_d)]
    loads = [moves.start(qkv, qkv_in), moves.start(att, att_in), moves.start(att_grad, grad_in)]
    load_middle = moves.start(middle, mid)
    slice_loads = {}

    def load_slice(source, number, name):
        columns = pl.ds(number * cut, cut)
        slice_loads[name] = moves.start(source.at[:, columns], branch.at[name[1] % 2])

    for index in range(min(2, groups)):
        load_slice(branch_all, order[index], ("out", index))
    early_loads = []
    if line.early:
        for index, (whose, upward, target) in enumerate(((1, True, groups - 1), (groups - 2, False, 0))):
            copy = moves.make(early.at[index], line.slot(upward, target).at[line.span(0), :])
            early_loads.append((whose, copy))
            pl.when(place.batch == whose)(copy.start)
    place.barrier(groups=True)
    scatter = Scatter(place, own, depth, *feed_refs[:5], feed_refs[5:])
    for whose, copy in early_loads:
        pl.when(place.batch == whose)(copy.wait)
    for target, copy in zip(order, parts):
        copy.wait()
        line.start(target, False)
    line.start_near()
    ticks = list(line.ticks())
    if line.early:
        line.tick(ticks.pop(0))
    for copy in feeds:
        copy.wait()
    tile = min(1024, depth)

    def partial(owner, target):
        lines = act_in[pl.ds(pl.multiple_of(owner * own, own), own), :]

        def columns(start):
            target[:, pl.ds(start, tile)] = dot(lines, w_d[:, pl.ds(start, tile)], 1, 0).astype(target.dtype)

        loop(depth, tile, columns)

    scatter.begin(partial)
    turns = depth // hidden
    weight_loads = [
        moves.start(
            w_qkv.at[part, pl.ds(turn * hidden, hidden), :],
            w_d.at[:, pl.ds((turn * 3 + part) * width, width)],
        )
        for turn in range(turns)
        for part in range(3)
    ]
    line.tick(ticks.pop(0))
    starts[...] = segment_starts(place.batch, lengths, scripts, places, rows)
    bias_out[...] = jnp.zeros_like(bias_out)
    key_grad[...] = jnp.zeros_like(key_grad)
    value_grad[...] = jnp.zeros_like(value_grad)
    for copy in loads:
        copy.wait()
    for index, target in enumerate(order):
        slice_loads["out", index].wait()
        out_line.own[target, :, :] = dot(att_in[...], branch[index % 2], 0, 0).astype(bf16)
        out_line.start(target, False)
        if index + 2 < groups:
            load_slice(branch_all, order[index + 2], ("out", index + 2))
    out_line.start_near()
    fit = rows // hidden
    down_parts = [branch.at[index // fit, pl.ds((index % fit) * hidden, hidden), :] for index in range(3)]
    down_loads = [moves.start(part, target) for part, target in zip((down0, down1, down2), down_parts)]
    scale = HEAD_DIM ** (-0.5)
    row_in = lax.broadcasted_iota(jnp.int32, (block, block), 0)
    col_in = lax.broadcasted_iota(jnp.int32, (block, block), 1)
    key_in = lax.broadcasted_iota(jnp.int32, (block, 1), 0)

    def attend(index):
        span = pl.ds(index * block, block)
        first = starts[:, span]
        queries, outer, inner, logs = [], [], [], []
        for head in range(heads):
            columns = pl.ds(head * HEAD_DIM, HEAD_DIM)
            queries.append(qkv_in[span, head_columns(0, head, width)])
            outer.append(grad_in[span, columns])
            product = grad_in[span, columns].astype(f32) * att_in[span, columns].astype(f32)
            inner.append(jnp.sum(product.T, axis=0, keepdims=True))
            logs.append(sums[pl.ds(head, 1), span])

        def against(key_block, carry, diagonal):
            key_span = pl.ds(pl.multiple_of(key_block * block, block), block)
            allowed = key_in + key_block * block >= first
            if diagonal:
                allowed = allowed & (row_in <= col_in)
            out = []
            for head in range(heads):
                columns = pl.ds(head * HEAD_DIM, HEAD_DIM)
                keys = qkv_in[key_span, head_columns(1, head, width)]
                values = qkv_in[key_span, head_columns(2, head, width)]
                scores = dot(keys, queries[head], 1, 1) * (scale * LOG2E)
                probs = jnp.exp2(jnp.where(allowed, scores - logs[head], NEGATIVE))
                value_grad[key_span, columns] += dot(probs.astype(bf16), outer[head], 1, 0)
                prob_grad = dot(values, outer[head], 1, 1)
                score_grad = (probs * (prob_grad - inner[head])).astype(bf16)
                key_grad[key_span, columns] += dot(score_grad, queries[head], 1, 0)
                out.append(carry[head] + dot(score_grad, keys, 0, 0))
            return tuple(out)

        carry = tuple(jnp.zeros((block, HEAD_DIM), f32) for head in range(heads))
        if index:
            carry = lax.fori_loop(0, index, lambda key_block, c: against(key_block, c, False), carry)
        carry = against(index, carry, True)
        for head in range(heads):
            query_grad = (carry[head] * scale).astype(bf16)
            qkv_in[span, head_columns(0, head, width)] = query_grad
            columns = pl.ds(head * HEAD_DIM, HEAD_DIM)
            bias_out[0:1, columns] += jnp.sum(query_grad.astype(f32), axis=0, keepdims=True)

    blocks = rows // block
    for index in range(blocks):
        attend(index)
        if index == blocks // 2:
            scatter.middle()
        if 0 < index < blocks - 1:
            line.tick(ticks.pop(0))
    kept = min(256, rows)

    def write(start):
        span = pl.ds(start, kept)
        qkv_in[span, pl.ds(width, width)] = (key_grad[span, :] * scale).astype(bf16)
        rounded = value_grad[span, :].astype(bf16)
        qkv_in[span, pl.ds(2 * width, width)] = rounded
        bias_out[1:2, :] += jnp.sum(rounded.astype(f32), axis=0, keepdims=True)

    loop(rows, kept, write)
    for number in ticks:
        line.tick(number)
    for copy in down_loads:
        copy.wait()
    add_parts(place, down_parts, key_grad, width)
    down_stores = [
        moves.start(piece, down_out.at[:, pl.ds(index * width, width)])
        for index, piece in enumerate(column_pieces(key_grad, hidden, cut, width))
    ]
    for index in range(min(2, groups)):
        load_slice(first_all, order[index], ("qkv", index))
    load_middle.wait()

    def close(start, count, value):
        span = pl.ds(start, count)
        result[span, :] = (mid[span, :] + value + down_bias[...]).astype(bf16)

    for half in range(plan.halves):
        scatter.end(close, half)
    stores = [moves.start(result, block_out)]
    load_grad = moves.start(middle_grad, mid)
    totals = [
        Total(place, *total_refs[index : index + 4], total_refs[index + 4 : index + 8]) for index in (0, 8, 16, 24)
    ]
    vectors2, spread2, vectors, spread = totals
    vectors2.value[...] = sums2[...]
    spread_rows(place, spread2.value, [bias_out[0:1, :], bias_out[1:2, :], in_sums[...]])
    vectors.value[...] = jnp.zeros_like(vectors.value)
    masks = [1] + plan.bits
    for mask in masks:
        pl.semaphore_signal(free, inc=1, device_id=place.at(mask), device_id_type=MESH)
    scatter.finish()
    scatter = Scatter(place, own, depth, *feed_refs[:5], first_sems)
    for copy in weight_loads:
        copy.wait()

    def first_partial(owner, target):
        lines = qkv_in[pl.ds(pl.multiple_of(owner * own, own), own), :]
        for turn in range(turns):
            target[:, pl.ds(turn * hidden, hidden)] = dot(
                lines, w_d[:, pl.ds(turn * 3 * width, 3 * width)], 1, 1
            ).astype(target.dtype)

    def qkv_slice(index):
        slice_loads["qkv", index].wait()
        qkv_line.part(order[index])[...] = dot(branch[index % 2], qkv_in[...], 0, 0).astype(bf16)
        qkv_line.start(order[index], False)
        if index + 2 < groups:
            load_slice(first_all, order[index + 2], ("qkv", index + 2))

    for index in range(groups):
        qkv_slice(index)
    qkv_line.start_near()
    pl.semaphore_wait(free, len(masks))
    out_ticks = list(out_line.ticks())

    def between(number):
        if number < 2:
            out_line.tick(out_ticks.pop(0))

    scatter.begin(first_partial, between)
    for number in out_ticks:
        out_line.tick(number)
    scatter.middle()
    pieces = line.add(value_grad, width)
    in_stores = [
        moves.start(piece, in_out.at[:, pl.ds(index * width, width)]) for index, piece in enumerate(pieces)
    ]
    ticks = list(qkv_line.ticks())
    qkv_line.tick(ticks.pop(0))
    qkv_line.tick(ticks.pop(0))
    load_grad.wait()
    stores.pop(0).wait()
    load_tok = moves.start(tok, result)
    load_tok.wait()

    def close_first(start, count, value):
        span = pl.ds(start, count)
        unit, inverse = norm_rows(result[span, :].astype(f32))
        sum_rows = mid[span, :] + norm_back(value, unit, inverse, gain[...])
        result[span, :] = sum_rows.astype(bf16)
        vectors.value[0:1, :] += jnp.sum(value * unit, axis=0, keepdims=True)
        vectors.value[1:2, :] += jnp.sum(value, axis=0, keepdims=True)

    for half in range(plan.halves):
        scatter.end(close_first, half)
    stores.append(moves.start(result, input_out))
    for number in ticks:
        qkv_line.tick(number)
    vectors.plane([vectors2, spread2])
    spread.value[...] = spread2.value[:, 0 : 2 * width]
    for total in (vectors, spread):
        total.begin()
    for copy in in_stores + down_stores:
        copy.wait()
    pieces = out_line.add(key_grad, width)
    stores += [
        moves.start(piece, out_out.at[:, pl.ds(index * width, width)]) for index, piece in enumerate(pieces)
    ]
    pieces = qkv_line.add(value_grad, width)
    stores += [moves.start(piece, qkv_out.at[index]) for index, piece in enumerate(pieces)]
    scatter.finish()
    line.finish()
    out_line.finish()
    qkv_line.finish()
    vectors2_out[...] = vectors2.value[...]
    spread2_out[...] = spread2.value[...]
    vectors.end(vectors_out)
    spread.end(spread_out)
    for copy in stores:
        copy.wait()


def run_back(
    plan, groups, block, order, qkv, att, att_grad, sums, activated, w_down, middle, down_bias, in_part, branch_all,
    sums2, in_sums, down_parts, early, w_qkv, tok, middle_grad, gain, first_all,
):
    own, depth = tok.shape
    rows, width = att.shape
    hidden = w_down.shape[0]
    cut = depth // groups
    return pl.pallas_call(
        functools.partial(back_kernel, plan, block),
        out_shape=(
            jax.ShapeDtypeStruct((own, depth), bf16),
            jax.ShapeDtypeStruct((own, depth), bf16),
            jax.ShapeDtypeStruct((hidden, cut), f32),
            jax.ShapeDtypeStruct((cut, hidden), f32),
            jax.ShapeDtypeStruct((width, cut), f32),
            jax.ShapeDtypeStruct((3, cut, width), f32),
            jax.ShapeDtypeStruct(sums2.shape, f32),
            jax.ShapeDtypeStruct((plan.devices, 2 * width + hidden), f32),
            jax.ShapeDtypeStruct((2, depth), f32),
            jax.ShapeDtypeStruct((plan.devices, 2 * width), f32),
        ),
        in_specs=[SMEM] * 3
        + [ANY, ANY, ANY, VMEM, ANY, ANY, ANY, VMEM, ANY, ANY, VMEM, VMEM, ANY, ANY, ANY, ANY, ANY, ANY, ANY, VMEM, ANY],
        out_specs=(ANY,) * 6 + (VMEM,) * 4,
        scratch_shapes=[
            pltpu.VMEM((rows, 3 * width), bf16),
            pltpu.VMEM((rows, width), bf16),
            pltpu.VMEM((rows, width), bf16),
            pltpu.VMEM((rows, hidden), bf16),
            pltpu.VMEM((hidden, depth), bf16),
            pltpu.VMEM((own, depth), f32),
            pltpu.VMEM((1, rows), jnp.int32),
            pltpu.VMEM((rows, width), f32),
            pltpu.VMEM((rows, width), f32),
            pltpu.VMEM((own, depth), bf16),
            pltpu.VMEM((2, rows, cut), bf16),
            pltpu.VMEM((2, width), f32),
            pltpu.SemaphoreType.DMA((96,)),
            pltpu.SemaphoreType.REGULAR,
        ]
        + Scatter.scratch(plan, own, depth, bf16)
        + Scatter.scratch(plan, own, depth, bf16)[5:]
        + Line.scratch(groups, cut, hidden, PIECES)
        + Line.scratch(groups, width, cut, 1)
        + Line.scratch(groups, cut, 3 * width, PIECES)[1:]
        + Total.scratch(plan, 1, sums2.shape)
        + Total.scratch(plan, 1, (plan.devices, 2 * width + hidden))
        + Total.scratch(plan, groups, (2, depth))
        + Total.scratch(plan, groups, (plan.devices, 2 * width)),
        compiler_params=params(3),
        name="back",
        cost_estimate=cost(145),
    )(
        *order, qkv, att, att_grad, sums, activated, w_down, middle, down_bias, in_part, branch_all, sums2, in_sums,
        *down_parts, early, w_qkv, tok, middle_grad, gain, first_all,
    )


def body(
    tokens,
    out_grad,
    seq_lengths,
    seq_scripts,
    seq_place,
    norm1_gain,
    norm1_shift,
    w_qkv,
    qv_bias,
    w_out,
    out_bias,
    norm2_gain,
    norm2_shift,
    w_in,
    in_bias,
    w_down,
    down_bias,
):
    own, depth = tokens.shape
    devices = lax.axis_size("mp")
    plan = Plan(devices)
    fine = Plan(devices, 2)
    rows = own * devices
    width = w_qkv.shape[2]
    block = min(512, rows)
    order = (seq_lengths, seq_scripts, seq_place)

    def line(vector):
        return vector.reshape(1, -1)

    (
        first_all, qkv, att, sums, grad_all, second_all, activated, hidden_grad, middle, in_part,
    ) = run_front(
        plan, fine, block, tokens, line(norm1_gain), line(norm1_shift), w_qkv, qv_bias, order, out_grad,
        w_out, line(out_bias), line(norm2_gain), line(norm2_shift), w_in, line(in_bias), w_down,
    )
    groups = lax.axis_size("batch")
    middle_grad, branch_all, att_grad, sums2, in_sums, *down_parts, in_part2, early = run_middle(
        fine, groups, hidden_grad, w_in, middle, out_grad, line(norm2_gain), w_out, activated, grad_all, second_all,
        in_part,
    )
    (
        block_out, input_grad, down_weight_grad, in_weight_grad, out_weight_grad, qkv_weight_grad,
        vectors2, spread2, vectors, spread,
    ) = run_back(
        plan, groups, block, order, qkv, att, att_grad, sums, activated, w_down, middle, line(down_bias),
        in_part2, branch_all, sums2, in_sums, down_parts, early, w_qkv, tokens, middle_grad, line(norm1_gain), first_all,
    )
    qv_bias_grad = jnp.stack([spread[:, :width].reshape(-1), spread[:, width:].reshape(-1)])
    return (
        block_out,
        input_grad,
        vectors[0],
        vectors[1],
        qkv_weight_grad,
        qv_bias_grad,
        out_weight_grad,
        vectors2[2],
        vectors2[0],
        vectors2[1],
        in_weight_grad,
        spread2[:, 2 * width :].reshape(-1),
        down_weight_grad,
        vectors2[3],
    )


def solution(mesh):
    return jax.shard_map(
        body,
        mesh=mesh,
        in_specs=(
            P(("batch", "mp"), None),
            P(("batch", "mp"), None),
            P(),
            P(),
            P(),
            P(),
            P(),
            P(None, None, "mp"),
            P(None, "mp"),
            P("mp", None),
            P(),
            P(),
            P(),
            P(None, "mp"),
            P("mp"),
            P("mp", None),
            P(),
        ),
        out_specs=(
            P(("batch", "mp"), None),
            P(("batch", "mp"), None),
            P(),
            P(),
            P(None, "batch", "mp"),
            P(),
            P("mp", "batch"),
            P(),
            P(),
            P(),
            P("batch", "mp"),
            P(),
            P("mp", "batch"),
            P(),
        ),
        check_vma=False,
    )
```

```python
import functools

import jax
import jax.numpy as jnp
from jax import lax
from jax.experimental import pallas as pl
from jax.experimental.pallas import tpu as pltpu
from jax.sharding import PartitionSpec as P

HEAD_DIM = 128
EPS = 1e-05
NEGATIVE = -1e30
LOG2E = 1.4426950408889634
f32 = jnp.float32
bf16 = jnp.bfloat16
MESH = pl.DeviceIdType.MESH
ANY = pl.BlockSpec(memory_space=pl.ANY)
VMEM = pl.BlockSpec(memory_space=pltpu.VMEM)
SMEM = pl.BlockSpec(memory_space=pltpu.SMEM)


def dot(left, right, contract_left, contract_right):
    return lax.dot_general(
        left,
        right,
        (((contract_left,), (contract_right,)), ((), ())),
        preferred_element_type=f32,
    )


def flip(index, mask):
    bit = 1
    while bit <= mask:
        if mask & bit:
            index = index + bit * (1 - 2 * lax.rem(lax.div(index, bit), 2))
        bit *= 2
    return index


def loop(count, step, body):
    def one(index, carry):
        body(pl.multiple_of(index * step, step))
        return carry

    lax.fori_loop(0, count // step, one, 0)


class Plan:
    def __init__(self, devices, halves=1):
        bits = []
        bit = 2
        while bit < devices:
            bits.append(bit)
            bit *= 2
        self.devices = devices
        self.bits = bits
        self.ways = [tuple(bits)] + ([tuple(reversed(bits))] if len(bits) > 1 else [])
        self.halves = halves
        self.orders = self.ways * halves
        self.parts = len(self.orders)
        self.offsets = list(range(0, devices, 2))
        self.keys = [(part, offset) for part in range(self.parts) for offset in self.offsets if offset]
        self.keys.sort(key=lambda key: (self.half(key[0]), bin(key[1]).count("1"), self.last(*key)))
        self.shares = [(part, offset) for offset in self.offsets for part in range(self.parts)]

    def half(self, part):
        return part // len(self.ways)

    def parts_of(self, half):
        return range(half * len(self.ways), (half + 1) * len(self.ways))

    def last(self, part, offset):
        steps = [step for step, bit in enumerate(self.orders[part]) if bit & offset]
        return max(steps) if steps else -1

    def bit(self, part, offset):
        return self.orders[part][self.last(part, offset)]

    def later(self, part, offset):
        order = self.orders[part]
        return [offset | order[step] for step in range(self.last(part, offset) + 1, len(order))]


class Place:
    def __init__(self, plan):
        self.plan = plan
        self.batch = lax.axis_index("batch")
        self.groups = lax.axis_size("batch")
        self.me = lax.axis_index("mp")

    def at(self, mask):
        return (self.batch, flip(self.me, mask))

    def beside(self, step):
        return (self.batch + step, self.me)

    def around(self, step):
        return (lax.rem(self.batch + step, self.groups), self.me)

    def barrier(self, groups=False):
        semaphore = pltpu.get_barrier_semaphore()
        partners = [self.at(mask) for mask in [1] + self.plan.bits]
        if groups:
            partners += [self.around(step) for step in range(1, self.groups)]
        for partner in partners:
            pl.semaphore_signal(semaphore, inc=1, device_id=partner, device_id_type=MESH)
        pl.semaphore_wait(semaphore, len(partners))


class Total:
    def __init__(self, place, value, sent, came, slots, sems):
        self.place, self.value, self.sent, self.came, self.slots = place, value, sent, came, slots
        self.send, self.recv, self.slot_send, self.slot_recv = sems

    def plane(self, others=()):
        totals = (self,) + tuple(others)
        for index, mask in enumerate([1] + self.place.plan.bits):
            copies = [
                pltpu.make_async_remote_copy(
                    src_ref=total.sent.at[index],
                    dst_ref=total.came.at[index],
                    send_sem=total.send.at[index],
                    recv_sem=total.recv.at[index],
                    device_id=self.place.at(mask),
                    device_id_type=MESH,
                )
                for total in totals
            ]
            for total, copy in zip(totals, copies):
                total.sent[index] = total.value[...]
                copy.start()
            for total, copy in zip(totals, copies):
                copy.wait_recv()
                total.value[...] = total.sent[index] + total.came[index]
                copy.wait_send()

    def slot(self, step):
        return pltpu.make_async_remote_copy(
            src_ref=self.value,
            dst_ref=self.slots.at[step],
            send_sem=self.slot_send.at[step - 1],
            recv_sem=self.slot_recv.at[step - 1],
            device_id=self.place.around(step),
            device_id_type=MESH,
        )

    def begin(self):
        self.slots[0] = self.value[...]
        for step in range(1, self.place.groups):
            self.slot(step).start()

    def end(self, result):
        for step in range(1, self.place.groups):
            self.slot(step).wait()
        groups = self.place.groups
        total = self.slots[self.place.batch]
        for group in range(1, groups):
            total = total + self.slots[lax.rem(self.place.batch + groups - group, groups)]
        result[...] = total

    @staticmethod
    def scratch(plan, groups, shape):
        rounds = len(plan.bits) + 1
        return [
            pltpu.VMEM(shape, f32),
            pltpu.VMEM((rounds,) + shape, f32),
            pltpu.VMEM((rounds,) + shape, f32),
            pltpu.VMEM((groups,) + shape, f32),
            pltpu.SemaphoreType.DMA((rounds,)),
            pltpu.SemaphoreType.DMA((rounds,)),
            pltpu.SemaphoreType.DMA((max(groups - 1, 1),)),
            pltpu.SemaphoreType.DMA((max(groups - 1, 1),)),
        ]


class Gather:
    def __init__(self, place, buf, own, rows, sems):
        self.place, self.plan, self.buf, self.own, self.rows = place, place.plan, buf, own, rows
        self.link_send, self.link_recv, self.core_send, self.core_recv = sems
        self.part_rows = rows // self.plan.parts

    def span(self, mask, part):
        block = flip(self.place.me, mask)
        start = block * self.rows + part * self.part_rows
        return self.buf.at[pl.ds(pl.multiple_of(start, self.part_rows), self.part_rows), :]

    def source(self, offset, part):
        if offset == 0 and self.own is not None:
            return self.own.at[pl.ds(part * self.part_rows, self.part_rows), :]
        return self.span(offset, part)

    def link(self, key):
        part, offset = key
        bit = self.plan.bit(part, offset)
        index = self.plan.keys.index(key)
        return pltpu.make_async_remote_copy(
            src_ref=self.source(offset ^ bit, part),
            dst_ref=self.span(offset ^ bit, part),
            send_sem=self.link_send.at[index],
            recv_sem=self.link_recv.at[index],
            device_id=self.place.at(bit),
            device_id_type=MESH,
        )

    def core(self, key):
        part, offset = key
        index = self.plan.shares.index(key)
        return pltpu.make_async_remote_copy(
            src_ref=self.source(offset, part),
            dst_ref=self.span(offset, part),
            send_sem=self.core_send.at[index],
            recv_sem=self.core_recv.at[index],
            device_id=self.place.at(1),
            device_id_type=MESH,
        )

    def landed(self, ref, semaphore):
        pltpu.make_async_remote_copy(
            src_ref=ref,
            dst_ref=ref,
            send_sem=semaphore,
            recv_sem=semaphore,
            device_id=self.place.at(1),
            device_id_type=MESH,
        ).wait_recv()

    def start(self, half=0, ahead=None):
        if ahead in (None, False):
            for part in self.plan.parts_of(half):
                self.core((part, 0)).start()
        for key in self.plan.keys:
            if bin(key[1]).count("1") == 1 and self.plan.half(key[0]) == half:
                if ahead is None or ahead == (self.plan.last(*key) == 0):
                    self.link(key).start()

    def arrive(self, key):
        part, offset = key
        self.landed(self.span(offset, part), self.link_recv.at[self.plan.keys.index(key)])
        for target in self.plan.later(part, offset):
            self.link((part, target)).start()
        self.core(key).start()

    def share(self, offset, half=0):
        for part in self.plan.parts_of(half):
            index = self.plan.shares.index((part, offset))
            self.landed(self.span(offset | 1, part), self.core_recv.at[index])

    def steps(self):
        result = []
        for half in range(self.plan.halves):
            for count in range(1, len(self.plan.bits) + 1):
                keys = [
                    key
                    for key in self.plan.keys
                    if self.plan.half(key[0]) == half and bin(key[1]).count("1") == count
                ]
                offsets = [offset for offset in self.plan.offsets if bin(offset).count("1") == count]
                result.append((half, keys, offsets))
        return result

    def pieces(self, offset, half):
        count = self.rows // self.plan.halves
        chip = lax.div(flip(self.place.me, offset), 2) * 2
        return [
            pl.ds(pl.multiple_of((chip + core) * self.rows + half * count, count), count) for core in range(2)
        ]

    def finish(self):
        for key in self.plan.keys:
            self.link(key).wait_send()
        for key in self.plan.shares:
            self.core(key).wait_send()

    @staticmethod
    def semaphores(plan):
        return [pltpu.SemaphoreType.DMA((len(plan.keys),))] * 2 + [
            pltpu.SemaphoreType.DMA((len(plan.shares),))
        ] * 2


class Spread:
    dtype = bf16

    def __init__(self, refs):
        self.refs = refs

    def __setitem__(self, index, value):
        count = self.refs[0].shape[0]
        for number, ref in enumerate(self.refs):
            ref[index] = value[number * count : (number + 1) * count]


class Scatter:
    def __init__(self, place, rows, width, core_out, core_in, kept, link_out, link_in, sems):
        self.place, self.plan, self.rows, self.width = place, place.plan, rows, width
        self.core_out, self.core_in, self.kept = core_out, core_in, kept
        self.link_out, self.link_in = link_out, link_in
        self.link_send, self.link_recv, self.core_send, self.core_recv = sems
        self.part_rows = rows // self.plan.parts
        self.step = min(32, self.part_rows)
        self.order = sorted(self.plan.offsets, key=lambda offset: -bin(offset).count("1"))

    def core(self, offset):
        index = offset // 2
        return pltpu.make_async_remote_copy(
            src_ref=self.core_out.at[index],
            dst_ref=self.core_in.at[index],
            send_sem=self.core_send.at[index],
            recv_sem=self.core_recv.at[index],
            device_id=self.place.at(1),
            device_id_type=MESH,
        )

    def link(self, key):
        index = self.plan.keys.index(key)
        return pltpu.make_async_remote_copy(
            src_ref=self.link_out.at[index],
            dst_ref=self.link_in.at[index],
            send_sem=self.link_send.at[index],
            recv_sem=self.link_recv.at[index],
            device_id=self.place.at(self.plan.bit(*key)),
            device_id_type=MESH,
        )

    def keep(self, offset):
        if offset == 0:
            return self.kept
        return Spread([self.link_out.at[self.plan.keys.index((part, offset))] for part in range(self.plan.parts)])

    def total(self, offset, part, start, arrived):
        rows = pl.ds(pl.multiple_of(part * self.part_rows + start, self.step), self.step)
        if offset:
            value = self.link_out[self.plan.keys.index((part, offset)), pl.ds(start, self.step), :].astype(f32)
        else:
            value = self.kept[rows, :].astype(f32)
        value += self.core_in[offset // 2, rows, :].astype(f32)
        for key in arrived:
            value += self.link_in[self.plan.keys.index(key), pl.ds(start, self.step), :].astype(f32)
        return value

    def pass_on(self, part, offset):
        arrived = [(part, target) for target in self.plan.later(part, offset)]
        for key in arrived:
            self.link(key).wait_recv()
        index = self.plan.keys.index((part, offset))

        def add(start):
            self.link_out[index, pl.ds(start, self.step), :] = self.total(
                offset, part, start, arrived
            ).astype(bf16)

        loop(self.part_rows, self.step, add)
        self.link((part, offset)).start()

    def free(self, offset, half):
        for part in self.plan.parts_of(half):
            if offset and not self.plan.later(part, offset):
                self.pass_on(part, offset)

    def bound(self, half):
        for offset in self.order:
            for part in self.plan.parts_of(half):
                if offset and self.plan.later(part, offset):
                    self.pass_on(part, offset)

    def begin(self, partial, between=None):
        for number, offset in enumerate(self.order):
            index = offset // 2
            if offset == 0:
                self.bound(0)
            partial(flip(self.place.me, offset | 1), self.core_out.at[index])
            self.core(offset).start()
            partial(flip(self.place.me, offset), self.keep(offset))
            self.core(offset).wait_recv()
            for half in range(self.plan.halves):
                self.free(offset, half)
            if between is not None:
                between(number)

    def middle(self):
        for half in range(1, self.plan.halves):
            self.bound(half)

    def end(self, use, half=0):
        for part in self.plan.parts_of(half):
            arrived = [(part, target) for target in self.plan.later(part, 0)]
            for key in arrived:
                self.link(key).wait_recv()

            def piece(start):
                row = pl.multiple_of(part * self.part_rows + start, self.step)
                use(row, self.step, self.total(0, part, start, arrived))

            loop(self.part_rows, self.step, piece)

    def finish(self):
        for key in self.plan.keys:
            self.link(key).wait_send()
        for offset in self.plan.offsets:
            self.core(offset).wait_send()

    @staticmethod
    def scratch(plan, rows, width, kept):
        chips, keys = len(plan.offsets), len(plan.keys)
        return [
            pltpu.VMEM((chips, rows, width), bf16),
            pltpu.VMEM((chips, rows, width), bf16),
            pltpu.VMEM((rows, width), kept),
            pltpu.VMEM((keys, rows // plan.parts, width), bf16),
            pltpu.VMEM((keys, rows // plan.parts, width), bf16),
            pltpu.SemaphoreType.DMA((keys,)),
            pltpu.SemaphoreType.DMA((keys,)),
            pltpu.SemaphoreType.DMA((chips,)),
            pltpu.SemaphoreType.DMA((chips,)),
        ]


class Slices:
    def __init__(self, ref, rows, columns):
        self.ref, self.shape = ref, (None, rows, columns)

    def part(self, target):
        rows = self.shape[1]
        start = target * rows
        start = start if isinstance(start, int) else pl.multiple_of(start, rows)
        return self.ref.at[pl.ds(start, rows), pl.ds(0, self.shape[2])]


def add_columns(parts, target, columns):
    rows, width = parts[0].shape
    step = min(32, rows)

    def rows_of(start):
        value = parts[0][pl.ds(start, step), :].astype(f32)
        for part in parts[1:]:
            value += part[pl.ds(start, step), :].astype(f32)
        for index in range(width // columns):
            lines = pl.ds(pl.multiple_of(index * rows + start, step), step)
            target[lines, :] = value[:, index * columns : (index + 1) * columns]

    loop(rows, step, rows_of)


def column_pieces(target, rows, width, columns):
    return [target.at[pl.ds(index * rows, rows), :] for index in range(width // columns)]


class Line:
    def __init__(self, place, own, up, down, pieces, sems, early=False):
        self.place, self.own, self.up, self.down, self.pieces = place, own, up, down, pieces
        self.early = early and place.groups > 2
        self.groups, self.batch = place.groups, place.batch
        self.rows = own.shape[1] // pieces
        self.step = min(32, self.rows)
        self.sems = sems

    def span(self, piece):
        start = piece * self.rows
        return pl.ds(start if isinstance(start, int) else pl.multiple_of(start, self.rows), self.rows)

    def part(self, target):
        return self.own.part(target) if isinstance(self.own, Slices) else self.own.at[target]

    def slot(self, upward, target):
        return self.up.at[target - 1] if upward else self.down.at[target]

    def copy(self, upward, target, piece, source):
        send, recv = self.sems[:2] if upward else self.sems[2:]
        index = target * self.pieces + piece
        return pltpu.make_async_remote_copy(
            src_ref=source.at[self.span(piece), :],
            dst_ref=self.slot(upward, target).at[self.span(piece), :],
            send_sem=send.at[index],
            recv_sem=recv.at[index],
            device_id=self.place.beside(1 if upward else -1),
            device_id_type=MESH,
        )

    def sent(self, target, farthest, pieces=None):
        pieces = list(range(self.pieces) if pieces is None else pieces)
        return [piece for piece in pieces if not (self.early and target == farthest and piece == 0)]

    def start(self, target, near=None, pieces=None):
        if target > 0 and near in (None, target == 1):

            @pl.when(self.batch == 0)
            def first():
                for piece in self.sent(target, self.groups - 1, pieces):
                    self.copy(True, target, piece, self.part(target)).start()

        if target < self.groups - 1 and near in (None, target == self.groups - 2):

            @pl.when(self.batch == self.groups - 1)
            def last():
                for piece in self.sent(target, 0, pieces):
                    self.copy(False, target, piece, self.part(target)).start()

    def start_near(self, pieces=None):
        for target in range(self.groups):
            self.start(target, True, pieces)

    def order(self):
        count = self.groups
        result = []
        for index in range((count + 1) // 2):
            for target in (count - 1 - index, index):
                if target not in result:
                    result.append(target)
        return result

    def ticks(self):
        return range(1, (self.groups - 1) * self.pieces + self.groups)

    def tick(self, number):
        for upward in (True, False):
            place = self.batch if upward else self.groups - 1 - self.batch
            for distance in range(2, self.groups):
                target = distance if upward else self.groups - 1 - distance
                piece = number - (self.groups - 1 - distance) * self.pieces - place
                due = (place > 0) & (place < distance) & (piece >= 0) & (piece < self.pieces)

                @pl.when(due)
                def forward():
                    slot = self.slot(upward, target)
                    copy = self.copy(upward, target, piece, slot)
                    if not (self.early and number == 1):
                        copy.wait_recv()

                    def add(start):
                        rows = pl.ds(pl.multiple_of(piece * self.rows + start, self.step), self.step)
                        total = slot[rows, :].astype(f32) + self.part(target)[rows, :].astype(f32)
                        slot[rows, :] = total.astype(bf16)

                    loop(self.rows, self.step, add)
                    copy.start()

    def export(self, outs, moves, columns=None):
        below, above = self.batch > 0, self.batch < self.groups - 1
        jobs = []
        for out, there, upward in ((outs[0], None, None), (outs[1], below, True), (outs[2], above, False)):
            slot = self.part(self.batch) if there is None else self.slot(upward, self.batch)
            if columns is None:
                copies = [moves.make(slot, out)]
            else:
                copies = [
                    moves.make(slot.at[:, pl.ds(part * columns, columns)], out.at[part])
                    for part in range(out.shape[0])
                ]
            jobs.append((there, copies))

            def begin():
                if there is not None:
                    for piece in range(self.pieces):
                        self.copy(upward, self.batch, piece, slot).wait_recv()
                for copy in copies:
                    copy.start()

            begin() if there is None else pl.when(there)(begin)

        def wait():
            for there, copies in jobs:

                def done():
                    for copy in copies:
                        copy.wait()

                done() if there is None else pl.when(there)(done)

        return wait

    def add(self, target, columns):
        below, above = self.batch > 0, self.batch < self.groups - 1
        for there, upward in ((below, True), (above, False)):

            @pl.when(there)
            def come():
                slot = self.slot(upward, self.batch)
                for piece in range(self.pieces):
                    self.copy(upward, self.batch, piece, slot).wait_recv()

        own = self.part(self.batch)

        def sides(chosen):
            slots = [self.slot(upward, self.batch) for upward in chosen]
            add_columns([own] + slots, target, columns)

        pl.when(jnp.logical_not(above))(lambda: sides([True]))
        pl.when(jnp.logical_not(below))(lambda: sides([False]))
        pl.when(below & above)(lambda: sides([True, False]))
        return column_pieces(target, own.shape[0], own.shape[1], columns)

    def finish(self):
        for target in range(self.groups):
            for upward in (True, False):
                if target == (0 if upward else self.groups - 1):
                    continue

                slot = self.slot(upward, target)
                farthest = self.groups - 1 if upward else 0
                passes = self.batch < target if upward else self.batch > target
                inner = self.batch > 0 if upward else self.batch < self.groups - 1

                @pl.when(passes)
                def sent():
                    for piece in self.sent(target, farthest):
                        self.copy(upward, target, piece, slot).wait_send()

                if self.early and target == farthest:

                    @pl.when(passes & inner)
                    def sent_first():
                        self.copy(upward, target, 0, slot).wait_send()

    @staticmethod
    def scratch(groups, rows, columns, pieces):
        return [
            pltpu.VMEM((groups, rows, columns), bf16),
            pltpu.VMEM((groups - 1, rows, columns), bf16),
            pltpu.VMEM((groups - 1, rows, columns), bf16),
        ] + [pltpu.SemaphoreType.DMA((groups * pieces,))] * 4


class Moves:
    def __init__(self, sems):
        self.sems, self.count = sems, 0

    def make(self, source, target):
        copy = pltpu.make_async_copy(source, target, self.sems.at[self.count])
        self.count += 1
        return copy

    def start(self, source, target):
        copy = self.make(source, target)
        copy.start()
        return copy


def norm_rows(rows):
    mean = jnp.mean(rows, axis=-1, keepdims=True)
    centred = rows - mean
    inverse = lax.rsqrt(jnp.mean(centred * centred, axis=-1, keepdims=True) + EPS)
    return centred * inverse, inverse


def norm_back(grad, unit, inverse, gain):
    scaled = grad * gain
    return inverse * (
        scaled
        - jnp.mean(scaled, axis=-1, keepdims=True)
        - unit * jnp.mean(scaled * unit, axis=-1, keepdims=True)
    )


def segment_starts(group, lengths, scripts, places, rows):
    position = lax.broadcasted_iota(jnp.int32, (1, rows), 1)
    first = jnp.zeros((1, rows), jnp.int32)
    count = lengths.shape[0]
    number = [lengths[index] for index in range(count)]
    script = [scripts[index] for index in range(count)]
    mine = [places[index] == group for index in range(count)]
    own = [jnp.where(mine[index], number[index], 0) for index in range(count)]
    total = own[0]
    for index in range(1, count):
        total = total + own[index]
    for index in range(count):
        offset = jnp.int32(0)
        for other in range(count):
            if other < index:
                offset = offset + jnp.where(script[other] <= script[index], own[other], 0)
            elif other > index:
                offset = offset + jnp.where(script[other] < script[index], own[other], 0)
        bound = jnp.where(mine[index], offset, 0)
        first = jnp.maximum(first, jnp.where(position >= bound, bound, 0))
    return jnp.maximum(first, jnp.where(position >= total, total, 0))


def head_columns(part, head, width):
    return pl.ds(part * width + head * HEAD_DIM, HEAD_DIM)


def params(number):
    return pltpu.CompilerParams(
        collective_id=number, has_side_effects=True, vmem_limit_bytes=62 * 2**20
    )


def cost(micros):
    return pl.CostEstimate(flops=micros * 10**9, bytes_accessed=10**7, transcendentals=0)


def joined(ref, pieces):
    return jnp.concatenate([ref[piece, :] for piece in pieces], axis=0)


def front_kernel(
    plan, fine, block, tok, gain1, shift1, w_qkv, qv_bias, lengths, scripts, places, out_grad,
    w_out, out_bias, gain, shift, w_in, in_bias, w_down,
    first_out, qkv_out, att_out, sum_out, grad_out, second_out, act_out, hidden_out, middle_out, bias_out,
    starts, sums, attended, w_o, w_i, w_d, grad_in, up, buf, act, back, middle, local, *rest,
):
    first_sems, grad_sems, gather_sems, scatter_refs = rest[:4], rest[4:8], rest[8:12], rest[12:]
    place = Place(plan)
    own, depth = tok.shape
    rows = buf.shape[0]
    width = w_qkv.shape[2]
    hidden_width = w_in.shape[1]
    chip_rows = 2 * own
    moves = Moves(local)
    qkv = act.at[:, pl.ds(0, 3 * width)]
    weights = back.at[pl.ds(0, depth), pl.ds(0, 3 * width)]
    loads = [
        moves.start(w_qkv.at[part], back.at[pl.ds(0, depth), pl.ds(part * width, width)]) for part in range(3)
    ]
    load_out = moves.start(w_out, w_o)
    load_down = moves.start(w_down, w_d)
    load_in = moves.start(w_in, w_i)
    place.barrier()
    grads = Gather(place, grad_out, out_grad, own, grad_sems)
    grads.start(0, True)
    step = min(32, own)
    mine = pl.multiple_of(place.me * own, own)

    def normalise(start):
        unit, _ = norm_rows(tok[pl.ds(start, step), :].astype(f32))
        buf[pl.ds(pl.multiple_of(mine + start, step), step), :] = (unit * gain1[...] + shift1[...]).astype(bf16)

    loop(own, step, normalise)
    gather = Gather(place, buf, None, own, first_sems)
    gather.start()
    stores = [moves.start(out_grad, grad_out.at[pl.ds(mine, own), :])]
    starts[...] = segment_starts(place.batch, lengths, scripts, places, rows)
    for copy in loads:
        copy.wait()

    def project(offset):
        chip = lax.div(flip(place.me, offset), 2)
        span = pl.ds(pl.multiple_of(chip * chip_rows, chip_rows), chip_rows)
        stores.append(moves.start(buf.at[span, :], first_out.at[span, :]))
        product = dot(buf[span, :], weights[...], 1, 0)
        qkv[span, 0:width] = (product[:, 0:width] + qv_bias[0:1, :]).astype(bf16)
        qkv[span, width : 2 * width] = product[:, width : 2 * width].astype(bf16)
        qkv[span, 2 * width : 3 * width] = (product[:, 2 * width :] + qv_bias[1:2, :]).astype(bf16)

    gather.share(0)
    project(0)
    steps = gather.steps()
    for number, (half, keys, offsets) in enumerate(steps):
        for key in keys:
            gather.arrive(key)
        if number == max(len(steps) - 2, 0):
            grads.start(0, False)
        for offset in offsets:
            gather.share(offset)
            project(offset)
    gather.finish()
    stores.append(moves.start(qkv, qkv_out))

    scale = HEAD_DIM ** (-0.5) * LOG2E
    heads = width // HEAD_DIM
    row_in = lax.broadcasted_iota(jnp.int32, (block, block), 0)
    col_in = lax.broadcasted_iota(jnp.int32, (block, block), 1)
    key_in = lax.broadcasted_iota(jnp.int32, (block, 1), 0)

    def attend(index):
        span = pl.ds(index * block, block)
        first = starts[:, span]
        queries = [qkv[span, head_columns(0, head, width)] for head in range(heads)]

        def against(key_block, carry, diagonal):
            key_span = pl.ds(pl.multiple_of(key_block * block, block), block)
            allowed = key_in + key_block * block >= first
            if diagonal:
                allowed = allowed & (row_in <= col_in)
            result = []
            for head in range(heads):
                top, total, mixed = carry[head]
                keys = qkv[key_span, head_columns(1, head, width)]
                values = qkv[key_span, head_columns(2, head, width)]
                scores = jnp.where(allowed, dot(keys, queries[head], 1, 1) * scale, NEGATIVE)
                new_top = jnp.maximum(top, jnp.max(scores, axis=0, keepdims=True))
                exps = jnp.exp2(scores - new_top)
                fade = jnp.exp2(top - new_top)
                total = total * fade + jnp.sum(exps, axis=0, keepdims=True)
                mixed = mixed * fade + dot(values, exps.astype(bf16), 0, 0)
                result.append((new_top, total, mixed))
            return tuple(result)

        carry = tuple(
            (
                jnp.full((1, block), NEGATIVE, f32),
                jnp.zeros((1, block), f32),
                jnp.zeros((HEAD_DIM, block), f32),
            )
            for head in range(heads)
        )
        if index:
            carry = lax.fori_loop(0, index, lambda key_block, c: against(key_block, c, False), carry)
        carry = against(index, carry, True)
        for head in range(heads):
            top, total, mixed = carry[head]
            attended[span, pl.ds(head * HEAD_DIM, HEAD_DIM)] = (mixed * (1.0 / total)).T.astype(bf16)
            sums[pl.ds(head, 1), span] = top + jnp.log2(total)

    blocks = rows // block
    waiting = [key for _, keys, _ in steps for key in keys]
    for index in range(blocks):
        attend(index)
        if index == blocks - 2:
            while waiting and plan.later(*waiting[0]) and bin(waiting[0][1]).count("1") == 1:
                grads.arrive(waiting.pop(0))
    for copy in stores:
        copy.wait()
    stores = [moves.start(attended, att_out), moves.start(sums, sum_out)]

    place = Place(fine)
    scatter = Scatter(place, own, depth, *scatter_refs[:5], scatter_refs[5:])
    load_out.wait()
    tile = min(1024, depth)

    def partial(owner, target):
        lines = attended[pl.ds(pl.multiple_of(owner * own, own), own), :]

        def columns(start):
            target[:, pl.ds(start, tile)] = dot(lines, w_o[:, pl.ds(start, tile)], 1, 0).astype(target.dtype)

        loop(depth, tile, columns)

    grad_loads = {}

    def load_grad(number):
        lines = pl.ds(number * own, own)
        grad_loads[number] = moves.start(grad_out.at[lines, :], grad_in.at[number % 2])

    def between(number):
        if number == max(len(plan.offsets) - 2, 0):
            for key in waiting:
                grads.arrive(key)
            for offset in plan.offsets:
                grads.share(offset)
            load_grad(0)
            load_grad(1)

    part_cols = min(512, hidden_width)
    chips = rows // own

    def raise_grad(number):
        grad_loads[number].wait()

        def columns(start):
            cols = pl.ds(start, part_cols)
            up[pl.ds(number * own, own), cols] = dot(grad_in[number % 2], w_d[cols, :], 1, 1)

        loop(hidden_width, part_cols, columns)
        if number + 2 < chips:
            load_grad(number + 2)

    scatter.begin(partial, between)
    load_down.wait()
    for number in range(chips):
        raise_grad(number)
    scatter.middle()
    grads.finish()

    def close(start, count, value):
        span = pl.ds(start, count)
        total = tok[span, :].astype(f32) + value + out_bias[...]
        middle[span, :] = total
        unit, _ = norm_rows(total)
        buf[pl.ds(pl.multiple_of(mine + start, count), count), :] = (unit * gain[...] + shift[...]).astype(bf16)

    gather = Gather(place, buf, None, own, gather_sems)
    for half in range(fine.halves):
        scatter.end(close, half)
        gather.start(half)
    scatter.finish()
    stores.append(moves.start(middle, middle_out))
    load_in.wait()
    bias_out[...] = jnp.zeros_like(bias_out)

    def expand(offset, half):
        pieces = gather.pieces(offset, half)
        count = own // fine.halves

        def columns(start):
            cols = pl.ds(start, part_cols)
            pre = dot(joined(buf, pieces), w_i[:, cols], 1, 0) + in_bias[:, cols]
            raised = jnp.concatenate([up[piece, cols] for piece in pieces], axis=0)
            root = 0.7978845608028654
            square = pre * pre
            inner = jnp.tanh(root * (pre + 0.044715 * (square * pre)))
            rise = 0.5 * (1.0 + inner)
            slope = rise + 0.5 * pre * (1.0 - inner * inner) * (root * (1.0 + 3 * 0.044715 * square))
            lifted = (pre * rise).astype(bf16)
            down = (raised * slope).astype(bf16)
            for index, piece in enumerate(pieces):
                act[piece, cols] = lifted[index * count : (index + 1) * count]
                back[piece, cols] = down[index * count : (index + 1) * count]
            bias_out[:, cols] += jnp.sum(down.astype(f32), axis=0, keepdims=True)

        loop(hidden_width, part_cols, columns)
        for piece in pieces:
            stores.append(moves.start(buf.at[piece, :], second_out.at[piece, :]))
            stores.append(moves.start(act.at[piece, :], act_out.at[piece, :]))
            stores.append(moves.start(back.at[piece, :], hidden_out.at[piece, :]))

    for half in range(fine.halves):
        gather.share(0, half)
        expand(0, half)
    for half, keys, offsets in gather.steps():
        for key in keys:
            gather.arrive(key)
        for offset in offsets:
            gather.share(offset, half)
            expand(offset, half)
    gather.finish()
    for copy in stores:
        copy.wait()


def run_front(
    plan, fine, block, tok, gain1, shift1, w_qkv, qv_bias, order, out_grad, w_out, out_bias, gain, shift, w_in, in_bias,
    w_down,
):
    own, depth = tok.shape
    rows = own * plan.devices
    width = w_qkv.shape[2]
    hidden = w_in.shape[1]
    return pl.pallas_call(
        functools.partial(front_kernel, plan, fine, block),
        out_shape=(
            jax.ShapeDtypeStruct((rows, depth), bf16),
            jax.ShapeDtypeStruct((rows, 3 * width), bf16),
            jax.ShapeDtypeStruct((rows, width), bf16),
            jax.ShapeDtypeStruct((8, rows), f32),
            jax.ShapeDtypeStruct((rows, depth), bf16),
            jax.ShapeDtypeStruct((rows, depth), bf16),
            jax.ShapeDtypeStruct((rows, hidden), bf16),
            jax.ShapeDtypeStruct((rows, hidden), bf16),
            jax.ShapeDtypeStruct((own, depth), f32),
            jax.ShapeDtypeStruct((1, hidden), f32),
        ),
        in_specs=[VMEM, VMEM, VMEM, ANY, VMEM, SMEM, SMEM, SMEM, ANY, ANY, VMEM, VMEM, VMEM, ANY, VMEM, ANY],
        out_specs=(ANY,) * 9 + (VMEM,),
        scratch_shapes=[
            pltpu.VMEM((1, rows), jnp.int32),
            pltpu.VMEM((8, rows), f32),
            pltpu.VMEM((rows, width), bf16),
            pltpu.VMEM((width, depth), bf16),
            pltpu.VMEM((depth, hidden), bf16),
            pltpu.VMEM((hidden, depth), bf16),
            pltpu.VMEM((2, own, depth), bf16),
            pltpu.VMEM((rows, hidden), f32),
            pltpu.VMEM((rows, depth), bf16),
            pltpu.VMEM((rows, hidden), bf16),
            pltpu.VMEM((max(rows, depth), hidden), bf16),
            pltpu.VMEM((own, depth), f32),
            pltpu.SemaphoreType.DMA((160,)),
        ]
        + Gather.semaphores(plan) * 2
        + Gather.semaphores(fine)
        + Scatter.scratch(fine, own, depth, bf16),
        compiler_params=params(0),
        name="front",
        cost_estimate=cost(150),
    )(tok, gain1, shift1, w_qkv, qv_bias, *order, out_grad, w_out, out_bias, gain, shift, w_in, in_bias, w_down)


PIECES = 2


def add_parts(place, parts, target, columns):
    below, above = place.batch > 0, place.batch < place.groups - 1
    pl.when(jnp.logical_not(above))(lambda: add_columns([parts[0], parts[1]], target, columns))
    pl.when(jnp.logical_not(below))(lambda: add_columns([parts[0], parts[2]], target, columns))
    pl.when(below & above)(lambda: add_columns(parts, target, columns))


def spread_rows(place, target, rows):
    mine = lax.broadcasted_iota(jnp.int32, (target.shape[0], 1), 0) == place.me
    start = 0
    for row in rows:
        target[:, pl.ds(start, row.shape[1])] = jnp.where(mine, row, 0.0)
        start += row.shape[1]


def middle_kernel(
    plan, hidden_grad, w_in, middle, out_grad, gain, w_out, activated, grad_all, second_all, in_sums,
    middle_grad_out, branch_out, att_grad_out, sums_out, in_sums_out, down_out0, down_out1, down_out2, in_part_out, early_out,
    h_in, w_i, w_o, buf, middle_grad, att_grad, act, staged, local, early_send, early_recv, *rest,
):
    down_outs = (down_out0, down_out1, down_out2)
    scatter_refs, gather_sems, line_refs, total_refs = rest[:9], rest[9:13], rest[13:20], rest[20:]
    place = Place(plan)
    own, depth = middle.shape
    rows = buf.shape[0]
    chip_rows = 2 * own
    hidden = w_in.shape[1]
    groups = place.groups
    cut = depth // groups
    moves = Moves(local)
    loads = [moves.start(hidden_grad, h_in), moves.start(w_in, w_i)]
    load_act = moves.start(activated, act)
    order = [index for pair in zip(range(groups - 1, -1, -1), range(groups)) for index in pair][:groups]
    load_grad = [
        moves.start(grad_all.at[:, pl.ds(target * cut, cut)], buf.at[:, pl.ds(target * cut, cut)])
        for target in order
    ]
    load_out = moves.start(w_out, w_o)
    place.barrier(groups=True)
    scatter = Scatter(place, own, depth, *scatter_refs[:5], scatter_refs[5:])
    line = Line(place, *line_refs[:3], PIECES, line_refs[3:])
    tile = min(1024, depth)

    def partial(owner, target):
        lines = h_in[pl.ds(pl.multiple_of(owner * own, own), own), :]

        def columns(start):
            target[:, pl.ds(start, tile)] = dot(lines, w_i[pl.ds(start, tile), :], 1, 1).astype(target.dtype)

        loop(depth, tile, columns)

    part = min(512, hidden)

    def down_slice(index):
        target = order[index]
        load_grad[index].wait()

        def piece(start):
            line.own[target, pl.ds(start, part), :] = dot(
                act[:, pl.ds(start, part)], buf[:, pl.ds(target * cut, cut)], 0, 0
            ).astype(bf16)

        loop(hidden, part, piece)
        line.start(target, False)

    for copy in loads:
        copy.wait()

    def between(number):
        if number == 0:
            load_act.wait()
            for index in range(groups // 2):
                down_slice(index)
        if number == min(2, len(plan.offsets) - 1):
            for index in range(groups // 2, groups):
                down_slice(index)
            line.start_near()

    scatter.begin(partial, between)

    in_stores = []
    in_loads = {}
    kept = set()

    def stored(number):
        if number not in kept:
            kept.add(number)
            in_stores[number].wait()

    def load_slice(number):
        columns = pl.ds(order[number] * cut, cut)
        in_loads[number] = moves.start(second_all.at[:, columns], act.at[:, pl.ds((number % 2) * cut, cut)])

    def in_slice(number):
        in_loads[number].wait()
        if number >= 2:
            stored(number - 2)
        slot = number % 2

        def piece(start):
            columns = pl.ds(start, part)
            staged[slot, :, columns] = dot(
                act[:, pl.ds(slot * cut, cut)], h_in[:, columns], 0, 0
            ).astype(bf16)

        loop(hidden, part, piece)
        in_stores.append(moves.start(staged.at[slot], in_part_out.at[order[number]]))
        if number + 2 < groups:
            load_slice(number + 2)

    ticks = list(line.ticks())
    for number in range(min(2, groups)):
        load_slice(number)
    line.tick(ticks.pop(0))
    scatter.middle()
    half_groups = groups // 2
    for number in range(half_groups):
        in_slice(number)
    line.tick(ticks.pop(0))
    mine = pl.multiple_of(place.me * own, own)
    totals = [
        Total(place, *total_refs[index : index + 4], total_refs[index + 4 : index + 8]) for index in (0, 8)
    ]
    own_sums = totals[0].value
    own_sums[...] = jnp.zeros_like(own_sums)
    totals[1].value[...] = in_sums[...]

    def close(start, count, value):
        span = pl.ds(start, count)
        unit, inverse = norm_rows(middle[span, :])
        sum_rows = out_grad[span, :].astype(f32) + norm_back(value, unit, inverse, gain[...])
        middle_grad[span, :] = sum_rows
        buf[pl.ds(pl.multiple_of(mine + start, count), count), :] = sum_rows.astype(bf16)
        own_sums[0:1, :] += jnp.sum(value * unit, axis=0, keepdims=True)
        own_sums[1:2, :] += jnp.sum(value, axis=0, keepdims=True)
        own_sums[2:3, :] += jnp.sum(sum_rows, axis=0, keepdims=True)
        own_sums[3:4, :] += jnp.sum(out_grad[span, :].astype(f32), axis=0, keepdims=True)

    gather = Gather(place, buf, None, own, gather_sems)
    for half in range(plan.halves):
        scatter.end(close, half)
        gather.start(half)
    for total in totals:
        total.begin()
    piece_rows = pl.ds(0, cut // PIECES)
    early = []
    if groups > 2:
        for index, (edge, step, target) in enumerate(((0, 1, groups - 1), (groups - 1, -1, 0))):
            early.append(
                (
                    edge,
                    step,
                    pltpu.make_async_remote_copy(
                        src_ref=in_part_out.at[target, piece_rows, :],
                        dst_ref=early_out.at[index],
                        send_sem=early_send.at[index],
                        recv_sem=early_recv.at[index],
                        device_id=place.beside(step),
                        device_id_type=MESH,
                    ),
                )
            )
        for number in range(2):
            stored(number)
        for edge, step, copy in early:
            pl.when(place.batch == edge)(copy.start)
    line.tick(ticks.pop(0))
    scatter.finish()
    stores = [moves.start(middle_grad, middle_grad_out)]
    load_out.wait()

    def project(offset, half):
        pieces = gather.pieces(offset, half)
        count = own // plan.halves
        product = dot(joined(buf, pieces), w_o[...], 1, 1).astype(bf16)
        for index, piece in enumerate(pieces):
            att_grad[piece, :] = product[index * count : (index + 1) * count]
            stores.append(moves.start(buf.at[piece, :], branch_out.at[piece, :]))

    for half in range(plan.halves):
        gather.share(0, half)
        project(0, half)
    for number in range(half_groups, groups):
        in_slice(number)
    line.tick(ticks.pop(0))
    for half, keys, offsets in gather.steps():
        for key in keys:
            gather.arrive(key)
        for offset in offsets:
            gather.share(offset, half)
            project(offset, half)
    stores.append(moves.start(att_grad, att_grad_out))
    for number in ticks:
        line.tick(number)
    exported = line.export(down_outs, moves)
    for total, total_out in zip(totals, (sums_out, in_sums_out)):
        total.end(total_out)
    gather.finish()
    line.finish()
    for edge, step, copy in early:
        pl.when(place.batch == edge)(copy.wait_send)
        pl.when(place.batch == edge + step)(copy.wait_recv)
    for number in range(groups):
        stored(number)
    for copy in stores:
        copy.wait()
    exported()


def run_middle(plan, groups, hidden_grad, w_in, middle, out_grad, gain, w_out, activated, grad_all, second_all, in_sums):
    own, depth = middle.shape
    rows = own * plan.devices
    width = w_out.shape[0]
    hidden = w_in.shape[1]
    cut = depth // groups
    return pl.pallas_call(
        functools.partial(middle_kernel, plan),
        out_shape=(
            jax.ShapeDtypeStruct((own, depth), f32),
            jax.ShapeDtypeStruct((rows, depth), bf16),
            jax.ShapeDtypeStruct((rows, width), bf16),
            jax.ShapeDtypeStruct((4, depth), f32),
            jax.ShapeDtypeStruct(in_sums.shape, f32),
        )
        + (jax.ShapeDtypeStruct((hidden, cut), bf16),) * 3
        + (
            jax.ShapeDtypeStruct((groups, cut, hidden), bf16),
            jax.ShapeDtypeStruct((2, cut // PIECES, hidden), bf16),
        ),
        in_specs=[ANY, ANY, VMEM, VMEM, VMEM, ANY, ANY, ANY, ANY, VMEM],
        out_specs=(ANY, ANY, ANY, VMEM, VMEM, ANY, ANY, ANY, ANY, ANY),
        scratch_shapes=[
            pltpu.VMEM((rows, hidden), bf16),
            pltpu.VMEM((depth, hidden), bf16),
            pltpu.VMEM((width, depth), bf16),
            pltpu.VMEM((rows, depth), bf16),
            pltpu.VMEM((own, depth), f32),
            pltpu.VMEM((rows, width), bf16),
            pltpu.VMEM((rows, max(hidden, 2 * cut)), bf16),
            pltpu.VMEM((2, cut, hidden), bf16),
            pltpu.SemaphoreType.DMA((64,)),
            pltpu.SemaphoreType.DMA((2,)),
            pltpu.SemaphoreType.DMA((2,)),
        ]
        + Scatter.scratch(plan, own, depth, bf16)
        + Gather.semaphores(plan)
        + Line.scratch(groups, hidden, cut, PIECES)
        + Total.scratch(plan, groups, (4, depth))
        + Total.scratch(plan, groups, in_sums.shape),
        compiler_params=params(2),
        name="middle",
        cost_estimate=cost(80),
    )(hidden_grad, w_in, middle, out_grad, gain, w_out, activated, grad_all, second_all, in_sums)


def back_kernel(
    plan, block, lengths, scripts, places, qkv, att, att_grad, sums, activated, w_down, middle, down_bias, in_part,
    branch_all, sums2, in_sums, down0, down1, down2, early, w_qkv, tok, middle_grad, gain, first_all,
    block_out, input_out, down_out, in_out, out_out, qkv_out, vectors2_out, spread2_out, vectors_out, spread_out,
    qkv_in, att_in, grad_in, act_in, w_d, mid, starts, key_grad, value_grad, result, branch, bias_out, local, free, *rest,
):
    feed_refs, first_sems, rest = rest[:9], rest[9:13], rest[13:]
    in_refs, out_refs, qkv_refs, total_refs = rest[:7], rest[7:14], rest[14:20], rest[20:]
    place = Place(plan)
    own, depth = tok.shape
    rows = qkv_in.shape[0]
    width = att_in.shape[1]
    hidden = w_down.shape[0]
    heads = width // HEAD_DIM
    groups = place.groups
    cut = depth // groups
    moves = Moves(local)
    line = Line(place, *in_refs[:3], PIECES, in_refs[3:], early=True)
    out_line = Line(place, *out_refs[:3], 1, out_refs[3:])
    qkv_line = Line(place, Slices(act_in, cut, 3 * width), *qkv_refs[:2], PIECES, qkv_refs[2:])
    order = line.order()
    parts = [moves.start(in_part.at[target], line.own.at[target]) for target in order]
    feeds = [moves.start(activated, act_in), moves.start(w_down, w_d)]
    loads = [moves.start(qkv, qkv_in), moves.start(att, att_in), moves.start(att_grad, grad_in)]
    load_middle = moves.start(middle, mid)
    slice_loads = {}

    def load_slice(source, number, name):
        columns = pl.ds(number * cut, cut)
        slice_loads[name] = moves.start(source.at[:, columns], branch.at[name[1] % 2])

    for index in range(min(2, groups)):
        load_slice(branch_all, order[index], ("out", index))
    early_loads = []
    if line.early:
        for index, (whose, upward, target) in enumerate(((1, True, groups - 1), (groups - 2, False, 0))):
            copy = moves.make(early.at[index], line.slot(upward, target).at[line.span(0), :])
            early_loads.append((whose, copy))
            pl.when(place.batch == whose)(copy.start)
    place.barrier(groups=True)
    scatter = Scatter(place, own, depth, *feed_refs[:5], feed_refs[5:])
    for whose, copy in early_loads:
        pl.when(place.batch == whose)(copy.wait)
    for target, copy in zip(order, parts):
        copy.wait()
        line.start(target, False)
    line.start_near()
    ticks = list(line.ticks())
    if line.early:
        line.tick(ticks.pop(0))
    for copy in feeds:
        copy.wait()
    tile = min(1024, depth)

    def partial(owner, target):
        lines = act_in[pl.ds(pl.multiple_of(owner * own, own), own), :]

        def columns(start):
            target[:, pl.ds(start, tile)] = dot(lines, w_d[:, pl.ds(start, tile)], 1, 0).astype(target.dtype)

        loop(depth, tile, columns)

    scatter.begin(partial)
    turns = depth // hidden
    weight_loads = [
        moves.start(
            w_qkv.at[part, pl.ds(turn * hidden, hidden), :],
            w_d.at[:, pl.ds((turn * 3 + part) * width, width)],
        )
        for turn in range(turns)
        for part in range(3)
    ]
    line.tick(ticks.pop(0))
    starts[...] = segment_starts(place.batch, lengths, scripts, places, rows)
    bias_out[...] = jnp.zeros_like(bias_out)
    key_grad[...] = jnp.zeros_like(key_grad)
    value_grad[...] = jnp.zeros_like(value_grad)
    for copy in loads:
        copy.wait()
    for index, target in enumerate(order):
        slice_loads["out", index].wait()
        out_line.own[target, :, :] = dot(att_in[...], branch[index % 2], 0, 0).astype(bf16)
        out_line.start(target, False)
        if index + 2 < groups:
            load_slice(branch_all, order[index + 2], ("out", index + 2))
    out_line.start_near()
    fit = rows // hidden
    down_parts = [branch.at[index // fit, pl.ds((index % fit) * hidden, hidden), :] for index in range(3)]
    down_loads = [moves.start(part, target) for part, target in zip((down0, down1, down2), down_parts)]
    scale = HEAD_DIM ** (-0.5)
    row_in = lax.broadcasted_iota(jnp.int32, (block, block), 0)
    col_in = lax.broadcasted_iota(jnp.int32, (block, block), 1)
    key_in = lax.broadcasted_iota(jnp.int32, (block, 1), 0)

    def attend(index):
        span = pl.ds(index * block, block)
        first = starts[:, span]
        queries, outer, inner, logs = [], [], [], []
        for head in range(heads):
            columns = pl.ds(head * HEAD_DIM, HEAD_DIM)
            queries.append(qkv_in[span, head_columns(0, head, width)])
            outer.append(grad_in[span, columns])
            product = grad_in[span, columns].astype(f32) * att_in[span, columns].astype(f32)
            inner.append(jnp.sum(product.T, axis=0, keepdims=True))
            logs.append(sums[pl.ds(head, 1), span])

        def against(key_block, carry, diagonal):
            key_span = pl.ds(pl.multiple_of(key_block * block, block), block)
            allowed = key_in + key_block * block >= first
            if diagonal:
                allowed = allowed & (row_in <= col_in)
            out = []
            for head in range(heads):
                columns = pl.ds(head * HEAD_DIM, HEAD_DIM)
                keys = qkv_in[key_span, head_columns(1, head, width)]
                values = qkv_in[key_span, head_columns(2, head, width)]
                scores = dot(keys, queries[head], 1, 1) * (scale * LOG2E)
                probs = jnp.exp2(jnp.where(allowed, scores - logs[head], NEGATIVE))
                value_grad[key_span, columns] += dot(probs.astype(bf16), outer[head], 1, 0)
                prob_grad = dot(values, outer[head], 1, 1)
                score_grad = (probs * (prob_grad - inner[head])).astype(bf16)
                key_grad[key_span, columns] += dot(score_grad, queries[head], 1, 0)
                out.append(carry[head] + dot(score_grad, keys, 0, 0))
            return tuple(out)

        carry = tuple(jnp.zeros((block, HEAD_DIM), f32) for head in range(heads))
        if index:
            carry = lax.fori_loop(0, index, lambda key_block, c: against(key_block, c, False), carry)
        carry = against(index, carry, True)
        for head in range(heads):
            query_grad = (carry[head] * scale).astype(bf16)
            qkv_in[span, head_columns(0, head, width)] = query_grad
            columns = pl.ds(head * HEAD_DIM, HEAD_DIM)
            bias_out[0:1, columns] += jnp.sum(query_grad.astype(f32), axis=0, keepdims=True)

    blocks = rows // block
    for index in range(blocks):
        attend(index)
        if index == blocks // 2:
            scatter.middle()
        if 0 < index < blocks - 1:
            line.tick(ticks.pop(0))
    kept = min(256, rows)

    def write(start):
        span = pl.ds(start, kept)
        qkv_in[span, pl.ds(width, width)] = (key_grad[span, :] * scale).astype(bf16)
        rounded = value_grad[span, :].astype(bf16)
        qkv_in[span, pl.ds(2 * width, width)] = rounded
        bias_out[1:2, :] += jnp.sum(rounded.astype(f32), axis=0, keepdims=True)

    loop(rows, kept, write)
    for number in ticks:
        line.tick(number)
    for copy in down_loads:
        copy.wait()
    add_parts(place, down_parts, key_grad, width)
    down_stores = [
        moves.start(piece, down_out.at[:, pl.ds(index * width, width)])
        for index, piece in enumerate(column_pieces(key_grad, hidden, cut, width))
    ]
    for index in range(min(2, groups)):
        load_slice(first_all, order[index], ("qkv", index))
    load_middle.wait()

    def close(start, count, value):
        span = pl.ds(start, count)
        result[span, :] = (mid[span, :] + value + down_bias[...]).astype(bf16)

    for half in range(plan.halves):
        scatter.end(close, half)
    stores = [moves.start(result, block_out)]
    load_grad = moves.start(middle_grad, mid)
    totals = [
        Total(place, *total_refs[index : index + 4], total_refs[index + 4 : index + 8]) for index in (0, 8, 16, 24)
    ]
    vectors2, spread2, vectors, spread = totals
    vectors2.value[...] = sums2[...]
    spread_rows(place, spread2.value, [bias_out[0:1, :], bias_out[1:2, :], in_sums[...]])
    vectors.value[...] = jnp.zeros_like(vectors.value)
    masks = [1] + plan.bits
    for mask in masks:
        pl.semaphore_signal(free, inc=1, device_id=place.at(mask), device_id_type=MESH)
    scatter.finish()
    scatter = Scatter(place, own, depth, *feed_refs[:5], first_sems)
    for copy in weight_loads:
        copy.wait()

    def first_partial(owner, target):
        lines = qkv_in[pl.ds(pl.multiple_of(owner * own, own), own), :]
        for turn in range(turns):
            target[:, pl.ds(turn * hidden, hidden)] = dot(
                lines, w_d[:, pl.ds(turn * 3 * width, 3 * width)], 1, 1
            ).astype(target.dtype)

    def qkv_slice(index):
        slice_loads["qkv", index].wait()
        qkv_line.part(order[index])[...] = dot(branch[index % 2], qkv_in[...], 0, 0).astype(bf16)
        qkv_line.start(order[index], False)
        if index + 2 < groups:
            load_slice(first_all, order[index + 2], ("qkv", index + 2))

    for index in range(groups):
        qkv_slice(index)
    qkv_line.start_near()
    pl.semaphore_wait(free, len(masks))
    out_ticks = list(out_line.ticks())

    def between(number):
        if number < 2:
            out_line.tick(out_ticks.pop(0))

    scatter.begin(first_partial, between)
    for number in out_ticks:
        out_line.tick(number)
    scatter.middle()
    pieces = line.add(value_grad, width)
    in_stores = [
        moves.start(piece, in_out.at[:, pl.ds(index * width, width)]) for index, piece in enumerate(pieces)
    ]
    ticks = list(qkv_line.ticks())
    qkv_line.tick(ticks.pop(0))
    qkv_line.tick(ticks.pop(0))
    load_grad.wait()
    stores.pop(0).wait()
    load_tok = moves.start(tok, result)
    load_tok.wait()

    def close_first(start, count, value):
        span = pl.ds(start, count)
        unit, inverse = norm_rows(result[span, :].astype(f32))
        sum_rows = mid[span, :] + norm_back(value, unit, inverse, gain[...])
        result[span, :] = sum_rows.astype(bf16)
        vectors.value[0:1, :] += jnp.sum(value * unit, axis=0, keepdims=True)
        vectors.value[1:2, :] += jnp.sum(value, axis=0, keepdims=True)

    for half in range(plan.halves):
        scatter.end(close_first, half)
    stores.append(moves.start(result, input_out))
    for number in ticks:
        qkv_line.tick(number)
    vectors.plane([vectors2, spread2])
    spread.value[...] = spread2.value[:, 0 : 2 * width]
    for total in (vectors, spread):
        total.begin()
    for copy in in_stores + down_stores:
        copy.wait()
    pieces = out_line.add(key_grad, width)
    stores += [
        moves.start(piece, out_out.at[:, pl.ds(index * width, width)]) for index, piece in enumerate(pieces)
    ]
    pieces = qkv_line.add(value_grad, width)
    stores += [moves.start(piece, qkv_out.at[index]) for index, piece in enumerate(pieces)]
    scatter.finish()
    line.finish()
    out_line.finish()
    qkv_line.finish()
    vectors2_out[...] = vectors2.value[...]
    spread2_out[...] = spread2.value[...]
    vectors.end(vectors_out)
    spread.end(spread_out)
    for copy in stores:
        copy.wait()


def run_back(
    plan, groups, block, order, qkv, att, att_grad, sums, activated, w_down, middle, down_bias, in_part, branch_all,
    sums2, in_sums, down_parts, early, w_qkv, tok, middle_grad, gain, first_all,
):
    own, depth = tok.shape
    rows, width = att.shape
    hidden = w_down.shape[0]
    cut = depth // groups
    return pl.pallas_call(
        functools.partial(back_kernel, plan, block),
        out_shape=(
            jax.ShapeDtypeStruct((own, depth), bf16),
            jax.ShapeDtypeStruct((own, depth), bf16),
            jax.ShapeDtypeStruct((hidden, cut), f32),
            jax.ShapeDtypeStruct((cut, hidden), f32),
            jax.ShapeDtypeStruct((width, cut), f32),
            jax.ShapeDtypeStruct((3, cut, width), f32),
            jax.ShapeDtypeStruct(sums2.shape, f32),
            jax.ShapeDtypeStruct((plan.devices, 2 * width + hidden), f32),
            jax.ShapeDtypeStruct((2, depth), f32),
            jax.ShapeDtypeStruct((plan.devices, 2 * width), f32),
        ),
        in_specs=[SMEM] * 3
        + [ANY, ANY, ANY, VMEM, ANY, ANY, ANY, VMEM, ANY, ANY, VMEM, VMEM, ANY, ANY, ANY, ANY, ANY, ANY, ANY, VMEM, ANY],
        out_specs=(ANY,) * 6 + (VMEM,) * 4,
        scratch_shapes=[
            pltpu.VMEM((rows, 3 * width), bf16),
            pltpu.VMEM((rows, width), bf16),
            pltpu.VMEM((rows, width), bf16),
            pltpu.VMEM((rows, hidden), bf16),
            pltpu.VMEM((hidden, depth), bf16),
            pltpu.VMEM((own, depth), f32),
            pltpu.VMEM((1, rows), jnp.int32),
            pltpu.VMEM((rows, width), f32),
            pltpu.VMEM((rows, width), f32),
            pltpu.VMEM((own, depth), bf16),
            pltpu.VMEM((2, rows, cut), bf16),
            pltpu.VMEM((2, width), f32),
            pltpu.SemaphoreType.DMA((96,)),
            pltpu.SemaphoreType.REGULAR,
        ]
        + Scatter.scratch(plan, own, depth, bf16)
        + Scatter.scratch(plan, own, depth, bf16)[5:]
        + Line.scratch(groups, cut, hidden, PIECES)
        + Line.scratch(groups, width, cut, 1)
        + Line.scratch(groups, cut, 3 * width, PIECES)[1:]
        + Total.scratch(plan, 1, sums2.shape)
        + Total.scratch(plan, 1, (plan.devices, 2 * width + hidden))
        + Total.scratch(plan, groups, (2, depth))
        + Total.scratch(plan, groups, (plan.devices, 2 * width)),
        compiler_params=params(3),
        name="back",
        cost_estimate=cost(145),
    )(
        *order, qkv, att, att_grad, sums, activated, w_down, middle, down_bias, in_part, branch_all, sums2, in_sums,
        *down_parts, early, w_qkv, tok, middle_grad, gain, first_all,
    )


def close_kernel(plan, *refs):
    large, (vectors, vectors2, spread, spread2) = refs[:6], refs[6:10]
    outs, vector_outs, (qv_out, in_out), held, sems = refs[10:16], refs[16:22], refs[22:24], refs[24:30], refs[30]
    loads = [pltpu.make_async_copy(large[index], held[index], sems.at[index]) for index in range(6)]
    copies = [pltpu.make_async_copy(held[index], outs[index], sems.at[6 + index]) for index in range(6)]
    for load in loads:
        load.start()
    rows = [vectors[0:1, :], vectors[1:2, :]] + [vectors2[index : index + 1, :] for index in range(4)]
    for row, out in zip(rows, vector_outs):
        out[...] = row
    width = spread.shape[1] // 2
    hidden = spread2.shape[1] - 2 * width
    for index in range(plan.devices):
        for part in range(2):
            qv_out[part : part + 1, pl.ds(index * width, width)] = spread[
                index : index + 1, part * width : (part + 1) * width
            ]
        in_out[:, pl.ds(index * hidden, hidden)] = spread2[index : index + 1, 2 * width :]
    for load, copy in zip(loads, copies):
        load.wait()
        copy.start()
    for copy in copies:
        copy.wait()


def run_close(plan, large, small):
    depth = small[0].shape[1]
    devices, double = small[2].shape
    hidden = small[3].shape[1] - double
    return pl.pallas_call(
        functools.partial(close_kernel, plan),
        out_shape=tuple(jax.ShapeDtypeStruct(array.shape, array.dtype) for array in large)
        + (jax.ShapeDtypeStruct((1, depth), f32),) * 6
        + (
            jax.ShapeDtypeStruct((2, devices * double // 2), f32),
            jax.ShapeDtypeStruct((1, devices * hidden), f32),
        ),
        in_specs=[ANY] * 6 + [VMEM] * 4,
        out_specs=(ANY,) * 6 + (VMEM,) * 8,
        scratch_shapes=[pltpu.VMEM(array.shape, array.dtype) for array in large] + [pltpu.SemaphoreType.DMA((12,))],
        compiler_params=pltpu.CompilerParams(vmem_limit_bytes=62 * 2**20),
        name="close",
    )(*large, *small)


def body(
    tokens,
    out_grad,
    seq_lengths,
    seq_scripts,
    seq_place,
    norm1_gain,
    norm1_shift,
    w_qkv,
    qv_bias,
    w_out,
    out_bias,
    norm2_gain,
    norm2_shift,
    w_in,
    in_bias,
    w_down,
    down_bias,
):
    own, depth = tokens.shape
    devices = lax.axis_size("mp")
    plan = Plan(devices)
    fine = Plan(devices, 2)
    rows = own * devices
    width = w_qkv.shape[2]
    block = min(512, rows)
    order = (seq_lengths, seq_scripts, seq_place)

    def line(vector):
        return vector.reshape(1, -1)

    (
        first_all, qkv, att, sums, grad_all, second_all, activated, hidden_grad, middle, in_part,
    ) = run_front(
        plan, fine, block, tokens, line(norm1_gain), line(norm1_shift), w_qkv, qv_bias, order, out_grad,
        w_out, line(out_bias), line(norm2_gain), line(norm2_shift), w_in, line(in_bias), w_down,
    )
    groups = lax.axis_size("batch")
    middle_grad, branch_all, att_grad, sums2, in_sums, *down_parts, in_part2, early = run_middle(
        fine, groups, hidden_grad, w_in, middle, out_grad, line(norm2_gain), w_out, activated, grad_all, second_all,
        in_part,
    )
    (
        block_out, input_grad, down_weight_grad, in_weight_grad, out_weight_grad, qkv_weight_grad,
        vectors2, spread2, vectors, spread,
    ) = run_back(
        plan, groups, block, order, qkv, att, att_grad, sums, activated, w_down, middle, line(down_bias),
        in_part2, branch_all, sums2, in_sums, down_parts, early, w_qkv, tokens, middle_grad, line(norm1_gain), first_all,
    )
    *large, gain1, shift1, gain2, shift2, out_b, down_b, qv_bias_grad, in_b = run_close(
        plan,
        (block_out, input_grad, qkv_weight_grad, out_weight_grad, in_weight_grad, down_weight_grad),
        (vectors, vectors2, spread, spread2),
    )
    return (
        large[0],
        large[1],
        gain1.reshape(-1),
        shift1.reshape(-1),
        large[2],
        qv_bias_grad,
        large[3],
        out_b.reshape(-1),
        gain2.reshape(-1),
        shift2.reshape(-1),
        large[4],
        in_b.reshape(-1),
        large[5],
        down_b.reshape(-1),
    )


def solution(mesh):
    return jax.shard_map(
        body,
        mesh=mesh,
        in_specs=(
            P(("batch", "mp"), None),
            P(("batch", "mp"), None),
            P(),
            P(),
            P(),
            P(),
            P(),
            P(None, None, "mp"),
            P(None, "mp"),
            P("mp", None),
            P(),
            P(),
            P(),
            P(None, "mp"),
            P("mp"),
            P("mp", None),
            P(),
        ),
        out_specs=(
            P(("batch", "mp"), None),
            P(("batch", "mp"), None),
            P(),
            P(),
            P(None, "batch", "mp"),
            P(),
            P("mp", "batch"),
            P(),
            P(),
            P(),
            P("batch", "mp"),
            P(),
            P("mp", "batch"),
            P(),
        ),
        check_vma=False,
    )
```

```python
import functools

import jax
import jax.numpy as jnp
from jax import lax
from jax.experimental import pallas as pl
from jax.experimental.pallas import tpu as pltpu
from jax.sharding import PartitionSpec as P

HEAD_DIM = 128
EPS = 1e-05
NEGATIVE = -1e30
LOG2E = 1.4426950408889634
f32 = jnp.float32
bf16 = jnp.bfloat16
MESH = pl.DeviceIdType.MESH
ANY = pl.BlockSpec(memory_space=pl.ANY)
VMEM = pl.BlockSpec(memory_space=pltpu.VMEM)
SMEM = pl.BlockSpec(memory_space=pltpu.SMEM)


def dot(left, right, contract_left, contract_right):
    return lax.dot_general(
        left,
        right,
        (((contract_left,), (contract_right,)), ((), ())),
        preferred_element_type=f32,
    )


def flip(index, mask):
    bit = 1
    while bit <= mask:
        if mask & bit:
            index = index + bit * (1 - 2 * lax.rem(lax.div(index, bit), 2))
        bit *= 2
    return index


def loop(count, step, body):
    def one(index, carry):
        body(pl.multiple_of(index * step, step))
        return carry

    lax.fori_loop(0, count // step, one, 0)


class Plan:
    def __init__(self, devices, halves=1):
        bits = []
        bit = 2
        while bit < devices:
            bits.append(bit)
            bit *= 2
        self.devices = devices
        self.bits = bits
        self.ways = [tuple(bits)] + ([tuple(reversed(bits))] if len(bits) > 1 else [])
        self.halves = halves
        self.orders = self.ways * halves
        self.parts = len(self.orders)
        self.offsets = list(range(0, devices, 2))
        self.keys = [(part, offset) for part in range(self.parts) for offset in self.offsets if offset]
        self.keys.sort(key=lambda key: (self.half(key[0]), bin(key[1]).count("1"), self.last(*key)))
        self.shares = [(part, offset) for offset in self.offsets for part in range(self.parts)]

    def half(self, part):
        return part // len(self.ways)

    def parts_of(self, half):
        return range(half * len(self.ways), (half + 1) * len(self.ways))

    def last(self, part, offset):
        steps = [step for step, bit in enumerate(self.orders[part]) if bit & offset]
        return max(steps) if steps else -1

    def bit(self, part, offset):
        return self.orders[part][self.last(part, offset)]

    def later(self, part, offset):
        order = self.orders[part]
        return [offset | order[step] for step in range(self.last(part, offset) + 1, len(order))]


class Place:
    def __init__(self, plan):
        self.plan = plan
        self.batch = lax.axis_index("batch")
        self.groups = lax.axis_size("batch")
        self.me = lax.axis_index("mp")

    def at(self, mask):
        return (self.batch, flip(self.me, mask))

    def beside(self, step):
        return (self.batch + step, self.me)

    def around(self, step):
        return (lax.rem(self.batch + step, self.groups), self.me)

    def barrier(self, groups=False):
        semaphore = pltpu.get_barrier_semaphore()
        partners = [self.at(mask) for mask in [1] + self.plan.bits]
        if groups:
            partners += [self.around(step) for step in range(1, self.groups)]
        for partner in partners:
            pl.semaphore_signal(semaphore, inc=1, device_id=partner, device_id_type=MESH)
        pl.semaphore_wait(semaphore, len(partners))


class Total:
    def __init__(self, place, value, sent, came, slots, sems):
        self.place, self.value, self.sent, self.came, self.slots = place, value, sent, came, slots
        self.send, self.recv, self.slot_send, self.slot_recv = sems

    def plane(self, others=()):
        totals = (self,) + tuple(others)
        for index, mask in enumerate([1] + self.place.plan.bits):
            copies = [
                pltpu.make_async_remote_copy(
                    src_ref=total.sent.at[index],
                    dst_ref=total.came.at[index],
                    send_sem=total.send.at[index],
                    recv_sem=total.recv.at[index],
                    device_id=self.place.at(mask),
                    device_id_type=MESH,
                )
                for total in totals
            ]
            for total, copy in zip(totals, copies):
                total.sent[index] = total.value[...]
                copy.start()
            for total, copy in zip(totals, copies):
                copy.wait_recv()
                total.value[...] = total.sent[index] + total.came[index]
                copy.wait_send()

    def slot(self, step):
        return pltpu.make_async_remote_copy(
            src_ref=self.value,
            dst_ref=self.slots.at[step],
            send_sem=self.slot_send.at[step - 1],
            recv_sem=self.slot_recv.at[step - 1],
            device_id=self.place.around(step),
            device_id_type=MESH,
        )

    def begin(self):
        self.slots[0] = self.value[...]
        for step in range(1, self.place.groups):
            self.slot(step).start()

    def end(self, result):
        for step in range(1, self.place.groups):
            self.slot(step).wait()
        groups = self.place.groups
        total = self.slots[self.place.batch]
        for group in range(1, groups):
            total = total + self.slots[lax.rem(self.place.batch + groups - group, groups)]
        result[...] = total

    @staticmethod
    def scratch(plan, groups, shape):
        rounds = len(plan.bits) + 1
        return [
            pltpu.VMEM(shape, f32),
            pltpu.VMEM((rounds,) + shape, f32),
            pltpu.VMEM((rounds,) + shape, f32),
            pltpu.VMEM((groups,) + shape, f32),
            pltpu.SemaphoreType.DMA((rounds,)),
            pltpu.SemaphoreType.DMA((rounds,)),
            pltpu.SemaphoreType.DMA((max(groups - 1, 1),)),
            pltpu.SemaphoreType.DMA((max(groups - 1, 1),)),
        ]


class Gather:
    def __init__(self, place, buf, own, rows, sems):
        self.place, self.plan, self.buf, self.own, self.rows = place, place.plan, buf, own, rows
        self.link_send, self.link_recv, self.core_send, self.core_recv = sems
        self.part_rows = rows // self.plan.parts

    def span(self, mask, part):
        block = flip(self.place.me, mask)
        start = block * self.rows + part * self.part_rows
        return self.buf.at[pl.ds(pl.multiple_of(start, self.part_rows), self.part_rows), :]

    def source(self, offset, part):
        if offset == 0 and self.own is not None:
            return self.own.at[pl.ds(part * self.part_rows, self.part_rows), :]
        return self.span(offset, part)

    def link(self, key):
        part, offset = key
        bit = self.plan.bit(part, offset)
        index = self.plan.keys.index(key)
        return pltpu.make_async_remote_copy(
            src_ref=self.source(offset ^ bit, part),
            dst_ref=self.span(offset ^ bit, part),
            send_sem=self.link_send.at[index],
            recv_sem=self.link_recv.at[index],
            device_id=self.place.at(bit),
            device_id_type=MESH,
        )

    def core(self, key):
        part, offset = key
        index = self.plan.shares.index(key)
        return pltpu.make_async_remote_copy(
            src_ref=self.source(offset, part),
            dst_ref=self.span(offset, part),
            send_sem=self.core_send.at[index],
            recv_sem=self.core_recv.at[index],
            device_id=self.place.at(1),
            device_id_type=MESH,
        )

    def landed(self, ref, semaphore):
        pltpu.make_async_remote_copy(
            src_ref=ref,
            dst_ref=ref,
            send_sem=semaphore,
            recv_sem=semaphore,
            device_id=self.place.at(1),
            device_id_type=MESH,
        ).wait_recv()

    def start(self, half=0, ahead=None):
        if ahead in (None, False):
            for part in self.plan.parts_of(half):
                self.core((part, 0)).start()
        for key in self.plan.keys:
            if bin(key[1]).count("1") == 1 and self.plan.half(key[0]) == half:
                if ahead is None or ahead == (self.plan.last(*key) == 0):
                    self.link(key).start()

    def arrive(self, key):
        part, offset = key
        self.landed(self.span(offset, part), self.link_recv.at[self.plan.keys.index(key)])
        for target in self.plan.later(part, offset):
            self.link((part, target)).start()
        self.core(key).start()

    def share(self, offset, half=0):
        for part in self.plan.parts_of(half):
            index = self.plan.shares.index((part, offset))
            self.landed(self.span(offset | 1, part), self.core_recv.at[index])

    def steps(self):
        result = []
        for half in range(self.plan.halves):
            for count in range(1, len(self.plan.bits) + 1):
                keys = [
                    key
                    for key in self.plan.keys
                    if self.plan.half(key[0]) == half and bin(key[1]).count("1") == count
                ]
                offsets = [offset for offset in self.plan.offsets if bin(offset).count("1") == count]
                result.append((half, keys, offsets))
        return result

    def pieces(self, offset, half):
        count = self.rows // self.plan.halves
        chip = lax.div(flip(self.place.me, offset), 2) * 2
        return [
            pl.ds(pl.multiple_of((chip + core) * self.rows + half * count, count), count) for core in range(2)
        ]

    def finish(self):
        for key in self.plan.keys:
            self.link(key).wait_send()
        for key in self.plan.shares:
            self.core(key).wait_send()

    @staticmethod
    def semaphores(plan):
        return [pltpu.SemaphoreType.DMA((len(plan.keys),))] * 2 + [
            pltpu.SemaphoreType.DMA((len(plan.shares),))
        ] * 2


class Spread:
    dtype = bf16

    def __init__(self, refs):
        self.refs = refs

    def __setitem__(self, index, value):
        count = self.refs[0].shape[0]
        for number, ref in enumerate(self.refs):
            ref[index] = value[number * count : (number + 1) * count]


class Scatter:
    def __init__(self, place, rows, width, core_out, core_in, kept, link_out, link_in, sems):
        self.place, self.plan, self.rows, self.width = place, place.plan, rows, width
        self.core_out, self.core_in, self.kept = core_out, core_in, kept
        self.link_out, self.link_in = link_out, link_in
        self.link_send, self.link_recv, self.core_send, self.core_recv = sems
        self.part_rows = rows // self.plan.parts
        self.step = min(32, self.part_rows)
        self.order = sorted(self.plan.offsets, key=lambda offset: -bin(offset).count("1"))

    def core(self, offset):
        index = offset // 2
        return pltpu.make_async_remote_copy(
            src_ref=self.core_out.at[index],
            dst_ref=self.core_in.at[index],
            send_sem=self.core_send.at[index],
            recv_sem=self.core_recv.at[index],
            device_id=self.place.at(1),
            device_id_type=MESH,
        )

    def link(self, key):
        index = self.plan.keys.index(key)
        return pltpu.make_async_remote_copy(
            src_ref=self.link_out.at[index],
            dst_ref=self.link_in.at[index],
            send_sem=self.link_send.at[index],
            recv_sem=self.link_recv.at[index],
            device_id=self.place.at(self.plan.bit(*key)),
            device_id_type=MESH,
        )

    def keep(self, offset):
        if offset == 0:
            return self.kept
        return Spread([self.link_out.at[self.plan.keys.index((part, offset))] for part in range(self.plan.parts)])

    def total(self, offset, part, start, arrived):
        rows = pl.ds(pl.multiple_of(part * self.part_rows + start, self.step), self.step)
        if offset:
            value = self.link_out[self.plan.keys.index((part, offset)), pl.ds(start, self.step), :].astype(f32)
        else:
            value = self.kept[rows, :].astype(f32)
        value += self.core_in[offset // 2, rows, :].astype(f32)
        for key in arrived:
            value += self.link_in[self.plan.keys.index(key), pl.ds(start, self.step), :].astype(f32)
        return value

    def pass_on(self, part, offset):
        arrived = [(part, target) for target in self.plan.later(part, offset)]
        for key in arrived:
            self.link(key).wait_recv()
        index = self.plan.keys.index((part, offset))

        def add(start):
            self.link_out[index, pl.ds(start, self.step), :] = self.total(
                offset, part, start, arrived
            ).astype(bf16)

        loop(self.part_rows, self.step, add)
        self.link((part, offset)).start()

    def free(self, offset, half):
        for part in self.plan.parts_of(half):
            if offset and not self.plan.later(part, offset):
                self.pass_on(part, offset)

    def bound(self, half):
        for offset in self.order:
            for part in self.plan.parts_of(half):
                if offset and self.plan.later(part, offset):
                    self.pass_on(part, offset)

    def begin(self, partial, between=None):
        for number, offset in enumerate(self.order):
            index = offset // 2
            if offset == 0:
                self.bound(0)
            partial(flip(self.place.me, offset | 1), self.core_out.at[index])
            self.core(offset).start()
            partial(flip(self.place.me, offset), self.keep(offset))
            self.core(offset).wait_recv()
            for half in range(self.plan.halves):
                self.free(offset, half)
            if between is not None:
                between(number)

    def middle(self):
        for half in range(1, self.plan.halves):
            self.bound(half)

    def end(self, use, half=0):
        for part in self.plan.parts_of(half):
            arrived = [(part, target) for target in self.plan.later(part, 0)]
            for key in arrived:
                self.link(key).wait_recv()

            def piece(start):
                row = pl.multiple_of(part * self.part_rows + start, self.step)
                use(row, self.step, self.total(0, part, start, arrived))

            loop(self.part_rows, self.step, piece)

    def finish(self):
        for key in self.plan.keys:
            self.link(key).wait_send()
        for offset in self.plan.offsets:
            self.core(offset).wait_send()

    @staticmethod
    def scratch(plan, rows, width, kept):
        chips, keys = len(plan.offsets), len(plan.keys)
        return [
            pltpu.VMEM((chips, rows, width), bf16),
            pltpu.VMEM((chips, rows, width), bf16),
            pltpu.VMEM((rows, width), kept),
            pltpu.VMEM((keys, rows // plan.parts, width), bf16),
            pltpu.VMEM((keys, rows // plan.parts, width), bf16),
            pltpu.SemaphoreType.DMA((keys,)),
            pltpu.SemaphoreType.DMA((keys,)),
            pltpu.SemaphoreType.DMA((chips,)),
            pltpu.SemaphoreType.DMA((chips,)),
        ]


class Slices:
    def __init__(self, ref, rows, columns):
        self.ref, self.shape = ref, (None, rows, columns)

    def part(self, target):
        rows = self.shape[1]
        start = target * rows
        start = start if isinstance(start, int) else pl.multiple_of(start, rows)
        return self.ref.at[pl.ds(start, rows), pl.ds(0, self.shape[2])]


def add_columns(parts, target, columns):
    rows, width = parts[0].shape
    step = min(32, rows)

    def rows_of(start):
        value = parts[0][pl.ds(start, step), :].astype(f32)
        for part in parts[1:]:
            value += part[pl.ds(start, step), :].astype(f32)
        for index in range(width // columns):
            lines = pl.ds(pl.multiple_of(index * rows + start, step), step)
            target[lines, :] = value[:, index * columns : (index + 1) * columns]

    loop(rows, step, rows_of)


def column_pieces(target, rows, width, columns):
    return [target.at[pl.ds(index * rows, rows), :] for index in range(width // columns)]


class Line:
    def __init__(self, place, own, up, down, pieces, sems, early=False):
        self.place, self.own, self.up, self.down, self.pieces = place, own, up, down, pieces
        self.early = early and place.groups > 2
        self.groups, self.batch = place.groups, place.batch
        self.rows = own.shape[1] // pieces
        self.step = min(32, self.rows)
        self.sems = sems

    def span(self, piece):
        start = piece * self.rows
        return pl.ds(start if isinstance(start, int) else pl.multiple_of(start, self.rows), self.rows)

    def part(self, target):
        return self.own.part(target) if isinstance(self.own, Slices) else self.own.at[target]

    def slot(self, upward, target):
        return self.up.at[target - 1] if upward else self.down.at[target]

    def copy(self, upward, target, piece, source):
        send, recv = self.sems[:2] if upward else self.sems[2:]
        index = target * self.pieces + piece
        return pltpu.make_async_remote_copy(
            src_ref=source.at[self.span(piece), :],
            dst_ref=self.slot(upward, target).at[self.span(piece), :],
            send_sem=send.at[index],
            recv_sem=recv.at[index],
            device_id=self.place.beside(1 if upward else -1),
            device_id_type=MESH,
        )

    def sent(self, target, farthest, pieces=None):
        pieces = list(range(self.pieces) if pieces is None else pieces)
        return [piece for piece in pieces if not (self.early and target == farthest and piece == 0)]

    def start(self, target, near=None, pieces=None):
        if target > 0 and near in (None, target == 1):

            @pl.when(self.batch == 0)
            def first():
                for piece in self.sent(target, self.groups - 1, pieces):
                    self.copy(True, target, piece, self.part(target)).start()

        if target < self.groups - 1 and near in (None, target == self.groups - 2):

            @pl.when(self.batch == self.groups - 1)
            def last():
                for piece in self.sent(target, 0, pieces):
                    self.copy(False, target, piece, self.part(target)).start()

    def start_near(self, pieces=None):
        for target in range(self.groups):
            self.start(target, True, pieces)

    def order(self):
        count = self.groups
        result = []
        for index in range((count + 1) // 2):
            for target in (count - 1 - index, index):
                if target not in result:
                    result.append(target)
        return result

    def ticks(self):
        return range(1, (self.groups - 1) * self.pieces + self.groups)

    def tick(self, number):
        for upward in (True, False):
            place = self.batch if upward else self.groups - 1 - self.batch
            for distance in range(2, self.groups):
                target = distance if upward else self.groups - 1 - distance
                piece = number - (self.groups - 1 - distance) * self.pieces - place
                due = (place > 0) & (place < distance) & (piece >= 0) & (piece < self.pieces)

                @pl.when(due)
                def forward():
                    slot = self.slot(upward, target)
                    copy = self.copy(upward, target, piece, slot)
                    if not (self.early and number == 1):
                        copy.wait_recv()

                    def add(start):
                        rows = pl.ds(pl.multiple_of(piece * self.rows + start, self.step), self.step)
                        total = slot[rows, :].astype(f32) + self.part(target)[rows, :].astype(f32)
                        slot[rows, :] = total.astype(bf16)

                    loop(self.rows, self.step, add)
                    copy.start()

    def export(self, outs, moves, columns=None):
        below, above = self.batch > 0, self.batch < self.groups - 1
        jobs = []
        for out, there, upward in ((outs[0], None, None), (outs[1], below, True), (outs[2], above, False)):
            slot = self.part(self.batch) if there is None else self.slot(upward, self.batch)
            if columns is None:
                copies = [moves.make(slot, out)]
            else:
                copies = [
                    moves.make(slot.at[:, pl.ds(part * columns, columns)], out.at[part])
                    for part in range(out.shape[0])
                ]
            jobs.append((there, copies))

            def begin():
                if there is not None:
                    for piece in range(self.pieces):
                        self.copy(upward, self.batch, piece, slot).wait_recv()
                for copy in copies:
                    copy.start()

            begin() if there is None else pl.when(there)(begin)

        def wait():
            for there, copies in jobs:

                def done():
                    for copy in copies:
                        copy.wait()

                done() if there is None else pl.when(there)(done)

        return wait

    def add(self, target, columns):
        below, above = self.batch > 0, self.batch < self.groups - 1
        for there, upward in ((below, True), (above, False)):

            @pl.when(there)
            def come():
                slot = self.slot(upward, self.batch)
                for piece in range(self.pieces):
                    self.copy(upward, self.batch, piece, slot).wait_recv()

        own = self.part(self.batch)

        def sides(chosen):
            slots = [self.slot(upward, self.batch) for upward in chosen]
            add_columns([own] + slots, target, columns)

        pl.when(jnp.logical_not(above))(lambda: sides([True]))
        pl.when(jnp.logical_not(below))(lambda: sides([False]))
        pl.when(below & above)(lambda: sides([True, False]))
        return column_pieces(target, own.shape[0], own.shape[1], columns)

    def finish(self):
        for target in range(self.groups):
            for upward in (True, False):
                if target == (0 if upward else self.groups - 1):
                    continue

                slot = self.slot(upward, target)
                farthest = self.groups - 1 if upward else 0
                passes = self.batch < target if upward else self.batch > target
                inner = self.batch > 0 if upward else self.batch < self.groups - 1

                @pl.when(passes)
                def sent():
                    for piece in self.sent(target, farthest):
                        self.copy(upward, target, piece, slot).wait_send()

                if self.early and target == farthest:

                    @pl.when(passes & inner)
                    def sent_first():
                        self.copy(upward, target, 0, slot).wait_send()

    @staticmethod
    def scratch(groups, rows, columns, pieces):
        return [
            pltpu.VMEM((groups, rows, columns), bf16),
            pltpu.VMEM((groups - 1, rows, columns), bf16),
            pltpu.VMEM((groups - 1, rows, columns), bf16),
        ] + [pltpu.SemaphoreType.DMA((groups * pieces,))] * 4


class Moves:
    def __init__(self, sems):
        self.sems, self.count = sems, 0

    def make(self, source, target):
        copy = pltpu.make_async_copy(source, target, self.sems.at[self.count])
        self.count += 1
        return copy

    def start(self, source, target):
        copy = self.make(source, target)
        copy.start()
        return copy


def norm_rows(rows):
    mean = jnp.mean(rows, axis=-1, keepdims=True)
    centred = rows - mean
    inverse = lax.rsqrt(jnp.mean(centred * centred, axis=-1, keepdims=True) + EPS)
    return centred * inverse, inverse


def norm_back(grad, unit, inverse, gain):
    scaled = grad * gain
    return inverse * (
        scaled
        - jnp.mean(scaled, axis=-1, keepdims=True)
        - unit * jnp.mean(scaled * unit, axis=-1, keepdims=True)
    )


def segment_starts(group, lengths, scripts, places, rows):
    position = lax.broadcasted_iota(jnp.int32, (1, rows), 1)
    first = jnp.zeros((1, rows), jnp.int32)
    count = lengths.shape[0]
    number = [lengths[index] for index in range(count)]
    script = [scripts[index] for index in range(count)]
    mine = [places[index] == group for index in range(count)]
    own = [jnp.where(mine[index], number[index], 0) for index in range(count)]
    total = own[0]
    for index in range(1, count):
        total = total + own[index]
    for index in range(count):
        offset = jnp.int32(0)
        for other in range(count):
            if other < index:
                offset = offset + jnp.where(script[other] <= script[index], own[other], 0)
            elif other > index:
                offset = offset + jnp.where(script[other] < script[index], own[other], 0)
        bound = jnp.where(mine[index], offset, 0)
        first = jnp.maximum(first, jnp.where(position >= bound, bound, 0))
    return jnp.maximum(first, jnp.where(position >= total, total, 0))


def head_columns(part, head, width):
    return pl.ds(part * width + head * HEAD_DIM, HEAD_DIM)


def params(number):
    return pltpu.CompilerParams(
        collective_id=number, has_side_effects=True, vmem_limit_bytes=62 * 2**20
    )


def cost(micros):
    return pl.CostEstimate(flops=micros * 10**9, bytes_accessed=10**7, transcendentals=0)


def joined(ref, pieces):
    return jnp.concatenate([ref[piece, :] for piece in pieces], axis=0)


def front_kernel(
    plan, fine, block, tok, gain1, shift1, w_qkv, qv_bias, lengths, scripts, places, out_grad,
    w_out, out_bias, gain, shift, w_in, in_bias, w_down,
    first_out, qkv_out, att_out, sum_out, grad_out, second_out, act_out, hidden_out, middle_out, bias_out,
    starts, sums, attended, w_o, w_i, w_d, grad_in, up, buf, act, back, middle, local, *rest,
):
    first_sems, grad_sems, gather_sems, scatter_refs = rest[:4], rest[4:8], rest[8:12], rest[12:]
    place = Place(plan)
    own, depth = tok.shape
    rows = buf.shape[0]
    width = w_qkv.shape[2]
    hidden_width = w_in.shape[1]
    chip_rows = 2 * own
    moves = Moves(local)
    qkv = act.at[:, pl.ds(0, 3 * width)]
    weights = back.at[pl.ds(0, depth), pl.ds(0, 3 * width)]
    loads = [
        moves.start(w_qkv.at[part], back.at[pl.ds(0, depth), pl.ds(part * width, width)]) for part in range(3)
    ]
    load_out = moves.start(w_out, w_o)
    load_down = moves.start(w_down, w_d)
    load_in = moves.start(w_in, w_i)
    place.barrier()
    grads = Gather(place, grad_out, out_grad, own, grad_sems)
    grads.start(0, True)
    step = min(32, own)
    mine = pl.multiple_of(place.me * own, own)

    def normalise(start):
        unit, _ = norm_rows(tok[pl.ds(start, step), :].astype(f32))
        buf[pl.ds(pl.multiple_of(mine + start, step), step), :] = (unit * gain1[...] + shift1[...]).astype(bf16)

    loop(own, step, normalise)
    gather = Gather(place, buf, None, own, first_sems)
    gather.start()
    stores = [moves.start(out_grad, grad_out.at[pl.ds(mine, own), :])]
    starts[...] = segment_starts(place.batch, lengths, scripts, places, rows)
    for copy in loads:
        copy.wait()

    def project(offset):
        chip = lax.div(flip(place.me, offset), 2)
        span = pl.ds(pl.multiple_of(chip * chip_rows, chip_rows), chip_rows)
        stores.append(moves.start(buf.at[span, :], first_out.at[span, :]))
        product = dot(buf[span, :], weights[...], 1, 0)
        qkv[span, 0:width] = (product[:, 0:width] + qv_bias[0:1, :]).astype(bf16)
        qkv[span, width : 2 * width] = product[:, width : 2 * width].astype(bf16)
        qkv[span, 2 * width : 3 * width] = (product[:, 2 * width :] + qv_bias[1:2, :]).astype(bf16)

    gather.share(0)
    project(0)
    steps = gather.steps()
    for number, (half, keys, offsets) in enumerate(steps):
        for key in keys:
            gather.arrive(key)
        if number == max(len(steps) - 2, 0):
            grads.start(0, False)
        for offset in offsets:
            gather.share(offset)
            project(offset)
    gather.finish()
    stores.append(moves.start(qkv, qkv_out))

    scale = HEAD_DIM ** (-0.5) * LOG2E
    heads = width // HEAD_DIM
    row_in = lax.broadcasted_iota(jnp.int32, (block, block), 0)
    col_in = lax.broadcasted_iota(jnp.int32, (block, block), 1)
    key_in = lax.broadcasted_iota(jnp.int32, (block, 1), 0)

    def attend(index):
        span = pl.ds(index * block, block)
        first = starts[:, span]
        queries = [qkv[span, head_columns(0, head, width)] for head in range(heads)]

        def against(key_block, carry, diagonal):
            key_span = pl.ds(pl.multiple_of(key_block * block, block), block)
            allowed = key_in + key_block * block >= first
            if diagonal:
                allowed = allowed & (row_in <= col_in)
            result = []
            for head in range(heads):
                top, total, mixed = carry[head]
                keys = qkv[key_span, head_columns(1, head, width)]
                values = qkv[key_span, head_columns(2, head, width)]
                scores = jnp.where(allowed, dot(keys, queries[head], 1, 1) * scale, NEGATIVE)
                new_top = jnp.maximum(top, jnp.max(scores, axis=0, keepdims=True))
                exps = jnp.exp2(scores - new_top)
                fade = jnp.exp2(top - new_top)
                total = total * fade + jnp.sum(exps, axis=0, keepdims=True)
                mixed = mixed * fade + dot(values, exps.astype(bf16), 0, 0)
                result.append((new_top, total, mixed))
            return tuple(result)

        carry = tuple(
            (
                jnp.full((1, block), NEGATIVE, f32),
                jnp.zeros((1, block), f32),
                jnp.zeros((HEAD_DIM, block), f32),
            )
            for head in range(heads)
        )
        if index:
            carry = lax.fori_loop(0, index, lambda key_block, c: against(key_block, c, False), carry)
        carry = against(index, carry, True)
        for head in range(heads):
            top, total, mixed = carry[head]
            attended[span, pl.ds(head * HEAD_DIM, HEAD_DIM)] = (mixed * (1.0 / total)).T.astype(bf16)
            sums[pl.ds(head, 1), span] = top + jnp.log2(total)

    blocks = rows // block
    waiting = [key for _, keys, _ in steps for key in keys]
    for index in range(blocks):
        attend(index)
        if index == blocks - 2:
            while waiting and plan.later(*waiting[0]) and bin(waiting[0][1]).count("1") == 1:
                grads.arrive(waiting.pop(0))
    for copy in stores:
        copy.wait()
    stores = [moves.start(attended, att_out), moves.start(sums, sum_out)]

    place = Place(fine)
    scatter = Scatter(place, own, depth, *scatter_refs[:5], scatter_refs[5:])
    load_out.wait()
    tile = min(1024, depth)

    def partial(owner, target):
        lines = attended[pl.ds(pl.multiple_of(owner * own, own), own), :]

        def columns(start):
            target[:, pl.ds(start, tile)] = dot(lines, w_o[:, pl.ds(start, tile)], 1, 0).astype(target.dtype)

        loop(depth, tile, columns)

    grad_loads = {}

    def load_grad(number):
        lines = pl.ds(number * own, own)
        grad_loads[number] = moves.start(grad_out.at[lines, :], grad_in.at[number % 2])

    def between(number):
        if number == max(len(plan.offsets) - 2, 0):
            for key in waiting:
                grads.arrive(key)
            for offset in plan.offsets:
                grads.share(offset)
            load_grad(0)
            load_grad(1)

    part_cols = min(512, hidden_width)
    chips = rows // own

    def raise_grad(number):
        grad_loads[number].wait()

        def columns(start):
            cols = pl.ds(start, part_cols)
            up[pl.ds(number * own, own), cols] = dot(grad_in[number % 2], w_d[cols, :], 1, 1)

        loop(hidden_width, part_cols, columns)
        if number + 2 < chips:
            load_grad(number + 2)

    scatter.begin(partial, between)
    load_down.wait()
    for number in range(chips):
        raise_grad(number)
    scatter.middle()
    grads.finish()

    def close(start, count, value):
        span = pl.ds(start, count)
        total = tok[span, :].astype(f32) + value + out_bias[...]
        middle[span, :] = total
        unit, _ = norm_rows(total)
        buf[pl.ds(pl.multiple_of(mine + start, count), count), :] = (unit * gain[...] + shift[...]).astype(bf16)

    gather = Gather(place, buf, None, own, gather_sems)
    for half in range(fine.halves):
        scatter.end(close, half)
        gather.start(half)
    scatter.finish()
    stores.append(moves.start(middle, middle_out))
    load_in.wait()
    bias_out[...] = jnp.zeros_like(bias_out)

    def expand(offset, half):
        pieces = gather.pieces(offset, half)
        count = own // fine.halves

        def columns(start):
            cols = pl.ds(start, part_cols)
            pre = dot(joined(buf, pieces), w_i[:, cols], 1, 0) + in_bias[:, cols]
            raised = jnp.concatenate([up[piece, cols] for piece in pieces], axis=0)
            root = 0.7978845608028654
            square = pre * pre
            inner = jnp.tanh(root * (pre + 0.044715 * (square * pre)))
            rise = 0.5 * (1.0 + inner)
            slope = rise + 0.5 * pre * (1.0 - inner * inner) * (root * (1.0 + 3 * 0.044715 * square))
            lifted = (pre * rise).astype(bf16)
            down = (raised * slope).astype(bf16)
            for index, piece in enumerate(pieces):
                act[piece, cols] = lifted[index * count : (index + 1) * count]
                back[piece, cols] = down[index * count : (index + 1) * count]
            bias_out[:, cols] += jnp.sum(down.astype(f32), axis=0, keepdims=True)

        loop(hidden_width, part_cols, columns)
        for piece in pieces:
            stores.append(moves.start(buf.at[piece, :], second_out.at[piece, :]))
            stores.append(moves.start(act.at[piece, :], act_out.at[piece, :]))
            stores.append(moves.start(back.at[piece, :], hidden_out.at[piece, :]))

    for half in range(fine.halves):
        gather.share(0, half)
        expand(0, half)
    for half, keys, offsets in gather.steps():
        for key in keys:
            gather.arrive(key)
        for offset in offsets:
            gather.share(offset, half)
            expand(offset, half)
    gather.finish()
    for copy in stores:
        copy.wait()


def run_front(
    plan, fine, block, tok, gain1, shift1, w_qkv, qv_bias, order, out_grad, w_out, out_bias, gain, shift, w_in, in_bias,
    w_down,
):
    own, depth = tok.shape
    rows = own * plan.devices
    width = w_qkv.shape[2]
    hidden = w_in.shape[1]
    return pl.pallas_call(
        functools.partial(front_kernel, plan, fine, block),
        out_shape=(
            jax.ShapeDtypeStruct((rows, depth), bf16),
            jax.ShapeDtypeStruct((rows, 3 * width), bf16),
            jax.ShapeDtypeStruct((rows, width), bf16),
            jax.ShapeDtypeStruct((8, rows), f32),
            jax.ShapeDtypeStruct((rows, depth), bf16),
            jax.ShapeDtypeStruct((rows, depth), bf16),
            jax.ShapeDtypeStruct((rows, hidden), bf16),
            jax.ShapeDtypeStruct((rows, hidden), bf16),
            jax.ShapeDtypeStruct((own, depth), f32),
            jax.ShapeDtypeStruct((1, hidden), f32),
        ),
        in_specs=[VMEM, VMEM, VMEM, ANY, VMEM, SMEM, SMEM, SMEM, ANY, ANY, VMEM, VMEM, VMEM, ANY, VMEM, ANY],
        out_specs=(ANY,) * 9 + (VMEM,),
        scratch_shapes=[
            pltpu.VMEM((1, rows), jnp.int32),
            pltpu.VMEM((8, rows), f32),
            pltpu.VMEM((rows, width), bf16),
            pltpu.VMEM((width, depth), bf16),
            pltpu.VMEM((depth, hidden), bf16),
            pltpu.VMEM((hidden, depth), bf16),
            pltpu.VMEM((2, own, depth), bf16),
            pltpu.VMEM((rows, hidden), f32),
            pltpu.VMEM((rows, depth), bf16),
            pltpu.VMEM((rows, hidden), bf16),
            pltpu.VMEM((max(rows, depth), hidden), bf16),
            pltpu.VMEM((own, depth), f32),
            pltpu.SemaphoreType.DMA((160,)),
        ]
        + Gather.semaphores(plan) * 2
        + Gather.semaphores(fine)
        + Scatter.scratch(fine, own, depth, bf16),
        compiler_params=params(0),
        name="front",
        cost_estimate=cost(150),
    )(tok, gain1, shift1, w_qkv, qv_bias, *order, out_grad, w_out, out_bias, gain, shift, w_in, in_bias, w_down)


PIECES = 2


def add_parts(place, parts, target, columns):
    below, above = place.batch > 0, place.batch < place.groups - 1
    pl.when(jnp.logical_not(above))(lambda: add_columns([parts[0], parts[1]], target, columns))
    pl.when(jnp.logical_not(below))(lambda: add_columns([parts[0], parts[2]], target, columns))
    pl.when(below & above)(lambda: add_columns(parts, target, columns))


def spread_rows(place, target, rows):
    mine = lax.broadcasted_iota(jnp.int32, (target.shape[0], 1), 0) == place.me
    start = 0
    for row in rows:
        target[:, pl.ds(start, row.shape[1])] = jnp.where(mine, row, 0.0)
        start += row.shape[1]


def middle_kernel(
    plan, hidden_grad, w_in, middle, out_grad, gain, w_out, activated, grad_all, second_all, in_sums,
    middle_grad_out, branch_out, att_grad_out, sums_out, in_sums_out, down_out0, down_out1, down_out2, in_part_out, early_out,
    h_in, w_i, w_o, buf, middle_grad, att_grad, act, staged, local, early_send, early_recv, *rest,
):
    down_outs = (down_out0, down_out1, down_out2)
    scatter_refs, gather_sems, line_refs, total_refs = rest[:9], rest[9:13], rest[13:20], rest[20:]
    place = Place(plan)
    own, depth = middle.shape
    rows = buf.shape[0]
    chip_rows = 2 * own
    hidden = w_in.shape[1]
    groups = place.groups
    cut = depth // groups
    moves = Moves(local)
    load_act = moves.start(activated, act)
    order = [index for pair in zip(range(groups - 1, -1, -1), range(groups)) for index in pair][:groups]

    def load_columns(targets):
        return [
            moves.start(grad_all.at[:, pl.ds(target * cut, cut)], buf.at[:, pl.ds(target * cut, cut)])
            for target in targets
        ]

    load_grad = load_columns(order[: groups // 2])
    loads = [moves.start(hidden_grad, h_in), moves.start(w_in, w_i)]
    load_grad += load_columns(order[groups // 2 :])
    load_out = moves.start(w_out, w_o)
    place.barrier(groups=True)
    scatter = Scatter(place, own, depth, *scatter_refs[:5], scatter_refs[5:])
    line = Line(place, *line_refs[:3], PIECES, line_refs[3:])
    tile = min(1024, depth)

    def partial(owner, target):
        lines = h_in[pl.ds(pl.multiple_of(owner * own, own), own), :]

        def columns(start):
            target[:, pl.ds(start, tile)] = dot(lines, w_i[pl.ds(start, tile), :], 1, 1).astype(target.dtype)

        loop(depth, tile, columns)

    part = min(512, hidden)

    def down_slice(index):
        target = order[index]
        load_grad[index].wait()

        def piece(start):
            line.own[target, pl.ds(start, part), :] = dot(
                act[:, pl.ds(start, part)], buf[:, pl.ds(target * cut, cut)], 0, 0
            ).astype(bf16)

        loop(hidden, part, piece)
        line.start(target, False)

    load_act.wait()
    for index in range(groups // 2):
        down_slice(index)
    for copy in loads:
        copy.wait()

    def between(number):
        if number == min(2, len(plan.offsets) - 1):
            for index in range(groups // 2, groups):
                down_slice(index)
            line.start_near()

    scatter.begin(partial, between)

    in_stores = []
    in_loads = {}
    kept = set()

    def stored(number):
        if number not in kept:
            kept.add(number)
            in_stores[number].wait()

    def load_slice(number):
        columns = pl.ds(order[number] * cut, cut)
        in_loads[number] = moves.start(second_all.at[:, columns], act.at[:, pl.ds((number % 2) * cut, cut)])

    def in_slice(number):
        in_loads[number].wait()
        if number >= 2:
            stored(number - 2)
        slot = number % 2

        def piece(start):
            columns = pl.ds(start, part)
            staged[slot, :, columns] = dot(
                act[:, pl.ds(slot * cut, cut)], h_in[:, columns], 0, 0
            ).astype(bf16)

        loop(hidden, part, piece)
        in_stores.append(moves.start(staged.at[slot], in_part_out.at[order[number]]))
        if number + 2 < groups:
            load_slice(number + 2)

    ticks = list(line.ticks())
    for number in range(min(2, groups)):
        load_slice(number)
    line.tick(ticks.pop(0))
    scatter.middle()
    half_groups = groups // 2
    for number in range(half_groups):
        in_slice(number)
    line.tick(ticks.pop(0))
    mine = pl.multiple_of(place.me * own, own)
    totals = [
        Total(place, *total_refs[index : index + 4], total_refs[index + 4 : index + 8]) for index in (0, 8)
    ]
    own_sums = totals[0].value
    own_sums[...] = jnp.zeros_like(own_sums)
    totals[1].value[...] = in_sums[...]

    def close(start, count, value):
        span = pl.ds(start, count)
        unit, inverse = norm_rows(middle[span, :])
        sum_rows = out_grad[span, :].astype(f32) + norm_back(value, unit, inverse, gain[...])
        middle_grad[span, :] = sum_rows
        buf[pl.ds(pl.multiple_of(mine + start, count), count), :] = sum_rows.astype(bf16)
        own_sums[0:1, :] += jnp.sum(value * unit, axis=0, keepdims=True)
        own_sums[1:2, :] += jnp.sum(value, axis=0, keepdims=True)
        own_sums[2:3, :] += jnp.sum(sum_rows, axis=0, keepdims=True)
        own_sums[3:4, :] += jnp.sum(out_grad[span, :].astype(f32), axis=0, keepdims=True)

    gather = Gather(place, buf, None, own, gather_sems)
    for half in range(plan.halves):
        scatter.end(close, half)
        gather.start(half)
    for total in totals:
        total.begin()
    piece_rows = pl.ds(0, cut // PIECES)
    early = []
    if groups > 2:
        for index, (edge, step, target) in enumerate(((0, 1, groups - 1), (groups - 1, -1, 0))):
            early.append(
                (
                    edge,
                    step,
                    pltpu.make_async_remote_copy(
                        src_ref=in_part_out.at[target, piece_rows, :],
                        dst_ref=early_out.at[index],
                        send_sem=early_send.at[index],
                        recv_sem=early_recv.at[index],
                        device_id=place.beside(step),
                        device_id_type=MESH,
                    ),
                )
            )
        for number in range(2):
            stored(number)
        for edge, step, copy in early:
            pl.when(place.batch == edge)(copy.start)
    line.tick(ticks.pop(0))
    scatter.finish()
    stores = [moves.start(middle_grad, middle_grad_out)]
    load_out.wait()

    def project(offset, half):
        pieces = gather.pieces(offset, half)
        count = own // plan.halves
        product = dot(joined(buf, pieces), w_o[...], 1, 1).astype(bf16)
        for index, piece in enumerate(pieces):
            att_grad[piece, :] = product[index * count : (index + 1) * count]
            stores.append(moves.start(buf.at[piece, :], branch_out.at[piece, :]))

    for half in range(plan.halves):
        gather.share(0, half)
        project(0, half)
    for number in range(half_groups, groups):
        in_slice(number)
    line.tick(ticks.pop(0))
    for half, keys, offsets in gather.steps():
        for key in keys:
            gather.arrive(key)
        for offset in offsets:
            gather.share(offset, half)
            project(offset, half)
    stores.append(moves.start(att_grad, att_grad_out))
    for number in ticks:
        line.tick(number)
    exported = line.export(down_outs, moves)
    for total, total_out in zip(totals, (sums_out, in_sums_out)):
        total.end(total_out)
    gather.finish()
    line.finish()
    for edge, step, copy in early:
        pl.when(place.batch == edge)(copy.wait_send)
        pl.when(place.batch == edge + step)(copy.wait_recv)
    for number in range(groups):
        stored(number)
    for copy in stores:
        copy.wait()
    exported()


def run_middle(plan, groups, hidden_grad, w_in, middle, out_grad, gain, w_out, activated, grad_all, second_all, in_sums):
    own, depth = middle.shape
    rows = own * plan.devices
    width = w_out.shape[0]
    hidden = w_in.shape[1]
    cut = depth // groups
    return pl.pallas_call(
        functools.partial(middle_kernel, plan),
        out_shape=(
            jax.ShapeDtypeStruct((own, depth), f32),
            jax.ShapeDtypeStruct((rows, depth), bf16),
            jax.ShapeDtypeStruct((rows, width), bf16),
            jax.ShapeDtypeStruct((4, depth), f32),
            jax.ShapeDtypeStruct(in_sums.shape, f32),
        )
        + (jax.ShapeDtypeStruct((hidden, cut), bf16),) * 3
        + (
            jax.ShapeDtypeStruct((groups, cut, hidden), bf16),
            jax.ShapeDtypeStruct((2, cut // PIECES, hidden), bf16),
        ),
        in_specs=[ANY, ANY, VMEM, VMEM, VMEM, ANY, ANY, ANY, ANY, VMEM],
        out_specs=(ANY, ANY, ANY, VMEM, VMEM, ANY, ANY, ANY, ANY, ANY),
        scratch_shapes=[
            pltpu.VMEM((rows, hidden), bf16),
            pltpu.VMEM((depth, hidden), bf16),
            pltpu.VMEM((width, depth), bf16),
            pltpu.VMEM((rows, depth), bf16),
            pltpu.VMEM((own, depth), f32),
            pltpu.VMEM((rows, width), bf16),
            pltpu.VMEM((rows, max(hidden, 2 * cut)), bf16),
            pltpu.VMEM((2, cut, hidden), bf16),
            pltpu.SemaphoreType.DMA((64,)),
            pltpu.SemaphoreType.DMA((2,)),
            pltpu.SemaphoreType.DMA((2,)),
        ]
        + Scatter.scratch(plan, own, depth, bf16)
        + Gather.semaphores(plan)
        + Line.scratch(groups, hidden, cut, PIECES)
        + Total.scratch(plan, groups, (4, depth))
        + Total.scratch(plan, groups, in_sums.shape),
        compiler_params=params(2),
        name="middle",
        cost_estimate=cost(80),
    )(hidden_grad, w_in, middle, out_grad, gain, w_out, activated, grad_all, second_all, in_sums)


def back_kernel(
    plan, block, lengths, scripts, places, qkv, att, att_grad, sums, activated, w_down, middle, down_bias, in_part,
    branch_all, sums2, in_sums, down0, down1, down2, early, w_qkv, tok, middle_grad, gain, first_all,
    block_out, input_out, down_out, in_out, out_out, qkv_out, vectors2_out, spread2_out, vectors_out, spread_out,
    qkv_in, att_in, grad_in, act_in, w_d, mid, starts, key_grad, value_grad, result, branch, bias_out, local, free, *rest,
):
    feed_refs, first_sems, rest = rest[:9], rest[9:13], rest[13:]
    in_refs, out_refs, qkv_refs, total_refs = rest[:7], rest[7:14], rest[14:20], rest[20:]
    place = Place(plan)
    own, depth = tok.shape
    rows = qkv_in.shape[0]
    width = att_in.shape[1]
    hidden = w_down.shape[0]
    heads = width // HEAD_DIM
    groups = place.groups
    cut = depth // groups
    moves = Moves(local)
    line = Line(place, *in_refs[:3], PIECES, in_refs[3:], early=True)
    out_line = Line(place, *out_refs[:3], 1, out_refs[3:])
    qkv_line = Line(place, Slices(act_in, cut, 3 * width), *qkv_refs[:2], PIECES, qkv_refs[2:])
    order = line.order()
    parts = [moves.start(in_part.at[target], line.own.at[target]) for target in order]
    feeds = [moves.start(activated, act_in), moves.start(w_down, w_d)]
    loads = [moves.start(qkv, qkv_in), moves.start(att, att_in), moves.start(att_grad, grad_in)]
    load_middle = moves.start(middle, mid)
    slice_loads = {}

    def load_slice(source, number, name):
        columns = pl.ds(number * cut, cut)
        slice_loads[name] = moves.start(source.at[:, columns], branch.at[name[1] % 2])

    for index in range(min(2, groups)):
        load_slice(branch_all, order[index], ("out", index))
    early_loads = []
    if line.early:
        for index, (whose, upward, target) in enumerate(((1, True, groups - 1), (groups - 2, False, 0))):
            copy = moves.make(early.at[index], line.slot(upward, target).at[line.span(0), :])
            early_loads.append((whose, copy))
            pl.when(place.batch == whose)(copy.start)
    place.barrier(groups=True)
    scatter = Scatter(place, own, depth, *feed_refs[:5], feed_refs[5:])
    for whose, copy in early_loads:
        pl.when(place.batch == whose)(copy.wait)
    for target, copy in zip(order, parts):
        copy.wait()
        line.start(target, False)
    line.start_near()
    ticks = list(line.ticks())
    if line.early:
        line.tick(ticks.pop(0))
    for copy in feeds:
        copy.wait()
    tile = min(1024, depth)

    def partial(owner, target):
        lines = act_in[pl.ds(pl.multiple_of(owner * own, own), own), :]

        def columns(start):
            target[:, pl.ds(start, tile)] = dot(lines, w_d[:, pl.ds(start, tile)], 1, 0).astype(target.dtype)

        loop(depth, tile, columns)

    scatter.begin(partial)
    turns = depth // hidden
    weight_loads = [
        moves.start(
            w_qkv.at[part, pl.ds(turn * hidden, hidden), :],
            w_d.at[:, pl.ds((turn * 3 + part) * width, width)],
        )
        for turn in range(turns)
        for part in range(3)
    ]
    line.tick(ticks.pop(0))
    starts[...] = segment_starts(place.batch, lengths, scripts, places, rows)
    bias_out[...] = jnp.zeros_like(bias_out)
    key_grad[...] = jnp.zeros_like(key_grad)
    value_grad[...] = jnp.zeros_like(value_grad)
    for copy in loads:
        copy.wait()
    for index, target in enumerate(order):
        slice_loads["out", index].wait()
        out_line.own[target, :, :] = dot(att_in[...], branch[index % 2], 0, 0).astype(bf16)
        out_line.start(target, False)
        if index + 2 < groups:
            load_slice(branch_all, order[index + 2], ("out", index + 2))
    out_line.start_near()
    fit = rows // hidden
    down_parts = [branch.at[index // fit, pl.ds((index % fit) * hidden, hidden), :] for index in range(3)]
    down_loads = [moves.start(part, target) for part, target in zip((down0, down1, down2), down_parts)]
    scale = HEAD_DIM ** (-0.5)
    row_in = lax.broadcasted_iota(jnp.int32, (block, block), 0)
    col_in = lax.broadcasted_iota(jnp.int32, (block, block), 1)
    key_in = lax.broadcasted_iota(jnp.int32, (block, 1), 0)

    def attend(index):
        span = pl.ds(index * block, block)
        first = starts[:, span]
        queries, outer, inner, logs = [], [], [], []
        for head in range(heads):
            columns = pl.ds(head * HEAD_DIM, HEAD_DIM)
            queries.append(qkv_in[span, head_columns(0, head, width)])
            outer.append(grad_in[span, columns])
            product = grad_in[span, columns].astype(f32) * att_in[span, columns].astype(f32)
            inner.append(jnp.sum(product.T, axis=0, keepdims=True))
            logs.append(sums[pl.ds(head, 1), span])

        def against(key_block, carry, diagonal):
            key_span = pl.ds(pl.multiple_of(key_block * block, block), block)
            allowed = key_in + key_block * block >= first
            if diagonal:
                allowed = allowed & (row_in <= col_in)
            out = []
            for head in range(heads):
                columns = pl.ds(head * HEAD_DIM, HEAD_DIM)
                keys = qkv_in[key_span, head_columns(1, head, width)]
                values = qkv_in[key_span, head_columns(2, head, width)]
                scores = dot(keys, queries[head], 1, 1) * (scale * LOG2E)
                probs = jnp.exp2(jnp.where(allowed, scores - logs[head], NEGATIVE))
                value_grad[key_span, columns] += dot(probs.astype(bf16), outer[head], 1, 0)
                prob_grad = dot(values, outer[head], 1, 1)
                score_grad = (probs * (prob_grad - inner[head])).astype(bf16)
                key_grad[key_span, columns] += dot(score_grad, queries[head], 1, 0)
                out.append(carry[head] + dot(score_grad, keys, 0, 0))
            return tuple(out)

        carry = tuple(jnp.zeros((block, HEAD_DIM), f32) for head in range(heads))
        if index:
            carry = lax.fori_loop(0, index, lambda key_block, c: against(key_block, c, False), carry)
        carry = against(index, carry, True)
        for head in range(heads):
            query_grad = (carry[head] * scale).astype(bf16)
            qkv_in[span, head_columns(0, head, width)] = query_grad
            columns = pl.ds(head * HEAD_DIM, HEAD_DIM)
            bias_out[0:1, columns] += jnp.sum(query_grad.astype(f32), axis=0, keepdims=True)

    blocks = rows // block
    for index in range(blocks):
        attend(index)
        if index == blocks // 2:
            scatter.middle()
        if 0 < index < blocks - 1:
            line.tick(ticks.pop(0))
    kept = min(256, rows)

    def write(start):
        span = pl.ds(start, kept)
        qkv_in[span, pl.ds(width, width)] = (key_grad[span, :] * scale).astype(bf16)
        rounded = value_grad[span, :].astype(bf16)
        qkv_in[span, pl.ds(2 * width, width)] = rounded
        bias_out[1:2, :] += jnp.sum(rounded.astype(f32), axis=0, keepdims=True)

    loop(rows, kept, write)
    for number in ticks:
        line.tick(number)
    for copy in down_loads:
        copy.wait()
    add_parts(place, down_parts, key_grad, width)
    down_stores = [
        moves.start(piece, down_out.at[:, pl.ds(index * width, width)])
        for index, piece in enumerate(column_pieces(key_grad, hidden, cut, width))
    ]
    for index in range(min(2, groups)):
        load_slice(first_all, order[index], ("qkv", index))
    load_middle.wait()

    def close(start, count, value):
        span = pl.ds(start, count)
        result[span, :] = (mid[span, :] + value + down_bias[...]).astype(bf16)

    for half in range(plan.halves):
        scatter.end(close, half)
    stores = [moves.start(result, block_out)]
    load_grad = moves.start(middle_grad, mid)
    totals = [
        Total(place, *total_refs[index : index + 4], total_refs[index + 4 : index + 8]) for index in (0, 8, 16, 24)
    ]
    vectors2, spread2, vectors, spread = totals
    vectors2.value[...] = sums2[...]
    spread_rows(place, spread2.value, [bias_out[0:1, :], bias_out[1:2, :], in_sums[...]])
    vectors.value[...] = jnp.zeros_like(vectors.value)
    masks = [1] + plan.bits
    for mask in masks:
        pl.semaphore_signal(free, inc=1, device_id=place.at(mask), device_id_type=MESH)
    scatter.finish()
    scatter = Scatter(place, own, depth, *feed_refs[:5], first_sems)
    for copy in weight_loads:
        copy.wait()

    def first_partial(owner, target):
        lines = qkv_in[pl.ds(pl.multiple_of(owner * own, own), own), :]
        for turn in range(turns):
            target[:, pl.ds(turn * hidden, hidden)] = dot(
                lines, w_d[:, pl.ds(turn * 3 * width, 3 * width)], 1, 1
            ).astype(target.dtype)

    def qkv_slice(index):
        slice_loads["qkv", index].wait()
        qkv_line.part(order[index])[...] = dot(branch[index % 2], qkv_in[...], 0, 0).astype(bf16)
        qkv_line.start(order[index], False)
        if index + 2 < groups:
            load_slice(first_all, order[index + 2], ("qkv", index + 2))

    for index in range(groups):
        qkv_slice(index)
    qkv_line.start_near()
    pl.semaphore_wait(free, len(masks))
    out_ticks = list(out_line.ticks())

    def between(number):
        if number < 2:
            out_line.tick(out_ticks.pop(0))

    scatter.begin(first_partial, between)
    for number in out_ticks:
        out_line.tick(number)
    scatter.middle()
    pieces = line.add(value_grad, width)
    in_stores = [
        moves.start(piece, in_out.at[:, pl.ds(index * width, width)]) for index, piece in enumerate(pieces)
    ]
    ticks = list(qkv_line.ticks())
    qkv_line.tick(ticks.pop(0))
    qkv_line.tick(ticks.pop(0))
    load_grad.wait()
    stores.pop(0).wait()
    load_tok = moves.start(tok, result)
    load_tok.wait()

    def close_first(start, count, value):
        span = pl.ds(start, count)
        unit, inverse = norm_rows(result[span, :].astype(f32))
        sum_rows = mid[span, :] + norm_back(value, unit, inverse, gain[...])
        result[span, :] = sum_rows.astype(bf16)
        vectors.value[0:1, :] += jnp.sum(value * unit, axis=0, keepdims=True)
        vectors.value[1:2, :] += jnp.sum(value, axis=0, keepdims=True)

    for half in range(plan.halves):
        scatter.end(close_first, half)
    stores.append(moves.start(result, input_out))
    for number in ticks:
        qkv_line.tick(number)
    vectors.plane([vectors2, spread2])
    spread.value[...] = spread2.value[:, 0 : 2 * width]
    for total in (vectors, spread):
        total.begin()
    for copy in in_stores + down_stores:
        copy.wait()
    pieces = out_line.add(key_grad, width)
    stores += [
        moves.start(piece, out_out.at[:, pl.ds(index * width, width)]) for index, piece in enumerate(pieces)
    ]
    pieces = qkv_line.add(value_grad, width)
    stores += [moves.start(piece, qkv_out.at[index]) for index, piece in enumerate(pieces)]
    scatter.finish()
    line.finish()
    out_line.finish()
    qkv_line.finish()
    vectors2_out[...] = vectors2.value[...]
    spread2_out[...] = spread2.value[...]
    vectors.end(vectors_out)
    spread.end(spread_out)
    for copy in stores:
        copy.wait()


def run_back(
    plan, groups, block, order, qkv, att, att_grad, sums, activated, w_down, middle, down_bias, in_part, branch_all,
    sums2, in_sums, down_parts, early, w_qkv, tok, middle_grad, gain, first_all,
):
    own, depth = tok.shape
    rows, width = att.shape
    hidden = w_down.shape[0]
    cut = depth // groups
    return pl.pallas_call(
        functools.partial(back_kernel, plan, block),
        out_shape=(
            jax.ShapeDtypeStruct((own, depth), bf16),
            jax.ShapeDtypeStruct((own, depth), bf16),
            jax.ShapeDtypeStruct((hidden, cut), f32),
            jax.ShapeDtypeStruct((cut, hidden), f32),
            jax.ShapeDtypeStruct((width, cut), f32),
            jax.ShapeDtypeStruct((3, cut, width), f32),
            jax.ShapeDtypeStruct(sums2.shape, f32),
            jax.ShapeDtypeStruct((plan.devices, 2 * width + hidden), f32),
            jax.ShapeDtypeStruct((2, depth), f32),
            jax.ShapeDtypeStruct((plan.devices, 2 * width), f32),
        ),
        in_specs=[SMEM] * 3
        + [ANY, ANY, ANY, VMEM, ANY, ANY, ANY, VMEM, ANY, ANY, VMEM, VMEM, ANY, ANY, ANY, ANY, ANY, ANY, ANY, VMEM, ANY],
        out_specs=(ANY,) * 6 + (VMEM,) * 4,
        scratch_shapes=[
            pltpu.VMEM((rows, 3 * width), bf16),
            pltpu.VMEM((rows, width), bf16),
            pltpu.VMEM((rows, width), bf16),
            pltpu.VMEM((rows, hidden), bf16),
            pltpu.VMEM((hidden, depth), bf16),
            pltpu.VMEM((own, depth), f32),
            pltpu.VMEM((1, rows), jnp.int32),
            pltpu.VMEM((rows, width), f32),
            pltpu.VMEM((rows, width), f32),
            pltpu.VMEM((own, depth), bf16),
            pltpu.VMEM((2, rows, cut), bf16),
            pltpu.VMEM((2, width), f32),
            pltpu.SemaphoreType.DMA((96,)),
            pltpu.SemaphoreType.REGULAR,
        ]
        + Scatter.scratch(plan, own, depth, bf16)
        + Scatter.scratch(plan, own, depth, bf16)[5:]
        + Line.scratch(groups, cut, hidden, PIECES)
        + Line.scratch(groups, width, cut, 1)
        + Line.scratch(groups, cut, 3 * width, PIECES)[1:]
        + Total.scratch(plan, 1, sums2.shape)
        + Total.scratch(plan, 1, (plan.devices, 2 * width + hidden))
        + Total.scratch(plan, groups, (2, depth))
        + Total.scratch(plan, groups, (plan.devices, 2 * width)),
        compiler_params=params(3),
        name="back",
        cost_estimate=cost(145),
    )(
        *order, qkv, att, att_grad, sums, activated, w_down, middle, down_bias, in_part, branch_all, sums2, in_sums,
        *down_parts, early, w_qkv, tok, middle_grad, gain, first_all,
    )


def close_kernel(plan, *refs):
    large, (vectors, vectors2, spread, spread2) = refs[:6], refs[6:10]
    outs, vector_outs, (qv_out, in_out), held, sems = refs[10:16], refs[16:22], refs[22:24], refs[24:30], refs[30]
    loads = [pltpu.make_async_copy(large[index], held[index], sems.at[index]) for index in range(6)]
    copies = [pltpu.make_async_copy(held[index], outs[index], sems.at[6 + index]) for index in range(6)]
    for load in loads:
        load.start()
    rows = [vectors[0:1, :], vectors[1:2, :]] + [vectors2[index : index + 1, :] for index in range(4)]
    for row, out in zip(rows, vector_outs):
        out[...] = row
    width = spread.shape[1] // 2
    hidden = spread2.shape[1] - 2 * width
    for index in range(plan.devices):
        for part in range(2):
            qv_out[part : part + 1, pl.ds(index * width, width)] = spread[
                index : index + 1, part * width : (part + 1) * width
            ]
        in_out[:, pl.ds(index * hidden, hidden)] = spread2[index : index + 1, 2 * width :]
    for load, copy in zip(loads, copies):
        load.wait()
        copy.start()
    for copy in copies:
        copy.wait()


def run_close(plan, large, small):
    depth = small[0].shape[1]
    devices, double = small[2].shape
    hidden = small[3].shape[1] - double
    return pl.pallas_call(
        functools.partial(close_kernel, plan),
        out_shape=tuple(jax.ShapeDtypeStruct(array.shape, array.dtype) for array in large)
        + (jax.ShapeDtypeStruct((1, depth), f32),) * 6
        + (
            jax.ShapeDtypeStruct((2, devices * double // 2), f32),
            jax.ShapeDtypeStruct((1, devices * hidden), f32),
        ),
        in_specs=[ANY] * 6 + [VMEM] * 4,
        out_specs=(ANY,) * 6 + (VMEM,) * 8,
        scratch_shapes=[pltpu.VMEM(array.shape, array.dtype) for array in large] + [pltpu.SemaphoreType.DMA((12,))],
        compiler_params=pltpu.CompilerParams(vmem_limit_bytes=62 * 2**20),
        name="close",
    )(*large, *small)


def body(
    tokens,
    out_grad,
    seq_lengths,
    seq_scripts,
    seq_place,
    norm1_gain,
    norm1_shift,
    w_qkv,
    qv_bias,
    w_out,
    out_bias,
    norm2_gain,
    norm2_shift,
    w_in,
    in_bias,
    w_down,
    down_bias,
):
    own, depth = tokens.shape
    devices = lax.axis_size("mp")
    plan = Plan(devices)
    fine = Plan(devices, 2)
    rows = own * devices
    width = w_qkv.shape[2]
    block = min(512, rows)
    order = (seq_lengths, seq_scripts, seq_place)

    def line(vector):
        return vector.reshape(1, -1)

    (
        first_all, qkv, att, sums, grad_all, second_all, activated, hidden_grad, middle, in_part,
    ) = run_front(
        plan, fine, block, tokens, line(norm1_gain), line(norm1_shift), w_qkv, qv_bias, order, out_grad,
        w_out, line(out_bias), line(norm2_gain), line(norm2_shift), w_in, line(in_bias), w_down,
    )
    groups = lax.axis_size("batch")
    middle_grad, branch_all, att_grad, sums2, in_sums, *down_parts, in_part2, early = run_middle(
        fine, groups, hidden_grad, w_in, middle, out_grad, line(norm2_gain), w_out, activated, grad_all, second_all,
        in_part,
    )
    (
        block_out, input_grad, down_weight_grad, in_weight_grad, out_weight_grad, qkv_weight_grad,
        vectors2, spread2, vectors, spread,
    ) = run_back(
        plan, groups, block, order, qkv, att, att_grad, sums, activated, w_down, middle, line(down_bias),
        in_part2, branch_all, sums2, in_sums, down_parts, early, w_qkv, tokens, middle_grad, line(norm1_gain), first_all,
    )
    *large, gain1, shift1, gain2, shift2, out_b, down_b, qv_bias_grad, in_b = run_close(
        plan,
        (block_out, input_grad, qkv_weight_grad, out_weight_grad, in_weight_grad, down_weight_grad),
        (vectors, vectors2, spread, spread2),
    )
    return (
        large[0],
        large[1],
        gain1.reshape(-1),
        shift1.reshape(-1),
        large[2],
        qv_bias_grad,
        large[3],
        out_b.reshape(-1),
        gain2.reshape(-1),
        shift2.reshape(-1),
        large[4],
        in_b.reshape(-1),
        large[5],
        down_b.reshape(-1),
    )


def solution(mesh):
    return jax.shard_map(
        body,
        mesh=mesh,
        in_specs=(
            P(("batch", "mp"), None),
            P(("batch", "mp"), None),
            P(),
            P(),
            P(),
            P(),
            P(),
            P(None, None, "mp"),
            P(None, "mp"),
            P("mp", None),
            P(),
            P(),
            P(),
            P(None, "mp"),
            P("mp"),
            P("mp", None),
            P(),
        ),
        out_specs=(
            P(("batch", "mp"), None),
            P(("batch", "mp"), None),
            P(),
            P(),
            P(None, "batch", "mp"),
            P(),
            P("mp", "batch"),
            P(),
            P(),
            P(),
            P("batch", "mp"),
            P(),
            P("mp", "batch"),
            P(),
        ),
        check_vma=False,
    )
```
